32 devices in a mesh: rows: 8 (over z, x), cols: 4 (over y, core).
Axes of the slice: x: 2, y: 2, z: 4, core: 2. Of those that a mesh axis runs over, the one named last changes fastest.
Arguments:
- block_list: int32 [64, 24], P('rows', 'cols'), may hold values from -1 to 63, as said below
- points: bfloat16 [16, 16384], P(None, 'rows'), may hold values from -4 to 4
- targets: float32 [32, 16384], P(None, 'rows'), may hold values from -6 to 6
Outputs:
- solution: float32 [32, 16384], P(None, 'rows')
- residual: float32 [32, 16384], P(None, 'rows')
The draws below stay inside these ranges and needn't reach their ends.
Inputs may be any that keep to these rules, and one draw needn't show every extreme that they name: `block_list`: A non-empty entry j of block row i satisfies j <= i. Within the 6 slots of a block row held by one index of cols, the entries lie in different groups of 8 consecutive blocks. Of all slots held by one device (8 block rows of 6 slots), at most 6 name blocks of any one group of 8 consecutive blocks, and in every draw some device reaches 6.
All inputs are finite; a program needn't handle non-finite values.
Results may differ from the reference program's by a relative error of at most 0.0057.
Values may be sent and summed in bfloat16 or wider, within the bound.
No kernel may reach another device: no remote copies, remote signals or barrier semaphores. Data moves between devices by JAX's collectives and lax.ppermute only.
A program may use at most 64 MiB of HBM per device.

```python
import math
import jax
import jax.numpy as jnp
from jax import lax

DIM = 16
OUTS = 32
BLOCK = 256
SLOTS = 24
BR_DEV = 8
ITERS = 2
NB = 64
NPTS = 16384
N_ROWS = 8
N_COLS = 4


def draw_points(key, part):
    spread = 0.7 ** jnp.arange(DIM, dtype=jnp.float32)
    width = 0.31
    cycle = 0.57 * width / math.sin(math.pi / BR_DEV)
    block_id = jnp.arange(NPTS, dtype=jnp.int32) // BLOCK
    family = (block_id % BR_DEV).astype(jnp.float32)
    turn = family * (2.0 * math.pi / BR_DEV)
    dims = jnp.arange(DIM, dtype=jnp.int32)[:, None]
    center = jnp.where(dims == 0, cycle * jnp.cos(turn)[None, :], jnp.where(dims == 1, cycle * jnp.sin(turn)[None, :], 0.0))
    keys_two = jax.random.split(key, 2)
    drift = jnp.clip(jax.random.normal(keys_two[0], (DIM, NB), jnp.float32), -3.0, 3.0) * 0.15
    drift_all = drift[:, block_id]
    noise = jnp.clip(jax.random.normal(keys_two[1], (DIM, NPTS), jnp.float32), -4.0, 4.0)
    return (center + width * spread[:, None] * (noise + drift_all)).astype(jnp.bfloat16)


def draw_targets(key, part):
    position = jnp.arange(NPTS, dtype=jnp.float32) / NPTS
    noise = jnp.clip(jax.random.normal(key, (OUTS, NPTS), jnp.float32), -3.5, 3.5)
    return noise * (0.5 * 3.0 ** position)[None, :]


def draw_block_list(key, part):
    slot_width = SLOTS // N_COLS
    slot_count = BR_DEV * slot_width
    group_keys = jax.random.split(key, N_ROWS * N_COLS)

    def one_share(share_key, group):
        row_dev = group // N_COLS
        keys_six = jax.random.split(share_key, 6)
        owner_order = jax.random.permutation(keys_six[0], N_ROWS).astype(jnp.int32)
        offset = jax.random.randint(keys_six[1], (), 0, N_ROWS, dtype=jnp.int32)
        serial = jnp.arange(slot_count, dtype=jnp.int32)
        steps_back = owner_order[(serial + offset) % N_ROWS]
        owners = row_dev - steps_back
        row_line = serial // slot_width
        shift_by = jax.random.randint(keys_six[2], (slot_count,), -1, 2, dtype=jnp.int32)
        any_family = jax.random.randint(keys_six[4], (slot_count,), 0, BR_DEV, dtype=jnp.int32)
        rare = jax.random.randint(keys_six[5], (slot_count,), 0, 8, dtype=jnp.int32)
        distant = jnp.where(rare == 0, any_family, (row_line + shift_by + BR_DEV) % BR_DEV)
        nearby = jnp.maximum(row_line - jax.random.randint(keys_six[3], (slot_count,), 0, 2, dtype=jnp.int32), 0)
        chosen = jnp.where(steps_back == 0, row_dev * BR_DEV + nearby, owners * BR_DEV + distant)
        return jnp.where(owners >= 0, chosen, -1).reshape(BR_DEV, slot_width)
    shares = jax.vmap(one_share)(group_keys, jnp.arange(N_ROWS * N_COLS, dtype=jnp.int32))
    shares = shares.reshape(N_ROWS, N_COLS, BR_DEV, slot_width).transpose(0, 2, 1, 3)
    return shares.reshape(N_ROWS * BR_DEV, SLOTS).astype(jnp.int32)


def setup_inputs(seed: int = 0) -> dict:
    splits = jax.random.split(jax.random.key(seed), 4)
    return {
        "block_list": draw_block_list(jax.random.fold_in(splits[3], 71), 0),
        "points": draw_points(jax.random.fold_in(splits[3], 71), 0),
        "targets": draw_targets(jax.random.fold_in(splits[3], 71), 0),
    }


REG = 1.5
RADIUS = 0.25

def wendland(left_x, right_x):
    left_f = left_x.astype(jnp.float32)
    right_f = right_x.astype(jnp.float32)
    left_sq = lax.optimization_barrier(jnp.sum(left_f * left_f, axis=1))
    right_sq = lax.optimization_barrier(jnp.sum(right_f * right_f, axis=1))
    inner_prod = jnp.einsum('nda,ndb->nab', left_f, right_f, precision=lax.Precision.HIGHEST)
    dist_sq = left_sq[:, :, None] + right_sq[:, None, :] - 2.0 * inner_prod
    scaled = jnp.sqrt(jnp.maximum(dist_sq, 0.0)) / RADIUS
    remain = jnp.maximum(1.0 - scaled, 0.0)
    square = remain * remain
    return square * square * (4.0 * scaled + 1.0)

def accumulate(coords, block_list, weights):
    count = coords.shape[0]
    slots_all = block_list.shape[1]
    channels = 1 if weights is None else weights.shape[1]

    def row_step(total, row):
        entries = block_list[row]
        is_live = entries >= 0
        clipped = jnp.maximum(entries, 0)
        off_diag = is_live & (entries != row)
        near_x = jnp.broadcast_to(coords[row][None], (slots_all,) + coords.shape[1:])
        values = jnp.where(is_live[:, None, None], wendland(near_x, coords[clipped]), 0.0)
        if weights is None:
            direct = lax.optimization_barrier(jnp.sum(values, axis=(0, 2)))[None, :]
            mirror = jnp.where(off_diag[:, None], lax.optimization_barrier(jnp.sum(values, axis=1)), 0.0)[:, None, :]
        else:
            kernel_f = lax.optimization_barrier(values.astype(jnp.bfloat16)).astype(jnp.float32)
            direct = jnp.einsum('sab,sob->oa', kernel_f, weights[clipped])
            mirror = jnp.einsum('sab,oa->sob', kernel_f, weights[row])
            mirror = jnp.where(off_diag[:, None, None], mirror, 0.0)
        total = total.at[row].add(direct)
        total = total.at[clipped].add(mirror)
        return (total, None)
    start = jnp.zeros((count, channels, coords.shape[2]), jnp.float32)
    return lax.scan(row_step, start, jnp.arange(count, dtype=jnp.int32))[0]

def reference(block_list, points, targets):
    coord_dim, npoints = points.shape
    count = npoints // BLOCK
    outputs = targets.shape[0]
    coords = points.reshape(coord_dim, count, BLOCK).transpose(1, 0, 2)
    degree = 1.0 + accumulate(coords, block_list, None)
    inv_root = 1.0 / jnp.sqrt(degree)

    def apply_matrix(direction):
        weights = lax.optimization_barrier((direction * inv_root).astype(jnp.bfloat16)).astype(jnp.float32)
        return REG * direction + inv_root * accumulate(coords, block_list, weights)
    resid = targets.reshape(outputs, count, BLOCK).transpose(1, 0, 2)
    direction = resid
    solution = jnp.zeros_like(resid)
    norm_now = lax.optimization_barrier(jnp.sum(resid * resid, axis=(0, 2)))
    for iteration in range(ITERS):
        applied = apply_matrix(direction)
        step_size = norm_now / lax.optimization_barrier(jnp.sum(direction * applied, axis=(0, 2)))
        solution = solution + step_size[None, :, None] * direction
        resid = resid - step_size[None, :, None] * applied
        norm_next = lax.optimization_barrier(jnp.sum(resid * resid, axis=(0, 2)))
        direction = resid + (norm_next / norm_now)[None, :, None] * direction
        norm_now = norm_next
    return (solution.transpose(1, 0, 2).reshape(outputs, npoints), resid.transpose(1, 0, 2).reshape(outputs, npoints))
```

```python
import functools

import jax
import jax.numpy as jnp
from jax import lax
from jax.experimental import pallas as pl
from jax.experimental.pallas import tpu as pltpu
from jax.sharding import PartitionSpec as P

REG = 1.5
RADIUS = 0.25
GROUP = 4
RING = 3
STRIP = 64
TINY = 1e-30
SHIFT = 0.375


def augment(x, first_ones):
    dim, n = x.shape
    norm = jnp.sum(x * x, axis=0, keepdims=True) / (RADIUS * RADIUS)
    high = norm.astype(jnp.bfloat16).astype(jnp.float32)
    rest = norm - high
    mid = rest.astype(jnp.bfloat16).astype(jnp.float32)
    low = rest - mid
    line = lax.broadcasted_iota(jnp.int32, (dim, n), 0)
    base = 3 if first_ones else 0
    ones_at = 0 if first_ones else 3
    tail = jnp.where((line >= ones_at) & (line < ones_at + 3), 1.0, 0.0)
    tail = jnp.where(line == base, high, tail)
    tail = jnp.where(line == base + 1, mid, tail)
    tail = jnp.where(line == base + 2, low, tail)
    return tail


def build_kernel(
    nb, block_len, own_rows, counts, own, x_ref, t_ref,
    k_hbm, jlist, groups, w_ref, inv_ref,
    mlist, kbuf, acc, lhs, sems,
):
    me = own[0]

    def copy_out(g):
        slot = lax.rem(g, RING)
        return pltpu.make_async_copy(kbuf.at[slot], k_hbm.at[g], sems.at[slot])

    ends = []
    pos = jnp.int32(0)
    for k in range(own_rows):

        def note(j, at, k=k):
            m = counts[k * nb + j]
            jlist[at] = j
            mlist[at] = m
            return at + jnp.where(m > 0, 1, 0)

        pos = lax.fori_loop(0, nb, note, pos, unroll=8)
        for u in range(GROUP):
            jlist[pos + u] = 0
            mlist[pos + u] = 0
        last = lax.div(pos + (GROUP - 1), GROUP)
        groups[k] = last
        ends.append(last)
        pos = last * GROUP

    scale = 1.0 / (RADIUS * RADIUS)
    for k in range(own_rows):
        begin = jnp.int32(0) if k == 0 else ends[k - 1]
        near = x_ref[me, :, k * block_len:(k + 1) * block_len].astype(jnp.float32)
        full = jnp.concatenate([near * (-2.0 * scale), augment(near, True)], axis=0)
        lhs[...] = full.T.astype(jnp.bfloat16)
        acc[...] = jnp.zeros_like(acc)

        def step(g, carry):
            slot = lax.rem(g, RING)

            @pl.when(g >= RING)
            def _():
                copy_out(g - RING).wait()

            for u in range(GROUP):
                j = jlist[g * GROUP + u]
                m = mlist[g * GROUP + u].astype(jnp.float32)
                dev = lax.div(j, own_rows)
                at = pl.multiple_of(lax.rem(j, own_rows) * block_len, block_len)
                far = x_ref[dev, :, pl.ds(at, block_len)]
                rhs = jnp.concatenate(
                    [far, augment(far.astype(jnp.float32), False).astype(jnp.bfloat16)], axis=0
                )
                for s in range(block_len // STRIP):
                    rows = slice(s * STRIP, (s + 1) * STRIP)
                    d = jnp.dot(lhs[rows, :], rhs, preferred_element_type=jnp.float32)
                    d = jnp.maximum(d, TINY)
                    sc = d * lax.rsqrt(d)
                    rem = jnp.maximum(1.0 - sc, 0.0)
                    sq = rem * rem
                    val = (sq * sq) * (sc * (4.0 * m) + m)
                    kbuf[slot, u, rows, :] = val.astype(jnp.bfloat16)
                    half = val[:, :128]
                    for h in range(1, block_len // 128):
                        half = half + val[:, h * 128:(h + 1) * 128]
                    acc[rows, :] += half
            copy_out(g).start()
            return carry

        lax.fori_loop(begin, ends[k], step, 0)
        degree = 1.0 + jnp.sum(acc[...].T, axis=0, keepdims=True)
        inv = 1.0 / jnp.sqrt(degree)
        cols = slice(k * block_len, (k + 1) * block_len)
        inv_ref[:, cols] = inv
        w_ref[:, cols] = (t_ref[:, cols] * inv).astype(jnp.bfloat16)

    def drain(g, carry):
        copy_out(g).wait()
        return carry

    lax.fori_loop(jnp.maximum(ends[-1] - RING, 0), ends[-1], drain, 0)


def apply_kernel(
    block_len, own_rows, first, jlist, groups, k_hbm, w_ref, inv_ref, prior_ref, *rest
):
    s_ref, kbuf, sems = rest[0], rest[-2], rest[-1]
    total = groups[own_rows - 1]

    def copy_in(g):
        slot = lax.rem(g, RING)
        return pltpu.make_async_copy(k_hbm.at[g], kbuf.at[slot], sems.at[slot])

    for p in range(RING - 1):

        @pl.when(p < total)
        def _(p=p):
            copy_in(p).start()

    for k in range(own_rows):
        begin = jnp.int32(0) if k == 0 else groups[k - 1]

        def step(g, acc):
            @pl.when(g + (RING - 1) < total)
            def _():
                copy_in(g + (RING - 1)).start()

            copy_in(g).wait()
            slot = lax.rem(g, RING)
            for u in range(GROUP):
                j = jlist[g * GROUP + u]
                dev = lax.div(j, own_rows)
                at = pl.multiple_of(lax.rem(j, own_rows) * block_len, block_len)
                acc = acc + lax.dot_general(
                    w_ref[dev, :, pl.ds(at, block_len)],
                    kbuf[slot, u],
                    (((1,), (1,)), ((), ())),
                    preferred_element_type=jnp.float32,
                )
            return acc

        acc = lax.fori_loop(begin, groups[k], step, jnp.zeros((s_ref.shape[0], block_len), jnp.float32))
        cols = slice(k * block_len, (k + 1) * block_len)
        inv = inv_ref[:, cols]
        s = acc * inv
        shift = SHIFT * prior_ref[:, cols]
        if first:
            s_ref[:, cols] = s
            rest[1][:, cols] = ((s - shift) * inv).astype(jnp.bfloat16)
        else:
            s_ref[:, cols] = s + shift


SMEM = pl.BlockSpec(memory_space=pltpu.SMEM)
VMEM = pl.BlockSpec(memory_space=pltpu.VMEM)
ANY = pl.BlockSpec(memory_space=pl.ANY)


def local(block_list, points, targets):
    n_rows = lax.axis_size("rows")
    n_cols = lax.axis_size("cols")
    row = lax.axis_index("rows")
    col = lax.axis_index("cols")
    block_rows, slots = block_list.shape
    dim, npoints = points.shape
    outputs = targets.shape[0]
    block_len = npoints // block_rows
    own_rows = block_rows // n_cols
    own_len = own_rows * block_len
    nb = block_rows * n_rows
    devices = n_rows * n_cols
    both = ("rows", "cols")
    capacity = -(-block_rows * slots // n_rows)
    bound = min(own_rows * nb, own_rows * slots * n_cols + devices * capacity)
    n_groups = -(-bound // GROUP) + own_rows
    me = row * n_cols + col

    own_points = lax.dynamic_slice_in_dim(points, col * own_len, own_len, 1)
    own_t = lax.dynamic_slice_in_dim(targets, col * own_len, own_len, 1)
    listed = jnp.pad(block_list + 1, ((0, 0), (0, 128 - slots)))
    coded = jnp.concatenate([listed // 32, listed % 32], axis=0).astype(jnp.bfloat16)
    packed = jnp.concatenate([own_points, coded], axis=1)
    gathered = lax.all_gather(packed, both, axis=0)
    codes = gathered[:, :, own_len:own_len + slots].astype(jnp.int32)
    entries = codes[:, :block_rows] * 32 + codes[:, block_rows:] - 1
    entries = entries.reshape(n_rows, n_cols, block_rows, slots)

    mine = me * own_rows + jnp.arange(own_rows, dtype=jnp.int32)
    names = jnp.arange(nb, dtype=jnp.int32)
    mirror = jnp.sum(
        (entries[None] == mine[:, None, None, None, None]).astype(jnp.int32), axis=(2, 4)
    ).reshape(own_rows, nb)
    own_entries = lax.dynamic_slice(
        entries, (row, 0, col * own_rows, 0), (1, n_cols, own_rows, slots)
    )[0].transpose(1, 0, 2).reshape(own_rows, n_cols * slots)
    direct = jnp.sum((own_entries[:, :, None] == names).astype(jnp.int32), axis=1)
    counts = direct + jnp.where(names[None, :] == mine[:, None], 0, mirror)

    k_mat, jlist, groups, w1, inv = pl.pallas_call(
        functools.partial(build_kernel, nb, block_len, own_rows),
        out_shape=(
            jax.ShapeDtypeStruct((n_groups, GROUP, block_len, block_len), jnp.bfloat16),
            jax.ShapeDtypeStruct(((n_groups + 1) * GROUP,), jnp.int32),
            jax.ShapeDtypeStruct((own_rows,), jnp.int32),
            jax.ShapeDtypeStruct((outputs, own_len), jnp.bfloat16),
            jax.ShapeDtypeStruct((1, own_len), jnp.float32),
        ),
        in_specs=[SMEM, SMEM, VMEM, VMEM],
        out_specs=(ANY, SMEM, SMEM, VMEM, VMEM),
        scratch_shapes=[
            pltpu.SMEM(((n_groups + 1) * GROUP,), jnp.int32),
            pltpu.VMEM((RING, GROUP, block_len, block_len), jnp.bfloat16),
            pltpu.VMEM((block_len, 128), jnp.float32),
            pltpu.VMEM((block_len, 2 * dim), jnp.bfloat16),
            pltpu.SemaphoreType.DMA((RING,)),
        ],
        compiler_params=pltpu.CompilerParams(vmem_limit_bytes=32 * 1024 * 1024),
        name="build",
    )(counts.reshape(own_rows * nb), me.reshape(1), gathered, own_t)

    def apply(first, w_all, prior):
        shapes = [
            jax.ShapeDtypeStruct((outputs, own_len), jnp.float32),
            jax.ShapeDtypeStruct((outputs, own_len), jnp.bfloat16),
        ]
        return pl.pallas_call(
            functools.partial(apply_kernel, block_len, own_rows, first),
            out_shape=shapes if first else shapes[:1],
            in_specs=[SMEM, SMEM, ANY, VMEM, VMEM, VMEM],
            out_specs=[VMEM, VMEM] if first else [VMEM],
            scratch_shapes=[
                pltpu.VMEM((RING, GROUP, block_len, block_len), jnp.bfloat16),
                pltpu.SemaphoreType.DMA((RING,)),
            ],
            compiler_params=pltpu.CompilerParams(vmem_limit_bytes=32 * 1024 * 1024),
            name="apply",
        )(jlist, groups, k_mat, w_all, inv, prior)

    s1, q1 = apply(True, lax.all_gather(w1, both, axis=0), own_t)
    (s2,) = apply(False, lax.all_gather(q1, both, axis=0), s1)

    pairs = jnp.stack(
        [
            jnp.sum(own_t * own_t, axis=1),
            jnp.sum(own_t * s1, axis=1),
            jnp.sum(s1 * s1, axis=1),
            jnp.sum(own_t * s2, axis=1),
            jnp.sum(s1 * s2, axis=1),
        ]
    )
    tt, ts1, s1s1, ts2, s1s2 = lax.psum(pairs, both)
    spread = lax.all_gather(jnp.stack([s1, s2]), "cols", axis=2, tiled=False)
    wide = spread.reshape(2, outputs, npoints)
    s1w, s2w = wide[0], wide[1]

    a1 = tt / (REG * tt + ts1)
    p = 1.0 - REG * a1
    new = p * p * tt - 2.0 * p * a1 * ts1 + a1 * a1 * s1s1
    u = p + new / tt
    dd = u * u * tt - 2.0 * u * a1 * ts1 + a1 * a1 * s1s1
    dmd = u * u * ts1 - u * a1 * (s1s1 + ts2) + a1 * a1 * s1s2
    a2 = new / (REG * dd + dmd)
    c = lambda v: v[:, None]
    sol = c(a1 + a2 * u) * targets - c(a2 * a1) * s1w
    res = (
        c(p - a2 * REG * u) * targets
        + c(-a1 - a2 * (u - REG * a1)) * s1w
        + c(a2 * a1) * s2w
    )
    return (sol, res)


def solution(mesh):
    placed = (P("rows", "cols"), P(None, "rows"), P(None, "rows"))
    return jax.shard_map(
        local,
        mesh=mesh,
        in_specs=placed,
        out_specs=(P(None, "rows"), P(None, "rows")),
        check_vma=False,
    )
```

```python
import functools

import jax
import jax.numpy as jnp
from jax import lax
from jax.experimental import pallas as pl
from jax.experimental.pallas import tpu as pltpu
from jax.sharding import PartitionSpec as P

REG = 1.5
RADIUS = 0.25
GROUP = 4
RING = 3
STRIP = 64
LANES = 128
TINY = 1e-30
SHIFT = 0.375
DIRECT_ROWS = 8

SMEM = pl.BlockSpec(memory_space=pltpu.SMEM)
VMEM = pl.BlockSpec(memory_space=pltpu.VMEM)
HBM = pl.BlockSpec(memory_space=pltpu.HBM)
F32 = jnp.float32
BF16 = jnp.bfloat16


def augment(x, first_ones):
    dim, n = x.shape
    norm = jnp.sum(x * x, axis=0, keepdims=True) / (RADIUS * RADIUS)
    high = norm.astype(BF16).astype(F32)
    rest = norm - high
    mid = rest.astype(BF16).astype(F32)
    low = rest - mid
    line = lax.broadcasted_iota(jnp.int32, (dim, n), 0)
    base = 3 if first_ones else 0
    ones_at = 0 if first_ones else 3
    tail = jnp.where((line >= ones_at) & (line < ones_at + 3), 1.0, 0.0)
    tail = jnp.where(line == base, high, tail)
    tail = jnp.where(line == base + 1, mid, tail)
    tail = jnp.where(line == base + 2, low, tail)
    return tail


def each_piece(pieces, row, visit):
    if len(pieces) == 1:

        def one(r, carry):
            visit(r, lambda *at: pieces[0][(r,) + at])
            return carry

        lax.fori_loop(0, pieces[0].shape[0], one, 0)
    else:
        for d, ref in enumerate(pieces):
            visit(row ^ d, lambda *at, ref=ref: ref[at])


def build_kernel(cfg, place, direct, near_ref, *refs):
    n_pieces, nb, block_len, own_rows, block_rows, n_sub, count_rows = cfg
    pieces, refs = refs[:n_pieces], refs[n_pieces:]
    k_hbm, ilist, jlist, groups, deg_ref = refs[:5]
    mlist, kbuf, acc, lhs, rhs, counts_v, counts, sems, count_sem = refs[5:]
    row, col = place[0], place[1]
    own_len = own_rows * block_len
    dim = near_ref.shape[0]
    scale = 1.0 / (RADIUS * RADIUS)

    def prepare(r, load):
        for k in range(own_rows):
            far = load(slice(None), slice(k * block_len, (k + 1) * block_len))
            rhs[r * own_rows + k, :dim, :] = far
            rhs[r * own_rows + k, dim:, :] = augment(far.astype(F32), False).astype(BF16)
        listed = load(slice(None), slice(own_len, own_len + LANES))
        counts_v[r] = listed.astype(F32)[:count_rows].astype(jnp.int32)

    each_piece(pieces, row, prepare)
    fetch = pltpu.make_async_copy(counts_v, counts, count_sem)
    fetch.start()
    for i in range(block_rows):
        near = near_ref[:, i * block_len:(i + 1) * block_len].astype(F32)
        full = jnp.concatenate([near * (-2.0 * scale), augment(near, True)], axis=0)
        lhs[i] = full.T.astype(BF16)
    acc[...] = jnp.zeros_like(acc)
    fetch.wait()

    def line(i, pos):
        me = row * block_rows + i

        def note(j, at):
            r, k = lax.div(j, own_rows), lax.rem(j, own_rows)
            name = r * block_rows + col * own_rows + k
            spot = k * nb + me
            mirrored = counts[r, lax.div(spot, LANES), lax.rem(spot, LANES)]
            m = direct[i, name] + jnp.where(name == me, 0, mirrored)
            ilist[at] = i
            jlist[at] = j
            mlist[at] = m
            return at + jnp.where(m > 0, 1, 0)

        return lax.fori_loop(0, n_sub, note, pos, unroll=8)

    pos = lax.fori_loop(0, block_rows, line, jnp.int32(0))
    for u in range(GROUP):
        ilist[pos + u] = 0
        jlist[pos + u] = 0
        mlist[pos + u] = 0
    total = lax.div(pos + (GROUP - 1), GROUP)
    groups[0] = total

    def copy_out(g):
        slot = lax.rem(g, RING)
        return pltpu.make_async_copy(kbuf.at[slot], k_hbm.at[g], sems.at[slot])

    def step(g, carry):
        slot = lax.rem(g, RING)

        @pl.when(g >= RING)
        def _():
            copy_out(g - RING).wait()

        for u in range(GROUP):
            i = ilist[g * GROUP + u]
            j = jlist[g * GROUP + u]
            m = mlist[g * GROUP + u].astype(F32)
            far = rhs[j]
            for s in range(block_len // STRIP):
                rows = slice(s * STRIP, (s + 1) * STRIP)
                d = jnp.dot(lhs[i, rows, :], far, preferred_element_type=F32)
                d = jnp.maximum(d, TINY)
                sc = d * lax.rsqrt(d)
                rem = jnp.maximum(1.0 - sc, 0.0)
                sq = rem * rem
                val = (sq * sq) * (sc * (4.0 * m) + m)
                kbuf[slot, u, rows, :] = val.astype(BF16)
                half = val[:, :LANES]
                for h in range(1, block_len // LANES):
                    half = half + val[:, h * LANES:(h + 1) * LANES]
                acc[i, rows, :] += half
        copy_out(g).start()
        return carry

    lax.fori_loop(0, total, step, 0)
    for i in range(block_rows):
        deg_ref[:, i * block_len:(i + 1) * block_len] = jnp.sum(acc[i].T, axis=0, keepdims=True)

    def drain(g, carry):
        copy_out(g).wait()
        return carry

    lax.fori_loop(jnp.maximum(total - RING, 0), total, drain, 0)


def scale_kernel(n_cols, place, t_ref, *refs):
    degs, (inv_ref, w_ref) = refs[:n_cols], refs[n_cols:]
    total = degs[0][...]
    for ref in degs[1:]:
        total = total + ref[...]
    inv_ref[...] = 1.0 / jnp.sqrt(1.0 + total)
    own_len = w_ref.shape[1]
    at = pl.ds(pl.multiple_of(place[1] * own_len, LANES), own_len)
    w_ref[...] = (t_ref[:, at] * inv_ref[:, at]).astype(BF16)


def apply_kernel(cfg, place, ilist, jlist, groups, k_hbm, *refs):
    n_pieces, n_cols, own_rows, block_len, products = cfg
    pieces, refs = refs[:n_pieces], refs[n_pieces:]
    if products:
        inv_ref, t_ref, refs = refs[0], refs[1], refs[2:]
        s_refs, refs = refs[:n_cols], refs[n_cols:]
    z_refs, refs = refs[:n_cols], refs[n_cols:]
    if products:
        dot_ref, refs = refs[0], refs[1:]
    w_all, z_acc, kbuf, sems = refs
    row, col = place[0], place[1]
    total = groups[0]

    def copy_in(g):
        slot = lax.rem(g, RING)
        return pltpu.make_async_copy(k_hbm.at[g], kbuf.at[slot], sems.at[slot])

    for p in range(RING - 1):

        @pl.when(p < total)
        def _(p=p):
            copy_in(p).start()

    def place_piece(r, load):
        for k in range(own_rows):
            w_all[r * own_rows + k] = load(slice(None), slice(k * block_len, (k + 1) * block_len))

    each_piece(pieces, row, place_piece)
    z_acc[...] = jnp.zeros_like(z_acc)

    def step(g, carry):
        @pl.when(g + (RING - 1) < total)
        def _():
            copy_in(g + (RING - 1)).start()

        copy_in(g).wait()
        slot = lax.rem(g, RING)
        parts = []
        for u in range(GROUP):
            parts.append(
                lax.dot_general(
                    w_all[jlist[g * GROUP + u]],
                    kbuf[slot, u],
                    (((1,), (1,)), ((), ())),
                    preferred_element_type=F32,
                )
            )
        for u in range(GROUP):
            z_acc[ilist[g * GROUP + u]] += parts[u]
        return carry

    lax.fori_loop(0, total, step, 0)
    own_len = own_rows * block_len
    for e in range(n_cols):
        for k in range(own_rows):
            z_refs[e][:, k * block_len:(k + 1) * block_len] = z_acc[(col ^ e) * own_rows + k]
    if products:
        ts2 = jnp.zeros((t_ref.shape[0], 1), F32)
        s1s2 = jnp.zeros((t_ref.shape[0], 1), F32)
        for e in range(n_cols):
            at = pl.ds(pl.multiple_of((col ^ e) * own_len, LANES), own_len)
            scaled = z_refs[e][...] * inv_ref[:, at]
            ts2 += jnp.sum(t_ref[:, at] * scaled, axis=1, keepdims=True)
            s1s2 += jnp.sum(s_refs[e][...] * scaled, axis=1, keepdims=True)
        t = t_ref[:, pl.ds(pl.multiple_of(col * own_len, LANES), own_len)]
        s1 = s_refs[0][...]
        tt = jnp.sum(t * t, axis=1, keepdims=True)
        ts1 = jnp.sum(t * s1, axis=1, keepdims=True)
        s1s1 = jnp.sum(s1 * s1, axis=1, keepdims=True)
        ts2 += SHIFT * ts1
        s1s2 += SHIFT * s1s1
        lane = lax.broadcasted_iota(jnp.int32, dot_ref.shape, 1)
        out = jnp.zeros(dot_ref.shape, F32)
        for n, v in enumerate((tt, ts1, s1s1, ts2, s1s2)):
            out = jnp.where(lane == n, v, out)
        dot_ref[...] = out


def first_kernel(n_cols, place, inv_ref, t_ref, *refs):
    zs, (s_ref, g_ref) = refs[:n_cols], refs[n_cols:]
    z = zs[0][...]
    for ref in zs[1:]:
        z = z + ref[...]
    own_len = z.shape[1]
    at = pl.ds(pl.multiple_of(place[1] * own_len, LANES), own_len)
    inv = inv_ref[:, at]
    s = z * inv
    s_ref[...] = s
    g_ref[...] = ((s - SHIFT * t_ref[:, at]) * inv).astype(BF16)


def second_kernel(n_cols, place, inv_ref, s1_ref, *refs):
    zs, dots, out_ref = refs[:n_cols], refs[n_cols:-1], refs[-1]
    z = zs[0][...]
    for ref in zs[1:]:
        z = z + ref[...]
    own_len = z.shape[1]
    at = pl.ds(pl.multiple_of(place[1] * own_len, LANES), own_len)
    out_ref[:, :own_len] = z * inv_ref[:, at] + SHIFT * s1_ref[...]
    total = dots[0][...]
    for ref in dots[1:]:
        total = total + ref[...]
    out_ref[:, own_len:] = total


def final_kernel(n_cols, place, t_ref, *refs):
    s1s, ends = refs[:n_cols], refs[n_cols:2 * n_cols]
    sol_ref, res_ref = refs[2 * n_cols:]
    own_len = s1s[0].shape[1]
    dots = ends[0][:, own_len:]
    for ref in ends[1:]:
        dots = dots + ref[:, own_len:]
    tt, ts1, s1s1, ts2, s1s2 = (dots[:, n:n + 1] for n in range(5))
    a1 = tt / (REG * tt + ts1)
    p = 1.0 - REG * a1
    new = p * p * tt - 2.0 * p * a1 * ts1 + a1 * a1 * s1s1
    u = p + new / tt
    dd = u * u * tt - 2.0 * u * a1 * ts1 + a1 * a1 * s1s1
    dmd = u * u * ts1 - u * a1 * (s1s1 + ts2) + a1 * a1 * s1s2
    a2 = new / (REG * dd + dmd)
    for e in range(n_cols):
        at = pl.ds(pl.multiple_of((place[1] ^ e) * own_len, LANES), own_len)
        t, s1, s2 = t_ref[:, at], s1s[e][...], ends[e][:, :own_len]
        sol_ref[:, at] = (a1 + a2 * u) * t - (a2 * a1) * s1
        res_ref[:, at] = (p - a2 * REG * u) * t - (a1 + a2 * (u - REG * a1)) * s1 + (a2 * a1) * s2


def swap(x, axis, d):
    size = lax.axis_size(axis)
    return lax.ppermute(x, axis, [(i, i ^ d) for i in range(size)])


def from_cols(x):
    return [x] + [swap(x, "cols", e) for e in range(1, lax.axis_size("cols"))]


def from_rows(x):
    size = lax.axis_size("rows")
    if size > DIRECT_ROWS:
        return [lax.all_gather(x, "rows")]
    return [x] + [swap(x, "rows", d) for d in range(1, size)]


def local(block_list, points, targets):
    n_rows = lax.axis_size("rows")
    n_cols = lax.axis_size("cols")
    row = lax.axis_index("rows")
    col = lax.axis_index("cols")
    block_rows, slots = block_list.shape
    dim, npoints = points.shape
    outputs = targets.shape[0]
    block_len = npoints // block_rows
    own_rows = block_rows // n_cols
    own_len = own_rows * block_len
    nb = block_rows * n_rows
    n_sub = own_rows * n_rows
    capacity = -(-block_rows * slots // n_rows)
    bound = min(block_rows * n_sub, n_cols * capacity * (n_rows + 1))
    n_groups = -(-bound // GROUP)
    list_len = n_groups * GROUP + GROUP
    place = jnp.stack([row, col])
    limit = pltpu.CompilerParams(vmem_limit_bytes=48 * 1024 * 1024)

    def shape(*dims, dtype=F32):
        return jax.ShapeDtypeStruct(dims, dtype)

    lists = jnp.concatenate(from_cols(block_list), axis=1)
    names = jnp.arange(nb, dtype=jnp.int32)
    direct = jnp.sum((lists[:, :, None] == names).astype(jnp.int32), axis=1)
    own_counts = lax.dynamic_slice_in_dim(direct, col * own_rows, own_rows, 0)
    count_rows = -(-own_rows * nb // LANES)
    coded = own_counts.reshape(-1)
    coded = jnp.pad(coded, (0, dim * LANES - coded.shape[0])).reshape(dim, LANES).astype(BF16)
    own_points = lax.dynamic_slice_in_dim(points, col * own_len, own_len, 1)
    pieces = from_rows(jnp.concatenate([own_points, coded], axis=1))

    k_mat, ilist, jlist, groups, degree = pl.pallas_call(
        functools.partial(
            build_kernel, (len(pieces), nb, block_len, own_rows, block_rows, n_sub, count_rows)
        ),
        out_shape=(
            shape(n_groups, GROUP, block_len, block_len, dtype=BF16),
            shape(list_len, dtype=jnp.int32),
            shape(list_len, dtype=jnp.int32),
            shape(1, dtype=jnp.int32),
            shape(1, npoints),
        ),
        in_specs=[SMEM, SMEM, VMEM] + [VMEM] * len(pieces),
        out_specs=(HBM, SMEM, SMEM, SMEM, VMEM),
        scratch_shapes=[
            pltpu.SMEM((list_len,), jnp.int32),
            pltpu.VMEM((RING, GROUP, block_len, block_len), BF16),
            pltpu.VMEM((block_rows, block_len, LANES), F32),
            pltpu.VMEM((block_rows, block_len, 2 * dim), BF16),
            pltpu.VMEM((n_sub, 2 * dim, block_len), BF16),
            pltpu.VMEM((n_rows, count_rows, LANES), jnp.int32),
            pltpu.SMEM((n_rows, count_rows, LANES), jnp.int32),
            pltpu.SemaphoreType.DMA((RING,)),
            pltpu.SemaphoreType.DMA,
        ],
        compiler_params=limit,
        name="build",
    )(place, direct, points, *pieces)

    inv, w1 = pl.pallas_call(
        functools.partial(scale_kernel, n_cols),
        out_shape=(shape(1, npoints), shape(outputs, own_len, dtype=BF16)),
        in_specs=[SMEM] + [VMEM] * (1 + n_cols),
        out_specs=(VMEM, VMEM),
        name="scale",
    )(place, targets, *from_cols(degree))

    def apply(w, s_pieces):
        pieces = from_rows(w)
        products = s_pieces is not None
        extra = [inv, targets, *s_pieces] if products else []
        out = [shape(outputs, own_len)] * n_cols + [shape(outputs, LANES)] * products
        return pl.pallas_call(
            functools.partial(
                apply_kernel, (len(pieces), n_cols, own_rows, block_len, products)
            ),
            out_shape=out,
            in_specs=[SMEM] * 4 + [HBM] + [VMEM] * (len(pieces) + len(extra)),
            out_specs=[VMEM] * len(out),
            scratch_shapes=[
                pltpu.VMEM((n_sub, outputs, block_len), BF16),
                pltpu.VMEM((block_rows, outputs, block_len), F32),
                pltpu.VMEM((RING, GROUP, block_len, block_len), BF16),
                pltpu.SemaphoreType.DMA((RING,)),
            ],
            compiler_params=limit,
            name="apply",
        )(place, ilist, jlist, groups, k_mat, *pieces, *extra)

    def deal(z):
        return [z[0]] + [swap(z[e], "cols", e) for e in range(1, n_cols)]

    s1, g = pl.pallas_call(
        functools.partial(first_kernel, n_cols),
        out_shape=(shape(outputs, own_len), shape(outputs, own_len, dtype=BF16)),
        in_specs=[SMEM] + [VMEM] * (2 + n_cols),
        out_specs=(VMEM, VMEM),
        name="first",
    )(place, inv, targets, *deal(apply(w1, None)))

    s1_pieces = from_cols(s1)
    *z2, dots = apply(g, s1_pieces)
    if n_rows > DIRECT_ROWS:
        dot_pieces = [lax.psum(dots, "rows")]
    else:
        dot_pieces = from_rows(dots)
    end = pl.pallas_call(
        functools.partial(second_kernel, n_cols),
        out_shape=shape(outputs, own_len + LANES),
        in_specs=[SMEM] + [VMEM] * (2 + n_cols + len(dot_pieces)),
        out_specs=VMEM,
        name="second",
    )(place, inv, s1, *deal(z2), *dot_pieces)

    return pl.pallas_call(
        functools.partial(final_kernel, n_cols),
        out_shape=(shape(outputs, npoints), shape(outputs, npoints)),
        in_specs=[SMEM] + [VMEM] * (1 + 2 * n_cols),
        out_specs=(VMEM, VMEM),
        name="final",
    )(place, targets, *s1_pieces, *from_cols(end))


def solution(mesh):
    placed = (P("rows", "cols"), P(None, "rows"), P(None, "rows"))
    return jax.shard_map(
        local,
        mesh=mesh,
        in_specs=placed,
        out_specs=(P(None, "rows"), P(None, "rows")),
        check_vma=False,
    )
```

```python
import functools

import jax
import jax.numpy as jnp
from jax import lax
from jax.experimental import pallas as pl
from jax.experimental.pallas import tpu as pltpu
from jax.sharding import PartitionSpec as P

REG = 1.5
RADIUS = 0.25
GROUP = 4
RING = 3
STRIP = 64
LANES = 128
TINY = 1e-30
SHIFT = 0.375
DIRECT_ROWS = 8
RESIDENT_BYTES = 20 * 1024 * 1024

SMEM = pl.BlockSpec(memory_space=pltpu.SMEM)
VMEM = pl.BlockSpec(memory_space=pltpu.VMEM)
HBM = pl.BlockSpec(memory_space=pltpu.HBM)
F32 = jnp.float32
BF16 = jnp.bfloat16


def augment(x, first_ones):
    dim, n = x.shape
    norm = jnp.sum(x * x, axis=0, keepdims=True) / (RADIUS * RADIUS)
    high = norm.astype(BF16).astype(F32)
    rest = norm - high
    mid = rest.astype(BF16).astype(F32)
    low = rest - mid
    line = lax.broadcasted_iota(jnp.int32, (dim, n), 0)
    base = 3 if first_ones else 0
    ones_at = 0 if first_ones else 3
    tail = jnp.where((line >= ones_at) & (line < ones_at + 3), 1.0, 0.0)
    tail = jnp.where(line == base, high, tail)
    tail = jnp.where(line == base + 1, mid, tail)
    tail = jnp.where(line == base + 2, low, tail)
    return tail


def each_piece(pieces, row, visit):
    if len(pieces) == 1:

        def one(r, carry):
            visit(r, lambda *at: pieces[0][(r,) + at])
            return carry

        lax.fori_loop(0, pieces[0].shape[0], one, 0)
    else:
        for parity, ref in enumerate(pieces):
            for k in range(ref.shape[0]):
                visit(row ^ (2 * k + parity), lambda *at, ref=ref, k=k: ref[(k,) + at])


def build_kernel(cfg, place, direct, near_ref, *refs):
    n_pieces, nb, block_len, own_rows, block_rows, n_sub, count_rows, resident = cfg
    pieces, refs = refs[:n_pieces], refs[n_pieces:]
    k_hbm, ilist, jlist, groups, deg_ref = refs[:5]
    mlist, acc, lhs, rhs, counts_v, counts, count_sem = refs[5:12]
    kbuf, sems = (None, None) if resident else refs[12:]
    row, col = place[0], place[1]
    own_len = own_rows * block_len
    dim = near_ref.shape[0]
    scale = 1.0 / (RADIUS * RADIUS)

    def prepare(r, load):
        for k in range(own_rows):
            far = load(slice(None), slice(k * block_len, (k + 1) * block_len))
            rhs[r * own_rows + k, :dim, :] = far
            rhs[r * own_rows + k, dim:, :] = augment(far.astype(F32), False).astype(BF16)
        listed = load(slice(None), slice(own_len, own_len + LANES))
        counts_v[r] = listed.astype(F32)[:count_rows].astype(jnp.int32)

    each_piece(pieces, row, prepare)
    fetch = pltpu.make_async_copy(counts_v, counts, count_sem)
    fetch.start()
    for i in range(block_rows):
        near = near_ref[:, i * block_len:(i + 1) * block_len].astype(F32)
        full = jnp.concatenate([near * (-2.0 * scale), augment(near, True)], axis=0)
        lhs[i] = full.T.astype(BF16)
    acc[...] = jnp.zeros_like(acc)
    fetch.wait()

    def line(i, pos):
        me = row * block_rows + i

        def note(j, at):
            r, k = lax.div(j, own_rows), lax.rem(j, own_rows)
            name = r * block_rows + col * own_rows + k
            spot = k * nb + me
            mirrored = counts[r, lax.div(spot, LANES), lax.rem(spot, LANES)]
            m = direct[i, name] + jnp.where(name == me, 0, mirrored)
            ilist[at] = i
            jlist[at] = j
            mlist[at] = m
            return at + jnp.where(m > 0, 1, 0)

        return lax.fori_loop(0, n_sub, note, pos, unroll=8)

    pos = lax.fori_loop(0, block_rows, line, jnp.int32(0))
    for u in range(GROUP):
        ilist[pos + u] = 0
        jlist[pos + u] = 0
        mlist[pos + u] = 0
    total = lax.div(pos + (GROUP - 1), GROUP)
    groups[0] = total

    def copy_out(g):
        slot = lax.rem(g, RING)
        return pltpu.make_async_copy(kbuf.at[slot], k_hbm.at[g], sems.at[slot])

    def step(g, carry):
        slot, target = (g, k_hbm) if resident else (lax.rem(g, RING), kbuf)
        if not resident:

            @pl.when(g >= RING)
            def _():
                copy_out(g - RING).wait()

        for u in range(GROUP):
            i = ilist[g * GROUP + u]
            j = jlist[g * GROUP + u]
            m = mlist[g * GROUP + u].astype(F32)
            far = rhs[j]
            for s in range(block_len // STRIP):
                rows = slice(s * STRIP, (s + 1) * STRIP)
                d = jnp.dot(lhs[i, rows, :], far, preferred_element_type=F32)
                d = jnp.maximum(d, TINY)
                sc = d * lax.rsqrt(d)
                rem = jnp.maximum(1.0 - sc, 0.0)
                sq = rem * rem
                val = (sq * sq) * (sc * (4.0 * m) + m)
                target[slot, u, rows, :] = val.astype(BF16)
                half = val[:, :LANES]
                for h in range(1, block_len // LANES):
                    half = half + val[:, h * LANES:(h + 1) * LANES]
                acc[i, rows, :] += half
        if not resident:
            copy_out(g).start()
        return carry

    lax.fori_loop(0, total, step, 0)
    for i in range(block_rows):
        deg_ref[:, i * block_len:(i + 1) * block_len] = jnp.sum(acc[i].T, axis=0, keepdims=True)

    def drain(g, carry):
        copy_out(g).wait()
        return carry

    if not resident:
        lax.fori_loop(jnp.maximum(total - RING, 0), total, drain, 0)


def apply_kernel(cfg, place, ilist, jlist, groups, k_mat, *refs):
    n_pieces, n_cols, own_rows, block_len, products, resident = cfg
    pieces, refs = refs[:n_pieces], refs[n_pieces:]
    if products:
        inv_ref, t_ref, refs = refs[0], refs[1], refs[2:]
        s_refs, refs = refs[:n_cols], refs[n_cols:]
    z_refs, refs = refs[:n_cols], refs[n_cols:]
    w_all, z_acc = refs[:2]
    kbuf, sems = (None, None) if resident else refs[2:]
    row, col = place[0], place[1]
    total = groups[0]

    def copy_in(g):
        slot = lax.rem(g, RING)
        return pltpu.make_async_copy(k_mat.at[g], kbuf.at[slot], sems.at[slot])

    if not resident:
        for p in range(RING - 1):

            @pl.when(p < total)
            def _(p=p):
                copy_in(p).start()

    def place_piece(r, load):
        for k in range(own_rows):
            w_all[r * own_rows + k] = load(slice(None), slice(k * block_len, (k + 1) * block_len))

    each_piece(pieces, row, place_piece)
    z_acc[...] = jnp.zeros_like(z_acc)

    def step(g, carry):
        slot, source = (g, k_mat) if resident else (lax.rem(g, RING), kbuf)
        if not resident:

            @pl.when(g + (RING - 1) < total)
            def _():
                copy_in(g + (RING - 1)).start()

            copy_in(g).wait()
        parts = []
        for u in range(GROUP):
            parts.append(
                lax.dot_general(
                    w_all[jlist[g * GROUP + u]],
                    source[slot, u],
                    (((1,), (1,)), ((), ())),
                    preferred_element_type=F32,
                )
            )
        for u in range(GROUP):
            z_acc[ilist[g * GROUP + u]] += parts[u]
        return carry

    lax.fori_loop(0, total, step, 0)
    own_len = own_rows * block_len
    for e in range(n_cols):
        for k in range(own_rows):
            z_refs[e][:, k * block_len:(k + 1) * block_len] = z_acc[(col ^ e) * own_rows + k]
    if products:
        ts2 = jnp.zeros((t_ref.shape[0], 1), F32)
        s1s2 = jnp.zeros((t_ref.shape[0], 1), F32)
        for e in range(n_cols):
            at = pl.ds(pl.multiple_of((col ^ e) * own_len, LANES), own_len)
            scaled = z_refs[e][:, :own_len] * inv_ref[:, at]
            ts2 += jnp.sum(t_ref[:, at] * scaled, axis=1, keepdims=True)
            s1s2 += jnp.sum(s_refs[e][...] * scaled, axis=1, keepdims=True)
        t = t_ref[:, pl.ds(pl.multiple_of(col * own_len, LANES), own_len)]
        s1 = s_refs[0][...]
        tt = jnp.sum(t * t, axis=1, keepdims=True)
        ts1 = jnp.sum(t * s1, axis=1, keepdims=True)
        s1s1 = jnp.sum(s1 * s1, axis=1, keepdims=True)
        ts2 += SHIFT * ts1
        s1s2 += SHIFT * s1s1
        lane = lax.broadcasted_iota(jnp.int32, (t_ref.shape[0], LANES), 1)
        out = jnp.zeros(lane.shape, F32)
        for n, v in enumerate((tt, ts1, s1s1, ts2, s1s2)):
            out = jnp.where(lane == n, v, out)
        for e in range(n_cols):
            z_refs[e][:, own_len:] = out


def final_kernel(n_cols, place, t_ref, dots_a, dots_b, *refs):
    s1s, ends = refs[:n_cols], refs[n_cols:2 * n_cols]
    sol_ref, res_ref = refs[2 * n_cols:]
    own_len = s1s[0].shape[1]
    dots = dots_a[...] + dots_b[...]
    tt, ts1, s1s1, ts2, s1s2 = (dots[:, n:n + 1] for n in range(5))
    a1 = tt / (REG * tt + ts1)
    p = 1.0 - REG * a1
    new = p * p * tt - 2.0 * p * a1 * ts1 + a1 * a1 * s1s1
    u = p + new / tt
    dd = u * u * tt - 2.0 * u * a1 * ts1 + a1 * a1 * s1s1
    dmd = u * u * ts1 - u * a1 * (s1s1 + ts2) + a1 * a1 * s1s2
    a2 = new / (REG * dd + dmd)
    for e in range(n_cols):
        at = pl.ds(pl.multiple_of((place[1] ^ e) * own_len, LANES), own_len)
        t, s1, s2 = t_ref[:, at], s1s[e][...], ends[e][...]
        sol_ref[:, at] = (a1 + a2 * u) * t - (a2 * a1) * s1
        res_ref[:, at] = (p - a2 * REG * u) * t - (a1 + a2 * (u - REG * a1)) * s1 + (a2 * a1) * s2


def swap(x, axis, d):
    size = lax.axis_size(axis)
    return lax.ppermute(x, axis, [(i, i ^ d) for i in range(size)])


def from_cols(x):
    return [x] + [swap(x, "cols", e) for e in range(1, lax.axis_size("cols"))]


def from_rows(x):
    size = lax.axis_size("rows")
    if size > DIRECT_ROWS:
        return [lax.all_gather(x, "rows")]
    same = jnp.stack([x] + [swap(x, "rows", d) for d in range(2, size, 2)])
    return [same, swap(same, "rows", 1)]


def local(block_list, points, targets):
    n_rows = lax.axis_size("rows")
    n_cols = lax.axis_size("cols")
    row = lax.axis_index("rows")
    col = lax.axis_index("cols")
    block_rows, slots = block_list.shape
    dim, npoints = points.shape
    outputs = targets.shape[0]
    block_len = npoints // block_rows
    own_rows = block_rows // n_cols
    own_len = own_rows * block_len
    nb = block_rows * n_rows
    n_sub = own_rows * n_rows
    capacity = -(-block_rows * slots // n_rows)
    bound = min(block_rows * n_sub, n_cols * capacity * (n_rows + 1))
    n_groups = -(-bound // GROUP)
    list_len = n_groups * GROUP + GROUP
    place = jnp.stack([row, col])
    k_shape = (n_groups, GROUP, block_len, block_len)
    resident = 2 * n_groups * GROUP * block_len * block_len <= RESIDENT_BYTES
    limit = pltpu.CompilerParams(vmem_limit_bytes=24 * 1024 * 1024)
    ring = [] if resident else [
        pltpu.VMEM((RING, GROUP, block_len, block_len), BF16),
        pltpu.SemaphoreType.DMA((RING,)),
    ]
    k_spec = VMEM if resident else HBM

    def shape(*dims, dtype=F32):
        return jax.ShapeDtypeStruct(dims, dtype)

    lists = jnp.concatenate(from_cols(block_list), axis=1)
    names = jnp.arange(nb, dtype=jnp.int32)
    direct = jnp.sum((lists[:, :, None] == names).astype(jnp.int32), axis=1)
    own_counts = lax.dynamic_slice_in_dim(direct, col * own_rows, own_rows, 0)
    count_rows = -(-own_rows * nb // LANES)
    coded = own_counts.reshape(-1)
    coded = jnp.pad(coded, (0, dim * LANES - coded.shape[0])).reshape(dim, LANES).astype(BF16)
    own_points = lax.dynamic_slice_in_dim(points, col * own_len, own_len, 1)
    pieces = from_rows(jnp.concatenate([own_points, coded], axis=1))

    k_mat, ilist, jlist, groups, degree = pl.pallas_call(
        functools.partial(
            build_kernel,
                (len(pieces), nb, block_len, own_rows, block_rows, n_sub, count_rows, resident),
        ),
        out_shape=(
            pltpu.VMEM(k_shape, BF16) if resident else shape(*k_shape, dtype=BF16),
            shape(list_len, dtype=jnp.int32),
            shape(list_len, dtype=jnp.int32),
            shape(1, dtype=jnp.int32),
            shape(1, npoints),
        ),
        in_specs=[SMEM, SMEM, VMEM] + [VMEM] * len(pieces),
        out_specs=(k_spec, SMEM, SMEM, SMEM, VMEM),
        scratch_shapes=[
            pltpu.SMEM((list_len,), jnp.int32),
            pltpu.VMEM((block_rows, block_len, LANES), F32),
            pltpu.VMEM((block_rows, block_len, 2 * dim), BF16),
            pltpu.VMEM((n_sub, 2 * dim, block_len), BF16),
            pltpu.VMEM((n_rows, count_rows, LANES), jnp.int32),
            pltpu.SMEM((n_rows, count_rows, LANES), jnp.int32),
            pltpu.SemaphoreType.DMA,
            *ring,
        ],
        compiler_params=limit,
        name="build",
    )(place, direct, points, *pieces)

    if resident:
        k_mat = pltpu.with_memory_space_constraint(k_mat, pltpu.VMEM)

    def own(x):
        return lax.dynamic_slice_in_dim(x, col * own_len, own_len, 1)

    own_t = own(targets)
    inv = 1.0 / jnp.sqrt(1.0 + sum(from_cols(degree)))
    own_inv = own(inv)
    w1 = (own_t * own_inv).astype(BF16)

    def apply(w, s_pieces):
        pieces = from_rows(w)
        products = s_pieces is not None
        extra = [inv, targets, *s_pieces] if products else []
        width = own_len + LANES if products else own_len
        z = pl.pallas_call(
            functools.partial(
                apply_kernel, (len(pieces), n_cols, own_rows, block_len, products, resident)
            ),
            out_shape=[shape(outputs, width)] * n_cols,
            in_specs=[SMEM] * 4 + [k_spec] + [VMEM] * (len(pieces) + len(extra)),
            out_specs=[VMEM] * n_cols,
            scratch_shapes=[
                pltpu.VMEM((n_sub, outputs, block_len), BF16),
                pltpu.VMEM((block_rows, outputs, block_len), F32),
                *ring,
            ],
            compiler_params=limit,
            name="apply",
        )(place, ilist, jlist, groups, k_mat, *pieces, *extra)
        return sum([z[0]] + [swap(z[e], "cols", e) for e in range(1, n_cols)])

    s1 = apply(w1, None) * own_inv
    g = ((s1 - SHIFT * own_t) * own_inv).astype(BF16)
    s1_pieces = from_cols(s1)
    z2 = apply(g, s1_pieces)
    s2 = z2[:, :own_len] * own_inv + SHIFT * s1
    dots = z2[:, own_len:]
    if n_rows > DIRECT_ROWS:
        dots = [lax.psum(dots, "rows"), jnp.zeros_like(dots)]
    else:
        dots = dots + sum(swap(dots, "rows", d) for d in range(2, n_rows, 2))
        dots = [dots, swap(dots, "rows", 1)]

    return pl.pallas_call(
        functools.partial(final_kernel, n_cols),
        out_shape=(shape(outputs, npoints), shape(outputs, npoints)),
        in_specs=[SMEM] + [VMEM] * (3 + 2 * n_cols),
        out_specs=(VMEM, VMEM),
        name="final",
    )(place, targets, *dots, *s1_pieces, *from_cols(s2))


def solution(mesh):
    placed = (P("rows", "cols"), P(None, "rows"), P(None, "rows"))
    return jax.shard_map(
        local,
        mesh=mesh,
        in_specs=placed,
        out_specs=(P(None, "rows"), P(None, "rows")),
        check_vma=False,
    )
```

```python
import functools

import jax
import jax.numpy as jnp
from jax import lax
from jax.experimental import pallas as pl
from jax.experimental.pallas import tpu as pltpu
from jax.sharding import PartitionSpec as P

REG = 1.5
RADIUS = 0.25
GROUP = 4
RING = 3
STRIP = 64
LANES = 128
TINY = 1e-30
SHIFT = 0.375
DIRECT_ROWS = 8
RESIDENT_BYTES = 20 * 1024 * 1024

SMEM = pl.BlockSpec(memory_space=pltpu.SMEM)
VMEM = pl.BlockSpec(memory_space=pltpu.VMEM)
HBM = pl.BlockSpec(memory_space=pltpu.HBM)
F32 = jnp.float32
BF16 = jnp.bfloat16


def augment(x, first_ones):
    dim, n = x.shape
    norm = jnp.sum(x * x, axis=0, keepdims=True) / (RADIUS * RADIUS)
    high = norm.astype(BF16).astype(F32)
    rest = norm - high
    mid = rest.astype(BF16).astype(F32)
    low = rest - mid
    line = lax.broadcasted_iota(jnp.int32, (dim, n), 0)
    base = 3 if first_ones else 0
    ones_at = 0 if first_ones else 3
    tail = jnp.where((line >= ones_at) & (line < ones_at + 3), 1.0, 0.0)
    tail = jnp.where(line == base, high, tail)
    tail = jnp.where(line == base + 1, mid, tail)
    tail = jnp.where(line == base + 2, low, tail)
    return tail


def each_piece(pieces, row, visit):
    if len(pieces) == 1:

        def one(r, carry):
            visit(r, lambda *at: pieces[0][(r,) + at])
            return carry

        lax.fori_loop(0, pieces[0].shape[0], one, 0)
    else:
        for parity, ref in enumerate(pieces):
            for k in range(ref.shape[0]):
                visit(row ^ (2 * k + parity), lambda *at, ref=ref, k=k: ref[(k,) + at])


def by_col(refs):
    own, across, pair = refs
    return own, pair.at[0], across, pair.at[1]


def build_kernel(cfg, place, direct, near_ref, *refs):
    n_pieces, nb, block_len, own_rows, block_rows, n_sub, count_rows, resident = cfg
    pieces, refs = refs[:n_pieces], refs[n_pieces:]
    k_hbm, ilist, jlist, groups, deg_ref = refs[:5]
    mlist, acc, lhs, rhs, counts_v, counts, count_sem = refs[5:12]
    kbuf, sems = (None, None) if resident else refs[12:]
    row, col = place[0], place[1]
    own_len = own_rows * block_len
    dim = near_ref.shape[0]
    scale = 1.0 / (RADIUS * RADIUS)

    def prepare(r, load):
        for k in range(own_rows):
            far = load(slice(None), slice(k * block_len, (k + 1) * block_len))
            rhs[r * own_rows + k, :dim, :] = far
            rhs[r * own_rows + k, dim:, :] = augment(far.astype(F32), False).astype(BF16)
        listed = load(slice(None), slice(own_len, own_len + LANES))
        counts_v[r] = listed.astype(F32)[:count_rows].astype(jnp.int32)

    each_piece(pieces, row, prepare)
    fetch = pltpu.make_async_copy(counts_v, counts, count_sem)
    fetch.start()
    for i in range(block_rows):
        near = near_ref[:, i * block_len:(i + 1) * block_len].astype(F32)
        full = jnp.concatenate([near * (-2.0 * scale), augment(near, True)], axis=0)
        lhs[i] = full.T.astype(BF16)
    acc[...] = jnp.zeros_like(acc)
    fetch.wait()

    def line(i, pos):
        me = row * block_rows + i

        def note(j, at):
            r, k = lax.div(j, own_rows), lax.rem(j, own_rows)
            name = r * block_rows + col * own_rows + k
            spot = k * nb + me
            mirrored = counts[r, lax.div(spot, LANES), lax.rem(spot, LANES)]
            m = direct[i, name] + jnp.where(name == me, 0, mirrored)
            ilist[at] = i
            jlist[at] = j
            mlist[at] = m
            return at + jnp.where(m > 0, 1, 0)

        return lax.fori_loop(0, n_sub, note, pos, unroll=8)

    pos = lax.fori_loop(0, block_rows, line, jnp.int32(0))
    for u in range(GROUP):
        ilist[pos + u] = 0
        jlist[pos + u] = 0
        mlist[pos + u] = 0
    total = lax.div(pos + (GROUP - 1), GROUP)
    groups[0] = total

    def copy_out(g):
        slot = lax.rem(g, RING)
        return pltpu.make_async_copy(kbuf.at[slot], k_hbm.at[g], sems.at[slot])

    def step(g, carry):
        slot, target = (g, k_hbm) if resident else (lax.rem(g, RING), kbuf)
        if not resident:

            @pl.when(g >= RING)
            def _():
                copy_out(g - RING).wait()

        for u in range(GROUP):
            i = ilist[g * GROUP + u]
            j = jlist[g * GROUP + u]
            m = mlist[g * GROUP + u].astype(F32)
            far = rhs[j]
            sums = jnp.zeros((8, block_len), F32)
            for s in range(block_len // STRIP):
                rows = slice(s * STRIP, (s + 1) * STRIP)
                d = jnp.dot(lhs[i, rows, :], far, preferred_element_type=F32)
                d = jnp.maximum(d, TINY)
                sc = d * lax.rsqrt(d)
                rem = jnp.maximum(1.0 - sc, 0.0)
                sq = rem * rem
                val = (sq * sq) * (sc * (4.0 * m) + m)
                target[slot, u, rows, :] = val.astype(BF16)
                for h in range(0, STRIP, 8):
                    sums = sums + val[h:h + 8]
            acc[j] += sums
        if not resident:
            copy_out(g).start()
        return carry

    lax.fori_loop(0, total, step, 0)
    deg_ref[...] = jnp.sum(acc[...], axis=1)

    def drain(g, carry):
        copy_out(g).wait()
        return carry

    if not resident:
        lax.fori_loop(jnp.maximum(total - RING, 0), total, drain, 0)


def apply_kernel(cfg, place, ilist, jlist, groups, k_mat, *refs):
    n_pieces, n_cols, own_rows, block_len, first, resident = cfg
    pieces, refs = refs[:n_pieces], refs[n_pieces:]
    if first:
        inv_ref, refs = refs[0], refs[1:]
    else:
        t_ref, s_refs, refs = refs[0], refs[1:4], refs[4:]
    near, near_y, cross = refs[:3]
    w_all, z_acc = refs[3:5]
    kbuf, sems = (None, None) if resident else refs[5:]
    row, col = place[0], place[1]
    total = groups[0]

    def copy_in(g):
        slot = lax.rem(g, RING)
        return pltpu.make_async_copy(k_mat.at[g], kbuf.at[slot], sems.at[slot])

    if not resident:
        for p in range(RING - 1):

            @pl.when(p < total)
            def _(p=p):
                copy_in(p).start()

    def place_piece(r, load):
        for k in range(own_rows):
            w = load(slice(None), slice(k * block_len, (k + 1) * block_len))
            if first:
                w = (w * inv_ref[pl.ds(r * own_rows + k, 1), :]).astype(BF16)
            w_all[r * own_rows + k] = w

    each_piece(pieces, row, place_piece)
    z_acc[...] = jnp.zeros_like(z_acc)

    def step(g, carry):
        slot, source = (g, k_mat) if resident else (lax.rem(g, RING), kbuf)
        if not resident:

            @pl.when(g + (RING - 1) < total)
            def _():
                copy_in(g + (RING - 1)).start()

            copy_in(g).wait()
        parts = []
        for u in range(GROUP):
            parts.append(
                lax.dot_general(
                    w_all[jlist[g * GROUP + u]],
                    source[slot, u],
                    (((1,), (1,)), ((), ())),
                    preferred_element_type=F32,
                )
            )
        for u in range(GROUP):
            z_acc[ilist[g * GROUP + u]] += parts[u]
        return carry

    lax.fori_loop(0, total, step, 0)
    own_len = own_rows * block_len
    z_refs = (near, cross.at[0], near_y, cross.at[1])
    for e in range(n_cols):
        for k in range(own_rows):
            z_refs[e][:, k * block_len:(k + 1) * block_len] = z_acc[(col ^ e) * own_rows + k]
    if not first:
        outputs = t_ref.shape[0]
        ts2 = jnp.zeros((outputs, 1), F32)
        s1s2 = jnp.zeros((outputs, 1), F32)
        for e, packed in enumerate(by_col(s_refs)):
            at = pl.ds(pl.multiple_of((col ^ e) * own_len, LANES), own_len)
            scaled = z_refs[e][:, :own_len] * packed[outputs:outputs + 1, :]
            ts2 += jnp.sum(t_ref[:, at] * scaled, axis=1, keepdims=True)
            s1s2 += jnp.sum(packed[:outputs, :] * scaled, axis=1, keepdims=True)
        t = t_ref[:, pl.ds(pl.multiple_of(col * own_len, LANES), own_len)]
        s1 = s_refs[0][:outputs, :]
        tt = jnp.sum(t * t, axis=1, keepdims=True)
        ts1 = jnp.sum(t * s1, axis=1, keepdims=True)
        s1s1 = jnp.sum(s1 * s1, axis=1, keepdims=True)
        ts2 += SHIFT * ts1
        s1s2 += SHIFT * s1s1
        lane = lax.broadcasted_iota(jnp.int32, (outputs, LANES), 1)
        out = jnp.zeros(lane.shape, F32)
        for n, v in enumerate((tt, ts1, s1s1, ts2, s1s2)):
            out = jnp.where(lane == n, v, out)
        for ref in z_refs:
            ref[:, own_len:] = out


def final_kernel(n_cols, place, t_ref, dots_a, dots_b, *refs):
    s1s, s2s = by_col(refs[:3]), by_col(refs[3:6])
    sol_ref, res_ref = refs[6:]
    outputs, own_len = s2s[0].shape
    dots = dots_a[...] + dots_b[...]
    tt, ts1, s1s1, ts2, s1s2 = (dots[:, n:n + 1] for n in range(5))
    a1 = tt / (REG * tt + ts1)
    p = 1.0 - REG * a1
    new = p * p * tt - 2.0 * p * a1 * ts1 + a1 * a1 * s1s1
    u = p + new / tt
    dd = u * u * tt - 2.0 * u * a1 * ts1 + a1 * a1 * s1s1
    dmd = u * u * ts1 - u * a1 * (s1s1 + ts2) + a1 * a1 * s1s2
    a2 = new / (REG * dd + dmd)
    for e in range(n_cols):
        at = pl.ds(pl.multiple_of((place[1] ^ e) * own_len, LANES), own_len)
        t, s1, s2 = t_ref[:, at], s1s[e][:outputs, :], s2s[e][...]
        sol_ref[:, at] = (a1 + a2 * u) * t - (a2 * a1) * s1
        res_ref[:, at] = (p - a2 * REG * u) * t - (a1 + a2 * (u - REG * a1)) * s1 + (a2 * a1) * s2


def swap(x, axis, d):
    size = lax.axis_size(axis)
    return lax.ppermute(x, axis, [(i, i ^ d) for i in range(size)])


def spread(x):
    across = swap(x, "cols", 2)
    return [x, across, swap(jnp.stack([x, across]), "cols", 1)]


def shared(near, near_y, cross):
    got = swap(cross, "cols", 1)
    far = swap(near_y + got[1], "cols", 2)
    return (near + got[0]) + far


def pair_sum(parts):
    while len(parts) > 1:
        parts = [a + b for a, b in zip(parts[::2], parts[1::2])]
    return parts[0]


def along_z(x):
    return [x] + [swap(x, "rows", d) for d in range(2, lax.axis_size("rows"), 2)]


def across_x(same):
    return [same, swap(same, "rows", 1)]


def local(block_list, points, targets):
    n_rows = lax.axis_size("rows")
    n_cols = lax.axis_size("cols")
    row = lax.axis_index("rows")
    col = lax.axis_index("cols")
    block_rows, slots = block_list.shape
    dim, npoints = points.shape
    outputs = targets.shape[0]
    block_len = npoints // block_rows
    own_rows = block_rows // n_cols
    own_len = own_rows * block_len
    nb = block_rows * n_rows
    n_sub = own_rows * n_rows
    capacity = -(-block_rows * slots // n_rows)
    bound = min(block_rows * n_sub, n_cols * capacity * (n_rows + 1))
    n_groups = -(-bound // GROUP)
    list_len = n_groups * GROUP + GROUP
    place = jnp.stack([row, col])
    k_shape = (n_groups, GROUP, block_len, block_len)
    resident = 2 * n_groups * GROUP * block_len * block_len <= RESIDENT_BYTES
    limit = pltpu.CompilerParams(vmem_limit_bytes=24 * 1024 * 1024)
    ring = [] if resident else [
        pltpu.VMEM((RING, GROUP, block_len, block_len), BF16),
        pltpu.SemaphoreType.DMA((RING,)),
    ]
    k_spec = VMEM if resident else HBM

    def shape(*dims, dtype=F32):
        return jax.ShapeDtypeStruct(dims, dtype)

    direct_rows = n_rows <= DIRECT_ROWS

    def own(x):
        return lax.dynamic_slice_in_dim(x, col * own_len, own_len, 1)

    def from_rows(x):
        return across_x(jnp.stack(along_z(x))) if direct_rows else [lax.all_gather(x, "rows")]

    def total_rows(x):
        if direct_rows:
            return pair_sum(across_x(pair_sum(along_z(x))))
        return lax.psum(x, "rows")

    lists = jnp.concatenate([block_list, swap(block_list, "cols", 1)], axis=1)
    lists = jnp.concatenate([lists, swap(lists, "cols", 2)], axis=1)
    names = jnp.arange(nb, dtype=jnp.int32)
    direct = jnp.sum((lists[:, :, None] == names).astype(jnp.int32), axis=1)
    own_counts = lax.dynamic_slice_in_dim(direct, col * own_rows, own_rows, 0)
    count_rows = -(-own_rows * nb // LANES)
    coded = own_counts.reshape(-1)
    coded = jnp.pad(coded, (0, dim * LANES - coded.shape[0])).reshape(dim, LANES).astype(BF16)
    packed = jnp.concatenate([own(points), coded], axis=1)
    own_t = own(targets)
    if direct_rows:
        packed, early_t = lax.optimization_barrier((packed, own_t))
        pieces = from_rows(packed)
        t_stack = jnp.stack(along_z(early_t))
    else:
        pieces = from_rows(packed)

    k_mat, ilist, jlist, groups, degree = pl.pallas_call(
        functools.partial(
            build_kernel,
                (len(pieces), nb, block_len, own_rows, block_rows, n_sub, count_rows, resident),
        ),
        out_shape=(
            pltpu.VMEM(k_shape, BF16) if resident else shape(*k_shape, dtype=BF16),
            shape(list_len, dtype=jnp.int32),
            shape(list_len, dtype=jnp.int32),
            shape(1, dtype=jnp.int32),
            shape(n_sub, block_len),
        ),
        in_specs=[SMEM, SMEM, VMEM] + [VMEM] * len(pieces),
        out_specs=(k_spec, SMEM, SMEM, SMEM, VMEM),
        scratch_shapes=[
            pltpu.SMEM((list_len,), jnp.int32),
            pltpu.VMEM((n_sub, 8, block_len), F32),
            pltpu.VMEM((block_rows, block_len, 2 * dim), BF16),
            pltpu.VMEM((n_sub, 2 * dim, block_len), BF16),
            pltpu.VMEM((n_rows, count_rows, LANES), jnp.int32),
            pltpu.SMEM((n_rows, count_rows, LANES), jnp.int32),
            pltpu.SemaphoreType.DMA,
            *ring,
        ],
        compiler_params=limit,
        name="build",
    )(place, direct, points, *pieces)

    if resident:
        k_mat = pltpu.with_memory_space_constraint(k_mat, pltpu.VMEM)

    t_pieces = across_x(t_stack) if direct_rows else from_rows(own_t)
    inv = 1.0 / jnp.sqrt(1.0 + total_rows(degree))
    own_inv = lax.dynamic_slice_in_dim(inv, row * own_rows, own_rows, 0).reshape(1, own_len)

    def apply(pieces, extra, width):
        first = len(extra) == 1
        return shared(*pl.pallas_call(
            functools.partial(
                apply_kernel, (len(pieces), n_cols, own_rows, block_len, first, resident)
            ),
            out_shape=[
                shape(outputs, width), shape(outputs, width), shape(2, outputs, width)
            ],
            in_specs=[SMEM] * 4 + [k_spec] + [VMEM] * (len(pieces) + len(extra)),
            out_specs=[VMEM] * 3,
            scratch_shapes=[
                pltpu.VMEM((n_sub, outputs, block_len), BF16),
                pltpu.VMEM((block_rows, outputs, block_len), F32),
                *ring,
            ],
            compiler_params=limit,
            name="apply",
        )(place, ilist, jlist, groups, k_mat, *pieces, *extra))

    s1 = apply(t_pieces, [inv], own_len) * own_inv
    g = ((s1 - SHIFT * own_t) * own_inv).astype(BF16)
    s1_all = spread(jnp.concatenate([s1, jnp.broadcast_to(own_inv, (8, own_len))], axis=0))
    z2 = apply(from_rows(g), [targets, *s1_all], own_len + LANES)
    s2 = z2[:, :own_len] * own_inv + SHIFT * s1
    dots = z2[:, own_len:]
    if direct_rows:
        dots = across_x(pair_sum(along_z(dots)))
    else:
        dots = [lax.psum(dots, "rows"), jnp.zeros_like(dots)]

    return pl.pallas_call(
        functools.partial(final_kernel, n_cols),
        out_shape=(shape(outputs, npoints), shape(outputs, npoints)),
        in_specs=[SMEM] + [VMEM] * 9,
        out_specs=(VMEM, VMEM),
        name="final",
    )(place, targets, *dots, *s1_all, *spread(s2))


def solution(mesh):
    placed = (P("rows", "cols"), P(None, "rows"), P(None, "rows"))
    return jax.shard_map(
        local,
        mesh=mesh,
        in_specs=placed,
        out_specs=(P(None, "rows"), P(None, "rows")),
        check_vma=False,
    )
```

```python
import functools

import jax
import jax.numpy as jnp
from jax import lax
from jax.experimental import pallas as pl
from jax.experimental.pallas import tpu as pltpu
from jax.sharding import PartitionSpec as P

REG = 1.5
RADIUS = 0.25
GROUP = 4
RING = 3
STRIP = 64
LANES = 128
TINY = 1e-30
SHIFT = 0.375
DIRECT_ROWS = 8
RESIDENT_BYTES = 20 * 1024 * 1024

SMEM = pl.BlockSpec(memory_space=pltpu.SMEM)
VMEM = pl.BlockSpec(memory_space=pltpu.VMEM)
HBM = pl.BlockSpec(memory_space=pltpu.HBM)
F32 = jnp.float32
BF16 = jnp.bfloat16


def pair_sum(parts):
    while len(parts) > 1:
        parts = [a + b for a, b in zip(parts[::2], parts[1::2])]
    return parts[0]


def augment(x, first_ones):
    dim, n = x.shape
    norm = jnp.sum(x * x, axis=0, keepdims=True) / (RADIUS * RADIUS)
    high = norm.astype(BF16).astype(F32)
    rest = norm - high
    mid = rest.astype(BF16).astype(F32)
    low = rest - mid
    line = lax.broadcasted_iota(jnp.int32, (dim, n), 0)
    base = 3 if first_ones else 0
    ones_at = 0 if first_ones else 3
    tail = jnp.where((line >= ones_at) & (line < ones_at + 3), 1.0, 0.0)
    tail = jnp.where(line == base, high, tail)
    tail = jnp.where(line == base + 1, mid, tail)
    tail = jnp.where(line == base + 2, low, tail)
    return tail


def each_piece(pieces, row, visit):
    if len(pieces) == 1:

        def one(r, carry):
            visit(r, lambda *at: pieces[0][(r,) + at])
            return carry

        lax.fori_loop(0, pieces[0].shape[0], one, 0)
    else:
        for parity, ref in enumerate(pieces):
            for k in range(ref.shape[0]):
                visit(row ^ (2 * k + parity), lambda *at, ref=ref, k=k: ref[(k,) + at])


def by_col(refs):
    own, across, pair = refs
    return own, pair.at[0], across, pair.at[1]


def build_kernel(cfg, place, direct, near_hbm, *refs):
    n_pieces, nb, block_len, own_rows, block_rows, n_sub, count_rows, resident = cfg
    pieces, refs = refs[:n_pieces], refs[n_pieces:]
    k_hbm, ilist, jlist, groups, deg_ref = refs[:5]
    mlist, acc, lhs, rhs, near_ref, counts_v, counts, count_sem, near_sem = refs[5:14]
    kbuf, sems = (None, None) if resident else refs[14:]
    near_copy = pltpu.make_async_copy(near_hbm, near_ref, near_sem)
    near_copy.start()
    row, col = place[0], place[1]
    own_len = own_rows * block_len
    dim = near_hbm.shape[0]
    scale = 1.0 / (RADIUS * RADIUS)

    def prepare(r, load):
        for k in range(own_rows):
            far = load(slice(None), slice(k * block_len, (k + 1) * block_len))
            rhs[r * own_rows + k, :dim, :] = far
            rhs[r * own_rows + k, dim:, :] = augment(far.astype(F32), False).astype(BF16)
        listed = load(slice(None), slice(own_len, own_len + LANES))
        counts_v[r] = listed.astype(F32)[:count_rows].astype(jnp.int32)

    each_piece(pieces, row, prepare)
    fetch = pltpu.make_async_copy(counts_v, counts, count_sem)
    fetch.start()
    near_copy.wait()
    for i in range(block_rows):
        near = near_ref[:, i * block_len:(i + 1) * block_len].astype(F32)
        full = jnp.concatenate([near * (-2.0 * scale), augment(near, True)], axis=0)
        lhs[i] = full.T.astype(BF16)
    acc[...] = jnp.zeros_like(acc)
    fetch.wait()

    pos = jnp.int32(0)
    for i in range(block_rows):
        me = row * block_rows + i
        spots = [k * nb + me for k in range(own_rows)]
        spots = [(lax.shift_right_logical(p, 7), p & (LANES - 1)) for p in spots]

        def note(r, at, i=i, me=me, spots=spots):
            for k in range(own_rows):
                name = r * block_rows + col * own_rows + k
                m = direct[i, name] + jnp.where(name == me, 0, counts[r, spots[k][0], spots[k][1]])
                ilist[at] = i
                jlist[at] = r * own_rows + k
                mlist[at] = m
                at = at + jnp.where(m > 0, 1, 0)
            return at

        pos = lax.fori_loop(0, n_sub // own_rows, note, pos, unroll=4)
    for u in range(GROUP):
        ilist[pos + u] = 0
        jlist[pos + u] = 0
        mlist[pos + u] = 0
    total = lax.div(pos + (GROUP - 1), GROUP)
    groups[0] = total

    def copy_out(g):
        slot = lax.rem(g, RING)
        return pltpu.make_async_copy(kbuf.at[slot], k_hbm.at[g], sems.at[slot])

    def step(g, carry):
        slot, target = (g, k_hbm) if resident else (lax.rem(g, RING), kbuf)
        if not resident:

            @pl.when(g >= RING)
            def _():
                copy_out(g - RING).wait()

        for u in range(GROUP):
            i = ilist[g * GROUP + u]
            j = jlist[g * GROUP + u]
            m = mlist[g * GROUP + u].astype(F32)
            far = rhs[j]
            sums = jnp.zeros((8, block_len), F32)
            for s in range(block_len // STRIP):
                rows = slice(s * STRIP, (s + 1) * STRIP)
                d = jnp.dot(lhs[i, rows, :], far, preferred_element_type=F32)
                d = jnp.maximum(d, TINY)
                sc = d * lax.rsqrt(d)
                rem = jnp.maximum(1.0 - sc, 0.0)
                sq = rem * rem
                val = (sq * sq) * (sc * (4.0 * m) + m)
                target[slot, u, rows, :] = val.astype(BF16)
                for h in range(0, STRIP, 8):
                    sums = sums + val[h:h + 8]
            acc[j] += sums
        if not resident:
            copy_out(g).start()
        return carry

    lax.fori_loop(0, total, step, 0)
    deg_ref[...] = jnp.sum(acc[...], axis=1)

    def drain(g, carry):
        copy_out(g).wait()
        return carry

    if not resident:
        lax.fori_loop(jnp.maximum(total - RING, 0), total, drain, 0)


def apply_kernel(cfg, place, ilist, jlist, groups, k_mat, *refs):
    n_pieces, n_cols, own_rows, block_len, first, resident = cfg
    pieces, refs = refs[:n_pieces], refs[n_pieces:]
    if first:
        inv_ref, refs = refs[0], refs[1:]
    else:
        t_ref, s_refs, refs = refs[0], refs[1:4], refs[4:]
    near, near_y, cross = refs[:3]
    if not first:
        dot_ref, refs = refs[3], refs[:3] + refs[4:]
    w_all, z_acc = refs[3:5]
    kbuf, sems = (None, None) if resident else refs[5:]
    row, col = place[0], place[1]
    total = groups[0]

    def copy_in(g):
        slot = lax.rem(g, RING)
        return pltpu.make_async_copy(k_mat.at[g], kbuf.at[slot], sems.at[slot])

    if not resident:
        for p in range(RING - 1):

            @pl.when(p < total)
            def _(p=p):
                copy_in(p).start()

    def place_piece(r, load):
        for k in range(own_rows):
            w = load(slice(None), slice(k * block_len, (k + 1) * block_len))
            if first:
                w = (w * inv_ref[pl.ds(r * own_rows + k, 1), :]).astype(BF16)
            w_all[r * own_rows + k] = w

    each_piece(pieces, row, place_piece)
    z_acc[...] = jnp.zeros_like(z_acc)

    def step(g, carry):
        slot, source = (g, k_mat) if resident else (lax.rem(g, RING), kbuf)
        if not resident:

            @pl.when(g + (RING - 1) < total)
            def _():
                copy_in(g + (RING - 1)).start()

            copy_in(g).wait()
        parts = []
        for u in range(GROUP):
            parts.append(
                lax.dot_general(
                    w_all[jlist[g * GROUP + u]],
                    source[slot, u],
                    (((1,), (1,)), ((), ())),
                    preferred_element_type=F32,
                )
            )
        for u in range(GROUP):
            z_acc[ilist[g * GROUP + u]] += parts[u]
        return carry

    lax.fori_loop(0, total, step, 0)
    own_len = own_rows * block_len
    z_refs = (near, cross.at[0], near_y, cross.at[1])
    for e in range(n_cols):
        for k in range(own_rows):
            z_refs[e][:, k * block_len:(k + 1) * block_len] = z_acc[(col ^ e) * own_rows + k]
    if not first:
        outputs = t_ref.shape[0]
        ts2 = jnp.zeros((outputs, 1), F32)
        s1s2 = jnp.zeros((outputs, 1), F32)
        for e, packed in enumerate(by_col(s_refs)):
            at = pl.ds(pl.multiple_of((col ^ e) * own_len, LANES), own_len)
            scaled = z_refs[e][...] * packed[outputs:outputs + 1, :]
            ts2 += jnp.sum(t_ref[:, at] * scaled, axis=1, keepdims=True)
            s1s2 += jnp.sum(packed[:outputs, :] * scaled, axis=1, keepdims=True)
        t = t_ref[:, pl.ds(pl.multiple_of(col * own_len, LANES), own_len)]
        s1 = s_refs[0][:outputs, :]
        tt = jnp.sum(t * t, axis=1, keepdims=True)
        ts1 = jnp.sum(t * s1, axis=1, keepdims=True)
        s1s1 = jnp.sum(s1 * s1, axis=1, keepdims=True)
        ts2 += SHIFT * ts1
        s1s2 += SHIFT * s1s1
        lane = lax.broadcasted_iota(jnp.int32, (outputs, LANES), 1)
        out = jnp.zeros(lane.shape, F32)
        for n, v in enumerate((tt, ts1, s1s1, ts2, s1s2)):
            out = jnp.where(lane == n, v, out)
        dot_ref[...] = out


def final_kernel(n_cols, place, t_ref, *refs):
    s1s, s2s = by_col(refs[:3]), by_col(refs[3:6])
    sol_ref, res_ref = refs[6:]
    outputs, own_len = s2s[0].shape[0], s2s[0].shape[1] - LANES
    dots = pair_sum([ref[:, own_len:] for ref in s2s])
    tt, ts1, s1s1, ts2, s1s2 = (dots[:, n:n + 1] for n in range(5))
    a1 = tt / (REG * tt + ts1)
    p = 1.0 - REG * a1
    new = p * p * tt - 2.0 * p * a1 * ts1 + a1 * a1 * s1s1
    u = p + new / tt
    dd = u * u * tt - 2.0 * u * a1 * ts1 + a1 * a1 * s1s1
    dmd = u * u * ts1 - u * a1 * (s1s1 + ts2) + a1 * a1 * s1s2
    a2 = new / (REG * dd + dmd)
    for e in range(n_cols):
        at = pl.ds(pl.multiple_of((place[1] ^ e) * own_len, LANES), own_len)
        t, s1, s2 = t_ref[:, at], s1s[e][:outputs, :], s2s[e][:, :own_len]
        sol_ref[:, at] = (a1 + a2 * u) * t - (a2 * a1) * s1
        res_ref[:, at] = (p - a2 * REG * u) * t - (a1 + a2 * (u - REG * a1)) * s1 + (a2 * a1) * s2


def swap(x, axis, d):
    size = lax.axis_size(axis)
    return lax.ppermute(x, axis, [(i, i ^ d) for i in range(size)])


def spread(x):
    across = swap(x, "cols", 2)
    return [x, across, swap(jnp.stack([x, across]), "cols", 1)]


def shared(near, near_y, cross):
    got = swap(cross, "cols", 1)
    far = swap(near_y + got[1], "cols", 2)
    return (near + got[0]) + far


def along_z(x):
    return [x] + [swap(x, "rows", d) for d in range(2, lax.axis_size("rows"), 2)]


def across_x(same):
    return [same, swap(same, "rows", 1)]


def local(block_list, points, targets):
    n_rows = lax.axis_size("rows")
    n_cols = lax.axis_size("cols")
    row = lax.axis_index("rows")
    col = lax.axis_index("cols")
    block_rows, slots = block_list.shape
    dim, npoints = points.shape
    outputs = targets.shape[0]
    block_len = npoints // block_rows
    own_rows = block_rows // n_cols
    own_len = own_rows * block_len
    nb = block_rows * n_rows
    n_sub = own_rows * n_rows
    capacity = -(-block_rows * slots // n_rows)
    bound = min(block_rows * n_sub, n_cols * capacity * (n_rows + 1))
    n_groups = -(-bound // GROUP)
    list_len = n_groups * GROUP + GROUP
    place = jnp.stack([row, col])
    k_shape = (n_groups, GROUP, block_len, block_len)
    resident = 2 * n_groups * GROUP * block_len * block_len <= RESIDENT_BYTES
    limit = pltpu.CompilerParams(vmem_limit_bytes=(8 if resident else 32) * 1024 * 1024)
    ring = [] if resident else [
        pltpu.VMEM((RING, GROUP, block_len, block_len), BF16),
        pltpu.SemaphoreType.DMA((RING,)),
    ]
    k_spec = VMEM if resident else HBM

    def shape(*dims, dtype=F32):
        return jax.ShapeDtypeStruct(dims, dtype)

    direct_rows = n_rows <= DIRECT_ROWS

    def own(x):
        return lax.dynamic_slice_in_dim(x, col * own_len, own_len, 1)

    def from_rows(x):
        return across_x(jnp.stack(along_z(x))) if direct_rows else [lax.all_gather(x, "rows")]

    def total_rows(x):
        if direct_rows:
            return pair_sum(across_x(pair_sum(along_z(x))))
        return lax.psum(x, "rows")

    lists = [block_list] + [swap(block_list, "cols", e) for e in range(1, n_cols)]
    names = jnp.arange(nb, dtype=jnp.int32)
    direct = sum(jnp.sum((x[:, :, None] == names).astype(jnp.int32), axis=1) for x in lists)
    own_counts = lax.dynamic_slice_in_dim(direct, col * own_rows, own_rows, 0)
    count_rows = -(-own_rows * nb // LANES)
    coded = own_counts.reshape(-1)
    coded = jnp.pad(coded, (0, dim * LANES - coded.shape[0])).reshape(dim, LANES).astype(BF16)
    packed = jnp.concatenate([own(points), coded], axis=1)
    own_t = own(targets)
    if direct_rows:
        packed, early_t = lax.optimization_barrier((packed, own_t))
        pieces = from_rows(packed)
        t_stack = jnp.stack(along_z(early_t))
        *pieces, t_stack = lax.optimization_barrier((*pieces, t_stack))
        t_pieces = across_x(t_stack)
    else:
        pieces = from_rows(packed)

    k_mat, ilist, jlist, groups, degree = pl.pallas_call(
        functools.partial(
            build_kernel,
                (len(pieces), nb, block_len, own_rows, block_rows, n_sub, count_rows, resident),
        ),
        out_shape=(
            pltpu.VMEM(k_shape, BF16) if resident else shape(*k_shape, dtype=BF16),
            shape(list_len, dtype=jnp.int32),
            shape(list_len, dtype=jnp.int32),
            shape(1, dtype=jnp.int32),
            shape(n_sub, block_len),
        ),
        in_specs=[SMEM, SMEM, HBM] + [VMEM] * len(pieces),
        out_specs=(k_spec, SMEM, SMEM, SMEM, VMEM),
        scratch_shapes=[
            pltpu.SMEM((list_len,), jnp.int32),
            pltpu.VMEM((n_sub, 8, block_len), F32),
            pltpu.VMEM((block_rows, block_len, 2 * dim), BF16),
            pltpu.VMEM((n_sub, 2 * dim, block_len), BF16),
            pltpu.VMEM((dim, npoints), BF16),
            pltpu.VMEM((n_rows, count_rows, LANES), jnp.int32),
            pltpu.SMEM((n_rows, count_rows, LANES), jnp.int32),
            pltpu.SemaphoreType.DMA,
            pltpu.SemaphoreType.DMA,
            *ring,
        ],
        compiler_params=limit,
        cost_estimate=pl.CostEstimate(
            flops=2 * 2 * dim * bound * block_len * block_len,
            bytes_accessed=2 * bound * block_len * block_len,
            transcendentals=bound * block_len * block_len,
        ),
        name="build",
    )(place, direct, pltpu.with_memory_space_constraint(points, pltpu.HBM), *pieces)

    if resident:
        k_mat = pltpu.with_memory_space_constraint(k_mat, pltpu.VMEM)

    if direct_rows:
        degree, *t_pieces = lax.optimization_barrier((degree, *t_pieces))
    else:
        t_pieces = from_rows(own_t)
    inv = 1.0 / jnp.sqrt(1.0 + total_rows(degree))
    own_inv = lax.dynamic_slice_in_dim(inv, row * own_rows, own_rows, 0).reshape(1, own_len)

    def apply(pieces, extra):
        first = len(extra) == 1
        out = [shape(outputs, own_len), shape(outputs, own_len), shape(2, outputs, own_len)]
        out += [] if first else [shape(outputs, LANES)]
        return pl.pallas_call(
            functools.partial(
                apply_kernel, (len(pieces), n_cols, own_rows, block_len, first, resident)
            ),
            out_shape=out,
            in_specs=[SMEM] * 4 + [k_spec] + [VMEM] * (len(pieces) + len(extra)),
            out_specs=[VMEM] * len(out),
            scratch_shapes=[
                pltpu.VMEM((n_sub, outputs, block_len), BF16),
                pltpu.VMEM((block_rows, outputs, block_len), F32),
                *ring,
            ],
            compiler_params=limit,
            name="apply",
        )(place, ilist, jlist, groups, k_mat, *pieces, *extra)

    s1 = shared(*apply(t_pieces, [inv])) * own_inv
    g = ((s1 - SHIFT * own_t) * own_inv).astype(BF16)
    s1_all = spread(jnp.concatenate([s1, jnp.broadcast_to(own_inv, (8, own_len))], axis=0))
    *z2, dots = apply(from_rows(g), [targets, *s1_all])
    if direct_rows:
        dots = pair_sum(along_z(pair_sum(across_x(dots))))
    else:
        dots = lax.psum(dots, "rows")
    s2 = shared(*z2) * own_inv + SHIFT * s1
    ends = spread(jnp.concatenate([s2, dots], axis=1))
    s1_all, ends = [
        [pltpu.with_memory_space_constraint(x, pltpu.VMEM) for x in xs] for xs in (s1_all, ends)
    ]

    return pl.pallas_call(
        functools.partial(final_kernel, n_cols),
        out_shape=(shape(outputs, npoints), shape(outputs, npoints)),
        in_specs=[SMEM] + [VMEM] * 7,
        out_specs=(VMEM, VMEM),
        name="final",
    )(place, targets, *s1_all, *ends)


def solution(mesh):
    placed = (P("rows", "cols"), P(None, "rows"), P(None, "rows"))
    return jax.shard_map(
        local,
        mesh=mesh,
        in_specs=placed,
        out_specs=(P(None, "rows"), P(None, "rows")),
        check_vma=False,
    )
```

```python
import functools
from typing import NamedTuple

import jax
import jax.numpy as jnp
from jax import lax
from jax.experimental import pallas as pl
from jax.experimental.pallas import tpu as pltpu
from jax.sharding import PartitionSpec as P

REG = 1.5
RADIUS = 0.25
GROUP_BITS = 2
GROUP = 1 << GROUP_BITS
CODE_BITS = 12
CODE = 1 << CODE_BITS
RING = 3
STRIP = 64
LANES = 128
TINY = 1e-30
SHIFT = 0.375
DIRECT_ROWS = 8
RESIDENT_BYTES = 20 * 1024 * 1024

SMEM = pl.BlockSpec(memory_space=pltpu.SMEM)
VMEM = pl.BlockSpec(memory_space=pltpu.VMEM)
HBM = pl.BlockSpec(memory_space=pltpu.HBM)
F32 = jnp.float32
BF16 = jnp.bfloat16


def pair_sum(parts):
    while len(parts) > 1:
        parts = [a + b for a, b in zip(parts[::2], parts[1::2])]
    return parts[0]


class Sizes(NamedTuple):
    parts: int
    resident: bool
    nb: int
    block_len: int
    own_rows: int
    block_rows: int
    count_rows: int


def augment(x, first_ones):
    dim, n = x.shape
    norm = jnp.sum(x * x, axis=0, keepdims=True) / (RADIUS * RADIUS)
    high = norm.astype(BF16).astype(F32)
    rest = norm - high
    mid = rest.astype(BF16).astype(F32)
    low = rest - mid
    line = lax.broadcasted_iota(jnp.int32, (dim, n), 0)
    base = 3 if first_ones else 0
    ones_at = 0 if first_ones else 3
    tail = jnp.where((line >= ones_at) & (line < ones_at + 3), 1.0, 0.0)
    tail = jnp.where(line == base, high, tail)
    tail = jnp.where(line == base + 1, mid, tail)
    tail = jnp.where(line == base + 2, low, tail)
    return tail


def row_of(cfg, place, part, z):
    if cfg.parts == 1:
        return z
    return 2 * z + (place[0] & 1 if part == 0 else 1 - (place[0] & 1))


def slot_of(cfg, place, n):
    return n if cfg.parts == 1 else lax.shift_right_logical(place[0], 1) ^ n


def build_kernel(cfg, part, place, direct, *refs):
    last = part == cfg.parts - 1
    if part == 0:
        near_hbm, piece, refs = refs[0], refs[1], refs[2:]
        k_mat, listed, deg_ref, lhs = refs[:4]
        near_ref, near_sem, refs = refs[4], refs[5], refs[6:]
        near_copy = pltpu.make_async_copy(near_hbm, near_ref, near_sem)
        near_copy.start()
    else:
        lhs, first_deg, piece = refs[:3]
        k_mat, listed, deg_ref = refs[3:6]
        refs = refs[6:]
    mlist, acc, rhs, counts_v, counts, count_sem = refs[:6]
    kbuf, sems = (None, None) if cfg.resident else refs[6:]
    row, col = place[0], place[1]
    own_rows, block_len, nb = cfg.own_rows, cfg.block_len, cfg.nb
    own_len = own_rows * block_len
    dim, held = piece.shape[1], piece.shape[0]
    scale = 1.0 / (RADIUS * RADIUS)

    def prepare(n, carry):
        z = slot_of(cfg, place, n)
        for k in range(own_rows):
            far = piece[n, :, k * block_len:(k + 1) * block_len]
            rhs[z * own_rows + k, :dim, :] = far
            rhs[z * own_rows + k, dim:, :] = augment(far.astype(F32), False).astype(BF16)
        named = piece[n, :, own_len:own_len + LANES]
        counts_v[z] = named.astype(F32)[:cfg.count_rows].astype(jnp.int32)
        return carry

    lax.fori_loop(0, held, prepare, 0, unroll=held <= 4)
    fetch = pltpu.make_async_copy(counts_v, counts, count_sem)
    fetch.start()
    if part == 0:
        near_copy.wait()
        for i in range(cfg.block_rows):
            near = near_ref[:, i * block_len:(i + 1) * block_len].astype(F32)
            full = jnp.concatenate([near * (-2.0 * scale), augment(near, True)], axis=0)
            lhs[i] = full.T.astype(BF16)
    acc[...] = jnp.zeros_like(acc)
    fetch.wait()

    pos = jnp.int32(0)
    for i in range(cfg.block_rows):
        me = row * cfg.block_rows + i
        spots = [k * nb + me for k in range(own_rows)]
        spots = [(lax.shift_right_logical(p, 7), p & (LANES - 1)) for p in spots]

        def note(z, at, i=i, me=me, spots=spots):
            for k in range(own_rows):
                name = row_of(cfg, place, part, z) * cfg.block_rows + col * own_rows + k
                m = direct[i, name] + jnp.where(name == me, 0, counts[z, spots[k][0], spots[k][1]])
                listed[at + 1] = i * CODE + z * own_rows + k
                mlist[at] = m
                at = at + jnp.where(m > 0, 1, 0)
            return at

        pos = lax.fori_loop(0, held, note, pos, unroll=4)
    for u in range(GROUP):
        listed[pos + u + 1] = 0
        mlist[pos + u] = 0
    total = lax.shift_right_logical(pos + (GROUP - 1), GROUP_BITS)
    listed[0] = total

    def copy_out(g):
        slot = lax.rem(g, RING)
        return pltpu.make_async_copy(kbuf.at[slot], k_mat.at[g], sems.at[slot])

    def step(g, carry):
        slot, target = (g, k_mat) if cfg.resident else (lax.rem(g, RING), kbuf)
        if not cfg.resident:

            @pl.when(g >= RING)
            def _():
                copy_out(g - RING).wait()

        for u in range(GROUP):
            code = listed[g * GROUP + u + 1]
            i, j = lax.shift_right_logical(code, CODE_BITS), code & (CODE - 1)
            m = mlist[g * GROUP + u].astype(F32)
            far = rhs[j]
            sums = jnp.zeros((8, block_len), F32)
            for s in range(block_len // STRIP):
                rows = slice(s * STRIP, (s + 1) * STRIP)
                d = jnp.dot(lhs[i, rows, :], far, preferred_element_type=F32)
                d = jnp.maximum(d, TINY)
                sc = d * lax.rsqrt(d)
                rem = jnp.maximum(1.0 - sc, 0.0)
                sq = rem * rem
                val = (sq * sq) * (sc * (4.0 * m) + m)
                target[slot, u, rows, :] = val.astype(BF16)
                for h in range(0, STRIP, 8):
                    sums = sums + val[h:h + 8]
            acc[j] += sums
        if not cfg.resident:
            copy_out(g).start()
        return carry

    lax.fori_loop(0, total, step, 0)
    if cfg.parts == 1 or not last:
        deg_ref[...] = jnp.sum(acc[...], axis=1)
    else:
        second = jnp.sum(acc[...], axis=1)
        for z in range(held):
            rows = slice(z * own_rows, (z + 1) * own_rows)
            for p, deg in enumerate((first_deg[rows, :], second[rows])):
                at = row_of(cfg, place, p, z) * own_rows
                for k in range(own_rows):
                    deg_ref[pl.ds(at + k, 1), :] = deg[k:k + 1]

    def drain(g, carry):
        copy_out(g).wait()
        return carry

    if not cfg.resident:
        lax.fori_loop(jnp.maximum(total - RING, 0), total, drain, 0)


def apply_kernel(cfg, parts, scaled, carried, finish, extra_k, place, *refs):
    n = len(parts)
    lists, ks, pieces, refs = refs[:n], refs[n:2 * n], refs[2 * n:3 * n], refs[3 * n + extra_k:]
    if scaled:
        inv_ref, refs = refs[0], refs[1:]
    if carried:
        z_in, refs = refs[0], refs[1:]
    products = finish and not scaled
    if products:
        t_ref, s_refs, refs = refs[0], refs[1:5], refs[5:]
    if finish:
        near, near_y, cross, refs = refs[0], refs[1], refs[2], refs[3:]
        if products:
            dot_ref, refs = refs[0], refs[1:]
        z_acc, refs = refs[0], refs[1:]
    else:
        z_acc, refs = refs[0], refs[1:]
    w_all, refs = refs[0], refs[1:]
    kbuf, sems = (None, None) if cfg.resident else refs
    col = place[1]
    own_rows, block_len = cfg.own_rows, cfg.block_len

    z_acc[...] = z_in[...] if carried else jnp.zeros_like(z_acc)
    for part, listed, k_mat, piece in zip(parts, lists, ks, pieces):
        total = listed[0]
        held = piece.shape[0]

        def copy_in(g, k_mat=k_mat):
            slot = lax.rem(g, RING)
            return pltpu.make_async_copy(k_mat.at[g], kbuf.at[slot], sems.at[slot])

        if not cfg.resident:
            for p in range(RING - 1):

                @pl.when(p < total)
                def _(p=p, copy_in=copy_in):
                    copy_in(p).start()

        def prepare(n, carry, part=part, piece=piece):
            z = slot_of(cfg, place, n)
            for k in range(own_rows):
                w = piece[n, :, k * block_len:(k + 1) * block_len]
                if scaled:
                    at = row_of(cfg, place, part, z) * own_rows + k
                    w = (w * inv_ref[pl.ds(at, 1), :]).astype(BF16)
                w_all[z * own_rows + k] = w
            return carry

        lax.fori_loop(0, held, prepare, 0, unroll=held <= 4)

        def step(g, carry, total=total, listed=listed, k_mat=k_mat, copy_in=copy_in):
            slot, source = (g, k_mat) if cfg.resident else (lax.rem(g, RING), kbuf)
            if not cfg.resident:

                @pl.when(g + (RING - 1) < total)
                def _():
                    copy_in(g + (RING - 1)).start()

                copy_in(g).wait()
            codes = [listed[g * GROUP + u + 1] for u in range(GROUP)]
            terms = [
                lax.dot_general(
                    w_all[code & (CODE - 1)],
                    source[slot, u],
                    (((1,), (1,)), ((), ())),
                    preferred_element_type=F32,
                )
                for u, code in enumerate(codes)
            ]
            for code, term in zip(codes, terms):
                z_acc[lax.shift_right_logical(code, CODE_BITS)] += term
            return carry

        lax.fori_loop(0, total, step, 0)
    if not finish:
        return
    own_len = own_rows * block_len
    z_refs = (near, cross.at[0], near_y, cross.at[1])
    for e in range(4):
        for k in range(own_rows):
            z_refs[e][:, k * block_len:(k + 1) * block_len] = z_acc[(col ^ e) * own_rows + k]
    if products:
        outputs = t_ref.shape[0]
        ts2 = jnp.zeros((outputs, 1), F32)
        s1s2 = jnp.zeros((outputs, 1), F32)
        for e, packed in enumerate(s_refs):
            at = pl.ds(pl.multiple_of((col ^ e) * own_len, LANES), own_len)
            grown = z_refs[e][...] * packed[outputs:outputs + 1, :]
            ts2 += jnp.sum(t_ref[:, at] * grown, axis=1, keepdims=True)
            s1s2 += jnp.sum(packed[:outputs, :] * grown, axis=1, keepdims=True)
        t = t_ref[:, pl.ds(pl.multiple_of(col * own_len, LANES), own_len)]
        s1 = s_refs[0][:outputs, :]
        tt = jnp.sum(t * t, axis=1, keepdims=True)
        ts1 = jnp.sum(t * s1, axis=1, keepdims=True)
        s1s1 = jnp.sum(s1 * s1, axis=1, keepdims=True)
        ts2 += SHIFT * ts1
        s1s2 += SHIFT * s1s1
        lane = lax.broadcasted_iota(jnp.int32, (outputs, LANES), 1)
        out = jnp.zeros(lane.shape, F32)
        for n, v in enumerate((tt, ts1, s1s1, ts2, s1s2)):
            out = jnp.where(lane == n, v, out)
        dot_ref[...] = out


def final_kernel(n_cols, place, t_ref, *refs):
    s1s, s2s = refs[:4], refs[4:8]
    sol_ref, res_ref = refs[8:]
    outputs, own_len = s2s[0].shape[0], s2s[0].shape[1] - LANES
    dots = pair_sum([ref[:, own_len:] for ref in s2s])
    tt, ts1, s1s1, ts2, s1s2 = (dots[:, n:n + 1] for n in range(5))
    a1 = tt / (REG * tt + ts1)
    p = 1.0 - REG * a1
    new = p * p * tt - 2.0 * p * a1 * ts1 + a1 * a1 * s1s1
    u = p + new / tt
    dd = u * u * tt - 2.0 * u * a1 * ts1 + a1 * a1 * s1s1
    dmd = u * u * ts1 - u * a1 * (s1s1 + ts2) + a1 * a1 * s1s2
    a2 = new / (REG * dd + dmd)
    for e in range(n_cols):
        at = pl.ds(pl.multiple_of((place[1] ^ e) * own_len, LANES), own_len)
        t, s1, s2 = t_ref[:, at], s1s[e][:outputs, :], s2s[e][:, :own_len]
        sol_ref[:, at] = (a1 + a2 * u) * t - (a2 * a1) * s1
        res_ref[:, at] = (p - a2 * REG * u) * t - (a1 + a2 * (u - REG * a1)) * s1 + (a2 * a1) * s2


def swap(x, axis, d):
    size = lax.axis_size(axis)
    return lax.ppermute(x, axis, [(i, i ^ d) for i in range(size)])


def half_shared(near, near_y, cross):
    got = swap(cross, "cols", 1)
    return near + got[0], near_y + got[1]


def shared(near, near_y):
    return near + swap(near_y, "cols", 2)


def along_z(x):
    return [x] + [swap(x, "rows", d) for d in range(2, lax.axis_size("rows"), 2)]


def across_x(same):
    return [same, swap(same, "rows", 1)]


def direct_cols(x):
    return [x] + [swap(x, "cols", e) for e in range(1, 4)]


def local(block_list, points, targets):
    n_rows = lax.axis_size("rows")
    n_cols = lax.axis_size("cols")
    row = lax.axis_index("rows")
    col = lax.axis_index("cols")
    block_rows, slots = block_list.shape
    dim, npoints = points.shape
    outputs = targets.shape[0]
    block_len = npoints // block_rows
    own_rows = block_rows // n_cols
    own_len = own_rows * block_len
    nb = block_rows * n_rows
    n_sub = own_rows * n_rows
    capacity = -(-block_rows * slots // n_rows)
    direct_rows = n_rows <= DIRECT_ROWS
    parts = 2 if direct_rows else 1
    n_part = n_sub // parts
    bound = min(block_rows * n_part, n_cols * capacity * (n_rows + 1))
    n_groups = -(-bound // GROUP)
    list_len = n_groups * GROUP + GROUP + 1
    place = jnp.stack([row, col])
    k_shape = (n_groups, GROUP, block_len, block_len)
    resident = parts * 2 * n_groups * GROUP * block_len * block_len <= RESIDENT_BYTES
    limit = pltpu.CompilerParams(vmem_limit_bytes=(8 if resident else 32) * 1024 * 1024)
    ring = [] if resident else [
        pltpu.VMEM((RING, GROUP, block_len, block_len), BF16),
        pltpu.SemaphoreType.DMA((RING,)),
    ]
    k_spec = VMEM if resident else HBM
    cfg = Sizes(
        parts, resident, nb, block_len, own_rows, block_rows, -(-own_rows * nb // LANES)
    )

    def shape(*dims, dtype=F32):
        return jax.ShapeDtypeStruct(dims, dtype)

    def own(x):
        return lax.dynamic_slice_in_dim(x, col * own_len, own_len, 1)

    def total_rows(x):
        if direct_rows:
            return pair_sum(across_x(pair_sum(along_z(x))))
        return lax.psum(x, "rows")

    lists = direct_cols(block_list)
    names = jnp.arange(nb, dtype=jnp.int32)
    direct = sum(jnp.sum((x[:, :, None] == names).astype(jnp.int32), axis=1) for x in lists)
    own_counts = lax.dynamic_slice_in_dim(direct, col * own_rows, own_rows, 0)
    coded = own_counts.reshape(-1)
    coded = jnp.pad(coded, (0, dim * LANES - coded.shape[0])).reshape(dim, LANES).astype(BF16)
    packed = jnp.concatenate([own(points), coded], axis=1)
    own_t = own(targets)

    def build(part, *operands):
        first, last = part == 0, part == parts - 1
        out = [
            pltpu.VMEM(k_shape, BF16) if resident else shape(*k_shape, dtype=BF16),
            shape(list_len, dtype=jnp.int32),
            shape(n_sub if last else n_part, block_len),
        ]
        out += [shape(block_rows, block_len, 2 * dim, dtype=BF16)] if first else []
        k_mat, *rest = pl.pallas_call(
            functools.partial(build_kernel, cfg, part),
            out_shape=out,
            in_specs=[SMEM, SMEM] + ([HBM, VMEM] if first else [VMEM] * 3),
            out_specs=[k_spec, SMEM] + [VMEM] * (len(out) - 2),
            scratch_shapes=([
                pltpu.VMEM((dim, npoints), BF16),
                pltpu.SemaphoreType.DMA,
            ] if first else []) + [
                pltpu.SMEM((list_len,), jnp.int32),
                pltpu.VMEM((n_part, 8, block_len), F32),
                pltpu.VMEM((n_part, 2 * dim, block_len), BF16),
                pltpu.VMEM((n_part // own_rows, cfg.count_rows, LANES), jnp.int32),
                pltpu.SMEM((n_part // own_rows, cfg.count_rows, LANES), jnp.int32),
                pltpu.SemaphoreType.DMA,
                *ring,
            ],
            compiler_params=limit,
            cost_estimate=pl.CostEstimate(
                flops=2 * 2 * dim * bound * block_len * block_len,
                bytes_accessed=2 * bound * block_len * block_len,
                transcendentals=bound * block_len * block_len,
            ),
            name="build",
        )(place, direct, *operands)
        if resident:
            k_mat = pltpu.with_memory_space_constraint(k_mat, pltpu.VMEM)
        return k_mat, *rest

    near = pltpu.with_memory_space_constraint(points, pltpu.HBM)
    if direct_rows:
        packed, early_t = lax.optimization_barrier((packed, own_t))
        same, other = across_x(jnp.stack(along_z(packed)))
        t_same = along_z(early_t)
        k0, list0, degree, lhs = build(0, near, same)
        degree, other, *t_same = lax.optimization_barrier((degree, other, *t_same))
        t_same, t_other = across_x(jnp.stack(t_same))
        other, t_same = lax.optimization_barrier((other, t_same))
        k1, list1, degree = build(1, lhs, degree, other)
        degree, t_other = lax.optimization_barrier((degree, t_other))
        t_pieces, k_mats, k_lists = [t_same, t_other], [k0, k1], [list0, list1]
    else:
        k0, list0, degree, _ = build(0, near, lax.all_gather(packed, "rows"))
        t_pieces, k_mats, k_lists = [lax.all_gather(own_t, "rows")], [k0], [list0]
    inv = 1.0 / jnp.sqrt(1.0 + total_rows(degree))
    own_inv = lax.dynamic_slice_in_dim(inv, row * own_rows, own_rows, 0).reshape(1, own_len)

    def apply(use, pieces, finish=True, inv=None, z_in=None, products=()):
        spare = [k for p, k in enumerate(k_mats) if p not in use]
        operands = [k_lists[p] for p in use] + [k_mats[p] for p in use] + pieces + spare
        specs = [SMEM] * len(use) + [k_spec] * len(use) + [VMEM] * len(pieces) + [k_spec] * len(spare)
        more = [x for x in (inv, z_in) if x is not None] + list(products)
        z_shape = (block_rows, outputs, block_len)
        if finish:
            out = [shape(outputs, own_len), shape(outputs, own_len), shape(2, outputs, own_len)]
            out += [shape(outputs, LANES)] if products else []
        else:
            out = [shape(*z_shape)]
        return pl.pallas_call(
            functools.partial(
                apply_kernel, cfg, use, inv is not None, z_in is not None, finish, len(spare)
            ),
            out_shape=out,
            in_specs=[SMEM] + specs + [VMEM] * len(more),
            out_specs=[VMEM] * len(out),
            scratch_shapes=([pltpu.VMEM(z_shape, F32)] if finish else []) + [
                pltpu.VMEM((n_part, outputs, block_len), BF16),
                *ring,
            ],
            compiler_params=limit,
            cost_estimate=pl.CostEstimate(
                flops=2 * len(use) * bound * outputs * block_len * block_len,
                bytes_accessed=len(use) * bound * block_len * block_len,
                transcendentals=0,
            ),
            name="apply",
        )(place, *operands, *more)

    s1 = shared(*half_shared(*apply(tuple(range(parts)), t_pieces, inv=inv))) * own_inv
    g = ((s1 - SHIFT * own_t) * own_inv).astype(BF16)
    s1_packed = jnp.concatenate([s1, jnp.broadcast_to(own_inv, (8, own_len))], axis=0)
    if direct_rows:
        g_same = jnp.stack(along_z(g))
        g_same, s1_packed = lax.optimization_barrier((g_same, s1_packed))
        _, g_other = across_x(g_same)
        s1_all = direct_cols(s1_packed)
        (z_part,) = apply((0,), [g_same], finish=False)
        z_part, g_other, *s1_all = lax.optimization_barrier((z_part, g_other, *s1_all))
        *z2, dots = apply((1,), [g_other], z_in=z_part, products=[targets, *s1_all])
        z2 = half_shared(*z2)
        dots = pair_sum(across_x(dots))
        dots, *z2 = lax.optimization_barrier((dots, *z2))
        s2 = shared(*z2)
        dots = pair_sum(along_z(dots))
    else:
        s1_all = direct_cols(s1_packed)
        *z2, dots = apply((0,), [lax.all_gather(g, "rows")], products=[targets, *s1_all])
        s2 = shared(*half_shared(*z2))
        dots = lax.psum(dots, "rows")
    s2 = s2 * own_inv + SHIFT * s1
    ends = direct_cols(jnp.concatenate([s2, dots], axis=1))
    s1_all, ends = [
        [pltpu.with_memory_space_constraint(x, pltpu.VMEM) for x in xs] for xs in (s1_all, ends)
    ]

    return pl.pallas_call(
        functools.partial(final_kernel, n_cols),
        out_shape=(shape(outputs, npoints), shape(outputs, npoints)),
        in_specs=[SMEM] + [VMEM] * 9,
        out_specs=(VMEM, VMEM),
        name="final",
    )(place, targets, *s1_all, *ends)


def solution(mesh):
    placed = (P("rows", "cols"), P(None, "rows"), P(None, "rows"))
    return jax.shard_map(
        local,
        mesh=mesh,
        in_specs=placed,
        out_specs=(P(None, "rows"), P(None, "rows")),
        check_vma=False,
    )
```

```python
import functools
from typing import NamedTuple

import jax
import jax.numpy as jnp
from jax import lax
from jax.experimental import pallas as pl
from jax.experimental.pallas import tpu as pltpu
from jax.sharding import PartitionSpec as P

REG = 1.5
RADIUS = 0.25
GROUP_BITS = 2
GROUP = 1 << GROUP_BITS
CODE_BITS = 12
CODE = 1 << CODE_BITS
RING = 3
STRIP = 64
LANES = 128
TINY = 1e-30
SHIFT = 0.375
DIRECT_ROWS = 8
ROOM_GROUPS = 8
RESIDENT_BYTES = 20 * 1024 * 1024

SMEM = pl.BlockSpec(memory_space=pltpu.SMEM)
VMEM = pl.BlockSpec(memory_space=pltpu.VMEM)
HBM = pl.BlockSpec(memory_space=pltpu.HBM)
F32 = jnp.float32
BF16 = jnp.bfloat16


def pair_sum(parts):
    while len(parts) > 1:
        parts = [a + b for a, b in zip(parts[::2], parts[1::2])]
    return parts[0]


class Sizes(NamedTuple):
    parts: int
    part_groups: int
    resident: bool
    nb: int
    block_len: int
    own_rows: int
    block_rows: int
    count_rows: int


def augment(x, first_ones):
    dim, n = x.shape
    norm = jnp.sum(x * x, axis=0, keepdims=True) / (RADIUS * RADIUS)
    high = norm.astype(BF16).astype(F32)
    rest = norm - high
    mid = rest.astype(BF16).astype(F32)
    low = rest - mid
    line = lax.broadcasted_iota(jnp.int32, (dim, n), 0)
    base = 3 if first_ones else 0
    ones_at = 0 if first_ones else 3
    tail = jnp.where((line >= ones_at) & (line < ones_at + 3), 1.0, 0.0)
    tail = jnp.where(line == base, high, tail)
    tail = jnp.where(line == base + 1, mid, tail)
    tail = jnp.where(line == base + 2, low, tail)
    return tail


def row_of(cfg, place, part, z):
    if cfg.parts == 1:
        return z
    return 2 * z + (place[0] & 1 if part == 0 else 1 - (place[0] & 1))


def slot_of(cfg, place, n):
    return n if cfg.parts == 1 else lax.shift_right_logical(place[0], 1) ^ n


def build_kernel(cfg, part, place, direct, *refs):
    last = part == cfg.parts - 1
    if part == 0:
        near_hbm, piece, refs = refs[0], refs[1], refs[2:]
        k_mat, listed, deg_ref, lhs = refs[:4]
        near_ref, near_sem, refs = refs[4], refs[5], refs[6:]
        near_copy = pltpu.make_async_copy(near_hbm, near_ref, near_sem)
        near_copy.start()
    else:
        lhs, first_deg, piece, _ = refs[:4]
        k_mat, listed, deg_ref = refs[4:7]
        refs = refs[7:]
    mlist, acc, rhs, counts_v, counts, count_sem = refs[:6]
    kbuf, sems = (None, None) if cfg.resident else refs[6:]
    row, col = place[0], place[1]
    own_rows, block_len, nb = cfg.own_rows, cfg.block_len, cfg.nb
    own_len = own_rows * block_len
    dim, held = piece.shape[1], piece.shape[0]
    scale = 1.0 / (RADIUS * RADIUS)

    def prepare(n, carry):
        z = slot_of(cfg, place, n)
        for k in range(own_rows):
            far = piece[n, :, k * block_len:(k + 1) * block_len]
            rhs[z * own_rows + k, :dim, :] = far
            rhs[z * own_rows + k, dim:, :] = augment(far.astype(F32), False).astype(BF16)
        named = piece[n, :, own_len:own_len + LANES]
        counts_v[z] = named.astype(F32)[:cfg.count_rows].astype(jnp.int32)
        return carry

    lax.fori_loop(0, held, prepare, 0, unroll=held <= 4)
    fetch = pltpu.make_async_copy(counts_v, counts, count_sem)
    fetch.start()
    if part == 0:
        near_copy.wait()
        for i in range(cfg.block_rows):
            near = near_ref[:, i * block_len:(i + 1) * block_len].astype(F32)
            full = jnp.concatenate([near * (-2.0 * scale), augment(near, True)], axis=0)
            lhs[i] = full.T.astype(BF16)
    acc[...] = jnp.zeros_like(acc)
    fetch.wait()

    pos = jnp.int32(0)
    for i in range(cfg.block_rows):
        me = row * cfg.block_rows + i
        spots = [k * nb + me for k in range(own_rows)]
        spots = [(lax.shift_right_logical(p, 7), p & (LANES - 1)) for p in spots]

        def note(z, at, i=i, me=me, spots=spots):
            for k in range(own_rows):
                name = row_of(cfg, place, part, z) * cfg.block_rows + col * own_rows + k
                m = direct[i, name] + jnp.where(name == me, 0, counts[z, spots[k][0], spots[k][1]])
                listed[at + 1] = i * CODE + z * own_rows + k
                mlist[at] = m
                at = at + jnp.where(m > 0, 1, 0)
            return at

        pos = lax.fori_loop(0, held, note, pos, unroll=4)
    for u in range(GROUP):
        listed[pos + u + 1] = 0
        mlist[pos + u] = 0
    total = lax.shift_right_logical(pos + (GROUP - 1), GROUP_BITS)
    listed[0] = total

    def copy_out(g):
        slot = lax.rem(g, RING)
        return pltpu.make_async_copy(kbuf.at[slot], k_mat.at[g], sems.at[slot])

    base = part * cfg.part_groups

    def step(g, carry):
        slot, target = (base + g, k_mat) if cfg.resident else (lax.rem(g, RING), kbuf)
        if not cfg.resident:

            @pl.when(g >= RING)
            def _():
                copy_out(g - RING).wait()

        for u in range(GROUP):
            code = listed[g * GROUP + u + 1]
            i, j = lax.shift_right_logical(code, CODE_BITS), code & (CODE - 1)
            m = mlist[g * GROUP + u].astype(F32)
            far = rhs[j]
            sums = jnp.zeros((8, block_len), F32)
            for s in range(block_len // STRIP):
                rows = slice(s * STRIP, (s + 1) * STRIP)
                d = jnp.dot(lhs[i, rows, :], far, preferred_element_type=F32)
                d = jnp.maximum(d, TINY)
                sc = d * lax.rsqrt(d)
                rem = jnp.maximum(1.0 - sc, 0.0)
                sq = rem * rem
                val = (sq * sq) * (sc * (4.0 * m) + m)
                target[slot, u, rows, :] = val.astype(BF16)
                for h in range(0, STRIP, 8):
                    sums = sums + val[h:h + 8]
            acc[j] += sums
        if not cfg.resident:
            copy_out(g).start()
        return carry

    lax.fori_loop(0, total, step, 0)
    if cfg.parts == 1 or not last:
        deg_ref[...] = jnp.sum(acc[...], axis=1)
    else:
        second = jnp.sum(acc[...], axis=1)
        for z in range(held):
            rows = slice(z * own_rows, (z + 1) * own_rows)
            for p, deg in enumerate((first_deg[rows, :], second[rows])):
                at = row_of(cfg, place, p, z) * own_rows
                for k in range(own_rows):
                    deg_ref[pl.ds(at + k, 1), :] = deg[k:k + 1]

    def drain(g, carry):
        copy_out(g).wait()
        return carry

    if not cfg.resident:
        lax.fori_loop(jnp.maximum(total - RING, 0), total, drain, 0)


def apply_kernel(cfg, parts, scaled, carried, finish, place, k_mat, *refs):
    n = len(parts)
    lists, pieces, refs = refs[:n], refs[n:2 * n], refs[2 * n:]
    if scaled:
        inv_ref, refs = refs[0], refs[1:]
    if carried:
        z_in, refs = refs[0], refs[1:]
    products = finish and not scaled
    if products:
        t_ref, s_refs, refs = refs[0], refs[1:5], refs[5:]
    if finish:
        near, near_y, cross, refs = refs[0], refs[1], refs[2], refs[3:]
        if products:
            dot_ref, refs = refs[0], refs[1:]
        z_acc, refs = refs[0], refs[1:]
    else:
        z_acc, refs = refs[0], refs[1:]
    w_all, refs = refs[0], refs[1:]
    kbuf, sems = (None, None) if cfg.resident else refs
    col = place[1]
    own_rows, block_len = cfg.own_rows, cfg.block_len

    z_acc[...] = z_in[...] if carried else jnp.zeros_like(z_acc)
    for part, listed, piece in zip(parts, lists, pieces):
        total = listed[0]
        base = part * cfg.part_groups
        held = piece.shape[0]

        def copy_in(g):
            slot = lax.rem(g, RING)
            return pltpu.make_async_copy(k_mat.at[g], kbuf.at[slot], sems.at[slot])

        if not cfg.resident:
            for p in range(RING - 1):

                @pl.when(p < total)
                def _(p=p, copy_in=copy_in):
                    copy_in(p).start()

        def prepare(n, carry, part=part, piece=piece):
            z = slot_of(cfg, place, n)
            for k in range(own_rows):
                w = piece[n, :, k * block_len:(k + 1) * block_len]
                if scaled:
                    at = row_of(cfg, place, part, z) * own_rows + k
                    w = (w * inv_ref[pl.ds(at, 1), :]).astype(BF16)
                w_all[z * own_rows + k] = w
            return carry

        lax.fori_loop(0, held, prepare, 0, unroll=held <= 4)

        def step(g, carry, total=total, listed=listed, base=base, copy_in=copy_in):
            slot, source = (base + g, k_mat) if cfg.resident else (lax.rem(g, RING), kbuf)
            if not cfg.resident:

                @pl.when(g + (RING - 1) < total)
                def _():
                    copy_in(g + (RING - 1)).start()

                copy_in(g).wait()
            codes = [listed[g * GROUP + u + 1] for u in range(GROUP)]
            terms = [
                lax.dot_general(
                    w_all[code & (CODE - 1)],
                    source[slot, u],
                    (((1,), (1,)), ((), ())),
                    preferred_element_type=F32,
                )
                for u, code in enumerate(codes)
            ]
            for code, term in zip(codes, terms):
                z_acc[lax.shift_right_logical(code, CODE_BITS)] += term
            return carry

        lax.fori_loop(0, total, step, 0)
    if not finish:
        return
    own_len = own_rows * block_len
    z_refs = (near, cross.at[0], near_y, cross.at[1])
    for e in range(4):
        for k in range(own_rows):
            z_refs[e][:, k * block_len:(k + 1) * block_len] = z_acc[(col ^ e) * own_rows + k]
    if products:
        outputs = t_ref.shape[0]
        ts2 = jnp.zeros((outputs, 1), F32)
        s1s2 = jnp.zeros((outputs, 1), F32)
        for e, packed in enumerate(s_refs):
            at = pl.ds(pl.multiple_of((col ^ e) * own_len, LANES), own_len)
            grown = z_refs[e][...] * packed[outputs:outputs + 1, :]
            ts2 += jnp.sum(t_ref[:, at] * grown, axis=1, keepdims=True)
            s1s2 += jnp.sum(packed[:outputs, :] * grown, axis=1, keepdims=True)
        t = t_ref[:, pl.ds(pl.multiple_of(col * own_len, LANES), own_len)]
        s1 = s_refs[0][:outputs, :]
        tt = jnp.sum(t * t, axis=1, keepdims=True)
        ts1 = jnp.sum(t * s1, axis=1, keepdims=True)
        s1s1 = jnp.sum(s1 * s1, axis=1, keepdims=True)
        ts2 += SHIFT * ts1
        s1s2 += SHIFT * s1s1
        lane = lax.broadcasted_iota(jnp.int32, (outputs, LANES), 1)
        out = jnp.zeros(lane.shape, F32)
        for n, v in enumerate((tt, ts1, s1s1, ts2, s1s2)):
            out = jnp.where(lane == n, v, out)
        dot_ref[...] = out


def first_kernel(near, far, inv_ref, t_ref, k_mat, s_ref, g_ref):
    outputs = t_ref.shape[0]
    inv = inv_ref[...]
    s = (near[...] + far[...]) * inv
    s_ref[:outputs, :] = s
    s_ref[outputs:, :] = jnp.broadcast_to(inv, (8, inv.shape[1]))
    g_ref[...] = ((s - SHIFT * t_ref[...]) * inv).astype(BF16)


def final_kernel(n_cols, place, t_ref, *refs):
    s1s, s2s = refs[:4], refs[4:8]
    sol_ref, res_ref = refs[8:]
    outputs, own_len = s2s[0].shape[0], s2s[0].shape[1] - LANES
    dots = pair_sum([ref[:, own_len:] for ref in s2s])
    tt, ts1, s1s1, ts2, s1s2 = (dots[:, n:n + 1] for n in range(5))
    a1 = tt / (REG * tt + ts1)
    p = 1.0 - REG * a1
    new = p * p * tt - 2.0 * p * a1 * ts1 + a1 * a1 * s1s1
    u = p + new / tt
    dd = u * u * tt - 2.0 * u * a1 * ts1 + a1 * a1 * s1s1
    dmd = u * u * ts1 - u * a1 * (s1s1 + ts2) + a1 * a1 * s1s2
    a2 = new / (REG * dd + dmd)
    for e in range(n_cols):
        at = pl.ds(pl.multiple_of((place[1] ^ e) * own_len, LANES), own_len)
        t, s1, s2 = t_ref[:, at], s1s[e][:outputs, :], s2s[e][:, :own_len]
        sol_ref[:, at] = (a1 + a2 * u) * t - (a2 * a1) * s1
        res_ref[:, at] = (p - a2 * REG * u) * t - (a1 + a2 * (u - REG * a1)) * s1 + (a2 * a1) * s2


def swap(x, axis, d):
    size = lax.axis_size(axis)
    return lax.ppermute(x, axis, [(i, i ^ d) for i in range(size)])


def half_shared(near, near_y, cross):
    got = swap(cross, "cols", 1)
    return near + got[0], near_y + got[1]


def shared(near, near_y):
    return near + swap(near_y, "cols", 2)


def along_z(x):
    return [x] + [swap(x, "rows", d) for d in range(2, lax.axis_size("rows"), 2)]


def across_x(same):
    return [same, swap(same, "rows", 1)]


def direct_cols(x):
    return [x] + [swap(x, "cols", e) for e in range(1, 4)]


def local(block_list, points, targets):
    n_rows = lax.axis_size("rows")
    n_cols = lax.axis_size("cols")
    row = lax.axis_index("rows")
    col = lax.axis_index("cols")
    block_rows, slots = block_list.shape
    dim, npoints = points.shape
    outputs = targets.shape[0]
    block_len = npoints // block_rows
    own_rows = block_rows // n_cols
    own_len = own_rows * block_len
    nb = block_rows * n_rows
    n_sub = own_rows * n_rows
    capacity = -(-block_rows * slots // n_rows)
    direct_rows = n_rows <= DIRECT_ROWS
    parts = 2 if direct_rows else 1
    n_part = n_sub // parts
    bound = min(block_rows * n_part, n_cols * capacity * (n_rows + 1))
    n_groups = -(-bound // GROUP)
    list_len = n_groups * GROUP + GROUP + 1
    place = jnp.stack([row, col])
    resident = parts * 2 * n_groups * GROUP * block_len * block_len <= RESIDENT_BYTES
    room = ROOM_GROUPS if resident else 0
    k_shape = (parts * n_groups + room, GROUP, block_len, block_len)
    limit = pltpu.CompilerParams(vmem_limit_bytes=(8 if resident else 32) * 1024 * 1024)
    ring = [] if resident else [
        pltpu.VMEM((RING, GROUP, block_len, block_len), BF16),
        pltpu.SemaphoreType.DMA((RING,)),
    ]
    k_spec = VMEM if resident else HBM
    cfg = Sizes(
        parts, n_groups, resident, nb, block_len, own_rows, block_rows, -(-own_rows * nb // LANES)
    )

    def shape(*dims, dtype=F32):
        return jax.ShapeDtypeStruct(dims, dtype)

    def own(x):
        return lax.dynamic_slice_in_dim(x, col * own_len, own_len, 1)

    def total_rows(x):
        if direct_rows:
            return pair_sum(across_x(pair_sum(along_z(x))))
        return lax.psum(x, "rows")

    lists = direct_cols(block_list)
    names = jnp.arange(nb, dtype=jnp.int32)
    direct = sum(jnp.sum((x[:, :, None] == names).astype(jnp.int32), axis=1) for x in lists)
    own_counts = lax.dynamic_slice_in_dim(direct, col * own_rows, own_rows, 0)
    coded = own_counts.reshape(-1)
    coded = jnp.pad(coded, (0, dim * LANES - coded.shape[0])).reshape(dim, LANES).astype(BF16)
    packed = jnp.concatenate([own(points), coded], axis=1)
    own_t = own(targets)

    def build(part, *operands):
        first, last = part == 0, part == parts - 1
        out = [
            pltpu.VMEM(k_shape, BF16) if resident else shape(*k_shape, dtype=BF16),
            shape(list_len, dtype=jnp.int32),
            shape(n_sub if last else n_part, block_len),
        ]
        out += [shape(block_rows, block_len, 2 * dim, dtype=BF16)] if first else []
        k_mat, *rest = pl.pallas_call(
            functools.partial(build_kernel, cfg, part),
            out_shape=out,
            in_specs=[SMEM, SMEM] + ([HBM, VMEM] if first else [VMEM] * 3 + [k_spec]),
            out_specs=[k_spec, SMEM] + [VMEM] * (len(out) - 2),
            scratch_shapes=([
                pltpu.VMEM((dim, npoints), BF16),
                pltpu.SemaphoreType.DMA,
            ] if first else []) + [
                pltpu.SMEM((list_len,), jnp.int32),
                pltpu.VMEM((n_part, 8, block_len), F32),
                pltpu.VMEM((n_part, 2 * dim, block_len), BF16),
                pltpu.VMEM((n_part // own_rows, cfg.count_rows, LANES), jnp.int32),
                pltpu.SMEM((n_part // own_rows, cfg.count_rows, LANES), jnp.int32),
                pltpu.SemaphoreType.DMA,
                *ring,
            ],
            compiler_params=limit,
            input_output_aliases={} if first else {5: 0},
            cost_estimate=pl.CostEstimate(
                flops=2 * 2 * dim * bound * block_len * block_len,
                bytes_accessed=2 * bound * block_len * block_len,
                transcendentals=bound * block_len * block_len,
            ),
            name="build",
        )(place, direct, *operands)
        if resident:
            k_mat = pltpu.with_memory_space_constraint(k_mat, pltpu.VMEM)
        return k_mat, *rest

    near = pltpu.with_memory_space_constraint(points, pltpu.HBM)
    if direct_rows:
        packed, early_t = lax.optimization_barrier((packed, own_t))
        same, other = across_x(jnp.stack(along_z(packed)))
        t_same = along_z(early_t)
        k_mat, list0, degree, lhs = build(0, near, same)
        degree, other, *t_same = lax.optimization_barrier((degree, other, *t_same))
        t_same, t_other = across_x(jnp.stack(t_same))
        other, t_same = lax.optimization_barrier((other, t_same))
        k_mat, list1, degree = build(1, lhs, degree, other, k_mat)
        degree, t_other = lax.optimization_barrier((degree, t_other))
        t_pieces, k_lists = [t_same, t_other], [list0, list1]
    else:
        k_mat, list0, degree, _ = build(0, near, lax.all_gather(packed, "rows"))
        t_pieces, k_lists = [lax.all_gather(own_t, "rows")], [list0]
    inv = 1.0 / jnp.sqrt(1.0 + total_rows(degree))
    own_inv = lax.dynamic_slice_in_dim(inv, row * own_rows, own_rows, 0).reshape(1, own_len)

    def apply(use, pieces, finish=True, inv=None, z_in=None, products=()):
        operands = [k_mat] + [k_lists[p] for p in use] + pieces
        specs = [k_spec] + [SMEM] * len(use) + [VMEM] * len(pieces)
        more = [x for x in (inv, z_in) if x is not None] + list(products)
        z_shape = (block_rows, outputs, block_len)
        if finish:
            out = [shape(outputs, own_len), shape(outputs, own_len), shape(2, outputs, own_len)]
            out += [shape(outputs, LANES)] if products else []
        else:
            out = [shape(*z_shape)]
        return pl.pallas_call(
            functools.partial(
                apply_kernel, cfg, use, inv is not None, z_in is not None, finish
            ),
            out_shape=out,
            in_specs=[SMEM] + specs + [VMEM] * len(more),
            out_specs=[VMEM] * len(out),
            scratch_shapes=([pltpu.VMEM(z_shape, F32)] if finish else []) + [
                pltpu.VMEM((n_part, outputs, block_len), BF16),
                *ring,
            ],
            compiler_params=limit,
            cost_estimate=pl.CostEstimate(
                flops=2 * len(use) * bound * outputs * block_len * block_len,
                bytes_accessed=len(use) * bound * block_len * block_len,
                transcendentals=0,
            ),
            name="apply",
        )(place, *operands, *more)

    z1, z1_y = half_shared(*apply(tuple(range(parts)), t_pieces, inv=inv))
    s1_packed, g = pl.pallas_call(
        first_kernel,
        out_shape=(shape(outputs + 8, own_len), shape(outputs, own_len, dtype=BF16)),
        in_specs=[VMEM] * 4 + [k_spec],
        out_specs=(VMEM, VMEM),
        compiler_params=limit,
        name="first",
    )(z1, swap(z1_y, "cols", 2), own_inv, own_t, k_mat)
    s1 = s1_packed[:outputs]
    if direct_rows:
        g_same = jnp.stack(along_z(g))
        g_same, s1_packed = lax.optimization_barrier((g_same, s1_packed))
        _, g_other = across_x(g_same)
        s1_all = direct_cols(s1_packed)
        (z_part,) = apply((0,), [g_same], finish=False)
        z_part, g_other, *s1_all = lax.optimization_barrier((z_part, g_other, *s1_all))
        *z2, dots = apply((1,), [g_other], z_in=z_part, products=[targets, *s1_all])
        dots = pair_sum(along_z(dots))
        s2 = shared(*half_shared(*z2))
        dots = pair_sum(across_x(dots))
    else:
        s1_all = direct_cols(s1_packed)
        *z2, dots = apply((0,), [lax.all_gather(g, "rows")], products=[targets, *s1_all])
        s2 = shared(*half_shared(*z2))
        dots = lax.psum(dots, "rows")
    s2 = s2 * own_inv + SHIFT * s1
    ends = direct_cols(jnp.concatenate([s2, dots], axis=1))
    s1_all, ends = [
        [pltpu.with_memory_space_constraint(x, pltpu.VMEM) for x in xs] for xs in (s1_all, ends)
    ]

    return pl.pallas_call(
        functools.partial(final_kernel, n_cols),
        out_shape=(shape(outputs, npoints), shape(outputs, npoints)),
        in_specs=[SMEM] + [VMEM] * 9,
        out_specs=(VMEM, VMEM),
        name="final",
    )(place, targets, *s1_all, *ends)


def solution(mesh):
    placed = (P("rows", "cols"), P(None, "rows"), P(None, "rows"))
    return jax.shard_map(
        local,
        mesh=mesh,
        in_specs=placed,
        out_specs=(P(None, "rows"), P(None, "rows")),
        check_vma=False,
    )
```

```python
import functools
from typing import NamedTuple

import jax
import jax.numpy as jnp
from jax import lax
from jax.experimental import pallas as pl
from jax.experimental.pallas import tpu as pltpu
from jax.sharding import PartitionSpec as P

REG = 1.5
RADIUS = 0.25
GROUP_BITS = 2
GROUP = 1 << GROUP_BITS
CODE_BITS = 12
CODE = 1 << CODE_BITS
RING = 3
STRIP = 32
LANES = 128
TINY = 1e-30
SHIFT = 0.375
DIRECT_ROWS = 8
RESIDENT_BYTES = 20 * 1024 * 1024

SMEM = pl.BlockSpec(memory_space=pltpu.SMEM)
VMEM = pl.BlockSpec(memory_space=pltpu.VMEM)
HBM = pl.BlockSpec(memory_space=pltpu.HBM)
F32 = jnp.float32
BF16 = jnp.bfloat16


def pair_sum(parts):
    while len(parts) > 1:
        parts = [a + b for a, b in zip(parts[::2], parts[1::2])]
    return parts[0]


class Sizes(NamedTuple):
    parts: int
    part_groups: int
    resident: bool
    nb: int
    block_len: int
    own_rows: int
    block_rows: int
    count_rows: int


def augment(x, first_ones):
    dim, n = x.shape
    norm = jnp.sum(x * x, axis=0, keepdims=True) / (RADIUS * RADIUS)
    high = norm.astype(BF16).astype(F32)
    rest = norm - high
    mid = rest.astype(BF16).astype(F32)
    low = rest - mid
    line = lax.broadcasted_iota(jnp.int32, (dim, n), 0)
    base = 3 if first_ones else 0
    ones_at = 0 if first_ones else 3
    tail = jnp.where((line >= ones_at) & (line < ones_at + 3), 1.0, 0.0)
    tail = jnp.where(line == base, high, tail)
    tail = jnp.where(line == base + 1, mid, tail)
    tail = jnp.where(line == base + 2, low, tail)
    return tail


def row_of(cfg, place, part, z):
    if cfg.parts == 1:
        return z
    return 2 * z + (place[0] & 1 if part == 0 else 1 - (place[0] & 1))


def slot_of(cfg, place, n):
    return n if cfg.parts == 1 else lax.shift_right_logical(place[0], 1) ^ n


def build_kernel(cfg, part, place, direct, *refs):
    last = part == cfg.parts - 1
    if part == 0:
        near_hbm, piece, refs = refs[0], refs[1], refs[2:]
        k_mat, listed, deg_ref, lhs = refs[:4]
        near_ref, near_sem, refs = refs[4], refs[5], refs[6:]
        near_copy = pltpu.make_async_copy(near_hbm, near_ref, near_sem)
        near_copy.start()
    else:
        lhs, first_deg, piece, _ = refs[:4]
        k_mat, listed, deg_ref = refs[4:7]
        refs = refs[7:]
    mlist, acc, rhs, counts_v, counts, count_sem = refs[:6]
    kbuf, sems = (None, None) if cfg.resident else refs[6:]
    row, col = place[0], place[1]
    own_rows, block_len, nb = cfg.own_rows, cfg.block_len, cfg.nb
    own_len = own_rows * block_len
    dim, held = piece.shape[1], piece.shape[0]
    scale = 1.0 / (RADIUS * RADIUS)

    def prepare(n, carry):
        z = slot_of(cfg, place, n)
        for k in range(own_rows):
            far = piece[n, :, k * block_len:(k + 1) * block_len]
            rhs[z * own_rows + k, :dim, :] = far
            rhs[z * own_rows + k, dim:, :] = augment(far.astype(F32), False).astype(BF16)
        named = piece[n, :, own_len:own_len + LANES]
        counts_v[z] = named.astype(F32)[:cfg.count_rows].astype(jnp.int32)
        return carry

    lax.fori_loop(0, held, prepare, 0, unroll=held <= 4)
    fetch = pltpu.make_async_copy(counts_v, counts, count_sem)
    fetch.start()
    if part == 0:
        near_copy.wait()
        for i in range(cfg.block_rows):
            near = near_ref[:, i * block_len:(i + 1) * block_len].astype(F32)
            full = jnp.concatenate([near * (-2.0 * scale), augment(near, True)], axis=0)
            lhs[i] = full.T.astype(BF16)
    acc[...] = jnp.zeros_like(acc)
    fetch.wait()

    pos = jnp.int32(0)
    for i in range(cfg.block_rows):
        me = row * cfg.block_rows + i
        spots = [k * nb + me for k in range(own_rows)]
        spots = [(lax.shift_right_logical(p, 7), p & (LANES - 1)) for p in spots]

        def note(z, at, i=i, me=me, spots=spots):
            for k in range(own_rows):
                name = row_of(cfg, place, part, z) * cfg.block_rows + col * own_rows + k
                m = direct[i, name] + jnp.where(name == me, 0, counts[z, spots[k][0], spots[k][1]])
                listed[at + 1] = i * CODE + z * own_rows + k
                mlist[at] = m
                at = at + jnp.where(m > 0, 1, 0)
            return at

        pos = lax.fori_loop(0, held, note, pos, unroll=4)
    for u in range(GROUP):
        listed[pos + u + 1] = 0
        mlist[pos + u] = 0
    total = lax.shift_right_logical(pos + (GROUP - 1), GROUP_BITS)
    listed[0] = total

    def copy_out(g):
        slot = lax.rem(g, RING)
        return pltpu.make_async_copy(kbuf.at[slot], k_mat.at[g], sems.at[slot])

    base = part * cfg.part_groups

    def step(g, carry):
        slot, target = (base + g, k_mat) if cfg.resident else (lax.rem(g, RING), kbuf)
        if not cfg.resident:

            @pl.when(g >= RING)
            def _():
                copy_out(g - RING).wait()

        for u in range(GROUP):
            code = listed[g * GROUP + u + 1]
            i, j = lax.shift_right_logical(code, CODE_BITS), code & (CODE - 1)
            m = mlist[g * GROUP + u].astype(F32)
            dist = jnp.dot(lhs[i], rhs[j], preferred_element_type=F32)
            sums = jnp.zeros((8, block_len), F32)
            for s in range(block_len // STRIP):
                rows = slice(s * STRIP, (s + 1) * STRIP)
                d = jnp.maximum(dist[rows], TINY)
                sc = d * lax.rsqrt(d)
                rem = jnp.maximum(1.0 - sc, 0.0)
                sq = rem * rem
                val = (sq * sq) * (sc * (4.0 * m) + m)
                target[slot, u, rows, :] = val.astype(BF16)
                for h in range(0, STRIP, 8):
                    sums = sums + val[h:h + 8]
            acc[j] += sums
        if not cfg.resident:
            copy_out(g).start()
        return carry

    lax.fori_loop(0, total, step, 0)
    if cfg.parts == 1 or not last:
        deg_ref[...] = jnp.sum(acc[...], axis=1)
    else:
        second = jnp.sum(acc[...], axis=1)
        for z in range(held):
            rows = slice(z * own_rows, (z + 1) * own_rows)
            for p, deg in enumerate((first_deg[rows, :], second[rows])):
                at = row_of(cfg, place, p, z) * own_rows
                for k in range(own_rows):
                    deg_ref[pl.ds(at + k, 1), :] = deg[k:k + 1]

    def drain(g, carry):
        copy_out(g).wait()
        return carry

    if not cfg.resident:
        lax.fori_loop(jnp.maximum(total - RING, 0), total, drain, 0)


def pieces_of(own, got):
    return own.at[0], got.at[0], own.at[1], got.at[1]


def apply_kernel(cfg, parts, scaled, carried, finish, place, k_mat, *refs):
    n = len(parts)
    lists, pieces, refs = refs[:n], refs[n:2 * n], refs[2 * n:]
    if scaled:
        inv_ref, refs = refs[0], refs[1:]
    if carried:
        z_in, refs = refs[0], refs[1:]
    products = finish and not scaled
    if products:
        t_ref, s_refs, refs = refs[0], pieces_of(refs[1], refs[2]), refs[3:]
    if products:
        near, near_y, cross, dot_ref, z_acc, refs = *refs[:5], refs[5:]
        z_refs = (near, cross.at[0], near_y, cross.at[1])
    elif finish:
        near, cross, z_acc, refs = *refs[:3], refs[3:]
    else:
        z_acc, refs = refs[0], refs[1:]
    w_all, refs = refs[0], refs[1:]
    kbuf, sems = (None, None) if cfg.resident else refs
    col = place[1]
    own_rows, block_len = cfg.own_rows, cfg.block_len

    z_acc[...] = z_in[...] if carried else jnp.zeros_like(z_acc)
    for part, listed, piece in zip(parts, lists, pieces):
        total = listed[0]
        base = part * cfg.part_groups
        held = piece.shape[0]

        def copy_in(g):
            slot = lax.rem(g, RING)
            return pltpu.make_async_copy(k_mat.at[g], kbuf.at[slot], sems.at[slot])

        if not cfg.resident:
            for p in range(RING - 1):

                @pl.when(p < total)
                def _(p=p, copy_in=copy_in):
                    copy_in(p).start()

        def prepare(n, carry, part=part, piece=piece):
            z = slot_of(cfg, place, n)
            for k in range(own_rows):
                w = piece[n, :, k * block_len:(k + 1) * block_len]
                if scaled:
                    at = row_of(cfg, place, part, z) * own_rows + k
                    w = (w * inv_ref[pl.ds(at, 1), :]).astype(BF16)
                w_all[z * own_rows + k] = w
            return carry

        lax.fori_loop(0, held, prepare, 0, unroll=held <= 4)

        def step(g, carry, total=total, listed=listed, base=base, copy_in=copy_in):
            slot, source = (base + g, k_mat) if cfg.resident else (lax.rem(g, RING), kbuf)
            if not cfg.resident:

                @pl.when(g + (RING - 1) < total)
                def _():
                    copy_in(g + (RING - 1)).start()

                copy_in(g).wait()
            codes = [listed[g * GROUP + u + 1] for u in range(GROUP)]
            terms = [
                lax.dot_general(
                    w_all[code & (CODE - 1)],
                    source[slot, u],
                    (((1,), (1,)), ((), ())),
                    preferred_element_type=F32,
                )
                for u, code in enumerate(codes)
            ]
            for code, term in zip(codes, terms):
                z_acc[lax.shift_right_logical(code, CODE_BITS)] += term
            return carry

        lax.fori_loop(0, total, step, 0)
    if not finish:
        return
    own_len = own_rows * block_len
    if scaled:
        outputs = (near.shape[0] - 8) // 2
        z_refs = [
            ref.at[pl.ds(outputs * h, outputs)] for h in range(2) for ref in (near, cross)
        ]
        for k in range(own_rows):
            cols = slice(k * block_len, (k + 1) * block_len)
            mine = inv_ref[pl.ds(place[0] * own_rows + k, 1), :]
            near[2 * outputs:, cols] = jnp.broadcast_to(mine, (8, block_len))
        cross[2 * outputs:, :] = jnp.zeros((8, own_len), F32)
    for e in range(4):
        for k in range(own_rows):
            z_refs[e][:, k * block_len:(k + 1) * block_len] = z_acc[(col ^ e) * own_rows + k]
    if products:
        outputs = t_ref.shape[0]
        ts2 = jnp.zeros((outputs, 1), F32)
        s1s2 = jnp.zeros((outputs, 1), F32)
        for e, packed in enumerate(s_refs):
            at = pl.ds(pl.multiple_of((col ^ e) * own_len, LANES), own_len)
            grown = z_refs[e][...] * packed[outputs:outputs + 1, :]
            ts2 += jnp.sum(t_ref[:, at] * grown, axis=1, keepdims=True)
            s1s2 += jnp.sum(packed[:outputs, :] * grown, axis=1, keepdims=True)
        t = t_ref[:, pl.ds(pl.multiple_of(col * own_len, LANES), own_len)]
        s1 = s_refs[0][:outputs, :]
        tt = jnp.sum(t * t, axis=1, keepdims=True)
        ts1 = jnp.sum(t * s1, axis=1, keepdims=True)
        s1s1 = jnp.sum(s1 * s1, axis=1, keepdims=True)
        ts2 += SHIFT * ts1
        s1s2 += SHIFT * s1s1
        lane = lax.broadcasted_iota(jnp.int32, (outputs, LANES), 1)
        out = jnp.zeros(lane.shape, F32)
        for n, v in enumerate((tt, ts1, s1s1, ts2, s1s2)):
            out = jnp.where(lane == n, v, out)
        dot_ref[...] = out


def final_kernel(place, t_ref, s1_own, s1_got, *refs):
    s2s, all_dots = refs[:4], refs[4:8]
    sol_hbm, res_hbm, sol_ref, res_ref, sems = refs[8:]
    s1s = pieces_of(s1_own, s1_got)
    outputs, own_len = s2s[0].shape
    dots = pair_sum([ref[...] for ref in all_dots])
    tt, ts1, s1s1, ts2, s1s2 = (dots[:, n:n + 1] for n in range(5))
    a1 = tt / (REG * tt + ts1)
    p = 1.0 - REG * a1
    new = p * p * tt - 2.0 * p * a1 * ts1 + a1 * a1 * s1s1
    u = p + new / tt
    dd = u * u * tt - 2.0 * u * a1 * ts1 + a1 * a1 * s1s1
    dmd = u * u * ts1 - u * a1 * (s1s1 + ts2) + a1 * a1 * s1s2
    a2 = new / (REG * dd + dmd)
    sol_t, sol_1 = a1 + a2 * u, a2 * a1
    res_t, res_1 = p - a2 * REG * u, a1 + a2 * (u - REG * a1)
    copies = []
    for e in range(4):
        at = pl.ds(pl.multiple_of((place[1] ^ e) * own_len, LANES), own_len)
        t, s1, s2 = t_ref[:, at], s1s[e][:outputs, :], s2s[e][...]
        sol_ref[e] = sol_t * t - sol_1 * s1
        res_ref[e] = res_t * t - res_1 * s1 + sol_1 * s2
        for n, (ref, hbm) in enumerate(((sol_ref, sol_hbm), (res_ref, res_hbm))):
            copy = pltpu.make_async_copy(ref.at[e], hbm.at[:, at], sems.at[n, e])
            copy.start()
            copies.append(copy)
    for copy in copies:
        copy.wait()


def swap(x, axis, d):
    size = lax.axis_size(axis)
    return lax.ppermute(x, axis, [(i, i ^ d) for i in range(size)])


def along_z(x):
    return [x] + [swap(x, "rows", d) for d in range(2, lax.axis_size("rows"), 2)]


def across_x(same):
    return [same, swap(same, "rows", 1)]


def direct_cols(x):
    return [x] + [swap(x, "cols", e) for e in range(1, 4)]


def local(block_list, points, targets):
    n_rows = lax.axis_size("rows")
    n_cols = lax.axis_size("cols")
    row = lax.axis_index("rows")
    col = lax.axis_index("cols")
    block_rows, slots = block_list.shape
    dim, npoints = points.shape
    outputs = targets.shape[0]
    block_len = npoints // block_rows
    own_rows = block_rows // n_cols
    own_len = own_rows * block_len
    nb = block_rows * n_rows
    n_sub = own_rows * n_rows
    capacity = -(-block_rows * slots // n_rows)
    direct_rows = n_rows <= DIRECT_ROWS
    parts = 2 if direct_rows else 1
    n_part = n_sub // parts
    bound = min(block_rows * n_part, n_cols * capacity * (n_rows + 1))
    n_groups = -(-bound // GROUP)
    list_len = n_groups * GROUP + GROUP + 1
    place = jnp.stack([row, col])
    resident = parts * 2 * n_groups * GROUP * block_len * block_len <= RESIDENT_BYTES
    k_shape = (parts * n_groups, GROUP, block_len, block_len)
    limit = pltpu.CompilerParams(vmem_limit_bytes=(8 if resident else 32) * 1024 * 1024)
    ring = [] if resident else [
        pltpu.VMEM((RING, GROUP, block_len, block_len), BF16),
        pltpu.SemaphoreType.DMA((RING,)),
    ]
    k_spec = VMEM if resident else HBM
    cfg = Sizes(
        parts, n_groups, resident, nb, block_len, own_rows, block_rows, -(-own_rows * nb // LANES)
    )

    def shape(*dims, dtype=F32):
        return jax.ShapeDtypeStruct(dims, dtype)

    def own(x):
        return lax.dynamic_slice_in_dim(x, col * own_len, own_len, 1)

    def total_rows(x):
        if direct_rows:
            return pair_sum(across_x(pair_sum(along_z(x))))
        return lax.psum(x, "rows")

    lists = direct_cols(block_list)
    names = jnp.arange(nb, dtype=jnp.int32)
    direct = sum(jnp.sum((x[:, :, None] == names).astype(jnp.int32), axis=1) for x in lists)
    own_counts = lax.dynamic_slice_in_dim(direct, col * own_rows, own_rows, 0)
    coded = own_counts.reshape(-1)
    coded = jnp.pad(coded, (0, dim * LANES - coded.shape[0])).reshape(dim, LANES).astype(BF16)
    packed = jnp.concatenate([own(points), coded], axis=1)
    own_t = own(targets)

    def build(part, *operands):
        first, last = part == 0, part == parts - 1
        out = [
            pltpu.VMEM(k_shape, BF16) if resident else shape(*k_shape, dtype=BF16),
            shape(list_len, dtype=jnp.int32),
            shape(n_sub if last else n_part, block_len),
        ]
        out += [shape(block_rows, block_len, 2 * dim, dtype=BF16)] if first else []
        k_mat, *rest = pl.pallas_call(
            functools.partial(build_kernel, cfg, part),
            out_shape=out,
            in_specs=[SMEM, SMEM] + ([HBM, VMEM] if first else [VMEM] * 3 + [k_spec]),
            out_specs=[k_spec, SMEM] + [VMEM] * (len(out) - 2),
            scratch_shapes=([
                pltpu.VMEM((dim, npoints), BF16),
                pltpu.SemaphoreType.DMA,
            ] if first else []) + [
                pltpu.SMEM((list_len,), jnp.int32),
                pltpu.VMEM((n_part, 8, block_len), F32),
                pltpu.VMEM((n_part, 2 * dim, block_len), BF16),
                pltpu.VMEM((n_part // own_rows, cfg.count_rows, LANES), jnp.int32),
                pltpu.SMEM((n_part // own_rows, cfg.count_rows, LANES), jnp.int32),
                pltpu.SemaphoreType.DMA,
                *ring,
            ],
            compiler_params=limit,
            input_output_aliases={} if first else {5: 0},
            cost_estimate=pl.CostEstimate(
                flops=2 * 2 * dim * bound * block_len * block_len,
                bytes_accessed=2 * bound * block_len * block_len,
                transcendentals=bound * block_len * block_len,
            ),
            name="build",
        )(place, direct, *operands)
        if resident:
            k_mat = pltpu.with_memory_space_constraint(k_mat, pltpu.VMEM)
        return k_mat, *rest

    near = pltpu.with_memory_space_constraint(points, pltpu.HBM)
    if direct_rows:
        packed, early_t = lax.optimization_barrier((packed, own_t))
        same, other = across_x(jnp.stack(along_z(packed)))
        t_same = along_z(early_t)
        k_mat, list0, degree, lhs = build(0, near, same)
        degree, other, *t_same = lax.optimization_barrier((degree, other, *t_same))
        t_same, t_other = across_x(jnp.stack(t_same))
        other, t_same = lax.optimization_barrier((other, t_same))
        k_mat, list1, degree = build(1, lhs, degree, other, k_mat)
        degree, t_other = lax.optimization_barrier((degree, t_other))
        t_pieces, k_lists = [t_same, t_other], [list0, list1]
    else:
        k_mat, list0, degree, _ = build(0, near, lax.all_gather(packed, "rows"))
        t_pieces, k_lists = [lax.all_gather(own_t, "rows")], [list0]
    inv = 1.0 / jnp.sqrt(1.0 + total_rows(degree))

    def apply(use, pieces, finish=True, inv=None, z_in=None, products=()):
        operands = [k_mat] + [k_lists[p] for p in use] + pieces
        specs = [k_spec] + [SMEM] * len(use) + [VMEM] * len(pieces)
        more = [x for x in (inv, z_in) if x is not None] + list(products)
        z_shape = (block_rows, outputs, block_len)
        if products:
            out = [shape(outputs, own_len), shape(outputs, own_len), shape(2, outputs, own_len)]
            out += [shape(outputs, LANES)]
        elif finish:
            out = [shape(2 * outputs + 8, own_len)] * 2
        else:
            out = [shape(*z_shape)]
        return pl.pallas_call(
            functools.partial(
                apply_kernel, cfg, use, inv is not None, z_in is not None, finish
            ),
            out_shape=out,
            in_specs=[SMEM] + specs + [VMEM] * len(more),
            out_specs=[VMEM] * len(out),
            scratch_shapes=([pltpu.VMEM(z_shape, F32)] if finish else []) + [
                pltpu.VMEM((n_part, outputs, block_len), BF16),
                *ring,
            ],
            compiler_params=limit,
            cost_estimate=pl.CostEstimate(
                flops=2 * len(use) * bound * outputs * block_len * block_len,
                bytes_accessed=len(use) * bound * block_len * block_len,
                transcendentals=0,
            ),
            name="apply",
        )(place, *operands, *more)

    near_z, cross_z = apply(tuple(range(parts)), t_pieces, inv=inv)
    half = near_z + swap(cross_z, "cols", 1)
    far = swap(half, "cols", 2)
    lo, hi, tail = slice(0, outputs), slice(outputs, 2 * outputs), slice(2 * outputs, None)
    own_inv, far_inv = half[2 * outputs:2 * outputs + 1], far[2 * outputs:2 * outputs + 1]
    s1 = (half[lo] + far[hi]) * own_inv
    g = ((s1 - SHIFT * own_t) * own_inv).astype(BF16)
    s1_own = jnp.stack([
        jnp.concatenate([s1, half[tail]], axis=0),
        jnp.concatenate([(half[hi] + far[lo]) * far_inv, far[tail]], axis=0),
    ])
    held_t = pltpu.with_memory_space_constraint(targets, pltpu.VMEM)
    if direct_rows:
        g_same = jnp.stack(along_z(g))
        g_same, s1_own = lax.optimization_barrier((g_same, s1_own))
        _, g_other = across_x(g_same)
        s1_got = swap(s1_own, "cols", 1)
        (z_part,) = apply((0,), [g_same], finish=False)
        z_part, g_other, s1_got = lax.optimization_barrier((z_part, g_other, s1_got))
        near_z, near_y, cross_z, dots = apply(
            (1,), [g_other], z_in=z_part, products=[held_t, s1_own, s1_got]
        )
        dots = pair_sum(along_z(dots))
    else:
        s1_got = swap(s1_own, "cols", 1)
        near_z, near_y, cross_z, dots = apply(
            (0,), [lax.all_gather(g, "rows")], products=[held_t, s1_own, s1_got]
        )
    got = swap(cross_z, "cols", 1)
    z2 = near_z + got[0] + swap(near_y + got[1], "cols", 2)
    s2 = direct_cols(z2 * own_inv + SHIFT * s1)
    dots = pair_sum(across_x(dots)) if direct_rows else lax.psum(dots, "rows")
    dots = direct_cols(dots)
    ends = [
        pltpu.with_memory_space_constraint(x, pltpu.VMEM) for x in (s1_own, s1_got, *s2, *dots)
    ]

    return pl.pallas_call(
        final_kernel,
        out_shape=(shape(outputs, npoints), shape(outputs, npoints)),
        in_specs=[SMEM] + [VMEM] * 11,
        out_specs=(HBM, HBM),
        scratch_shapes=[
            pltpu.VMEM((4, outputs, own_len), F32),
            pltpu.VMEM((4, outputs, own_len), F32),
            pltpu.SemaphoreType.DMA((2, 4)),
        ],
        compiler_params=limit,
        name="final",
    )(place, held_t, *ends)


def solution(mesh):
    placed = (P("rows", "cols"), P(None, "rows"), P(None, "rows"))
    return jax.shard_map(
        local,
        mesh=mesh,
        in_specs=placed,
        out_specs=(P(None, "rows"), P(None, "rows")),
        check_vma=False,
    )
```

```python
import functools
from typing import NamedTuple

import jax
import jax.numpy as jnp
from jax import lax
from jax.experimental import pallas as pl
from jax.experimental.pallas import tpu as pltpu
from jax.sharding import PartitionSpec as P

REG = 1.5
RADIUS = 0.25
GROUP_BITS = 2
GROUP = 1 << GROUP_BITS
CODE_BITS = 12
CODE = 1 << CODE_BITS
RING = 3
STRIP = 32
LANES = 128
TINY = 1e-30
SHIFT = 0.375
DIRECT_ROWS = 8
RESIDENT_BYTES = 20 * 1024 * 1024

SMEM = pl.BlockSpec(memory_space=pltpu.SMEM)
VMEM = pl.BlockSpec(memory_space=pltpu.VMEM)
HBM = pl.BlockSpec(memory_space=pltpu.HBM)
F32 = jnp.float32
BF16 = jnp.bfloat16


def pair_sum(parts):
    while len(parts) > 1:
        parts = [a + b for a, b in zip(parts[::2], parts[1::2])]
    return parts[0]


class Sizes(NamedTuple):
    parts: int
    part_groups: int
    resident: bool
    nb: int
    block_len: int
    own_rows: int
    block_rows: int
    count_rows: int


def augment(x, first_ones):
    dim, n = x.shape
    norm = jnp.sum(x * x, axis=0, keepdims=True) / (RADIUS * RADIUS)
    high = norm.astype(BF16).astype(F32)
    rest = norm - high
    mid = rest.astype(BF16).astype(F32)
    low = rest - mid
    line = lax.broadcasted_iota(jnp.int32, (dim, n), 0)
    base = 3 if first_ones else 0
    ones_at = 0 if first_ones else 3
    tail = jnp.where((line >= ones_at) & (line < ones_at + 3), 1.0, 0.0)
    tail = jnp.where(line == base, high, tail)
    tail = jnp.where(line == base + 1, mid, tail)
    tail = jnp.where(line == base + 2, low, tail)
    return tail


def row_of(cfg, place, part, z):
    if cfg.parts == 1:
        return z
    return 2 * z + (place[0] & 1 if part == 0 else 1 - (place[0] & 1))


def slot_of(cfg, place, n):
    return n if cfg.parts == 1 else lax.shift_right_logical(place[0], 1) ^ n


def build_kernel(cfg, part, place, direct, *refs):
    last = part == cfg.parts - 1
    if part == 0:
        near_hbm, piece, refs = refs[0], refs[1], refs[2:]
        k_mat, listed, deg_ref, lhs = refs[:4]
        near_ref, near_sem, refs = refs[4], refs[5], refs[6:]
        near_copy = pltpu.make_async_copy(near_hbm, near_ref, near_sem)
        near_copy.start()
    else:
        lhs, first_deg, piece, _ = refs[:4]
        k_mat, listed, deg_ref = refs[4:7]
        refs = refs[7:]
    mlist, acc, rhs, counts_v, counts, count_sem = refs[:6]
    kbuf, sems = (None, None) if cfg.resident else refs[6:]
    row, col = place[0], place[1]
    own_rows, block_len, nb = cfg.own_rows, cfg.block_len, cfg.nb
    own_len = own_rows * block_len
    dim, held = piece.shape[1], piece.shape[0]
    scale = 1.0 / (RADIUS * RADIUS)

    def prepare(n, carry):
        z = slot_of(cfg, place, n)
        for k in range(own_rows):
            far = piece[n, :, k * block_len:(k + 1) * block_len]
            rhs[z * own_rows + k, :dim, :] = far
            rhs[z * own_rows + k, dim:, :] = augment(far.astype(F32), False).astype(BF16)
        named = piece[n, :, own_len:own_len + LANES]
        counts_v[z] = named.astype(F32)[:cfg.count_rows].astype(jnp.int32)
        return carry

    lax.fori_loop(0, held, prepare, 0, unroll=held <= 4)
    fetch = pltpu.make_async_copy(counts_v, counts, count_sem)
    fetch.start()
    if part == 0:
        near_copy.wait()
        for i in range(cfg.block_rows):
            near = near_ref[:, i * block_len:(i + 1) * block_len].astype(F32)
            full = jnp.concatenate([near * (-2.0 * scale), augment(near, True)], axis=0)
            lhs[i] = full.T.astype(BF16)
    acc[...] = jnp.zeros_like(acc)
    fetch.wait()

    pos = jnp.int32(0)
    for i in range(cfg.block_rows):
        me = row * cfg.block_rows + i
        spots = [k * nb + me for k in range(own_rows)]
        spots = [(lax.shift_right_logical(p, 7), p & (LANES - 1)) for p in spots]

        def note(z, at, i=i, me=me, spots=spots):
            for k in range(own_rows):
                name = row_of(cfg, place, part, z) * cfg.block_rows + col * own_rows + k
                m = direct[i, name] + jnp.where(name == me, 0, counts[z, spots[k][0], spots[k][1]])
                listed[at + 1] = i * CODE + z * own_rows + k
                mlist[at] = m
                at = at + jnp.where(m > 0, 1, 0)
            return at

        pos = lax.fori_loop(0, held, note, pos, unroll=4)
    for u in range(GROUP):
        listed[pos + u + 1] = 0
        mlist[pos + u] = 0
    total = lax.shift_right_logical(pos + (GROUP - 1), GROUP_BITS)
    listed[0] = total

    def copy_out(g):
        slot = lax.rem(g, RING)
        return pltpu.make_async_copy(kbuf.at[slot], k_mat.at[g], sems.at[slot])

    base = part * cfg.part_groups

    def step(g, carry):
        slot, target = (base + g, k_mat) if cfg.resident else (lax.rem(g, RING), kbuf)
        if not cfg.resident:

            @pl.when(g >= RING)
            def _():
                copy_out(g - RING).wait()

        for u in range(GROUP):
            code = listed[g * GROUP + u + 1]
            i, j = lax.shift_right_logical(code, CODE_BITS), code & (CODE - 1)
            m = mlist[g * GROUP + u].astype(F32)
            dist = jnp.dot(lhs[i], rhs[j], preferred_element_type=F32)
            sums = jnp.zeros((8, block_len), F32)
            for s in range(block_len // STRIP):
                rows = slice(s * STRIP, (s + 1) * STRIP)
                d = jnp.maximum(dist[rows], TINY)
                sc = d * lax.rsqrt(d)
                rem = jnp.maximum(1.0 - sc, 0.0)
                sq = rem * rem
                val = (sq * sq) * (sc * (4.0 * m) + m)
                target[slot, u, rows, :] = val.astype(BF16)
                for h in range(0, STRIP, 8):
                    sums = sums + val[h:h + 8]
            acc[j] += sums
        if not cfg.resident:
            copy_out(g).start()
        return carry

    lax.fori_loop(0, total, step, 0)
    if cfg.parts == 1 or not last:
        deg_ref[...] = jnp.sum(acc[...], axis=1)
    else:
        second = jnp.sum(acc[...], axis=1)
        for z in range(held):
            rows = slice(z * own_rows, (z + 1) * own_rows)
            for p, deg in enumerate((first_deg[rows, :], second[rows])):
                at = row_of(cfg, place, p, z) * own_rows
                for k in range(own_rows):
                    deg_ref[pl.ds(at + k, 1), :] = deg[k:k + 1]

    def drain(g, carry):
        copy_out(g).wait()
        return carry

    if not cfg.resident:
        lax.fori_loop(jnp.maximum(total - RING, 0), total, drain, 0)


def pieces_of(own, got):
    return own.at[0], got.at[0], own.at[1], got.at[1]


def apply_kernel(cfg, parts, scaled, carried, finish, place, k_mat, *refs):
    n = len(parts)
    lists, pieces, refs = refs[:n], refs[n:2 * n], refs[2 * n:]
    if scaled:
        inv_ref, refs = refs[0], refs[1:]
    if carried:
        z_in, refs = refs[0], refs[1:]
    products = finish and not scaled
    if products:
        t_ref, s_refs, refs = refs[0], pieces_of(refs[1], refs[2]), refs[3:]
    if finish:
        near, near_y, cross, extra, z_acc, refs = *refs[:5], refs[5:]
        z_refs = (near, cross.at[0], near_y, cross.at[1])
    else:
        z_acc, refs = refs[0], refs[1:]
    w_all, refs = refs[0], refs[1:]
    kbuf, sems = (None, None) if cfg.resident else refs
    col = place[1]
    own_rows, block_len = cfg.own_rows, cfg.block_len

    z_acc[...] = z_in[...] if carried else jnp.zeros_like(z_acc)
    for part, listed, piece in zip(parts, lists, pieces):
        total = listed[0]
        base = part * cfg.part_groups
        held = piece.shape[0]

        def copy_in(g):
            slot = lax.rem(g, RING)
            return pltpu.make_async_copy(k_mat.at[g], kbuf.at[slot], sems.at[slot])

        if not cfg.resident:
            for p in range(RING - 1):

                @pl.when(p < total)
                def _(p=p, copy_in=copy_in):
                    copy_in(p).start()

        def prepare(n, carry, part=part, piece=piece):
            z = slot_of(cfg, place, n)
            for k in range(own_rows):
                w = piece[n, :, k * block_len:(k + 1) * block_len]
                if scaled:
                    at = row_of(cfg, place, part, z) * own_rows + k
                    w = (w * inv_ref[pl.ds(at, 1), :]).astype(BF16)
                w_all[z * own_rows + k] = w
            return carry

        lax.fori_loop(0, held, prepare, 0, unroll=held <= 4)

        def step(g, carry, total=total, listed=listed, base=base, copy_in=copy_in):
            slot, source = (base + g, k_mat) if cfg.resident else (lax.rem(g, RING), kbuf)
            if not cfg.resident:

                @pl.when(g + (RING - 1) < total)
                def _():
                    copy_in(g + (RING - 1)).start()

                copy_in(g).wait()
            codes = [listed[g * GROUP + u + 1] for u in range(GROUP)]
            terms = [
                lax.dot_general(
                    w_all[code & (CODE - 1)],
                    source[slot, u],
                    (((1,), (1,)), ((), ())),
                    preferred_element_type=F32,
                )
                for u, code in enumerate(codes)
            ]
            for code, term in zip(codes, terms):
                z_acc[lax.shift_right_logical(code, CODE_BITS)] += term
            return carry

        lax.fori_loop(0, total, step, 0)
    if not finish:
        return
    own_len = own_rows * block_len
    if scaled:
        for k in range(own_rows):
            mine = inv_ref[pl.ds(place[0] * own_rows + k, 1), :]
            extra[:, k * block_len:(k + 1) * block_len] = jnp.broadcast_to(mine, (8, block_len))
    for e in range(4):
        for k in range(own_rows):
            z_refs[e][:, k * block_len:(k + 1) * block_len] = z_acc[(col ^ e) * own_rows + k]
    if products:
        outputs = t_ref.shape[0]
        ts2 = jnp.zeros((outputs, 1), F32)
        s1s2 = jnp.zeros((outputs, 1), F32)
        for e, packed in enumerate(s_refs):
            at = pl.ds(pl.multiple_of((col ^ e) * own_len, LANES), own_len)
            grown = z_refs[e][...] * packed[outputs:outputs + 1, :]
            ts2 += jnp.sum(t_ref[:, at] * grown, axis=1, keepdims=True)
            s1s2 += jnp.sum(packed[:outputs, :] * grown, axis=1, keepdims=True)
        t = t_ref[:, pl.ds(pl.multiple_of(col * own_len, LANES), own_len)]
        s1 = s_refs[0][:outputs, :]
        tt = jnp.sum(t * t, axis=1, keepdims=True)
        ts1 = jnp.sum(t * s1, axis=1, keepdims=True)
        s1s1 = jnp.sum(s1 * s1, axis=1, keepdims=True)
        ts2 += SHIFT * ts1
        s1s2 += SHIFT * s1s1
        lane = lax.broadcasted_iota(jnp.int32, (outputs, LANES), 1)
        out = jnp.zeros(lane.shape, F32)
        for n, v in enumerate((tt, ts1, s1s1, ts2, s1s2)):
            out = jnp.where(lane == n, v, out)
        extra[...] = out


def final_kernel(place, t_ref, s1_own, s1_got, *refs):
    grown, all_dots = pieces_of(refs[0], refs[1]), refs[2:6]
    sol_hbm, res_hbm, sol_ref, res_ref, sems = refs[6:]
    s1s = pieces_of(s1_own, s1_got)
    outputs, own_len = grown[0].shape
    dots = pair_sum([ref[...] for ref in all_dots])
    tt, ts1, s1s1, ts2, s1s2 = (dots[:, n:n + 1] for n in range(5))
    a1 = tt / (REG * tt + ts1)
    p = 1.0 - REG * a1
    new = p * p * tt - 2.0 * p * a1 * ts1 + a1 * a1 * s1s1
    u = p + new / tt
    dd = u * u * tt - 2.0 * u * a1 * ts1 + a1 * a1 * s1s1
    dmd = u * u * ts1 - u * a1 * (s1s1 + ts2) + a1 * a1 * s1s2
    a2 = new / (REG * dd + dmd)
    sol_t, sol_1 = a1 + a2 * u, a2 * a1
    res_t, res_1 = p - a2 * REG * u, a1 + a2 * (u - REG * a1)
    copies = []
    for e in range(4):
        at = pl.ds(pl.multiple_of((place[1] ^ e) * own_len, LANES), own_len)
        t, s1 = t_ref[:, at], s1s[e][:outputs, :]
        s2 = grown[e][...] + SHIFT * s1
        sol_ref[e] = sol_t * t - sol_1 * s1
        res_ref[e] = res_t * t - res_1 * s1 + sol_1 * s2
        for n, (ref, hbm) in enumerate(((sol_ref, sol_hbm), (res_ref, res_hbm))):
            copy = pltpu.make_async_copy(ref.at[e], hbm.at[:, at], sems.at[n, e])
            copy.start()
            copies.append(copy)
    for copy in copies:
        copy.wait()


def swap(x, axis, d):
    size = lax.axis_size(axis)
    return lax.ppermute(x, axis, [(i, i ^ d) for i in range(size)])


def along_z(x):
    return [x] + [swap(x, "rows", d) for d in range(2, lax.axis_size("rows"), 2)]


def across_x(same):
    return [same, swap(same, "rows", 1)]


def direct_cols(x):
    return [x] + [swap(x, "cols", e) for e in range(1, 4)]


def local(block_list, points, targets):
    n_rows = lax.axis_size("rows")
    n_cols = lax.axis_size("cols")
    row = lax.axis_index("rows")
    col = lax.axis_index("cols")
    block_rows, slots = block_list.shape
    dim, npoints = points.shape
    outputs = targets.shape[0]
    block_len = npoints // block_rows
    own_rows = block_rows // n_cols
    own_len = own_rows * block_len
    nb = block_rows * n_rows
    n_sub = own_rows * n_rows
    capacity = -(-block_rows * slots // n_rows)
    direct_rows = n_rows <= DIRECT_ROWS
    parts = 2 if direct_rows else 1
    n_part = n_sub // parts
    bound = min(block_rows * n_part, n_cols * capacity * (n_rows + 1))
    n_groups = -(-bound // GROUP)
    list_len = n_groups * GROUP + GROUP + 1
    place = jnp.stack([row, col])
    resident = parts * 2 * n_groups * GROUP * block_len * block_len <= RESIDENT_BYTES
    k_shape = (parts * n_groups, GROUP, block_len, block_len)
    limit = pltpu.CompilerParams(vmem_limit_bytes=(8 if resident else 32) * 1024 * 1024)
    ring = [] if resident else [
        pltpu.VMEM((RING, GROUP, block_len, block_len), BF16),
        pltpu.SemaphoreType.DMA((RING,)),
    ]
    k_spec = VMEM if resident else HBM
    cfg = Sizes(
        parts, n_groups, resident, nb, block_len, own_rows, block_rows, -(-own_rows * nb // LANES)
    )

    def shape(*dims, dtype=F32):
        return jax.ShapeDtypeStruct(dims, dtype)

    def own(x):
        return lax.dynamic_slice_in_dim(x, col * own_len, own_len, 1)

    def total_rows(x):
        if direct_rows:
            return pair_sum(across_x(pair_sum(along_z(x))))
        return lax.psum(x, "rows")

    lists = direct_cols(block_list)
    names = jnp.arange(nb, dtype=jnp.int32)
    direct = sum(jnp.sum((x[:, :, None] == names).astype(jnp.int32), axis=1) for x in lists)
    own_counts = lax.dynamic_slice_in_dim(direct, col * own_rows, own_rows, 0)
    coded = own_counts.reshape(-1)
    coded = jnp.pad(coded, (0, dim * LANES - coded.shape[0])).reshape(dim, LANES).astype(BF16)
    packed = jnp.concatenate([own(points), coded], axis=1)
    own_t = own(targets)

    def build(part, *operands):
        first, last = part == 0, part == parts - 1
        out = [
            pltpu.VMEM(k_shape, BF16) if resident else shape(*k_shape, dtype=BF16),
            shape(list_len, dtype=jnp.int32),
            shape(n_sub if last else n_part, block_len),
        ]
        out += [shape(block_rows, block_len, 2 * dim, dtype=BF16)] if first else []
        k_mat, *rest = pl.pallas_call(
            functools.partial(build_kernel, cfg, part),
            out_shape=out,
            in_specs=[SMEM, SMEM] + ([HBM, VMEM] if first else [VMEM] * 3 + [k_spec]),
            out_specs=[k_spec, SMEM] + [VMEM] * (len(out) - 2),
            scratch_shapes=([
                pltpu.VMEM((dim, npoints), BF16),
                pltpu.SemaphoreType.DMA,
            ] if first else []) + [
                pltpu.SMEM((list_len,), jnp.int32),
                pltpu.VMEM((n_part, 8, block_len), F32),
                pltpu.VMEM((n_part, 2 * dim, block_len), BF16),
                pltpu.VMEM((n_part // own_rows, cfg.count_rows, LANES), jnp.int32),
                pltpu.SMEM((n_part // own_rows, cfg.count_rows, LANES), jnp.int32),
                pltpu.SemaphoreType.DMA,
                *ring,
            ],
            compiler_params=limit,
            input_output_aliases={} if first else {5: 0},
            cost_estimate=pl.CostEstimate(
                flops=2 * 2 * dim * bound * block_len * block_len,
                bytes_accessed=2 * bound * block_len * block_len,
                transcendentals=bound * block_len * block_len,
            ),
            name="build",
        )(place, direct, *operands)
        if resident:
            k_mat = pltpu.with_memory_space_constraint(k_mat, pltpu.VMEM)
        return k_mat, *rest

    near = pltpu.with_memory_space_constraint(points, pltpu.HBM)
    if direct_rows:
        packed, early_t = lax.optimization_barrier((packed, own_t))
        same, other = across_x(jnp.stack(along_z(packed)))
        t_same = along_z(early_t)
        k_mat, list0, degree, lhs = build(0, near, same)
        degree, other, *t_same = lax.optimization_barrier((degree, other, *t_same))
        t_same, t_other = across_x(jnp.stack(t_same))
        other, t_same = lax.optimization_barrier((other, t_same))
        k_mat, list1, degree = build(1, lhs, degree, other, k_mat)
        degree, t_other = lax.optimization_barrier((degree, t_other))
        t_pieces, k_lists = [t_same, t_other], [list0, list1]
    else:
        k_mat, list0, degree, _ = build(0, near, lax.all_gather(packed, "rows"))
        t_pieces, k_lists = [lax.all_gather(own_t, "rows")], [list0]
    inv = 1.0 / jnp.sqrt(1.0 + total_rows(degree))

    def apply(use, pieces, finish=True, inv=None, z_in=None, products=()):
        operands = [k_mat] + [k_lists[p] for p in use] + pieces
        specs = [k_spec] + [SMEM] * len(use) + [VMEM] * len(pieces)
        more = [x for x in (inv, z_in) if x is not None] + list(products)
        z_shape = (block_rows, outputs, block_len)
        if finish:
            out = [shape(outputs, own_len)] * 2 + [shape(2, outputs, own_len)]
            out += [shape(outputs, LANES) if products else shape(8, own_len)]
        else:
            out = [shape(*z_shape)]
        return pl.pallas_call(
            functools.partial(
                apply_kernel, cfg, use, inv is not None, z_in is not None, finish
            ),
            out_shape=out,
            in_specs=[SMEM] + specs + [VMEM] * len(more),
            out_specs=[VMEM] * len(out),
            scratch_shapes=([pltpu.VMEM(z_shape, F32)] if finish else []) + [
                pltpu.VMEM((n_part, outputs, block_len), BF16),
                *ring,
            ],
            compiler_params=limit,
            cost_estimate=pl.CostEstimate(
                flops=2 * len(use) * bound * outputs * block_len * block_len,
                bytes_accessed=len(use) * bound * block_len * block_len,
                transcendentals=0,
            ),
            name="apply",
        )(place, *operands, *more)

    near_z, near_y, cross_z, tail = apply(tuple(range(parts)), t_pieces, inv=inv)
    got = swap(cross_z, "cols", 1)
    half, half_y = near_z + got[0], near_y + got[1]
    own_inv = tail[:1]
    s1 = (half + swap(half_y, "cols", 2)) * own_inv
    g = ((s1 - SHIFT * own_t) * own_inv).astype(BF16)
    g, half, half_y = lax.optimization_barrier((g, half, half_y))
    far = swap(jnp.concatenate([half, tail], axis=0), "cols", 2)
    s1_own = jnp.stack([
        jnp.concatenate([s1, tail], axis=0),
        jnp.concatenate([(half_y + far[:outputs]) * far[outputs:outputs + 1], far[outputs:]], axis=0),
    ])
    held_t = pltpu.with_memory_space_constraint(targets, pltpu.VMEM)
    if direct_rows:
        g_same = jnp.stack(along_z(g))
        g_same, s1_own = lax.optimization_barrier((g_same, s1_own))
        _, g_other = across_x(g_same)
        s1_got = swap(s1_own, "cols", 1)
        (z_part,) = apply((0,), [g_same], finish=False)
        z_part, g_other, s1_got = lax.optimization_barrier((z_part, g_other, s1_got))
        *z2, dots = apply(
            (1,), [g_other], z_in=z_part, products=[held_t, s1_own, s1_got]
        )
        dots = pair_sum(along_z(dots))
    else:
        s1_got = swap(s1_own, "cols", 1)
        *z2, dots = apply(
            (0,), [lax.all_gather(g, "rows")], products=[held_t, s1_own, s1_got]
        )
    got = swap(z2[2], "cols", 1)
    halves = jnp.stack([z2[0] + got[0], z2[1] + got[1]])
    halves = lax.reduce_precision(halves, 8, 7)
    far = swap(halves.astype(BF16), "cols", 2).astype(F32)
    grown = jnp.stack([
        (halves[0] + far[1]) * own_inv,
        (halves[1] + far[0]) * s1_own[1, outputs:outputs + 1],
    ])
    dots = pair_sum(across_x(dots)) if direct_rows else lax.psum(dots, "rows")
    dots = direct_cols(dots)
    ends = (s1_own, s1_got, grown, swap(grown, "cols", 1), *dots)
    ends = [pltpu.with_memory_space_constraint(x, pltpu.VMEM) for x in ends]

    return pl.pallas_call(
        final_kernel,
        out_shape=(shape(outputs, npoints), shape(outputs, npoints)),
        in_specs=[SMEM] + [VMEM] * 9,
        out_specs=(HBM, HBM),
        scratch_shapes=[
            pltpu.VMEM((4, outputs, own_len), F32),
            pltpu.VMEM((4, outputs, own_len), F32),
            pltpu.SemaphoreType.DMA((2, 4)),
        ],
        compiler_params=limit,
        name="final",
    )(place, held_t, *ends)


def solution(mesh):
    placed = (P("rows", "cols"), P(None, "rows"), P(None, "rows"))
    return jax.shard_map(
        local,
        mesh=mesh,
        in_specs=placed,
        out_specs=(P(None, "rows"), P(None, "rows")),
        check_vma=False,
    )
```

```python
import functools
from typing import NamedTuple

import jax
import jax.numpy as jnp
from jax import lax
from jax.experimental import pallas as pl
from jax.experimental.pallas import tpu as pltpu
from jax.sharding import PartitionSpec as P

REG = 1.5
RADIUS = 0.25
GROUP_BITS = 2
GROUP = 1 << GROUP_BITS
CODE_BITS = 12
CODE = 1 << CODE_BITS
RING = 3
STRIP = 32
LANES = 128
TINY = 1e-30
SHIFT = 0.375
DIRECT_ROWS = 8
RESIDENT_BYTES = 20 * 1024 * 1024

SMEM = pl.BlockSpec(memory_space=pltpu.SMEM)
VMEM = pl.BlockSpec(memory_space=pltpu.VMEM)
HBM = pl.BlockSpec(memory_space=pltpu.HBM)
F32 = jnp.float32
BF16 = jnp.bfloat16


def pair_sum(parts):
    while len(parts) > 1:
        parts = [a + b for a, b in zip(parts[::2], parts[1::2])]
    return parts[0]


class Sizes(NamedTuple):
    parts: int
    part_groups: int
    resident: bool
    nb: int
    block_len: int
    own_rows: int
    block_rows: int
    count_rows: int


def augment(x, first_ones):
    dim, n = x.shape
    norm = jnp.sum(x * x, axis=0, keepdims=True) / (RADIUS * RADIUS)
    high = norm.astype(BF16).astype(F32)
    rest = norm - high
    mid = rest.astype(BF16).astype(F32)
    low = rest - mid
    line = lax.broadcasted_iota(jnp.int32, (dim, n), 0)
    base = 3 if first_ones else 0
    ones_at = 0 if first_ones else 3
    tail = jnp.where((line >= ones_at) & (line < ones_at + 3), 1.0, 0.0)
    tail = jnp.where(line == base, high, tail)
    tail = jnp.where(line == base + 1, mid, tail)
    tail = jnp.where(line == base + 2, low, tail)
    return tail


def row_of(cfg, place, part, z):
    if cfg.parts == 1:
        return z
    return 2 * z + (place[0] & 1 if part == 0 else 1 - (place[0] & 1))


def slot_of(cfg, place, n):
    return n if cfg.parts == 1 else lax.shift_right_logical(place[0], 1) ^ n


def build_kernel(cfg, part, place, direct, *refs):
    last = part == cfg.parts - 1
    if part == 0:
        near_hbm, piece, refs = refs[0], refs[1], refs[2:]
        k_mat, listed, deg_ref, lhs = refs[:4]
        near_ref, near_sem, refs = refs[4], refs[5], refs[6:]
        near_copy = pltpu.make_async_copy(near_hbm, near_ref, near_sem)
        near_copy.start()
    else:
        lhs, first_deg, piece, _ = refs[:4]
        k_mat, listed, deg_ref = refs[4:7]
        refs = refs[7:]
    mlist, acc, rhs, counts_v, counts, count_sem = refs[:6]
    kbuf, sems = (None, None) if cfg.resident else refs[6:]
    row, col = place[0], place[1]
    own_rows, block_len, nb = cfg.own_rows, cfg.block_len, cfg.nb
    own_len = own_rows * block_len
    dim, held = piece.shape[1], piece.shape[0]
    scale = 1.0 / (RADIUS * RADIUS)

    def prepare(n, carry):
        z = slot_of(cfg, place, n)
        for k in range(own_rows):
            far = piece[n, :, k * block_len:(k + 1) * block_len]
            rhs[z * own_rows + k, :dim, :] = far
            rhs[z * own_rows + k, dim:, :] = augment(far.astype(F32), False).astype(BF16)
        named = piece[n, :, own_len:own_len + LANES]
        counts_v[z] = named.astype(F32)[:cfg.count_rows].astype(jnp.int32)
        return carry

    lax.fori_loop(0, held, prepare, 0, unroll=held <= 4)
    fetch = pltpu.make_async_copy(counts_v, counts, count_sem)
    fetch.start()
    if part == 0:
        near_copy.wait()
        for i in range(cfg.block_rows):
            near = near_ref[:, i * block_len:(i + 1) * block_len].astype(F32)
            full = jnp.concatenate([near * (-2.0 * scale), augment(near, True)], axis=0)
            lhs[i] = full.T.astype(BF16)
    acc[...] = jnp.zeros_like(acc)
    fetch.wait()

    pos = jnp.int32(0)
    for i in range(cfg.block_rows):
        me = row * cfg.block_rows + i
        spots = [k * nb + me for k in range(own_rows)]
        spots = [(lax.shift_right_logical(p, 7), p & (LANES - 1)) for p in spots]

        def note(z, at, i=i, me=me, spots=spots):
            for k in range(own_rows):
                name = row_of(cfg, place, part, z) * cfg.block_rows + col * own_rows + k
                m = direct[i, name] + jnp.where(name == me, 0, counts[z, spots[k][0], spots[k][1]])
                listed[at + 1] = i * CODE + z * own_rows + k
                mlist[at] = m
                at = at + jnp.where(m > 0, 1, 0)
            return at

        pos = lax.fori_loop(0, held, note, pos, unroll=4)
    for u in range(GROUP):
        listed[pos + u + 1] = 0
        mlist[pos + u] = 0
    total = lax.shift_right_logical(pos + (GROUP - 1), GROUP_BITS)
    listed[0] = total

    def copy_out(g):
        slot = lax.rem(g, RING)
        return pltpu.make_async_copy(kbuf.at[slot], k_mat.at[g], sems.at[slot])

    base = part * cfg.part_groups

    def step(g, carry):
        slot, target = (base + g, k_mat) if cfg.resident else (lax.rem(g, RING), kbuf)
        if not cfg.resident:

            @pl.when(g >= RING)
            def _():
                copy_out(g - RING).wait()

        for u in range(GROUP):
            code = listed[g * GROUP + u + 1]
            i, j = lax.shift_right_logical(code, CODE_BITS), code & (CODE - 1)
            m = mlist[g * GROUP + u].astype(F32)
            dist = jnp.dot(lhs[i], rhs[j], preferred_element_type=F32)
            sums = jnp.zeros((8, block_len), F32)
            for s in range(block_len // STRIP):
                rows = slice(s * STRIP, (s + 1) * STRIP)
                d = jnp.maximum(dist[rows], TINY)
                sc = d * lax.rsqrt(d)
                rem = jnp.maximum(1.0 - sc, 0.0)
                sq = rem * rem
                val = (sq * sq) * (sc * (4.0 * m) + m)
                target[slot, u, rows, :] = val.astype(BF16)
                for h in range(0, STRIP, 8):
                    sums = sums + val[h:h + 8]
            acc[j] += sums
        if not cfg.resident:
            copy_out(g).start()
        return carry

    lax.fori_loop(0, total, step, 0)
    if cfg.parts == 1 or not last:
        deg_ref[...] = jnp.sum(acc[...], axis=1)
    else:
        second = jnp.sum(acc[...], axis=1)
        for z in range(held):
            rows = slice(z * own_rows, (z + 1) * own_rows)
            for p, deg in enumerate((first_deg[rows, :], second[rows])):
                at = row_of(cfg, place, p, z) * own_rows
                for k in range(own_rows):
                    deg_ref[pl.ds(at + k, 1), :] = deg[k:k + 1]

    def drain(g, carry):
        copy_out(g).wait()
        return carry

    if not cfg.resident:
        lax.fori_loop(jnp.maximum(total - RING, 0), total, drain, 0)


def pieces_of(own, got):
    return own.at[0], got.at[0], own.at[1], got.at[1]


def walk(cfg, part, listed, k_mat, kbuf, sems, product, total_ref, by_row):
    total = listed[0]
    base = part * cfg.part_groups

    def copy_in(g):
        slot = lax.rem(g, RING)
        return pltpu.make_async_copy(k_mat.at[g], kbuf.at[slot], sems.at[slot])

    if not cfg.resident:
        for p in range(RING - 1):

            @pl.when(p < total)
            def _(p=p):
                copy_in(p).start()

    def step(g, carry):
        slot, source = (base + g, k_mat) if cfg.resident else (lax.rem(g, RING), kbuf)
        if not cfg.resident:

            @pl.when(g + (RING - 1) < total)
            def _():
                copy_in(g + (RING - 1)).start()

            copy_in(g).wait()
        codes = [listed[g * GROUP + u + 1] for u in range(GROUP)]
        pairs = [(lax.shift_right_logical(code, CODE_BITS), code & (CODE - 1)) for code in codes]
        terms = [product(i, j, source[slot, u]) for u, (i, j) in enumerate(pairs)]
        for (i, j), term in zip(pairs, terms):
            total_ref[i if by_row else j] += term
        return carry

    lax.fori_loop(0, total, step, 0)


def first_kernel(cfg, place, k_mat, *refs):
    n = cfg.parts
    lists, pieces, inv_ref, refs = refs[:n], refs[n:2 * n], refs[2 * n], refs[2 * n + 1:]
    near, near_y, cross, own_inv, z_acc, w_all, *ring = refs
    kbuf, sems = ring or (None, None)
    col = place[1]
    own_rows, block_len = cfg.own_rows, cfg.block_len
    z_acc[...] = jnp.zeros_like(z_acc)
    for part, (listed, piece) in enumerate(zip(lists, pieces)):
        held = piece.shape[0]

        def prepare(m, carry, part=part, piece=piece):
            z = slot_of(cfg, place, m)
            for k in range(own_rows):
                w = piece[m, :, k * block_len:(k + 1) * block_len]
                at = row_of(cfg, place, part, z) * own_rows + k
                w_all[z * own_rows + k] = (w * inv_ref[pl.ds(at, 1), :]).astype(BF16)
            return carry

        lax.fori_loop(0, held, prepare, 0, unroll=held <= 4)

        def product(i, j, block):
            return lax.dot_general(
                w_all[j], block, (((1,), (1,)), ((), ())), preferred_element_type=F32
            )

        walk(cfg, part, listed, k_mat, kbuf, sems, product, z_acc, True)
    for k in range(own_rows):
        cols = slice(k * block_len, (k + 1) * block_len)
        mine = inv_ref[pl.ds(place[0] * own_rows + k, 1), :]
        own_inv[:, cols] = jnp.broadcast_to(mine, (8, block_len))
        for e, ref in enumerate((near, cross.at[0], near_y, cross.at[1])):
            ref[:, cols] = z_acc[(col ^ e) * own_rows + k]


def second_kernel(cfg, part, place, k_mat, listed, t_ref, s1_own, s1_got, out, z_acc, w_all, *ring):
    kbuf, sems = ring or (None, None)
    own_rows, block_len = cfg.own_rows, cfg.block_len
    outputs = t_ref.shape[0]
    for e, packed in enumerate(pieces_of(s1_own, s1_got)):
        share = place[1] ^ e
        for k in range(own_rows):
            cols = slice(k * block_len, (k + 1) * block_len)
            i = share * own_rows + k
            t = t_ref[:, pl.ds(pl.multiple_of(i * block_len, LANES), block_len)]
            g = (packed[:outputs, cols] - SHIFT * t) * packed[outputs:outputs + 1, cols]
            w_all[i] = g.astype(BF16)
    z_acc[...] = jnp.zeros_like(z_acc)

    def product(i, j, block):
        return jnp.dot(w_all[i], block, preferred_element_type=F32)

    walk(cfg, part, listed, k_mat, kbuf, sems, product, z_acc, False)

    def hand_out(m, carry):
        z = slot_of(cfg, place, m)
        for k in range(own_rows):
            out[m, :, k * block_len:(k + 1) * block_len] = z_acc[z * own_rows + k].astype(out.dtype)
        return carry

    held = out.shape[0]
    lax.fori_loop(0, held, hand_out, 0, unroll=held <= 4)


def product_kernel(place, t_ref, s1_own, *refs):
    zs, grown_ref, dot_ref = refs[:-2], refs[-2], refs[-1]
    outputs, own_len = grown_ref.shape
    z = zs[0][...].astype(F32)
    for ref in zs[1:]:
        z = z + ref[...].astype(F32)
    grown = z * s1_own[0, outputs:outputs + 1, :]
    grown_ref[...] = grown
    s1 = s1_own[0, :outputs, :]
    s2 = grown + SHIFT * s1
    t = t_ref[:, pl.ds(pl.multiple_of(place[1] * own_len, LANES), own_len)]
    lane = lax.broadcasted_iota(jnp.int32, (outputs, LANES), 1)
    out = jnp.zeros(lane.shape, F32)
    for n, (a, b) in enumerate(((t, t), (t, s1), (s1, s1), (t, s2), (s1, s2))):
        out = jnp.where(lane == n, jnp.sum(a * b, axis=1, keepdims=True), out)
    dot_ref[...] = out


def final_kernel(place, t_ref, s1_own, s1_got, *refs):
    grown, all_dots = pieces_of(refs[0], refs[1]), refs[2:6]
    sol_hbm, res_hbm, sol_ref, res_ref, sems = refs[6:]
    s1s = pieces_of(s1_own, s1_got)
    outputs, own_len = grown[0].shape
    dots = pair_sum([ref[...] for ref in all_dots])
    tt, ts1, s1s1, ts2, s1s2 = (dots[:, n:n + 1] for n in range(5))
    a1 = tt / (REG * tt + ts1)
    p = 1.0 - REG * a1
    new = p * p * tt - 2.0 * p * a1 * ts1 + a1 * a1 * s1s1
    u = p + new / tt
    dd = u * u * tt - 2.0 * u * a1 * ts1 + a1 * a1 * s1s1
    dmd = u * u * ts1 - u * a1 * (s1s1 + ts2) + a1 * a1 * s1s2
    a2 = new / (REG * dd + dmd)
    sol_t, sol_1 = a1 + a2 * u, a2 * a1
    res_t, res_1 = p - a2 * REG * u, a1 + a2 * (u - REG * a1)
    copies = []
    for e in range(4):
        at = pl.ds(pl.multiple_of((place[1] ^ e) * own_len, LANES), own_len)
        t, s1 = t_ref[:, at], s1s[e][:outputs, :]
        s2 = grown[e][...] + SHIFT * s1
        sol_ref[e] = sol_t * t - sol_1 * s1
        res_ref[e] = res_t * t - res_1 * s1 + sol_1 * s2
        for n, (ref, hbm) in enumerate(((sol_ref, sol_hbm), (res_ref, res_hbm))):
            copy = pltpu.make_async_copy(ref.at[e], hbm.at[:, at], sems.at[n, e])
            copy.start()
            copies.append(copy)
    for copy in copies:
        copy.wait()


def swap(x, axis, d):
    size = lax.axis_size(axis)
    return lax.ppermute(x, axis, [(i, i ^ d) for i in range(size)])


def along_z(x):
    return [x] + [swap(x, "rows", d) for d in range(2, lax.axis_size("rows"), 2)]


def across_x(same):
    return [same, swap(same, "rows", 1)]


def direct_cols(x):
    return [x] + [swap(x, "cols", e) for e in range(1, 4)]


def local(block_list, points, targets):
    n_rows = lax.axis_size("rows")
    n_cols = lax.axis_size("cols")
    row = lax.axis_index("rows")
    col = lax.axis_index("cols")
    block_rows, slots = block_list.shape
    dim, npoints = points.shape
    outputs = targets.shape[0]
    block_len = npoints // block_rows
    own_rows = block_rows // n_cols
    own_len = own_rows * block_len
    nb = block_rows * n_rows
    n_sub = own_rows * n_rows
    capacity = -(-block_rows * slots // n_rows)
    direct_rows = n_rows <= DIRECT_ROWS
    parts = 2 if direct_rows else 1
    n_part = n_sub // parts
    bound = min(block_rows * n_part, n_cols * capacity * (n_rows + 1))
    n_groups = -(-bound // GROUP)
    list_len = n_groups * GROUP + GROUP + 1
    place = jnp.stack([row, col])
    resident = parts * 2 * n_groups * GROUP * block_len * block_len <= RESIDENT_BYTES
    k_shape = (parts * n_groups, GROUP, block_len, block_len)
    limit = pltpu.CompilerParams(vmem_limit_bytes=(8 if resident else 32) * 1024 * 1024)
    ring = [] if resident else [
        pltpu.VMEM((RING, GROUP, block_len, block_len), BF16),
        pltpu.SemaphoreType.DMA((RING,)),
    ]
    k_spec = VMEM if resident else HBM
    cfg = Sizes(
        parts, n_groups, resident, nb, block_len, own_rows, block_rows, -(-own_rows * nb // LANES)
    )

    def shape(*dims, dtype=F32):
        return jax.ShapeDtypeStruct(dims, dtype)

    def own(x):
        return lax.dynamic_slice_in_dim(x, col * own_len, own_len, 1)

    def total_rows(x):
        if direct_rows:
            return pair_sum(across_x(pair_sum(along_z(x))))
        return lax.psum(x, "rows")

    lists = direct_cols(block_list)
    names = jnp.arange(nb, dtype=jnp.int32)
    direct = sum(jnp.sum((x[:, :, None] == names).astype(jnp.int32), axis=1) for x in lists)
    own_counts = lax.dynamic_slice_in_dim(direct, col * own_rows, own_rows, 0)
    coded = own_counts.reshape(-1)
    coded = jnp.pad(coded, (0, dim * LANES - coded.shape[0])).reshape(dim, LANES).astype(BF16)
    packed = jnp.concatenate([own(points), coded], axis=1)
    own_t = own(targets)

    def build(part, *operands):
        first, last = part == 0, part == parts - 1
        out = [
            pltpu.VMEM(k_shape, BF16) if resident else shape(*k_shape, dtype=BF16),
            shape(list_len, dtype=jnp.int32),
            shape(n_sub if last else n_part, block_len),
        ]
        out += [shape(block_rows, block_len, 2 * dim, dtype=BF16)] if first else []
        k_mat, *rest = pl.pallas_call(
            functools.partial(build_kernel, cfg, part),
            out_shape=out,
            in_specs=[SMEM, SMEM] + ([HBM, VMEM] if first else [VMEM] * 3 + [k_spec]),
            out_specs=[k_spec, SMEM] + [VMEM] * (len(out) - 2),
            scratch_shapes=([
                pltpu.VMEM((dim, npoints), BF16),
                pltpu.SemaphoreType.DMA,
            ] if first else []) + [
                pltpu.SMEM((list_len,), jnp.int32),
                pltpu.VMEM((n_part, 8, block_len), F32),
                pltpu.VMEM((n_part, 2 * dim, block_len), BF16),
                pltpu.VMEM((n_part // own_rows, cfg.count_rows, LANES), jnp.int32),
                pltpu.SMEM((n_part // own_rows, cfg.count_rows, LANES), jnp.int32),
                pltpu.SemaphoreType.DMA,
                *ring,
            ],
            compiler_params=limit,
            input_output_aliases={} if first else {5: 0},
            cost_estimate=pl.CostEstimate(
                flops=2 * 2 * dim * bound * block_len * block_len,
                bytes_accessed=2 * bound * block_len * block_len,
                transcendentals=bound * block_len * block_len,
            ),
            name="build",
        )(place, direct, *operands)
        if resident:
            k_mat = pltpu.with_memory_space_constraint(k_mat, pltpu.VMEM)
        return k_mat, *rest

    near = pltpu.with_memory_space_constraint(points, pltpu.HBM)
    if direct_rows:
        packed, early_t = lax.optimization_barrier((packed, own_t))
        same, other = across_x(jnp.stack(along_z(packed)))
        t_same = along_z(early_t)
        k_mat, list0, degree, lhs = build(0, near, same)
        degree, other, *t_same = lax.optimization_barrier((degree, other, *t_same))
        t_same, t_other = across_x(jnp.stack(t_same))
        other, t_same = lax.optimization_barrier((other, t_same))
        k_mat, list1, degree = build(1, lhs, degree, other, k_mat)
        degree, t_other = lax.optimization_barrier((degree, t_other))
        t_pieces, k_lists = [t_same, t_other], [list0, list1]
    else:
        k_mat, list0, degree, _ = build(0, near, lax.all_gather(packed, "rows"))
        t_pieces, k_lists = [lax.all_gather(own_t, "rows")], [list0]
    inv = 1.0 / jnp.sqrt(1.0 + total_rows(degree))

    def cost(n):
        return pl.CostEstimate(
            flops=2 * n * bound * outputs * block_len * block_len,
            bytes_accessed=n * bound * block_len * block_len,
            transcendentals=0,
        )

    near_z, near_y, cross_z, tail = pl.pallas_call(
        functools.partial(first_kernel, cfg),
        out_shape=[shape(outputs, own_len)] * 2 + [shape(2, outputs, own_len), shape(8, own_len)],
        in_specs=[SMEM, k_spec] + [SMEM] * parts + [VMEM] * (parts + 1),
        out_specs=[VMEM] * 4,
        scratch_shapes=[
            pltpu.VMEM((block_rows, outputs, block_len), F32),
            pltpu.VMEM((n_part, outputs, block_len), BF16),
            *ring,
        ],
        compiler_params=limit,
        cost_estimate=cost(parts),
        name="first",
    )(place, k_mat, *k_lists, *t_pieces, inv)

    got = swap(cross_z, "cols", 1)
    half = jnp.concatenate([near_z + got[0], near_y + got[1], tail], axis=0)
    far = swap(half, "cols", 2)
    lo, hi, end = slice(0, outputs), slice(outputs, 2 * outputs), slice(2 * outputs, None)
    s1_own = jnp.stack([
        jnp.concatenate([(half[lo] + far[hi]) * tail[:1], tail], axis=0),
        jnp.concatenate([(half[hi] + far[lo]) * far[end][:1], far[end]], axis=0),
    ])
    s1_got = swap(s1_own, "cols", 1)
    held_t = pltpu.with_memory_space_constraint(targets, pltpu.VMEM)

    def second(part, dtype):
        return pl.pallas_call(
            functools.partial(second_kernel, cfg, part),
            out_shape=shape(n_part // own_rows, outputs, own_len, dtype=dtype),
            in_specs=[SMEM, k_spec, SMEM] + [VMEM] * 3,
            out_specs=VMEM,
            scratch_shapes=[
                pltpu.VMEM((n_part, outputs, block_len), F32),
                pltpu.VMEM((block_rows, outputs, block_len), BF16),
                *ring,
            ],
            compiler_params=limit,
            cost_estimate=cost(1),
            name="second",
        )(place, k_mat, k_lists[part], held_t, s1_own, s1_got)

    if direct_rows:
        z2_other = swap(second(1, BF16), "rows", 1)
        z2_same = second(0, F32)
        z2_same, z2_other = lax.optimization_barrier((z2_same, z2_other))
        z2 = z2_same + z2_other.astype(F32)
        z2 = [z2[0]] + [swap(z2[n].astype(BF16), "rows", 2 * n) for n in range(1, n_rows // 2)]
    else:
        z2 = [lax.psum_scatter(second(0, F32), "rows", scatter_dimension=0)]
    grown, dots = pl.pallas_call(
        product_kernel,
        out_shape=(shape(outputs, own_len), shape(outputs, LANES)),
        in_specs=[SMEM] + [VMEM] * (2 + len(z2)),
        out_specs=(VMEM, VMEM),
        compiler_params=limit,
        name="products",
    )(place, held_t, s1_own, *z2)
    if direct_rows:
        dots = pair_sum(across_x(pair_sum(along_z(dots))))
    else:
        dots = lax.psum(dots, "rows")
    grown = jnp.stack([grown, swap(grown, "cols", 2)])
    ends = (s1_own, s1_got, grown, swap(grown, "cols", 1), *direct_cols(dots))
    ends = [pltpu.with_memory_space_constraint(x, pltpu.VMEM) for x in ends]

    return pl.pallas_call(
        final_kernel,
        out_shape=(shape(outputs, npoints), shape(outputs, npoints)),
        in_specs=[SMEM] + [VMEM] * 9,
        out_specs=(HBM, HBM),
        scratch_shapes=[
            pltpu.VMEM((4, outputs, own_len), F32),
            pltpu.VMEM((4, outputs, own_len), F32),
            pltpu.SemaphoreType.DMA((2, 4)),
        ],
        compiler_params=limit,
        name="final",
    )(place, held_t, *ends)


def solution(mesh):
    placed = (P("rows", "cols"), P(None, "rows"), P(None, "rows"))
    return jax.shard_map(
        local,
        mesh=mesh,
        in_specs=placed,
        out_specs=(P(None, "rows"), P(None, "rows")),
        check_vma=False,
    )
```

```python
import functools
from typing import NamedTuple

import jax
import jax.numpy as jnp
from jax import lax
from jax.experimental import pallas as pl
from jax.experimental.pallas import tpu as pltpu
from jax.sharding import PartitionSpec as P

REG = 1.5
RADIUS = 0.25
GROUP_BITS = 2
GROUP = 1 << GROUP_BITS
CODE_BITS = 12
CODE = 1 << CODE_BITS
RING = 3
STRIP = 32
LANES = 128
TINY = 1e-30
SHIFT = 0.375
DIRECT_ROWS = 8
RESIDENT_BYTES = 20 * 1024 * 1024

SMEM = pl.BlockSpec(memory_space=pltpu.SMEM)
VMEM = pl.BlockSpec(memory_space=pltpu.VMEM)
HBM = pl.BlockSpec(memory_space=pltpu.HBM)
F32 = jnp.float32
BF16 = jnp.bfloat16


def pair_sum(parts):
    while len(parts) > 1:
        parts = [a + b for a, b in zip(parts[::2], parts[1::2])]
    return parts[0]


class Sizes(NamedTuple):
    parts: int
    part_groups: int
    resident: bool
    nb: int
    block_len: int
    own_rows: int
    block_rows: int
    count_rows: int


def augment(x, first_ones):
    dim, n = x.shape
    norm = jnp.sum(x * x, axis=0, keepdims=True) / (RADIUS * RADIUS)
    high = norm.astype(BF16).astype(F32)
    rest = norm - high
    mid = rest.astype(BF16).astype(F32)
    low = rest - mid
    line = lax.broadcasted_iota(jnp.int32, (dim, n), 0)
    base = 3 if first_ones else 0
    ones_at = 0 if first_ones else 3
    tail = jnp.where((line >= ones_at) & (line < ones_at + 3), 1.0, 0.0)
    tail = jnp.where(line == base, high, tail)
    tail = jnp.where(line == base + 1, mid, tail)
    tail = jnp.where(line == base + 2, low, tail)
    return tail


def row_of(cfg, place, part, z):
    if cfg.parts == 1:
        return z
    return 2 * z + (place[0] & 1 if part == 0 else 1 - (place[0] & 1))


def slot_of(cfg, place, n):
    return n if cfg.parts == 1 else lax.shift_right_logical(place[0], 1) ^ n


def build_kernel(cfg, part, place, direct, *refs):
    last = part == cfg.parts - 1
    if part == 0:
        near_hbm, piece, refs = refs[0], refs[1], refs[2:]
        k_mat, listed, deg_ref, lhs = refs[:4]
        near_ref, near_sem, refs = refs[4], refs[5], refs[6:]
        near_copy = pltpu.make_async_copy(near_hbm, near_ref, near_sem)
        near_copy.start()
    else:
        lhs, first_deg, piece, _ = refs[:4]
        k_mat, listed, deg_ref = refs[4:7]
        refs = refs[7:]
    mlist, acc, rhs, counts_v, counts, count_sem = refs[:6]
    kbuf, sems = (None, None) if cfg.resident else refs[6:]
    row, col = place[0], place[1]
    own_rows, block_len, nb = cfg.own_rows, cfg.block_len, cfg.nb
    own_len = own_rows * block_len
    dim, held = piece.shape[1], piece.shape[0]
    scale = 1.0 / (RADIUS * RADIUS)

    def prepare(n, carry):
        z = slot_of(cfg, place, n)
        for k in range(own_rows):
            far = piece[n, :, k * block_len:(k + 1) * block_len]
            rhs[z * own_rows + k, :dim, :] = far
            rhs[z * own_rows + k, dim:, :] = augment(far.astype(F32), False).astype(BF16)
        named = piece[n, :, own_len:own_len + LANES]
        counts_v[z] = named.astype(F32)[:cfg.count_rows].astype(jnp.int32)
        return carry

    lax.fori_loop(0, held, prepare, 0, unroll=held <= 4)
    fetch = pltpu.make_async_copy(counts_v, counts, count_sem)
    fetch.start()
    if part == 0:
        near_copy.wait()
        for i in range(cfg.block_rows):
            near = near_ref[:, i * block_len:(i + 1) * block_len].astype(F32)
            full = jnp.concatenate([near * (-2.0 * scale), augment(near, True)], axis=0)
            lhs[i] = full.T.astype(BF16)
    acc[...] = jnp.zeros_like(acc)
    fetch.wait()

    pos = jnp.int32(0)
    for i in range(cfg.block_rows):
        me = row * cfg.block_rows + i
        spots = [k * nb + me for k in range(own_rows)]
        spots = [(lax.shift_right_logical(p, 7), p & (LANES - 1)) for p in spots]

        def note(z, at, i=i, me=me, spots=spots):
            for k in range(own_rows):
                name = row_of(cfg, place, part, z) * cfg.block_rows + col * own_rows + k
                m = direct[i, name] + jnp.where(name == me, 0, counts[z, spots[k][0], spots[k][1]])
                listed[at + 1] = i * CODE + z * own_rows + k
                mlist[at] = m
                at = at + jnp.where(m > 0, 1, 0)
            return at

        pos = lax.fori_loop(0, held, note, pos, unroll=4)
    for u in range(GROUP):
        listed[pos + u + 1] = 0
        mlist[pos + u] = 0
    total = lax.shift_right_logical(pos + (GROUP - 1), GROUP_BITS)
    listed[0] = total

    def copy_out(g):
        slot = lax.rem(g, RING)
        return pltpu.make_async_copy(kbuf.at[slot], k_mat.at[g], sems.at[slot])

    base = part * cfg.part_groups

    def step(g, carry):
        slot, target = (base + g, k_mat) if cfg.resident else (lax.rem(g, RING), kbuf)
        if not cfg.resident:

            @pl.when(g >= RING)
            def _():
                copy_out(g - RING).wait()

        for u in range(GROUP):
            code = listed[g * GROUP + u + 1]
            i, j = lax.shift_right_logical(code, CODE_BITS), code & (CODE - 1)
            m = mlist[g * GROUP + u].astype(F32)
            dist = jnp.dot(lhs[i], rhs[j], preferred_element_type=F32)
            sums = jnp.zeros((8, block_len), F32)
            for s in range(block_len // STRIP):
                rows = slice(s * STRIP, (s + 1) * STRIP)
                d = jnp.maximum(dist[rows], TINY)
                sc = d * lax.rsqrt(d)
                rem = jnp.maximum(1.0 - sc, 0.0)
                sq = rem * rem
                val = (sq * sq) * (sc * (4.0 * m) + m)
                target[slot, u, rows, :] = val.astype(BF16)
                for h in range(0, STRIP, 8):
                    sums = sums + val[h:h + 8]
            acc[j] += sums
        if not cfg.resident:
            copy_out(g).start()
        return carry

    lax.fori_loop(0, total, step, 0)
    if cfg.parts == 1 or not last:
        deg_ref[...] = jnp.sum(acc[...], axis=1)
    else:
        second = jnp.sum(acc[...], axis=1)
        for z in range(held):
            rows = slice(z * own_rows, (z + 1) * own_rows)
            for p, deg in enumerate((first_deg[rows, :], second[rows])):
                at = row_of(cfg, place, p, z) * own_rows
                for k in range(own_rows):
                    deg_ref[pl.ds(at + k, 1), :] = deg[k:k + 1]

    def drain(g, carry):
        copy_out(g).wait()
        return carry

    if not cfg.resident:
        lax.fori_loop(jnp.maximum(total - RING, 0), total, drain, 0)


def pieces_of(own, got):
    return own.at[0], got.at[0], own.at[1], got.at[1]


def walk(cfg, part, listed, k_mat, kbuf, sems, product, total_ref, by_row):
    total = listed[0]
    base = part * cfg.part_groups

    def copy_in(g):
        slot = lax.rem(g, RING)
        return pltpu.make_async_copy(k_mat.at[g], kbuf.at[slot], sems.at[slot])

    if not cfg.resident:
        for p in range(RING - 1):

            @pl.when(p < total)
            def _(p=p):
                copy_in(p).start()

    def step(g, carry):
        slot, source = (base + g, k_mat) if cfg.resident else (lax.rem(g, RING), kbuf)
        if not cfg.resident:

            @pl.when(g + (RING - 1) < total)
            def _():
                copy_in(g + (RING - 1)).start()

            copy_in(g).wait()
        codes = [listed[g * GROUP + u + 1] for u in range(GROUP)]
        pairs = [(lax.shift_right_logical(code, CODE_BITS), code & (CODE - 1)) for code in codes]
        terms = [product(i, j, source[slot, u]) for u, (i, j) in enumerate(pairs)]
        for (i, j), term in zip(pairs, terms):
            total_ref[i if by_row else j] += term
        return carry

    lax.fori_loop(0, total, step, 0)


def first_kernel(cfg, place, k_mat, *refs):
    n = cfg.parts
    lists, pieces, refs = refs[:n], refs[n:2 * n], refs[2 * n:]
    lent, refs = (refs[:n], refs[n:]) if n > 1 else (None, refs)
    inv_ref, near, near_y, cross, own_inv, z_acc, w_all, *ring = refs
    kbuf, sems = ring or (None, None)
    col = place[1]
    own_rows, block_len = cfg.own_rows, cfg.block_len
    z_acc[...] = jnp.zeros_like(z_acc)
    for part, (listed, piece) in enumerate(zip(lists, pieces)):
        held = piece.shape[0]

        def prepare(m, load, part=part):
            z = slot_of(cfg, place, m)
            for k in range(own_rows):
                w = load(slice(k * block_len, (k + 1) * block_len))
                at = row_of(cfg, place, part, z) * own_rows + k
                w_all[z * own_rows + k] = (w * inv_ref[pl.ds(at, 1), :]).astype(BF16)

        if lent is None:

            def one(m, carry, piece=piece, prepare=prepare):
                prepare(m, lambda cols: piece[m, :, cols])
                return carry

            lax.fori_loop(0, held, one, 0)
        else:
            own_len = own_rows * block_len

            @pl.when(col & 1 == 1)
            def _(piece=piece, prepare=prepare):
                for m in range(held):
                    prepare(m, lambda cols, m=m: piece[m, :, own_len:][:, cols])

            @pl.when(col & 1 == 0)
            def _(piece=lent[part], prepare=prepare):
                for m in range(held):
                    prepare(m, lambda cols, m=m: piece[m, :, cols])

        def product(i, j, block):
            return lax.dot_general(
                w_all[j], block, (((1,), (1,)), ((), ())), preferred_element_type=F32
            )

        walk(cfg, part, listed, k_mat, kbuf, sems, product, z_acc, True)
    for k in range(own_rows):
        cols = slice(k * block_len, (k + 1) * block_len)
        mine = inv_ref[pl.ds(place[0] * own_rows + k, 1), :]
        own_inv[:, cols] = jnp.broadcast_to(mine, (8, block_len))
        for e, ref in enumerate((near, cross.at[0], near_y, cross.at[1])):
            ref[:, cols] = z_acc[(col ^ e) * own_rows + k]


def second_kernel(cfg, part, place, k_mat, listed, t_ref, s1_own, s1_got, out, z_acc, w_all, *ring):
    kbuf, sems = ring or (None, None)
    own_rows, block_len = cfg.own_rows, cfg.block_len
    outputs = t_ref.shape[0]
    for e, packed in enumerate(pieces_of(s1_own, s1_got)):
        share = place[1] ^ e
        for k in range(own_rows):
            cols = slice(k * block_len, (k + 1) * block_len)
            i = share * own_rows + k
            t = t_ref[:, pl.ds(pl.multiple_of(i * block_len, LANES), block_len)]
            g = (packed[:outputs, cols] - SHIFT * t) * packed[outputs:outputs + 1, cols]
            w_all[i] = g.astype(BF16)
    z_acc[...] = jnp.zeros_like(z_acc)

    def product(i, j, block):
        return jnp.dot(w_all[i], block, preferred_element_type=F32)

    walk(cfg, part, listed, k_mat, kbuf, sems, product, z_acc, False)

    def hand_out(m, carry):
        z = slot_of(cfg, place, m)
        for k in range(own_rows):
            out[m, :, k * block_len:(k + 1) * block_len] = z_acc[z * own_rows + k].astype(out.dtype)
        return carry

    held = out.shape[0]
    lax.fori_loop(0, held, hand_out, 0, unroll=held <= 4)


def product_kernel(place, t_ref, s1_own, *refs):
    zs, grown_ref, dot_ref = refs[:-2], refs[-2], refs[-1]
    outputs, own_len = grown_ref.shape
    z = zs[0][...].astype(F32)
    for ref in zs[1:]:
        z = z + ref[...].astype(F32)
    grown = z * s1_own[0, outputs:outputs + 1, :]
    grown_ref[...] = grown
    s1 = s1_own[0, :outputs, :]
    s2 = grown + SHIFT * s1
    t = t_ref[:, pl.ds(pl.multiple_of(place[1] * own_len, LANES), own_len)]
    lane = lax.broadcasted_iota(jnp.int32, (outputs, LANES), 1)
    out = jnp.zeros(lane.shape, F32)
    for n, (a, b) in enumerate(((t, t), (t, s1), (s1, s1), (t, s2), (s1, s2))):
        out = jnp.where(lane == n, jnp.sum(a * b, axis=1, keepdims=True), out)
    dot_ref[...] = out


def final_kernel(place, t_ref, s1_own, s1_got, *refs):
    grown, all_dots = pieces_of(refs[0], refs[1]), refs[2:4]
    sol_hbm, res_hbm, sol_ref, res_ref, sems = refs[4:]
    s1s = pieces_of(s1_own, s1_got)
    outputs, own_len = grown[0].shape
    dots = jnp.where(place[1] & 1 == 1, all_dots[0][...], all_dots[1][...])
    tt, ts1, s1s1, ts2, s1s2 = (dots[:, n:n + 1] for n in range(5))
    a1 = tt / (REG * tt + ts1)
    p = 1.0 - REG * a1
    new = p * p * tt - 2.0 * p * a1 * ts1 + a1 * a1 * s1s1
    u = p + new / tt
    dd = u * u * tt - 2.0 * u * a1 * ts1 + a1 * a1 * s1s1
    dmd = u * u * ts1 - u * a1 * (s1s1 + ts2) + a1 * a1 * s1s2
    a2 = new / (REG * dd + dmd)
    sol_t, sol_1 = a1 + a2 * u, a2 * a1
    res_t, res_1 = p - a2 * REG * u, a1 + a2 * (u - REG * a1)
    copies = []
    for e in range(4):
        at = pl.ds(pl.multiple_of((place[1] ^ e) * own_len, LANES), own_len)
        t, s1 = t_ref[:, at], s1s[e][:outputs, :]
        s2 = grown[e][...] + SHIFT * s1
        sol_ref[e] = sol_t * t - sol_1 * s1
        res_ref[e] = res_t * t - res_1 * s1 + sol_1 * s2
        for n, (ref, hbm) in enumerate(((sol_ref, sol_hbm), (res_ref, res_hbm))):
            copy = pltpu.make_async_copy(ref.at[e], hbm.at[:, at], sems.at[n, e])
            copy.start()
            copies.append(copy)
    for copy in copies:
        copy.wait()


def swap(x, axis, d):
    size = lax.axis_size(axis)
    return lax.ppermute(x, axis, [(i, i ^ d) for i in range(size)])


def odd_swap(x, row_d, col_d):
    n_rows, n_cols = lax.axis_size("rows"), lax.axis_size("cols")
    pairs = [
        (r * n_cols + c, (r ^ row_d) * n_cols + (c ^ col_d))
        for r in range(n_rows)
        for c in range(1, n_cols, 2)
    ]
    return lax.ppermute(x, ("rows", "cols"), pairs)


def lend(x):
    size = lax.axis_size("cols")
    return lax.ppermute(x, "cols", [(c, c ^ 1) for c in range(1, size, 2)])


def along_z(x):
    return [x] + [swap(x, "rows", d) for d in range(2, lax.axis_size("rows"), 2)]


def across_x(same):
    return [same, swap(same, "rows", 1)]


def direct_cols(x):
    return [x] + [swap(x, "cols", e) for e in range(1, 4)]


def local(block_list, points, targets):
    n_rows = lax.axis_size("rows")
    n_cols = lax.axis_size("cols")
    row = lax.axis_index("rows")
    col = lax.axis_index("cols")
    block_rows, slots = block_list.shape
    dim, npoints = points.shape
    outputs = targets.shape[0]
    block_len = npoints // block_rows
    own_rows = block_rows // n_cols
    own_len = own_rows * block_len
    nb = block_rows * n_rows
    n_sub = own_rows * n_rows
    capacity = -(-block_rows * slots // n_rows)
    direct_rows = n_rows <= DIRECT_ROWS
    parts = 2 if direct_rows else 1
    n_part = n_sub // parts
    bound = min(block_rows * n_part, n_cols * capacity * (n_rows + 1))
    n_groups = -(-bound // GROUP)
    list_len = n_groups * GROUP + GROUP + 1
    place = jnp.stack([row, col])
    resident = parts * 2 * n_groups * GROUP * block_len * block_len <= RESIDENT_BYTES
    k_shape = (parts * n_groups, GROUP, block_len, block_len)
    limit = pltpu.CompilerParams(vmem_limit_bytes=(8 if resident else 32) * 1024 * 1024)
    ring = [] if resident else [
        pltpu.VMEM((RING, GROUP, block_len, block_len), BF16),
        pltpu.SemaphoreType.DMA((RING,)),
    ]
    k_spec = VMEM if resident else HBM
    cfg = Sizes(
        parts, n_groups, resident, nb, block_len, own_rows, block_rows, -(-own_rows * nb // LANES)
    )

    def shape(*dims, dtype=F32):
        return jax.ShapeDtypeStruct(dims, dtype)

    def own(x):
        return lax.dynamic_slice_in_dim(x, col * own_len, own_len, 1)

    def total_rows(x):
        if direct_rows:
            return pair_sum(across_x(pair_sum(along_z(x))))
        return lax.psum(x, "rows")

    lists = direct_cols(block_list)
    names = jnp.arange(nb, dtype=jnp.int32)
    direct = sum(jnp.sum((x[:, :, None] == names).astype(jnp.int32), axis=1) for x in lists)
    own_counts = lax.dynamic_slice_in_dim(direct, col * own_rows, own_rows, 0)
    coded = own_counts.reshape(-1)
    coded = jnp.pad(coded, (0, dim * LANES - coded.shape[0])).reshape(dim, LANES).astype(BF16)
    packed = jnp.concatenate([own(points), coded], axis=1)

    def build(part, *operands):
        first, last = part == 0, part == parts - 1
        out = [
            pltpu.VMEM(k_shape, BF16) if resident else shape(*k_shape, dtype=BF16),
            shape(list_len, dtype=jnp.int32),
            shape(n_sub if last else n_part, block_len),
        ]
        out += [shape(block_rows, block_len, 2 * dim, dtype=BF16)] if first else []
        k_mat, *rest = pl.pallas_call(
            functools.partial(build_kernel, cfg, part),
            out_shape=out,
            in_specs=[SMEM, SMEM] + ([HBM, VMEM] if first else [VMEM] * 3 + [k_spec]),
            out_specs=[k_spec, SMEM] + [VMEM] * (len(out) - 2),
            scratch_shapes=([
                pltpu.VMEM((dim, npoints), BF16),
                pltpu.SemaphoreType.DMA,
            ] if first else []) + [
                pltpu.SMEM((list_len,), jnp.int32),
                pltpu.VMEM((n_part, 8, block_len), F32),
                pltpu.VMEM((n_part, 2 * dim, block_len), BF16),
                pltpu.VMEM((n_part // own_rows, cfg.count_rows, LANES), jnp.int32),
                pltpu.SMEM((n_part // own_rows, cfg.count_rows, LANES), jnp.int32),
                pltpu.SemaphoreType.DMA,
                *ring,
            ],
            compiler_params=limit,
            input_output_aliases={} if first else {5: 0},
            cost_estimate=pl.CostEstimate(
                flops=2 * 2 * dim * bound * block_len * block_len,
                bytes_accessed=2 * bound * block_len * block_len,
                transcendentals=bound * block_len * block_len,
            ),
            name="build",
        )(place, direct, *operands)
        if resident:
            k_mat = pltpu.with_memory_space_constraint(k_mat, pltpu.VMEM)
        return k_mat, *rest

    near = pltpu.with_memory_space_constraint(points, pltpu.HBM)
    if direct_rows:
        both_t = lax.dynamic_slice_in_dim(targets, (col - (col & 1)) * own_len, 2 * own_len, 1)
        packed, both_t = lax.optimization_barrier((packed, both_t))
        same, other = across_x(jnp.stack(along_z(packed)))
        t_same = [both_t] + [odd_swap(both_t, d, 0) for d in range(2, n_rows, 2)]
        k_mat, list0, degree, lhs = build(0, near, same)
        degree, other, *t_same = lax.optimization_barrier((degree, other, *t_same))
        t_same = jnp.stack(t_same)
        t_other = odd_swap(t_same, 1, 0)
        other, t_same = lax.optimization_barrier((other, t_same))
        k_mat, list1, degree = build(1, lhs, degree, other, k_mat)
        degree, t_other = lax.optimization_barrier((degree, t_other))
        t_pieces = [t_same, t_other, lend(t_same), lend(t_other)]
        k_lists = [list0, list1]
    else:
        k_mat, list0, degree, _ = build(0, near, lax.all_gather(packed, "rows"))
        t_pieces, k_lists = [lax.all_gather(own(targets), "rows")], [list0]
    inv = 1.0 / jnp.sqrt(1.0 + total_rows(degree))

    def cost(n):
        return pl.CostEstimate(
            flops=2 * n * bound * outputs * block_len * block_len,
            bytes_accessed=n * bound * block_len * block_len,
            transcendentals=0,
        )

    near_z, near_y, cross_z, tail = pl.pallas_call(
        functools.partial(first_kernel, cfg),
        out_shape=[shape(outputs, own_len)] * 2 + [shape(2, outputs, own_len), shape(8, own_len)],
        in_specs=[SMEM, k_spec] + [SMEM] * parts + [VMEM] * (len(t_pieces) + 1),
        out_specs=[VMEM] * 4,
        scratch_shapes=[
            pltpu.VMEM((block_rows, outputs, block_len), F32),
            pltpu.VMEM((n_part, outputs, block_len), BF16),
            *ring,
        ],
        compiler_params=limit,
        cost_estimate=cost(parts),
        name="first",
    )(place, k_mat, *k_lists, *t_pieces, inv)

    got = swap(cross_z, "cols", 1)
    half = jnp.concatenate([near_z + got[0], near_y + got[1], tail], axis=0)
    far = swap(half, "cols", 2)
    lo, hi, end = slice(0, outputs), slice(outputs, 2 * outputs), slice(2 * outputs, None)
    s1_own = jnp.stack([
        jnp.concatenate([(half[lo] + far[hi]) * tail[:1], tail], axis=0),
        jnp.concatenate([(half[hi] + far[lo]) * far[end][:1], far[end]], axis=0),
    ])
    s1_got = swap(s1_own, "cols", 1)
    held_t = pltpu.with_memory_space_constraint(targets, pltpu.VMEM)

    def second(part, dtype):
        return pl.pallas_call(
            functools.partial(second_kernel, cfg, part),
            out_shape=shape(n_part // own_rows, outputs, own_len, dtype=dtype),
            in_specs=[SMEM, k_spec, SMEM] + [VMEM] * 3,
            out_specs=VMEM,
            scratch_shapes=[
                pltpu.VMEM((n_part, outputs, block_len), F32),
                pltpu.VMEM((block_rows, outputs, block_len), BF16),
                *ring,
            ],
            compiler_params=limit,
            cost_estimate=cost(1),
            name="second",
        )(place, k_mat, k_lists[part], held_t, s1_own, s1_got)

    if direct_rows:
        z2_other = swap(second(1, BF16), "rows", 1)
        z2_same = second(0, F32)
        z2_same, z2_other = lax.optimization_barrier((z2_same, z2_other))
        z2 = z2_same + z2_other.astype(F32)
        z2 = [z2[0]] + [swap(z2[n].astype(BF16), "rows", 2 * n) for n in range(1, n_rows // 2)]
    else:
        z2 = [lax.psum_scatter(second(0, F32), "rows", scatter_dimension=0)]
    grown, dots = pl.pallas_call(
        product_kernel,
        out_shape=(shape(outputs, own_len), shape(outputs, LANES)),
        in_specs=[SMEM] + [VMEM] * (2 + len(z2)),
        out_specs=(VMEM, VMEM),
        compiler_params=limit,
        name="products",
    )(place, held_t, s1_own, *z2)
    if direct_rows:
        dots = dots + swap(dots, "cols", 1)
        dots = pair_sum([dots] + [odd_swap(dots, d, 0) for d in range(2, n_rows, 2)])
        dots = pair_sum([dots, odd_swap(dots, 1, 0), odd_swap(dots, 0, 2), odd_swap(dots, 1, 2)])
        dots = [dots, lend(dots)]
    else:
        dots = [lax.psum(dots, ("rows", "cols"))] * 2
    grown = jnp.stack([grown, swap(grown, "cols", 2)])
    ends = (s1_own, s1_got, grown, swap(grown, "cols", 1), *dots)
    ends = [pltpu.with_memory_space_constraint(x, pltpu.VMEM) for x in ends]

    return pl.pallas_call(
        final_kernel,
        out_shape=(shape(outputs, npoints), shape(outputs, npoints)),
        in_specs=[SMEM] + [VMEM] * 7,
        out_specs=(HBM, HBM),
        scratch_shapes=[
            pltpu.VMEM((4, outputs, own_len), F32),
            pltpu.VMEM((4, outputs, own_len), F32),
            pltpu.SemaphoreType.DMA((2, 4)),
        ],
        compiler_params=limit,
        name="final",
    )(place, held_t, *ends)


def solution(mesh):
    placed = (P("rows", "cols"), P(None, "rows"), P(None, "rows"))
    return jax.shard_map(
        local,
        mesh=mesh,
        in_specs=placed,
        out_specs=(P(None, "rows"), P(None, "rows")),
        check_vma=False,
    )
```

```python
import functools
from typing import NamedTuple

import jax
import jax.numpy as jnp
from jax import lax
from jax.experimental import pallas as pl
from jax.experimental.pallas import tpu as pltpu
from jax.sharding import PartitionSpec as P

REG = 1.5
RADIUS = 0.25
GROUP_BITS = 2
GROUP = 1 << GROUP_BITS
CODE_BITS = 12
CODE = 1 << CODE_BITS
RING = 3
STRIP = 32
LANES = 128
TINY = 1e-30
SHIFT = 0.375
DIRECT_ROWS = 8
RESIDENT_BYTES = 20 * 1024 * 1024

SMEM = pl.BlockSpec(memory_space=pltpu.SMEM)
VMEM = pl.BlockSpec(memory_space=pltpu.VMEM)
HBM = pl.BlockSpec(memory_space=pltpu.HBM)
F32 = jnp.float32
BF16 = jnp.bfloat16


def pair_sum(parts):
    while len(parts) > 1:
        parts = [a + b for a, b in zip(parts[::2], parts[1::2])]
    return parts[0]


class Sizes(NamedTuple):
    parts: int
    part_groups: int
    resident: bool
    nb: int
    block_len: int
    own_rows: int
    block_rows: int
    count_rows: int


def augment(x, first_ones):
    dim, n = x.shape
    norm = jnp.sum(x * x, axis=0, keepdims=True) / (RADIUS * RADIUS)
    high = norm.astype(BF16).astype(F32)
    rest = norm - high
    mid = rest.astype(BF16).astype(F32)
    low = rest - mid
    line = lax.broadcasted_iota(jnp.int32, (dim, n), 0)
    base = 3 if first_ones else 0
    ones_at = 0 if first_ones else 3
    tail = jnp.where((line >= ones_at) & (line < ones_at + 3), 1.0, 0.0)
    tail = jnp.where(line == base, high, tail)
    tail = jnp.where(line == base + 1, mid, tail)
    tail = jnp.where(line == base + 2, low, tail)
    return tail


def row_of(cfg, place, part, z):
    if cfg.parts == 1:
        return z
    return 2 * z + (place[0] & 1 if part == 0 else 1 - (place[0] & 1))


def slot_of(cfg, place, n):
    return n if cfg.parts == 1 else lax.shift_right_logical(place[0], 1) ^ n


def build_kernel(cfg, part, place, direct, *refs):
    last = part == cfg.parts - 1
    if part == 0:
        near_hbm, piece, refs = refs[0], refs[1], refs[2:]
        k_mat, listed, deg_ref, lhs = refs[:4]
        near_ref, near_sem, refs = refs[4], refs[5], refs[6:]
        near_copy = pltpu.make_async_copy(near_hbm, near_ref, near_sem)
        near_copy.start()
    else:
        lhs, first_deg, piece, _ = refs[:4]
        k_mat, listed, deg_ref = refs[4:7]
        refs = refs[7:]
    mlist, acc, rhs, dist, counts_v, counts, count_sem = refs[:7]
    kbuf, sems = (None, None) if cfg.resident else refs[7:]
    row, col = place[0], place[1]
    own_rows, block_len, nb = cfg.own_rows, cfg.block_len, cfg.nb
    own_len = own_rows * block_len
    dim, held = piece.shape[1], piece.shape[0]
    scale = 1.0 / (RADIUS * RADIUS)

    def count(n, carry):
        named = piece[n, :, own_len:own_len + LANES]
        counts_v[slot_of(cfg, place, n)] = named.astype(F32)[:cfg.count_rows].astype(jnp.int32)
        return carry

    def prepare(n, carry):
        z = slot_of(cfg, place, n)
        for k in range(own_rows):
            far = piece[n, :, k * block_len:(k + 1) * block_len]
            rhs[z * own_rows + k, :dim, :] = far
            rhs[z * own_rows + k, dim:, :] = augment(far.astype(F32), False).astype(BF16)
        return carry

    lax.fori_loop(0, held, count, 0, unroll=held <= 4)
    fetch = pltpu.make_async_copy(counts_v, counts, count_sem)
    fetch.start()
    lax.fori_loop(0, held, prepare, 0, unroll=held <= 4)
    acc[...] = jnp.zeros_like(acc)
    if part == 0:
        near_copy.wait()
        for i in range(cfg.block_rows):
            near = near_ref[:, i * block_len:(i + 1) * block_len].astype(F32)
            full = jnp.concatenate([near * (-2.0 * scale), augment(near, True)], axis=0)
            lhs[i] = full.T.astype(BF16)
    fetch.wait()

    pos = jnp.int32(0)
    for i in range(cfg.block_rows):
        me = row * cfg.block_rows + i
        spots = [k * nb + me for k in range(own_rows)]
        spots = [(lax.shift_right_logical(p, 7), p & (LANES - 1)) for p in spots]

        def note(z, at, i=i, me=me, spots=spots):
            for k in range(own_rows):
                name = row_of(cfg, place, part, z) * cfg.block_rows + col * own_rows + k
                m = direct[i, name] + jnp.where(name == me, 0, counts[z, spots[k][0], spots[k][1]])
                listed[at + 1] = i * CODE + z * own_rows + k
                mlist[at] = m
                at = at + jnp.where(m > 0, 1, 0)
            return at

        if held <= 4:
            for z in range(held):
                pos = note(z, pos)
        else:
            pos = lax.fori_loop(0, held, note, pos, unroll=4)
    for u in range(GROUP):
        listed[pos + u + 1] = 0
        mlist[pos + u] = 0
    total = lax.shift_right_logical(pos + (GROUP - 1), GROUP_BITS)
    listed[0] = total

    def copy_out(g):
        slot = lax.rem(g, RING)
        return pltpu.make_async_copy(kbuf.at[slot], k_mat.at[g], sems.at[slot])

    base = part * cfg.part_groups

    def distances(e, slot):
        code = listed[e + 1]
        i, j = lax.shift_right_logical(code, CODE_BITS), code & (CODE - 1)
        dist[slot] = jnp.dot(lhs[i], rhs[j], preferred_element_type=F32)

    distances(0, 0)

    def step(g, carry):
        slot, target = (base + g, k_mat) if cfg.resident else (lax.rem(g, RING), kbuf)
        if not cfg.resident:

            @pl.when(g >= RING)
            def _():
                copy_out(g - RING).wait()

        for u in range(GROUP):
            distances(g * GROUP + u + 1, (u + 1) % 2)
            j = listed[g * GROUP + u + 1] & (CODE - 1)
            m = mlist[g * GROUP + u].astype(F32)
            sums = jnp.zeros((8, block_len), F32)
            for s in range(block_len // STRIP):
                rows = slice(s * STRIP, (s + 1) * STRIP)
                d = jnp.maximum(dist[u % 2, rows, :], TINY)
                sc = d * lax.rsqrt(d)
                rem = jnp.maximum(1.0 - sc, 0.0)
                sq = rem * rem
                val = (sq * sq) * (sc * (4.0 * m) + m)
                target[slot, u, rows, :] = val.astype(BF16)
                for h in range(0, STRIP, 8):
                    sums = sums + val[h:h + 8]
            acc[j] += sums
        if not cfg.resident:
            copy_out(g).start()
        return carry

    lax.fori_loop(0, total, step, 0)
    if cfg.parts == 1 or not last:
        deg_ref[...] = jnp.sum(acc[...], axis=1)
    else:
        second = jnp.sum(acc[...], axis=1)
        for z in range(held):
            rows = slice(z * own_rows, (z + 1) * own_rows)
            for p, deg in enumerate((first_deg[rows, :], second[rows])):
                at = row_of(cfg, place, p, z) * own_rows
                for k in range(own_rows):
                    deg_ref[pl.ds(at + k, 1), :] = deg[k:k + 1]

    def drain(g, carry):
        copy_out(g).wait()
        return carry

    if not cfg.resident:
        lax.fori_loop(jnp.maximum(total - RING, 0), total, drain, 0)


def pieces_of(own, got):
    return own.at[0], got.at[0], own.at[1], got.at[1]


def walk(cfg, part, listed, k_mat, kbuf, sems, product, total_ref, by_row):
    total = listed[0]
    base = part * cfg.part_groups

    def copy_in(g):
        slot = lax.rem(g, RING)
        return pltpu.make_async_copy(k_mat.at[g], kbuf.at[slot], sems.at[slot])

    if not cfg.resident:
        for p in range(RING - 1):

            @pl.when(p < total)
            def _(p=p):
                copy_in(p).start()

    def step(g, carry):
        slot, source = (base + g, k_mat) if cfg.resident else (lax.rem(g, RING), kbuf)
        if not cfg.resident:

            @pl.when(g + (RING - 1) < total)
            def _():
                copy_in(g + (RING - 1)).start()

            copy_in(g).wait()
        codes = [listed[g * GROUP + u + 1] for u in range(GROUP)]
        pairs = [(lax.shift_right_logical(code, CODE_BITS), code & (CODE - 1)) for code in codes]
        terms = [product(i, j, source[slot, u]) for u, (i, j) in enumerate(pairs)]
        for (i, j), term in zip(pairs, terms):
            total_ref[i if by_row else j] += term
        return carry

    lax.fori_loop(0, total, step, 0)


def first_kernel(cfg, place, k_mat, *refs):
    n = cfg.parts
    lists, pieces, inv_ref, refs = refs[:n], refs[n:2 * n], refs[2 * n], refs[2 * n + 1:]
    near, near_y, cross, own_inv, z_acc, w_all, *ring = refs
    kbuf, sems = ring or (None, None)
    col = place[1]
    own_rows, block_len = cfg.own_rows, cfg.block_len
    z_acc[...] = jnp.zeros_like(z_acc)
    for part, (listed, piece) in enumerate(zip(lists, pieces)):
        held = piece.shape[0]

        def prepare(m, carry, part=part, piece=piece):
            z = slot_of(cfg, place, m)
            for k in range(own_rows):
                w = piece[m, :, k * block_len:(k + 1) * block_len]
                at = row_of(cfg, place, part, z) * own_rows + k
                w_all[z * own_rows + k] = (w * inv_ref[pl.ds(at, 1), :]).astype(BF16)
            return carry

        lax.fori_loop(0, held, prepare, 0, unroll=held <= 4)

        def product(i, j, block):
            return lax.dot_general(
                w_all[j], block, (((1,), (1,)), ((), ())), preferred_element_type=F32
            )

        walk(cfg, part, listed, k_mat, kbuf, sems, product, z_acc, True)
    for k in range(own_rows):
        cols = slice(k * block_len, (k + 1) * block_len)
        mine = inv_ref[pl.ds(place[0] * own_rows + k, 1), :]
        own_inv[:, cols] = jnp.broadcast_to(mine, (8, block_len))
        for e, ref in enumerate((near, cross.at[0], near_y, cross.at[1])):
            ref[:, cols] = z_acc[(col ^ e) * own_rows + k]


def second_kernel(cfg, part, place, k_mat, listed, t_ref, s1_own, s1_got, out, z_acc, w_all, *ring):
    kbuf, sems = ring or (None, None)
    own_rows, block_len = cfg.own_rows, cfg.block_len
    outputs = t_ref.shape[0]
    for e, packed in enumerate(pieces_of(s1_own, s1_got)):
        share = place[1] ^ e
        for k in range(own_rows):
            cols = slice(k * block_len, (k + 1) * block_len)
            i = share * own_rows + k
            t = t_ref[:, pl.ds(pl.multiple_of(i * block_len, LANES), block_len)]
            g = (packed[:outputs, cols] - SHIFT * t) * packed[outputs:outputs + 1, cols]
            w_all[i] = g.astype(BF16)
    z_acc[...] = jnp.zeros_like(z_acc)

    def product(i, j, block):
        return jnp.dot(w_all[i], block, preferred_element_type=F32)

    walk(cfg, part, listed, k_mat, kbuf, sems, product, z_acc, False)

    def hand_out(m, carry):
        z = slot_of(cfg, place, m)
        for k in range(own_rows):
            out[m, :, k * block_len:(k + 1) * block_len] = z_acc[z * own_rows + k].astype(out.dtype)
        return carry

    held = out.shape[0]
    lax.fori_loop(0, held, hand_out, 0, unroll=held <= 4)


def product_kernel(place, t_ref, s1_own, *refs):
    zs, grown_ref, dot_ref = refs[:-2], refs[-2], refs[-1]
    outputs, own_len = grown_ref.shape
    z = zs[0][...].astype(F32)
    for ref in zs[1:]:
        z = z + ref[...].astype(F32)
    grown = z * s1_own[0, outputs:outputs + 1, :]
    grown_ref[...] = grown
    s1 = s1_own[0, :outputs, :]
    s2 = grown + SHIFT * s1
    t = t_ref[:, pl.ds(pl.multiple_of(place[1] * own_len, LANES), own_len)]
    lane = lax.broadcasted_iota(jnp.int32, (outputs, LANES), 1)
    out = jnp.zeros(lane.shape, F32)
    for n, (a, b) in enumerate(((t, t), (t, s1), (s1, s1), (t, s2), (s1, s2))):
        out = jnp.where(lane == n, jnp.sum(a * b, axis=1, keepdims=True), out)
    dot_ref[...] = out


def final_kernel(place, t_ref, s1_own, s1_got, *refs):
    grown, all_dots = pieces_of(refs[0], refs[1]), refs[2:6]
    sol_hbm, res_hbm, sol_ref, res_ref, sems = refs[6:]
    s1s = pieces_of(s1_own, s1_got)
    outputs, own_len = grown[0].shape
    dots = pair_sum([ref[...] for ref in all_dots])
    tt, ts1, s1s1, ts2, s1s2 = (dots[:, n:n + 1] for n in range(5))
    a1 = tt / (REG * tt + ts1)
    p = 1.0 - REG * a1
    new = p * p * tt - 2.0 * p * a1 * ts1 + a1 * a1 * s1s1
    u = p + new / tt
    dd = u * u * tt - 2.0 * u * a1 * ts1 + a1 * a1 * s1s1
    dmd = u * u * ts1 - u * a1 * (s1s1 + ts2) + a1 * a1 * s1s2
    a2 = new / (REG * dd + dmd)
    sol_t, sol_1 = a1 + a2 * u, a2 * a1
    res_t, res_1 = p - a2 * REG * u, a1 + a2 * (u - REG * a1)
    copies = []
    for e in range(4):
        at = pl.ds(pl.multiple_of((place[1] ^ e) * own_len, LANES), own_len)
        t, s1 = t_ref[:, at], s1s[e][:outputs, :]
        s2 = grown[e][...] + SHIFT * s1
        sol_ref[e] = sol_t * t - sol_1 * s1
        res_ref[e] = res_t * t - res_1 * s1 + sol_1 * s2
        for n, (ref, hbm) in enumerate(((sol_ref, sol_hbm), (res_ref, res_hbm))):
            copy = pltpu.make_async_copy(ref.at[e], hbm.at[:, at], sems.at[n, e])
            copy.start()
            copies.append(copy)
    for copy in copies:
        copy.wait()


def swap(x, axis, d):
    size = lax.axis_size(axis)
    return lax.ppermute(x, axis, [(i, i ^ d) for i in range(size)])


def along_z(x):
    return [x] + [swap(x, "rows", d) for d in range(2, lax.axis_size("rows"), 2)]


def across_x(same):
    return [same, swap(same, "rows", 1)]


def direct_cols(x):
    return [x] + [swap(x, "cols", e) for e in range(1, 4)]


def local(block_list, points, targets):
    n_rows = lax.axis_size("rows")
    n_cols = lax.axis_size("cols")
    row = lax.axis_index("rows")
    col = lax.axis_index("cols")
    block_rows, slots = block_list.shape
    dim, npoints = points.shape
    outputs = targets.shape[0]
    block_len = npoints // block_rows
    own_rows = block_rows // n_cols
    own_len = own_rows * block_len
    nb = block_rows * n_rows
    n_sub = own_rows * n_rows
    capacity = -(-block_rows * slots // n_rows)
    direct_rows = n_rows <= DIRECT_ROWS
    parts = 2 if direct_rows else 1
    n_part = n_sub // parts
    bound = min(block_rows * n_part, n_cols * capacity * (n_rows + 1))
    n_groups = -(-bound // GROUP)
    list_len = n_groups * GROUP + GROUP + 1
    place = jnp.stack([row, col])
    resident = parts * 2 * n_groups * GROUP * block_len * block_len <= RESIDENT_BYTES
    k_shape = (parts * n_groups, GROUP, block_len, block_len)
    limit = pltpu.CompilerParams(vmem_limit_bytes=(8 if resident else 32) * 1024 * 1024)
    ring = [] if resident else [
        pltpu.VMEM((RING, GROUP, block_len, block_len), BF16),
        pltpu.SemaphoreType.DMA((RING,)),
    ]
    k_spec = VMEM if resident else HBM
    cfg = Sizes(
        parts, n_groups, resident, nb, block_len, own_rows, block_rows, -(-own_rows * nb // LANES)
    )

    def shape(*dims, dtype=F32):
        return jax.ShapeDtypeStruct(dims, dtype)

    def own(x):
        return lax.dynamic_slice_in_dim(x, col * own_len, own_len, 1)

    def total_rows(x):
        if direct_rows:
            return pair_sum(across_x(pair_sum(along_z(x))))
        return lax.psum(x, "rows")

    lists = direct_cols(block_list)
    names = jnp.arange(nb, dtype=jnp.int32)
    direct = sum(jnp.sum((x[:, :, None] == names).astype(jnp.int32), axis=1) for x in lists)
    own_counts = lax.dynamic_slice_in_dim(direct, col * own_rows, own_rows, 0)
    coded = own_counts.reshape(-1)
    coded = jnp.pad(coded, (0, dim * LANES - coded.shape[0])).reshape(dim, LANES).astype(BF16)
    packed = jnp.concatenate([own(points), coded], axis=1)
    own_t = own(targets)

    def build(part, *operands):
        first, last = part == 0, part == parts - 1
        out = [
            pltpu.VMEM(k_shape, BF16) if resident else shape(*k_shape, dtype=BF16),
            shape(list_len, dtype=jnp.int32),
            shape(n_sub if last else n_part, block_len),
        ]
        out += [shape(block_rows, block_len, 2 * dim, dtype=BF16)] if first else []
        k_mat, *rest = pl.pallas_call(
            functools.partial(build_kernel, cfg, part),
            out_shape=out,
            in_specs=[SMEM, SMEM] + ([HBM, VMEM] if first else [VMEM] * 3 + [k_spec]),
            out_specs=[k_spec, SMEM] + [VMEM] * (len(out) - 2),
            scratch_shapes=([
                pltpu.VMEM((dim, npoints), BF16),
                pltpu.SemaphoreType.DMA,
            ] if first else []) + [
                pltpu.SMEM((list_len,), jnp.int32),
                pltpu.VMEM((n_part, 8, block_len), F32),
                pltpu.VMEM((n_part, 2 * dim, block_len), BF16),
                pltpu.VMEM((2, block_len, block_len), F32),
                pltpu.VMEM((n_part // own_rows, cfg.count_rows, LANES), jnp.int32),
                pltpu.SMEM((n_part // own_rows, cfg.count_rows, LANES), jnp.int32),
                pltpu.SemaphoreType.DMA,
                *ring,
            ],
            compiler_params=limit,
            input_output_aliases={} if first else {5: 0},
            cost_estimate=pl.CostEstimate(
                flops=2 * 2 * dim * bound * block_len * block_len,
                bytes_accessed=2 * bound * block_len * block_len,
                transcendentals=bound * block_len * block_len,
            ),
            name="build",
        )(place, direct, *operands)
        if resident:
            k_mat = pltpu.with_memory_space_constraint(k_mat, pltpu.VMEM)
        return k_mat, *rest

    near = pltpu.with_memory_space_constraint(points, pltpu.HBM)
    if direct_rows:
        packed, early_t = lax.optimization_barrier((packed, own_t))
        same, other = across_x(jnp.stack(along_z(packed)))
        t_same = along_z(early_t)
        k_mat, list0, degree, lhs = build(0, near, same)
        degree, other, *t_same = lax.optimization_barrier((degree, other, *t_same))
        t_same, t_other = across_x(jnp.stack(t_same))
        other, t_same = lax.optimization_barrier((other, t_same))
        k_mat, list1, degree = build(1, lhs, degree, other, k_mat)
        degree, t_other = lax.optimization_barrier((degree, t_other))
        t_pieces, k_lists = [t_same, t_other], [list0, list1]
    else:
        k_mat, list0, degree, _ = build(0, near, lax.all_gather(packed, "rows"))
        t_pieces, k_lists = [lax.all_gather(own_t, "rows")], [list0]
    inv = 1.0 / jnp.sqrt(1.0 + total_rows(degree))

    def cost(n):
        return pl.CostEstimate(
            flops=2 * n * bound * outputs * block_len * block_len,
            bytes_accessed=n * bound * block_len * block_len,
            transcendentals=0,
        )

    near_z, near_y, cross_z, tail = pl.pallas_call(
        functools.partial(first_kernel, cfg),
        out_shape=[shape(outputs, own_len)] * 2 + [shape(2, outputs, own_len), shape(8, own_len)],
        in_specs=[SMEM, k_spec] + [SMEM] * parts + [VMEM] * (parts + 1),
        out_specs=[VMEM] * 4,
        scratch_shapes=[
            pltpu.VMEM((block_rows, outputs, block_len), F32),
            pltpu.VMEM((n_part, outputs, block_len), BF16),
            *ring,
        ],
        compiler_params=limit,
        cost_estimate=cost(parts),
        name="first",
    )(place, k_mat, *k_lists, *t_pieces, inv)

    got = swap(cross_z, "cols", 1)
    half = jnp.concatenate([near_z + got[0], near_y + got[1], tail], axis=0)
    far = swap(half, "cols", 2)
    lo, hi, end = slice(0, outputs), slice(outputs, 2 * outputs), slice(2 * outputs, None)
    s1_own = jnp.stack([
        jnp.concatenate([(half[lo] + far[hi]) * tail[:1], tail], axis=0),
        jnp.concatenate([(half[hi] + far[lo]) * far[end][:1], far[end]], axis=0),
    ])
    s1_got = swap(s1_own, "cols", 1)
    held_t = pltpu.with_memory_space_constraint(targets, pltpu.VMEM)

    def second(part, dtype):
        return pl.pallas_call(
            functools.partial(second_kernel, cfg, part),
            out_shape=shape(n_part // own_rows, outputs, own_len, dtype=dtype),
            in_specs=[SMEM, k_spec, SMEM] + [VMEM] * 3,
            out_specs=VMEM,
            scratch_shapes=[
                pltpu.VMEM((n_part, outputs, block_len), F32),
                pltpu.VMEM((block_rows, outputs, block_len), BF16),
                *ring,
            ],
            compiler_params=limit,
            cost_estimate=cost(1),
            name="second",
        )(place, k_mat, k_lists[part], held_t, s1_own, s1_got)

    if direct_rows:
        z2_other = swap(second(1, BF16), "rows", 1)
        z2_same = second(0, F32)
        z2_same, z2_other = lax.optimization_barrier((z2_same, z2_other))
        z2 = z2_same + z2_other.astype(F32)
        z2 = [z2[0]] + [swap(z2[n].astype(BF16), "rows", 2 * n) for n in range(1, n_rows // 2)]
    else:
        z2 = [lax.psum_scatter(second(0, F32), "rows", scatter_dimension=0)]
    grown, dots = pl.pallas_call(
        product_kernel,
        out_shape=(shape(outputs, own_len), shape(outputs, LANES)),
        in_specs=[SMEM] + [VMEM] * (2 + len(z2)),
        out_specs=(VMEM, VMEM),
        compiler_params=limit,
        name="products",
    )(place, held_t, s1_own, *z2)
    if direct_rows:
        dots = pair_sum(across_x(pair_sum(along_z(dots))))
    else:
        dots = lax.psum(dots, "rows")
    grown = jnp.stack([grown, swap(grown, "cols", 2)])
    ends = (s1_own, s1_got, grown, swap(grown, "cols", 1), *direct_cols(dots))
    ends = [pltpu.with_memory_space_constraint(x, pltpu.VMEM) for x in ends]

    return pl.pallas_call(
        final_kernel,
        out_shape=(shape(outputs, npoints), shape(outputs, npoints)),
        in_specs=[SMEM] + [VMEM] * 9,
        out_specs=(HBM, HBM),
        scratch_shapes=[
            pltpu.VMEM((4, outputs, own_len), F32),
            pltpu.VMEM((4, outputs, own_len), F32),
            pltpu.SemaphoreType.DMA((2, 4)),
        ],
        compiler_params=limit,
        name="final",
    )(place, held_t, *ends)


def solution(mesh):
    placed = (P("rows", "cols"), P(None, "rows"), P(None, "rows"))
    return jax.shard_map(
        local,
        mesh=mesh,
        in_specs=placed,
        out_specs=(P(None, "rows"), P(None, "rows")),
        check_vma=False,
    )
```

```python
import functools
from typing import NamedTuple

import jax
import jax.numpy as jnp
from jax import lax
from jax.experimental import pallas as pl
from jax.experimental.pallas import tpu as pltpu
from jax.sharding import PartitionSpec as P

REG = 1.5
RADIUS = 0.25
GROUP_BITS = 2
GROUP = 1 << GROUP_BITS
CODE_BITS = 12
CODE = 1 << CODE_BITS
RING = 3
STRIP = 32
LANES = 128
TINY = 1e-30
SHIFT = 0.375
DIRECT_ROWS = 8
RESIDENT_BYTES = 20 * 1024 * 1024

SMEM = pl.BlockSpec(memory_space=pltpu.SMEM)
VMEM = pl.BlockSpec(memory_space=pltpu.VMEM)
HBM = pl.BlockSpec(memory_space=pltpu.HBM)
F32 = jnp.float32
BF16 = jnp.bfloat16


def pair_sum(parts):
    while len(parts) > 1:
        parts = [a + b for a, b in zip(parts[::2], parts[1::2])]
    return parts[0]


class Sizes(NamedTuple):
    parts: int
    part_groups: int
    resident: bool
    nb: int
    block_len: int
    own_rows: int
    block_rows: int
    count_rows: int


def augment(x, first_ones):
    dim, n = x.shape
    norm = jnp.sum(x * x, axis=0, keepdims=True) / (RADIUS * RADIUS)
    high = norm.astype(BF16).astype(F32)
    rest = norm - high
    mid = rest.astype(BF16).astype(F32)
    low = rest - mid
    line = lax.broadcasted_iota(jnp.int32, (dim, n), 0)
    base = 3 if first_ones else 0
    ones_at = 0 if first_ones else 3
    tail = jnp.where((line >= ones_at) & (line < ones_at + 3), 1.0, 0.0)
    tail = jnp.where(line == base, high, tail)
    tail = jnp.where(line == base + 1, mid, tail)
    tail = jnp.where(line == base + 2, low, tail)
    return tail


def row_of(cfg, place, part, z):
    if cfg.parts == 1:
        return z
    return 2 * z + (place[0] & 1 if part == 0 else 1 - (place[0] & 1))


def slot_of(cfg, place, n):
    return n if cfg.parts == 1 else lax.shift_right_logical(place[0], 1) ^ n


def build_kernel(cfg, part, place, direct, *refs):
    last = part == cfg.parts - 1
    if part == 0:
        near_hbm, piece, refs = refs[0], refs[1], refs[2:]
        k_mat, listed, deg_ref, lhs = refs[:4]
        near_ref, near_sem, refs = refs[4], refs[5], refs[6:]
        near_copy = pltpu.make_async_copy(near_hbm, near_ref, near_sem)
        near_copy.start()
    else:
        lhs, first_deg, piece, _ = refs[:4]
        k_mat, listed, deg_ref = refs[4:7]
        refs = refs[7:]
    mlist, acc, rhs, dist, counts_v, counts, count_sem = refs[:7]
    kbuf, sems = (None, None) if cfg.resident else refs[7:]
    row, col = place[0], place[1]
    own_rows, block_len, nb = cfg.own_rows, cfg.block_len, cfg.nb
    own_len = own_rows * block_len
    dim, held = piece.shape[1], piece.shape[0]
    scale = 1.0 / (RADIUS * RADIUS)

    def count(n, carry):
        named = piece[n, :, own_len:own_len + LANES]
        counts_v[slot_of(cfg, place, n)] = named.astype(F32)[:cfg.count_rows].astype(jnp.int32)
        return carry

    def prepare(n, carry):
        z = slot_of(cfg, place, n)
        for k in range(own_rows):
            far = piece[n, :, k * block_len:(k + 1) * block_len]
            rhs[z * own_rows + k, :dim, :] = far
            rhs[z * own_rows + k, dim:, :] = augment(far.astype(F32), False).astype(BF16)
        return carry

    lax.fori_loop(0, held, count, 0, unroll=held <= 4)
    fetch = pltpu.make_async_copy(counts_v, counts, count_sem)
    fetch.start()
    lax.fori_loop(0, held, prepare, 0, unroll=held <= 4)
    acc[...] = jnp.zeros_like(acc)
    if part == 0:
        near_copy.wait()
        for i in range(cfg.block_rows):
            near = near_ref[:, i * block_len:(i + 1) * block_len].astype(F32)
            full = jnp.concatenate([near * (-2.0 * scale), augment(near, True)], axis=0)
            lhs[i] = full.T.astype(BF16)
    fetch.wait()

    pos = jnp.int32(0)
    for i in range(cfg.block_rows):
        me = row * cfg.block_rows + i
        spots = [k * nb + me for k in range(own_rows)]
        spots = [(lax.shift_right_logical(p, 7), p & (LANES - 1)) for p in spots]

        def note(z, at, i=i, me=me, spots=spots):
            for k in range(own_rows):
                name = row_of(cfg, place, part, z) * cfg.block_rows + col * own_rows + k
                m = direct[i, name] + jnp.where(name == me, 0, counts[z, spots[k][0], spots[k][1]])
                listed[at + 1] = i * CODE + z * own_rows + k
                mlist[at] = m
                at = at + jnp.where(m > 0, 1, 0)
            return at

        if held <= 4:
            for z in range(held):
                pos = note(z, pos)
        else:
            pos = lax.fori_loop(0, held, note, pos, unroll=4)
    for u in range(GROUP):
        listed[pos + u + 1] = 0
        mlist[pos + u] = 0
    total = lax.shift_right_logical(pos + (GROUP - 1), GROUP_BITS)
    listed[0] = total

    def copy_out(g):
        slot = lax.rem(g, RING)
        return pltpu.make_async_copy(kbuf.at[slot], k_mat.at[g], sems.at[slot])

    base = part * cfg.part_groups

    def distances(e, slot):
        code = listed[e + 1]
        i, j = lax.shift_right_logical(code, CODE_BITS), code & (CODE - 1)
        dist[slot] = jnp.dot(lhs[i], rhs[j], preferred_element_type=F32)

    distances(0, 0)

    def step(g, carry):
        slot, target = (base + g, k_mat) if cfg.resident else (lax.rem(g, RING), kbuf)
        if not cfg.resident:

            @pl.when(g >= RING)
            def _():
                copy_out(g - RING).wait()

        for u in range(GROUP):
            distances(g * GROUP + u + 1, (u + 1) % 2)
            j = listed[g * GROUP + u + 1] & (CODE - 1)
            m = mlist[g * GROUP + u].astype(F32)
            sums = jnp.zeros((8, block_len), F32)
            for s in range(block_len // STRIP):
                rows = slice(s * STRIP, (s + 1) * STRIP)
                d = jnp.maximum(dist[u % 2, rows, :], TINY)
                sc = d * lax.rsqrt(d)
                rem = jnp.maximum(1.0 - sc, 0.0)
                sq = rem * rem
                val = (sq * sq) * (sc * (4.0 * m) + m)
                target[slot, u, rows, :] = val.astype(BF16)
                for h in range(0, STRIP, 8):
                    sums = sums + val[h:h + 8]
            acc[j] += sums
        if not cfg.resident:
            copy_out(g).start()
        return carry

    lax.fori_loop(0, total, step, 0)
    if cfg.parts == 1 or not last:
        deg_ref[...] = jnp.sum(acc[...], axis=1)
    else:
        second = jnp.sum(acc[...], axis=1)
        for z in range(held):
            rows = slice(z * own_rows, (z + 1) * own_rows)
            for p, deg in enumerate((first_deg[rows, :], second[rows])):
                at = row_of(cfg, place, p, z) * own_rows
                for k in range(own_rows):
                    deg_ref[pl.ds(at + k, 1), :] = deg[k:k + 1]

    def drain(g, carry):
        copy_out(g).wait()
        return carry

    if not cfg.resident:
        lax.fori_loop(jnp.maximum(total - RING, 0), total, drain, 0)


def pieces_of(own, got):
    return own.at[0], got.at[0], own.at[1], got.at[1]


def walk(cfg, part, listed, k_mat, kbuf, sems, product, total_ref, by_row):
    total = listed[0]
    base = part * cfg.part_groups

    def copy_in(g):
        slot = lax.rem(g, RING)
        return pltpu.make_async_copy(k_mat.at[g], kbuf.at[slot], sems.at[slot])

    if not cfg.resident:
        for p in range(RING - 1):

            @pl.when(p < total)
            def _(p=p):
                copy_in(p).start()

    def step(g, carry):
        slot, source = (base + g, k_mat) if cfg.resident else (lax.rem(g, RING), kbuf)
        if not cfg.resident:

            @pl.when(g + (RING - 1) < total)
            def _():
                copy_in(g + (RING - 1)).start()

            copy_in(g).wait()
        codes = [listed[g * GROUP + u + 1] for u in range(GROUP)]
        pairs = [(lax.shift_right_logical(code, CODE_BITS), code & (CODE - 1)) for code in codes]
        terms = [product(i, j, source[slot, u]) for u, (i, j) in enumerate(pairs)]
        for (i, j), term in zip(pairs, terms):
            total_ref[i if by_row else j] += term
        return carry

    lax.fori_loop(0, total, step, 0)


def first_kernel(cfg, place, k_mat, *refs):
    n = cfg.parts
    lists, pieces, inv_ref, refs = refs[:n], refs[n:2 * n], refs[2 * n], refs[2 * n + 1:]
    near, near_y, cross, own_inv, z_acc, w_all, *ring = refs
    kbuf, sems = ring or (None, None)
    col = place[1]
    own_rows, block_len = cfg.own_rows, cfg.block_len
    z_acc[...] = jnp.zeros_like(z_acc)
    for part, (listed, piece) in enumerate(zip(lists, pieces)):
        held = piece.shape[0]

        def prepare(m, carry, part=part, piece=piece):
            z = slot_of(cfg, place, m)
            for k in range(own_rows):
                w = piece[m, :, k * block_len:(k + 1) * block_len]
                at = row_of(cfg, place, part, z) * own_rows + k
                w_all[z * own_rows + k] = (w * inv_ref[pl.ds(at, 1), :]).astype(BF16)
            return carry

        lax.fori_loop(0, held, prepare, 0, unroll=held <= 4)

        def product(i, j, block):
            return lax.dot_general(
                w_all[j], block, (((1,), (1,)), ((), ())), preferred_element_type=F32
            )

        walk(cfg, part, listed, k_mat, kbuf, sems, product, z_acc, True)
    for k in range(own_rows):
        cols = slice(k * block_len, (k + 1) * block_len)
        mine = inv_ref[pl.ds(place[0] * own_rows + k, 1), :]
        own_inv[:, cols] = jnp.broadcast_to(mine, (8, block_len))
        for e, ref in enumerate((near, cross.at[0], near_y, cross.at[1])):
            ref[:, cols] = z_acc[(col ^ e) * own_rows + k]


def second_kernel(cfg, part, place, k_mat, listed, t_ref, s1_own, s1_got, out, z_acc, w_all, *ring):
    kbuf, sems = ring or (None, None)
    own_rows, block_len = cfg.own_rows, cfg.block_len
    outputs = t_ref.shape[0]
    for e, packed in enumerate(pieces_of(s1_own, s1_got)):
        share = place[1] ^ e
        for k in range(own_rows):
            cols = slice(k * block_len, (k + 1) * block_len)
            i = share * own_rows + k
            t = t_ref[:, pl.ds(pl.multiple_of(i * block_len, LANES), block_len)]
            g = (packed[:outputs, cols] - SHIFT * t) * packed[outputs:outputs + 1, cols]
            w_all[i] = g.astype(BF16)
    z_acc[...] = jnp.zeros_like(z_acc)

    def product(i, j, block):
        return jnp.dot(w_all[i], block, preferred_element_type=F32)

    walk(cfg, part, listed, k_mat, kbuf, sems, product, z_acc, False)

    def hand_out(m, carry):
        z = slot_of(cfg, place, m)
        for k in range(own_rows):
            out[m, :, k * block_len:(k + 1) * block_len] = z_acc[z * own_rows + k].astype(out.dtype)
        return carry

    held = out.shape[0]
    lax.fori_loop(0, held, hand_out, 0, unroll=held <= 4)


N_DOTS = 5


def meet_kernel(cfg, place, z_same, z_other, t_same, inv_ref, s1_own, *refs):
    gs, (own_z, own_dots, *outs) = refs[:4], refs[4:]
    own_rows, block_len = cfg.own_rows, cfg.block_len
    outputs, own_len = own_z.shape
    tz = jnp.zeros((outputs, 1), F32)
    gz = jnp.zeros((outputs, 1), F32)
    for n in range(4):
        z = z_same[n] + z_other[n].astype(F32)
        if n == 0:
            own_z[...] = z
        else:
            outs[n - 1][:, :own_len] = z.astype(BF16)
        gz += jnp.sum(gs[n][...].astype(F32) * z, axis=1, keepdims=True)
        at = row_of(cfg, place, 0, slot_of(cfg, place, n)) * own_rows
        for k in range(own_rows):
            cols = slice(k * block_len, (k + 1) * block_len)
            scaled = t_same[n, :, cols] * inv_ref[pl.ds(at + k, 1), :]
            tz += jnp.sum(scaled * z[:, cols], axis=1, keepdims=True)
    t, s1 = t_same[0], s1_own[0, :outputs, :]
    tt = jnp.sum(t * t, axis=1, keepdims=True)
    ts1 = jnp.sum(t * s1, axis=1, keepdims=True)
    s1s1 = jnp.sum(s1 * s1, axis=1, keepdims=True)
    dots = (tt, ts1, s1s1, tz + SHIFT * ts1, gz + SHIFT * (tz + s1s1))
    lane = lax.broadcasted_iota(jnp.int32, (outputs, LANES), 1)
    tile = jnp.zeros(lane.shape, F32)
    for n, v in enumerate(dots):
        for part in range(3):
            head = v.astype(BF16).astype(F32)
            tile = jnp.where(lane == part * N_DOTS + n, head, tile)
            v = v - head
    own_dots[...] = tile.astype(BF16)
    for out in outs:
        out[:, own_len:] = tile.astype(BF16)


def product_kernel(own_z, own_dots, s1_own, *refs):
    got, grown_ref, dot_ref = refs[:3], refs[3], refs[4]
    outputs, own_len = grown_ref.shape
    z = own_z[...]
    for ref in got:
        z = z + ref[:, :own_len].astype(F32)
    grown_ref[...] = z * s1_own[0, outputs:outputs + 1, :]
    tiles = [own_dots[...]] + [ref[:, own_len:] for ref in got]
    total = pair_sum([tile.astype(F32) for tile in tiles])
    out = total
    for part in range(1, 3):
        out = out + pltpu.roll(total, LANES - part * N_DOTS, 1)
    dot_ref[...] = out


def final_kernel(place, t_ref, s1_own, s1_got, *refs):
    grown, all_dots = pieces_of(refs[0], refs[1]), refs[2:6]
    sol_hbm, res_hbm, sol_ref, res_ref, sems = refs[6:]
    s1s = pieces_of(s1_own, s1_got)
    outputs, own_len = grown[0].shape
    dots = pair_sum([ref[...] for ref in all_dots])
    tt, ts1, s1s1, ts2, s1s2 = (dots[:, n:n + 1] for n in range(5))
    a1 = tt / (REG * tt + ts1)
    p = 1.0 - REG * a1
    new = p * p * tt - 2.0 * p * a1 * ts1 + a1 * a1 * s1s1
    u = p + new / tt
    dd = u * u * tt - 2.0 * u * a1 * ts1 + a1 * a1 * s1s1
    dmd = u * u * ts1 - u * a1 * (s1s1 + ts2) + a1 * a1 * s1s2
    a2 = new / (REG * dd + dmd)
    sol_t, sol_1 = a1 + a2 * u, a2 * a1
    res_t, res_1 = p - a2 * REG * u, a1 + a2 * (u - REG * a1)
    copies = []
    for e in range(4):
        at = pl.ds(pl.multiple_of((place[1] ^ e) * own_len, LANES), own_len)
        t, s1 = t_ref[:, at], s1s[e][:outputs, :]
        s2 = grown[e][...] + SHIFT * s1
        sol_ref[e] = sol_t * t - sol_1 * s1
        res_ref[e] = res_t * t - res_1 * s1 + sol_1 * s2
        for n, (ref, hbm) in enumerate(((sol_ref, sol_hbm), (res_ref, res_hbm))):
            copy = pltpu.make_async_copy(ref.at[e], hbm.at[:, at], sems.at[n, e])
            copy.start()
            copies.append(copy)
    for copy in copies:
        copy.wait()


def swap(x, axis, d):
    size = lax.axis_size(axis)
    return lax.ppermute(x, axis, [(i, i ^ d) for i in range(size)])


def along_z(x):
    return [x] + [swap(x, "rows", d) for d in range(2, lax.axis_size("rows"), 2)]


def across_x(same):
    return [same, swap(same, "rows", 1)]


def direct_cols(x):
    return [x] + [swap(x, "cols", e) for e in range(1, 4)]


def local(block_list, points, targets):
    n_rows = lax.axis_size("rows")
    n_cols = lax.axis_size("cols")
    row = lax.axis_index("rows")
    col = lax.axis_index("cols")
    block_rows, slots = block_list.shape
    dim, npoints = points.shape
    outputs = targets.shape[0]
    block_len = npoints // block_rows
    own_rows = block_rows // n_cols
    own_len = own_rows * block_len
    nb = block_rows * n_rows
    n_sub = own_rows * n_rows
    capacity = -(-block_rows * slots // n_rows)
    direct_rows = n_rows <= DIRECT_ROWS
    parts = 2 if direct_rows else 1
    n_part = n_sub // parts
    bound = min(block_rows * n_part, n_cols * capacity * (n_rows + 1))
    n_groups = -(-bound // GROUP)
    list_len = n_groups * GROUP + GROUP + 1
    place = jnp.stack([row, col])
    resident = parts * 2 * n_groups * GROUP * block_len * block_len <= RESIDENT_BYTES
    k_shape = (parts * n_groups, GROUP, block_len, block_len)
    limit = pltpu.CompilerParams(vmem_limit_bytes=(8 if resident else 32) * 1024 * 1024)
    ring = [] if resident else [
        pltpu.VMEM((RING, GROUP, block_len, block_len), BF16),
        pltpu.SemaphoreType.DMA((RING,)),
    ]
    k_spec = VMEM if resident else HBM
    cfg = Sizes(
        parts, n_groups, resident, nb, block_len, own_rows, block_rows, -(-own_rows * nb // LANES)
    )

    def shape(*dims, dtype=F32):
        return jax.ShapeDtypeStruct(dims, dtype)

    def own(x):
        return lax.dynamic_slice_in_dim(x, col * own_len, own_len, 1)

    def total_rows(x):
        if direct_rows:
            return pair_sum(across_x(pair_sum(along_z(x))))
        return lax.psum(x, "rows")

    lists = direct_cols(block_list)
    names = jnp.arange(nb, dtype=jnp.int32)
    direct = sum(jnp.sum((x[:, :, None] == names).astype(jnp.int32), axis=1) for x in lists)
    own_counts = lax.dynamic_slice_in_dim(direct, col * own_rows, own_rows, 0)
    coded = own_counts.reshape(-1)
    coded = jnp.pad(coded, (0, dim * LANES - coded.shape[0])).reshape(dim, LANES).astype(BF16)
    packed = jnp.concatenate([own(points), coded], axis=1)
    own_t = own(targets)

    def build(part, *operands):
        first, last = part == 0, part == parts - 1
        out = [
            pltpu.VMEM(k_shape, BF16) if resident else shape(*k_shape, dtype=BF16),
            shape(list_len, dtype=jnp.int32),
            shape(n_sub if last else n_part, block_len),
        ]
        out += [shape(block_rows, block_len, 2 * dim, dtype=BF16)] if first else []
        k_mat, *rest = pl.pallas_call(
            functools.partial(build_kernel, cfg, part),
            out_shape=out,
            in_specs=[SMEM, SMEM] + ([HBM, VMEM] if first else [VMEM] * 3 + [k_spec]),
            out_specs=[k_spec, SMEM] + [VMEM] * (len(out) - 2),
            scratch_shapes=([
                pltpu.VMEM((dim, npoints), BF16),
                pltpu.SemaphoreType.DMA,
            ] if first else []) + [
                pltpu.SMEM((list_len,), jnp.int32),
                pltpu.VMEM((n_part, 8, block_len), F32),
                pltpu.VMEM((n_part, 2 * dim, block_len), BF16),
                pltpu.VMEM((2, block_len, block_len), F32),
                pltpu.VMEM((n_part // own_rows, cfg.count_rows, LANES), jnp.int32),
                pltpu.SMEM((n_part // own_rows, cfg.count_rows, LANES), jnp.int32),
                pltpu.SemaphoreType.DMA,
                *ring,
            ],
            compiler_params=limit,
            input_output_aliases={} if first else {5: 0},
            cost_estimate=pl.CostEstimate(
                flops=2 * 2 * dim * bound * block_len * block_len,
                bytes_accessed=2 * bound * block_len * block_len,
                transcendentals=bound * block_len * block_len,
            ),
            name="build",
        )(place, direct, *operands)
        if resident:
            k_mat = pltpu.with_memory_space_constraint(k_mat, pltpu.VMEM)
        return k_mat, *rest

    near = pltpu.with_memory_space_constraint(points, pltpu.HBM)
    if direct_rows:
        packed, early_t = lax.optimization_barrier((packed, own_t))
        same, other = across_x(jnp.stack(along_z(packed)))
        t_same = along_z(early_t)
        k_mat, list0, degree, lhs = build(0, near, same)
        degree, other, *t_same = lax.optimization_barrier((degree, other, *t_same))
        t_same, t_other = across_x(jnp.stack(t_same))
        other, t_same = lax.optimization_barrier((other, t_same))
        k_mat, list1, degree = build(1, lhs, degree, other, k_mat)
        degree, t_other = lax.optimization_barrier((degree, t_other))
        t_pieces, k_lists = [t_same, t_other], [list0, list1]
    else:
        k_mat, list0, degree, _ = build(0, near, lax.all_gather(packed, "rows"))
        t_pieces, k_lists = [lax.all_gather(own_t, "rows")], [list0]
    inv = 1.0 / jnp.sqrt(1.0 + total_rows(degree))

    def cost(n):
        return pl.CostEstimate(
            flops=2 * n * bound * outputs * block_len * block_len,
            bytes_accessed=n * bound * block_len * block_len,
            transcendentals=0,
        )

    near_z, near_y, cross_z, tail = pl.pallas_call(
        functools.partial(first_kernel, cfg),
        out_shape=[shape(outputs, own_len)] * 2 + [shape(2, outputs, own_len), shape(8, own_len)],
        in_specs=[SMEM, k_spec] + [SMEM] * parts + [VMEM] * (parts + 1),
        out_specs=[VMEM] * 4,
        scratch_shapes=[
            pltpu.VMEM((block_rows, outputs, block_len), F32),
            pltpu.VMEM((n_part, outputs, block_len), BF16),
            *ring,
        ],
        compiler_params=limit,
        cost_estimate=cost(parts),
        name="first",
    )(place, k_mat, *k_lists, *t_pieces, inv)

    got = swap(cross_z, "cols", 1)
    half = jnp.concatenate([near_z + got[0], near_y + got[1], tail], axis=0)
    far = swap(half, "cols", 2)
    lo, hi, end = slice(0, outputs), slice(outputs, 2 * outputs), slice(2 * outputs, None)
    s1_own = jnp.stack([
        jnp.concatenate([(half[lo] + far[hi]) * tail[:1], tail], axis=0),
        jnp.concatenate([(half[hi] + far[lo]) * far[end][:1], far[end]], axis=0),
    ])
    s1_got = swap(s1_own, "cols", 1)
    held_t = pltpu.with_memory_space_constraint(targets, pltpu.VMEM)

    def second(part, dtype):
        return pl.pallas_call(
            functools.partial(second_kernel, cfg, part),
            out_shape=shape(n_part // own_rows, outputs, own_len, dtype=dtype),
            in_specs=[SMEM, k_spec, SMEM] + [VMEM] * 3,
            out_specs=VMEM,
            scratch_shapes=[
                pltpu.VMEM((n_part, outputs, block_len), F32),
                pltpu.VMEM((block_rows, outputs, block_len), BF16),
                *ring,
            ],
            compiler_params=limit,
            cost_estimate=cost(1),
            name="second",
        )(place, k_mat, k_lists[part], held_t, s1_own, s1_got)

    if direct_rows:
        g = ((s1_own[0, :outputs] - SHIFT * own_t) * tail[:1]).astype(BF16)
        z2_other, g = lax.optimization_barrier((second(1, BF16), g))
        z2_other = swap(z2_other, "rows", 1)
        gs = along_z(g)
        z2_same = second(0, F32)
        z2_same, z2_other, *gs = lax.optimization_barrier((z2_same, z2_other, *gs))
        row_piece = shape(outputs, own_len + LANES, dtype=BF16)
        own_z, own_dots, *sends = pl.pallas_call(
            functools.partial(meet_kernel, cfg),
            out_shape=[shape(outputs, own_len), shape(outputs, LANES, dtype=BF16)] + [row_piece] * 3,
            in_specs=[SMEM] + [VMEM] * 9,
            out_specs=[VMEM] * 5,
            compiler_params=limit,
            name="meet",
        )(place, z2_same, z2_other, t_pieces[0], inv, s1_own, *gs)
        grown, dots = pl.pallas_call(
            product_kernel,
            out_shape=(shape(outputs, own_len), shape(outputs, LANES)),
            in_specs=[VMEM] * 6,
            out_specs=(VMEM, VMEM),
            compiler_params=limit,
            name="products",
        )(own_z, own_dots, s1_own, *[swap(x, "rows", 2 * n + 2) for n, x in enumerate(sends)])
        dots = pair_sum(across_x(dots))
    else:
        z2 = lax.psum_scatter(second(0, F32), "rows", scatter_dimension=0)
        grown = z2 * tail[:1]
        own_s1 = s1_own[0, :outputs]
        own_t, s2 = own(targets), grown + SHIFT * own_s1
        dots = [(own_t, own_t), (own_t, own_s1), (own_s1, own_s1), (own_t, s2), (own_s1, s2)]
        dots = jnp.stack([jnp.sum(x * y, axis=1) for x, y in dots], axis=1)
        dots = lax.psum(jnp.pad(dots, ((0, 0), (0, LANES - N_DOTS))), "rows")
    grown = jnp.stack([grown, swap(grown, "cols", 2)])
    grown, dots = lax.optimization_barrier((grown, dots))
    ends = (s1_own, s1_got, grown, swap(grown, "cols", 1), *direct_cols(dots))
    ends = [pltpu.with_memory_space_constraint(x, pltpu.VMEM) for x in ends]

    return pl.pallas_call(
        final_kernel,
        out_shape=(shape(outputs, npoints), shape(outputs, npoints)),
        in_specs=[SMEM] + [VMEM] * 9,
        out_specs=(HBM, HBM),
        scratch_shapes=[
            pltpu.VMEM((4, outputs, own_len), F32),
            pltpu.VMEM((4, outputs, own_len), F32),
            pltpu.SemaphoreType.DMA((2, 4)),
        ],
        compiler_params=limit,
        name="final",
    )(place, held_t, *ends)


def solution(mesh):
    placed = (P("rows", "cols"), P(None, "rows"), P(None, "rows"))
    return jax.shard_map(
        local,
        mesh=mesh,
        in_specs=placed,
        out_specs=(P(None, "rows"), P(None, "rows")),
        check_vma=False,
    )
```

```python
import functools
from typing import NamedTuple

import jax
import jax.numpy as jnp
from jax import lax
from jax.experimental import pallas as pl
from jax.experimental.pallas import tpu as pltpu
from jax.sharding import PartitionSpec as P

REG = 1.5
RADIUS = 0.25
GROUP_BITS = 2
GROUP = 1 << GROUP_BITS
CODE_BITS = 12
CODE = 1 << CODE_BITS
RING = 3
STRIP = 32
LANES = 128
TINY = 1e-30
SHIFT = 0.375
DIRECT_ROWS = 8
RESIDENT_BYTES = 20 * 1024 * 1024

VMEM = pl.BlockSpec(memory_space=pltpu.VMEM)
HBM = pl.BlockSpec(memory_space=pltpu.HBM)
F32 = jnp.float32
BF16 = jnp.bfloat16


def pair_sum(parts):
    while len(parts) > 1:
        parts = [a + b for a, b in zip(parts[::2], parts[1::2])]
    return parts[0]


def position():
    return lax.axis_index("rows"), lax.axis_index("cols")


class Sizes(NamedTuple):
    parts: int
    part_groups: int
    resident: bool
    nb: int
    block_len: int
    own_rows: int
    block_rows: int
    count_rows: int


def augment(x, first_ones):
    dim, n = x.shape
    norm = jnp.sum(x * x, axis=0, keepdims=True) / (RADIUS * RADIUS)
    high = norm.astype(BF16).astype(F32)
    rest = norm - high
    mid = rest.astype(BF16).astype(F32)
    low = rest - mid
    line = lax.broadcasted_iota(jnp.int32, (dim, n), 0)
    base = 3 if first_ones else 0
    ones_at = 0 if first_ones else 3
    tail = jnp.where((line >= ones_at) & (line < ones_at + 3), 1.0, 0.0)
    tail = jnp.where(line == base, high, tail)
    tail = jnp.where(line == base + 1, mid, tail)
    tail = jnp.where(line == base + 2, low, tail)
    return tail


def row_of(cfg, place, part, z):
    if cfg.parts == 1:
        return z
    return 2 * z + (place[0] & 1 if part == 0 else 1 - (place[0] & 1))


def slot_of(cfg, place, n):
    return n if cfg.parts == 1 else lax.shift_right_logical(place[0], 1) ^ n


def build_kernel(cfg, part, direct_v, *refs):
    last = part == cfg.parts - 1
    place = position()
    if part == 0:
        near_hbm, piece, refs = refs[0], refs[1], refs[2:]
        k_mat, list_v, deg_ref, lhs = refs[:4]
        near_ref, near_sem, refs = refs[4], refs[5], refs[6:]
        near_copy = pltpu.make_async_copy(near_hbm, near_ref, near_sem)
        near_copy.start()
    else:
        lhs, first_deg, piece, _ = refs[:4]
        k_mat, list_v, deg_ref = refs[4:7]
        refs = refs[7:]
    listed, mlist, acc, rhs, dist, direct, counts_v, counts, copy_sems = refs[:9]
    kbuf, sems = (None, None) if cfg.resident else refs[9:]
    direct_copy = pltpu.make_async_copy(direct_v, direct, copy_sems.at[0])
    direct_copy.start()
    row, col = place[0], place[1]
    own_rows, block_len, nb = cfg.own_rows, cfg.block_len, cfg.nb
    own_len = own_rows * block_len
    dim, held = piece.shape[1], piece.shape[0]
    scale = 1.0 / (RADIUS * RADIUS)

    def count(n, carry):
        named = piece[n, :, own_len:own_len + LANES]
        counts_v[slot_of(cfg, place, n)] = named.astype(F32)[:cfg.count_rows].astype(jnp.int32)
        return carry

    def prepare(n, carry):
        z = slot_of(cfg, place, n)
        for k in range(own_rows):
            far = piece[n, :, k * block_len:(k + 1) * block_len]
            rhs[z * own_rows + k, :dim, :] = far
            rhs[z * own_rows + k, dim:, :] = augment(far.astype(F32), False).astype(BF16)
        return carry

    lax.fori_loop(0, held, count, 0, unroll=held <= 4)
    fetch = pltpu.make_async_copy(counts_v, counts, copy_sems.at[1])
    fetch.start()
    lax.fori_loop(0, held, prepare, 0, unroll=held <= 4)
    acc[...] = jnp.zeros_like(acc)
    if part == 0:
        near_copy.wait()
        for i in range(cfg.block_rows):
            near = near_ref[:, i * block_len:(i + 1) * block_len].astype(F32)
            full = jnp.concatenate([near * (-2.0 * scale), augment(near, True)], axis=0)
            lhs[i] = full.T.astype(BF16)
    direct_copy.wait()
    fetch.wait()

    pos = jnp.int32(0)
    for i in range(cfg.block_rows):
        me = row * cfg.block_rows + i
        spots = [k * nb + me for k in range(own_rows)]
        spots = [(lax.shift_right_logical(p, 7), p & (LANES - 1)) for p in spots]

        def note(z, at, i=i, me=me, spots=spots):
            for k in range(own_rows):
                name = row_of(cfg, place, part, z) * cfg.block_rows + col * own_rows + k
                m = direct[i, name] + jnp.where(name == me, 0, counts[z, spots[k][0], spots[k][1]])
                listed[0, at + 1] = i * CODE + z * own_rows + k
                mlist[at] = m
                at = at + jnp.where(m > 0, 1, 0)
            return at

        if held <= 4:
            for z in range(held):
                pos = note(z, pos)
        else:
            pos = lax.fori_loop(0, held, note, pos, unroll=4)
    for u in range(GROUP):
        listed[0, pos + u + 1] = 0
        mlist[pos + u] = 0
    total = lax.shift_right_logical(pos + (GROUP - 1), GROUP_BITS)
    listed[0, 0] = total
    list_copy = pltpu.make_async_copy(listed, list_v, copy_sems.at[2])
    list_copy.start()

    def copy_out(g):
        slot = lax.rem(g, RING)
        return pltpu.make_async_copy(kbuf.at[slot], k_mat.at[g], sems.at[slot])

    base = part * cfg.part_groups

    def distances(e, slot):
        code = listed[0, e + 1]
        i, j = lax.shift_right_logical(code, CODE_BITS), code & (CODE - 1)
        dist[slot] = jnp.dot(lhs[i], rhs[j], preferred_element_type=F32)

    distances(0, 0)

    def step(g, carry):
        slot, target = (base + g, k_mat) if cfg.resident else (lax.rem(g, RING), kbuf)
        if not cfg.resident:

            @pl.when(g >= RING)
            def _():
                copy_out(g - RING).wait()

        for u in range(GROUP):
            distances(g * GROUP + u + 1, (u + 1) % 2)
            j = listed[0, g * GROUP + u + 1] & (CODE - 1)
            m = mlist[g * GROUP + u].astype(F32)
            sums = jnp.zeros((8, block_len), F32)
            for s in range(block_len // STRIP):
                rows = slice(s * STRIP, (s + 1) * STRIP)
                d = jnp.maximum(dist[u % 2, rows, :], TINY)
                sc = d * lax.rsqrt(d)
                rem = jnp.maximum(1.0 - sc, 0.0)
                sq = rem * rem
                val = (sq * sq) * (sc * (4.0 * m) + m)
                target[slot, u, rows, :] = val.astype(BF16)
                for h in range(0, STRIP, 8):
                    sums = sums + val[h:h + 8]
            acc[j] += sums
        if not cfg.resident:
            copy_out(g).start()
        return carry

    lax.fori_loop(0, total, step, 0)
    if cfg.parts == 1 or not last:
        deg_ref[...] = jnp.sum(acc[...], axis=1)
    else:
        second = jnp.sum(acc[...], axis=1)
        for z in range(held):
            rows = slice(z * own_rows, (z + 1) * own_rows)
            for p, deg in enumerate((first_deg[rows, :], second[rows])):
                at = row_of(cfg, place, p, z) * own_rows
                for k in range(own_rows):
                    deg_ref[pl.ds(at + k, 1), :] = deg[k:k + 1]

    def drain(g, carry):
        copy_out(g).wait()
        return carry

    if not cfg.resident:
        lax.fori_loop(jnp.maximum(total - RING, 0), total, drain, 0)
    list_copy.wait()


def pieces_of(own, got):
    return own.at[0], got.at[0], own.at[1], got.at[1]


def walk(cfg, part, listed, k_mat, kbuf, sems, product, total_ref, by_row):
    total = listed[0, 0]
    base = part * cfg.part_groups

    def copy_in(g):
        slot = lax.rem(g, RING)
        return pltpu.make_async_copy(k_mat.at[g], kbuf.at[slot], sems.at[slot])

    if not cfg.resident:
        for p in range(RING - 1):

            @pl.when(p < total)
            def _(p=p):
                copy_in(p).start()

    def step(g, carry):
        slot, source = (base + g, k_mat) if cfg.resident else (lax.rem(g, RING), kbuf)
        if not cfg.resident:

            @pl.when(g + (RING - 1) < total)
            def _():
                copy_in(g + (RING - 1)).start()

            copy_in(g).wait()
        codes = [listed[0, g * GROUP + u + 1] for u in range(GROUP)]
        pairs = [(lax.shift_right_logical(code, CODE_BITS), code & (CODE - 1)) for code in codes]
        terms = [product(i, j, source[slot, u]) for u, (i, j) in enumerate(pairs)]
        for (i, j), term in zip(pairs, terms):
            total_ref[i if by_row else j] += term
        return carry

    lax.fori_loop(0, total, step, 0)


def first_kernel(cfg, k_mat, *refs):
    n = cfg.parts
    lists, pieces, inv_ref, refs = refs[:n], refs[n:2 * n], refs[2 * n], refs[2 * n + 1:]
    near, near_y, cross, own_inv, z_acc, w_all, listed, list_sems, *ring = refs
    kbuf, sems = ring or (None, None)
    place = position()
    col = place[1]
    copies = [
        pltpu.make_async_copy(lists[p], listed.at[p], list_sems.at[p]) for p in range(n)
    ]
    for copy in copies:
        copy.start()
    own_rows, block_len = cfg.own_rows, cfg.block_len
    z_acc[...] = jnp.zeros_like(z_acc)
    for part, piece in enumerate(pieces):
        held = piece.shape[0]

        def prepare(m, carry, part=part, piece=piece):
            z = slot_of(cfg, place, m)
            for k in range(own_rows):
                w = piece[m, :, k * block_len:(k + 1) * block_len]
                at = row_of(cfg, place, part, z) * own_rows + k
                w_all[z * own_rows + k] = (w * inv_ref[pl.ds(at, 1), :]).astype(BF16)
            return carry

        lax.fori_loop(0, held, prepare, 0, unroll=held <= 4)

        def product(i, j, block):
            return lax.dot_general(
                w_all[j], block, (((1,), (1,)), ((), ())), preferred_element_type=F32
            )

        copies[part].wait()
        walk(cfg, part, listed.at[part], k_mat, kbuf, sems, product, z_acc, True)
    for k in range(own_rows):
        cols = slice(k * block_len, (k + 1) * block_len)
        mine = inv_ref[pl.ds(place[0] * own_rows + k, 1), :]
        own_inv[:, cols] = jnp.broadcast_to(mine, (8, block_len))
        for e, ref in enumerate((near, cross.at[0], near_y, cross.at[1])):
            ref[:, cols] = z_acc[(col ^ e) * own_rows + k]


def second_kernel(cfg, part, k_mat, list_v, t_ref, s1_own, s1_got, out, z_acc, w_all, listed, list_sem, *ring):
    kbuf, sems = ring or (None, None)
    place = position()
    own_rows, block_len = cfg.own_rows, cfg.block_len
    outputs = t_ref.shape[0]
    list_copy = pltpu.make_async_copy(list_v, listed, list_sem)
    list_copy.start()
    for e, packed in enumerate(pieces_of(s1_own, s1_got)):
        share = place[1] ^ e
        for k in range(own_rows):
            cols = slice(k * block_len, (k + 1) * block_len)
            i = share * own_rows + k
            t = t_ref[:, pl.ds(pl.multiple_of(i * block_len, LANES), block_len)]
            g = (packed[:outputs, cols] - SHIFT * t) * packed[outputs:outputs + 1, cols]
            w_all[i] = g.astype(BF16)
    z_acc[...] = jnp.zeros_like(z_acc)

    def product(i, j, block):
        return jnp.dot(w_all[i], block, preferred_element_type=F32)

    list_copy.wait()
    walk(cfg, part, listed, k_mat, kbuf, sems, product, z_acc, False)

    def hand_out(m, carry):
        z = slot_of(cfg, place, m)
        for k in range(own_rows):
            out[m, :, k * block_len:(k + 1) * block_len] = z_acc[z * own_rows + k].astype(out.dtype)
        return carry

    held = out.shape[0]
    lax.fori_loop(0, held, hand_out, 0, unroll=held <= 4)


N_DOTS = 5


def meet_kernel(cfg, z_same, z_other, t_same, inv_ref, s1_own, *refs):
    gs, (own_z, own_dots, *outs) = refs[:4], refs[4:]
    own_rows, block_len = cfg.own_rows, cfg.block_len
    outputs, own_len = own_z.shape
    place = position()
    tz = jnp.zeros((outputs, 1), F32)
    gz = jnp.zeros((outputs, 1), F32)
    for n in range(4):
        z = z_same[n] + z_other[n].astype(F32)
        if n == 0:
            own_z[...] = z
        else:
            outs[n - 1][:, :own_len] = z.astype(BF16)
        gz += jnp.sum(gs[n][...].astype(F32) * z, axis=1, keepdims=True)
        at = row_of(cfg, place, 0, slot_of(cfg, place, n)) * own_rows
        for k in range(own_rows):
            cols = slice(k * block_len, (k + 1) * block_len)
            scaled = t_same[n, :, cols] * inv_ref[pl.ds(at + k, 1), :]
            tz += jnp.sum(scaled * z[:, cols], axis=1, keepdims=True)
    t, s1 = t_same[0], s1_own[0, :outputs, :]
    tt = jnp.sum(t * t, axis=1, keepdims=True)
    ts1 = jnp.sum(t * s1, axis=1, keepdims=True)
    s1s1 = jnp.sum(s1 * s1, axis=1, keepdims=True)
    dots = (tt, ts1, s1s1, tz + SHIFT * ts1, gz + SHIFT * (tz + s1s1))
    lane = lax.broadcasted_iota(jnp.int32, (outputs, LANES), 1)
    tile = jnp.zeros(lane.shape, F32)
    for n, v in enumerate(dots):
        for part in range(3):
            head = v.astype(BF16).astype(F32)
            tile = jnp.where(lane == part * N_DOTS + n, head, tile)
            v = v - head
    own_dots[...] = tile.astype(BF16)
    for out in outs:
        out[:, own_len:] = tile.astype(BF16)


def product_kernel(own_z, own_dots, s1_own, *refs):
    got, grown_ref, dot_ref = refs[:3], refs[3], refs[4]
    outputs, own_len = grown_ref.shape
    z = own_z[...]
    for ref in got:
        z = z + ref[:, :own_len].astype(F32)
    grown_ref[...] = z * s1_own[0, outputs:outputs + 1, :]
    tiles = [own_dots[...]] + [ref[:, own_len:] for ref in got]
    total = pair_sum([tile.astype(F32) for tile in tiles])
    out = total
    for part in range(1, 3):
        out = out + pltpu.roll(total, LANES - part * N_DOTS, 1)
    dot_ref[...] = out


def final_kernel(t_ref, s1_own, s1_got, *refs):
    grown, all_dots = pieces_of(refs[0], refs[1]), refs[2:6]
    sol_hbm, res_hbm, sol_ref, res_ref, sems = refs[6:]
    s1s = pieces_of(s1_own, s1_got)
    outputs, own_len = grown[0].shape
    place = position()
    dots = pair_sum([ref[...] for ref in all_dots])
    tt, ts1, s1s1, ts2, s1s2 = (dots[:, n:n + 1] for n in range(5))
    a1 = tt / (REG * tt + ts1)
    p = 1.0 - REG * a1
    new = p * p * tt - 2.0 * p * a1 * ts1 + a1 * a1 * s1s1
    u = p + new / tt
    dd = u * u * tt - 2.0 * u * a1 * ts1 + a1 * a1 * s1s1
    dmd = u * u * ts1 - u * a1 * (s1s1 + ts2) + a1 * a1 * s1s2
    a2 = new / (REG * dd + dmd)
    sol_t, sol_1 = a1 + a2 * u, a2 * a1
    res_t, res_1 = p - a2 * REG * u, a1 + a2 * (u - REG * a1)
    copies = []
    for e in range(4):
        at = pl.ds(pl.multiple_of((place[1] ^ e) * own_len, LANES), own_len)
        t, s1 = t_ref[:, at], s1s[e][:outputs, :]
        s2 = grown[e][...] + SHIFT * s1
        sol_ref[e] = sol_t * t - sol_1 * s1
        res_ref[e] = res_t * t - res_1 * s1 + sol_1 * s2
        for n, (ref, hbm) in enumerate(((sol_ref, sol_hbm), (res_ref, res_hbm))):
            copy = pltpu.make_async_copy(ref.at[e], hbm.at[:, at], sems.at[n, e])
            copy.start()
            copies.append(copy)
    for copy in copies:
        copy.wait()


def swap(x, axis, d):
    size = lax.axis_size(axis)
    return lax.ppermute(x, axis, [(i, i ^ d) for i in range(size)])


def along_z(x):
    return [x] + [swap(x, "rows", d) for d in range(2, lax.axis_size("rows"), 2)]


def across_x(same):
    return [same, swap(same, "rows", 1)]


def direct_cols(x):
    return [x] + [swap(x, "cols", e) for e in range(1, 4)]


def local(block_list, points, targets):
    n_rows = lax.axis_size("rows")
    n_cols = lax.axis_size("cols")
    row = lax.axis_index("rows")
    col = lax.axis_index("cols")
    block_rows, slots = block_list.shape
    dim, npoints = points.shape
    outputs = targets.shape[0]
    block_len = npoints // block_rows
    own_rows = block_rows // n_cols
    own_len = own_rows * block_len
    nb = block_rows * n_rows
    n_sub = own_rows * n_rows
    capacity = -(-block_rows * slots // n_rows)
    direct_rows = n_rows <= DIRECT_ROWS
    parts = 2 if direct_rows else 1
    n_part = n_sub // parts
    bound = min(block_rows * n_part, n_cols * capacity * (n_rows + 1))
    n_groups = -(-bound // GROUP)
    list_len = -(-(n_groups * GROUP + GROUP + 1) // LANES) * LANES
    resident = parts * 2 * n_groups * GROUP * block_len * block_len <= RESIDENT_BYTES
    k_shape = (parts * n_groups, GROUP, block_len, block_len)
    limit = pltpu.CompilerParams(vmem_limit_bytes=(8 if resident else 32) * 1024 * 1024)
    ring = [] if resident else [
        pltpu.VMEM((RING, GROUP, block_len, block_len), BF16),
        pltpu.SemaphoreType.DMA((RING,)),
    ]
    k_spec = VMEM if resident else HBM
    cfg = Sizes(
        parts, n_groups, resident, nb, block_len, own_rows, block_rows, -(-own_rows * nb // LANES)
    )

    def shape(*dims, dtype=F32):
        return jax.ShapeDtypeStruct(dims, dtype)

    def own(x):
        return lax.dynamic_slice_in_dim(x, col * own_len, own_len, 1)

    def total_rows(x):
        if direct_rows:
            return pair_sum(across_x(pair_sum(along_z(x))))
        return lax.psum(x, "rows")

    lists = direct_cols(block_list)
    names = jnp.arange(nb, dtype=jnp.int32)
    direct = sum(jnp.sum((x[:, :, None] == names).astype(jnp.int32), axis=1) for x in lists)
    own_counts = lax.dynamic_slice_in_dim(direct, col * own_rows, own_rows, 0)
    coded = own_counts.reshape(-1)
    coded = jnp.pad(coded, (0, dim * LANES - coded.shape[0])).reshape(dim, LANES).astype(BF16)
    packed = jnp.concatenate([own(points), coded], axis=1)
    own_t = own(targets)

    def build(part, *operands):
        first, last = part == 0, part == parts - 1
        out = [
            pltpu.VMEM(k_shape, BF16) if resident else shape(*k_shape, dtype=BF16),
            shape(1, list_len, dtype=jnp.int32),
            shape(n_sub if last else n_part, block_len),
        ]
        out += [shape(block_rows, block_len, 2 * dim, dtype=BF16)] if first else []
        k_mat, *rest = pl.pallas_call(
            functools.partial(build_kernel, cfg, part),
            out_shape=out,
            in_specs=[VMEM] + ([HBM, VMEM] if first else [VMEM] * 3 + [k_spec]),
            out_specs=[k_spec] + [VMEM] * (len(out) - 1),
            scratch_shapes=([
                pltpu.VMEM((dim, npoints), BF16),
                pltpu.SemaphoreType.DMA,
            ] if first else []) + [
                pltpu.SMEM((1, list_len), jnp.int32),
                pltpu.SMEM((list_len,), jnp.int32),
                pltpu.VMEM((n_part, 8, block_len), F32),
                pltpu.VMEM((n_part, 2 * dim, block_len), BF16),
                pltpu.VMEM((2, block_len, block_len), F32),
                pltpu.SMEM((block_rows, nb), jnp.int32),
                pltpu.VMEM((n_part // own_rows, cfg.count_rows, LANES), jnp.int32),
                pltpu.SMEM((n_part // own_rows, cfg.count_rows, LANES), jnp.int32),
                pltpu.SemaphoreType.DMA((3,)),
                *ring,
            ],
            compiler_params=limit,
            input_output_aliases={} if first else {4: 0},
            cost_estimate=pl.CostEstimate(
                flops=2 * 2 * dim * bound * block_len * block_len,
                bytes_accessed=2 * bound * block_len * block_len,
                transcendentals=bound * block_len * block_len,
            ),
            name="build",
        )(direct, *operands)
        if resident:
            k_mat = pltpu.with_memory_space_constraint(k_mat, pltpu.VMEM)
        return k_mat, *rest

    near = pltpu.with_memory_space_constraint(points, pltpu.HBM)
    if direct_rows:
        packed, early_t = lax.optimization_barrier((packed, own_t))
        same, other = across_x(jnp.stack(along_z(packed)))
        t_same = along_z(early_t)
        k_mat, list0, degree, lhs = build(0, near, same)
        degree, other, *t_same = lax.optimization_barrier((degree, other, *t_same))
        t_same, t_other = across_x(jnp.stack(t_same))
        other, t_same = lax.optimization_barrier((other, t_same))
        k_mat, list1, degree = build(1, lhs, degree, other, k_mat)
        degree, t_other = lax.optimization_barrier((degree, t_other))
        t_pieces, k_lists = [t_same, t_other], [list0, list1]
    else:
        k_mat, list0, degree, _ = build(0, near, lax.all_gather(packed, "rows"))
        t_pieces, k_lists = [lax.all_gather(own_t, "rows")], [list0]
    inv = 1.0 / jnp.sqrt(1.0 + total_rows(degree))

    def cost(n):
        return pl.CostEstimate(
            flops=2 * n * bound * outputs * block_len * block_len,
            bytes_accessed=n * bound * block_len * block_len,
            transcendentals=0,
        )

    near_z, near_y, cross_z, tail = pl.pallas_call(
        functools.partial(first_kernel, cfg),
        out_shape=[shape(outputs, own_len)] * 2 + [shape(2, outputs, own_len), shape(8, own_len)],
        in_specs=[k_spec] + [VMEM] * (2 * parts + 1),
        out_specs=[VMEM] * 4,
        scratch_shapes=[
            pltpu.VMEM((block_rows, outputs, block_len), F32),
            pltpu.VMEM((n_part, outputs, block_len), BF16),
            pltpu.SMEM((parts, 1, list_len), jnp.int32),
            pltpu.SemaphoreType.DMA((parts,)),
            *ring,
        ],
        compiler_params=limit,
        cost_estimate=cost(parts),
        name="first",
    )(k_mat, *k_lists, *t_pieces, inv)

    got = swap(cross_z, "cols", 1)
    half = jnp.concatenate([near_z + got[0], near_y + got[1], tail], axis=0)
    far = swap(half, "cols", 2)
    lo, hi, end = slice(0, outputs), slice(outputs, 2 * outputs), slice(2 * outputs, None)
    s1_own = jnp.stack([
        jnp.concatenate([(half[lo] + far[hi]) * tail[:1], tail], axis=0),
        jnp.concatenate([(half[hi] + far[lo]) * far[end][:1], far[end]], axis=0),
    ])
    s1_got = swap(s1_own, "cols", 1)
    held_t = pltpu.with_memory_space_constraint(targets, pltpu.VMEM)

    def second(part, dtype):
        return pl.pallas_call(
            functools.partial(second_kernel, cfg, part),
            out_shape=shape(n_part // own_rows, outputs, own_len, dtype=dtype),
            in_specs=[k_spec] + [VMEM] * 4,
            out_specs=VMEM,
            scratch_shapes=[
                pltpu.VMEM((n_part, outputs, block_len), F32),
                pltpu.VMEM((block_rows, outputs, block_len), BF16),
                pltpu.SMEM((1, list_len), jnp.int32),
                pltpu.SemaphoreType.DMA,
                *ring,
            ],
            compiler_params=limit,
            cost_estimate=cost(1),
            name="second",
        )(k_mat, k_lists[part], held_t, s1_own, s1_got)

    if direct_rows:
        g = ((s1_own[0, :outputs] - SHIFT * own_t) * tail[:1]).astype(BF16)
        z2_other, g = lax.optimization_barrier((second(1, BF16), g))
        z2_other = swap(z2_other, "rows", 1)
        gs = along_z(g)
        z2_same = second(0, F32)
        z2_same, z2_other, *gs = lax.optimization_barrier((z2_same, z2_other, *gs))
        row_piece = shape(outputs, own_len + LANES, dtype=BF16)
        own_z, own_dots, *sends = pl.pallas_call(
            functools.partial(meet_kernel, cfg),
            out_shape=[shape(outputs, own_len), shape(outputs, LANES, dtype=BF16)] + [row_piece] * 3,
            in_specs=[VMEM] * 9,
            out_specs=[VMEM] * 5,
            compiler_params=limit,
            name="meet",
        )(z2_same, z2_other, t_pieces[0], inv, s1_own, *gs)
        got = [swap(sends[n], "rows", 2 * n + 2) for n in (2, 1, 0)][::-1]
        grown, dots = pl.pallas_call(
            product_kernel,
            out_shape=(shape(outputs, own_len), shape(outputs, LANES)),
            in_specs=[VMEM] * 6,
            out_specs=(VMEM, VMEM),
            compiler_params=limit,
            name="products",
        )(own_z, own_dots, s1_own, *got)
        dots = pair_sum(across_x(dots))
    else:
        z2 = lax.psum_scatter(second(0, F32), "rows", scatter_dimension=0)
        grown = z2 * tail[:1]
        own_s1 = s1_own[0, :outputs]
        own_t, s2 = own(targets), grown + SHIFT * own_s1
        dots = [(own_t, own_t), (own_t, own_s1), (own_s1, own_s1), (own_t, s2), (own_s1, s2)]
        dots = jnp.stack([jnp.sum(x * y, axis=1) for x, y in dots], axis=1)
        dots = lax.psum(jnp.pad(dots, ((0, 0), (0, LANES - N_DOTS))), "rows")
    grown = jnp.stack([grown, swap(grown, "cols", 2)])
    grown, dots = lax.optimization_barrier((grown, dots))
    ends = (s1_own, s1_got, grown, swap(grown, "cols", 1), *direct_cols(dots))
    ends = [pltpu.with_memory_space_constraint(x, pltpu.VMEM) for x in ends]

    return pl.pallas_call(
        final_kernel,
        out_shape=(shape(outputs, npoints), shape(outputs, npoints)),
        in_specs=[VMEM] * 9,
        out_specs=(HBM, HBM),
        scratch_shapes=[
            pltpu.VMEM((4, outputs, own_len), F32),
            pltpu.VMEM((4, outputs, own_len), F32),
            pltpu.SemaphoreType.DMA((2, 4)),
        ],
        compiler_params=limit,
        name="final",
    )(held_t, *ends)


def solution(mesh):
    placed = (P("rows", "cols"), P(None, "rows"), P(None, "rows"))
    return jax.shard_map(
        local,
        mesh=mesh,
        in_specs=placed,
        out_specs=(P(None, "rows"), P(None, "rows")),
        check_vma=False,
    )
```

```python
import functools
from typing import NamedTuple

import jax
import jax.numpy as jnp
from jax import lax
from jax.experimental import pallas as pl
from jax.experimental.pallas import tpu as pltpu
from jax.sharding import PartitionSpec as P

REG = 1.5
RADIUS = 0.25
GROUP_BITS = 2
GROUP = 1 << GROUP_BITS
CODE_BITS = 12
CODE = 1 << CODE_BITS
RING = 3
STRIP = 32
LANES = 128
TINY = 1e-30
SHIFT = 0.375
DIRECT_ROWS = 8
RESIDENT_BYTES = 20 * 1024 * 1024

VMEM = pl.BlockSpec(memory_space=pltpu.VMEM)
HBM = pl.BlockSpec(memory_space=pltpu.HBM)
F32 = jnp.float32
BF16 = jnp.bfloat16


def pair_sum(parts):
    while len(parts) > 1:
        parts = [a + b for a, b in zip(parts[::2], parts[1::2])]
    return parts[0]


def position():
    return lax.axis_index("rows"), lax.axis_index("cols")


class Sizes(NamedTuple):
    parts: int
    part_groups: int
    resident: bool
    nb: int
    block_len: int
    own_rows: int
    block_rows: int
    count_rows: int


def augment(x, first_ones):
    dim, n = x.shape
    norm = jnp.sum(x * x, axis=0, keepdims=True) / (RADIUS * RADIUS)
    high = norm.astype(BF16).astype(F32)
    rest = norm - high
    mid = rest.astype(BF16).astype(F32)
    low = rest - mid
    line = lax.broadcasted_iota(jnp.int32, (dim, n), 0)
    base = 3 if first_ones else 0
    ones_at = 0 if first_ones else 3
    tail = jnp.where((line >= ones_at) & (line < ones_at + 3), 1.0, 0.0)
    tail = jnp.where(line == base, high, tail)
    tail = jnp.where(line == base + 1, mid, tail)
    tail = jnp.where(line == base + 2, low, tail)
    return tail


def row_of(cfg, place, part, z):
    if cfg.parts == 1:
        return z
    return 2 * z + (place[0] & 1 if part == 0 else 1 - (place[0] & 1))


def slot_of(cfg, place, n):
    return n if cfg.parts == 1 else lax.shift_right_logical(place[0], 1) ^ n


def build_kernel(cfg, part, direct_v, *refs):
    last = part == cfg.parts - 1
    place = position()
    if part == 0:
        near_hbm, piece, refs = refs[0], refs[1], refs[2:]
        k_mat, list_v, deg_ref, lhs = refs[:4]
        near_ref, near_sem, refs = refs[4], refs[5], refs[6:]
        near_copy = pltpu.make_async_copy(near_hbm, near_ref, near_sem)
        near_copy.start()
    else:
        lhs, first_deg, piece, _ = refs[:4]
        k_mat, list_v, deg_ref = refs[4:7]
        refs = refs[7:]
    listed, mlist, acc, rhs, dist, direct, counts_v, counts, copy_sems = refs[:9]
    kbuf, sems = (None, None) if cfg.resident else refs[9:]
    direct_copy = pltpu.make_async_copy(direct_v, direct, copy_sems.at[0])
    direct_copy.start()
    row, col = place[0], place[1]
    own_rows, block_len, nb = cfg.own_rows, cfg.block_len, cfg.nb
    own_len = own_rows * block_len
    dim, held = piece.shape[1], piece.shape[0]
    scale = 1.0 / (RADIUS * RADIUS)

    def count(n, carry):
        named = piece[n, :, own_len:own_len + LANES]
        counts_v[slot_of(cfg, place, n)] = named.astype(F32)[:cfg.count_rows].astype(jnp.int32)
        return carry

    def prepare(n, carry):
        z = slot_of(cfg, place, n)
        for k in range(own_rows):
            far = piece[n, :, k * block_len:(k + 1) * block_len]
            rhs[z * own_rows + k, :dim, :] = far
            rhs[z * own_rows + k, dim:, :] = augment(far.astype(F32), False).astype(BF16)
        return carry

    lax.fori_loop(0, held, count, 0, unroll=held <= 4)
    fetch = pltpu.make_async_copy(counts_v, counts, copy_sems.at[1])
    fetch.start()
    lax.fori_loop(0, held, prepare, 0, unroll=held <= 4)
    acc[...] = jnp.zeros_like(acc)
    if part == 0:
        near_copy.wait()
        for i in range(cfg.block_rows):
            near = near_ref[:, i * block_len:(i + 1) * block_len].astype(F32)
            full = jnp.concatenate([near * (-2.0 * scale), augment(near, True)], axis=0)
            lhs[i] = full.T.astype(BF16)
    direct_copy.wait()
    fetch.wait()

    pos = jnp.int32(0)
    for i in range(cfg.block_rows):
        me = row * cfg.block_rows + i
        spots = [k * nb + me for k in range(own_rows)]
        spots = [(lax.shift_right_logical(p, 7), p & (LANES - 1)) for p in spots]

        def note(z, at, i=i, me=me, spots=spots):
            for k in range(own_rows):
                name = row_of(cfg, place, part, z) * cfg.block_rows + col * own_rows + k
                m = direct[i, name] + jnp.where(name == me, 0, counts[z, spots[k][0], spots[k][1]])
                listed[0, at + 1] = i * CODE + z * own_rows + k
                mlist[at] = m
                at = at + jnp.where(m > 0, 1, 0)
            return at

        if held <= 4:
            for z in range(held):
                pos = note(z, pos)
        else:
            pos = lax.fori_loop(0, held, note, pos, unroll=4)
    for u in range(GROUP):
        listed[0, pos + u + 1] = 0
        mlist[pos + u] = 0
    total = lax.shift_right_logical(pos + (GROUP - 1), GROUP_BITS)
    listed[0, 0] = total
    list_copy = pltpu.make_async_copy(listed, list_v, copy_sems.at[2])
    list_copy.start()

    def copy_out(g):
        slot = lax.rem(g, RING)
        return pltpu.make_async_copy(kbuf.at[slot], k_mat.at[g], sems.at[slot])

    base = part * cfg.part_groups

    def distances(e, slot):
        code = listed[0, e + 1]
        i, j = lax.shift_right_logical(code, CODE_BITS), code & (CODE - 1)
        dist[slot] = jnp.dot(lhs[i], rhs[j], preferred_element_type=F32)

    distances(0, 0)

    def step(g, carry):
        slot, target = (base + g, k_mat) if cfg.resident else (lax.rem(g, RING), kbuf)
        if not cfg.resident:

            @pl.when(g >= RING)
            def _():
                copy_out(g - RING).wait()

        for u in range(GROUP):
            distances(g * GROUP + u + 1, (u + 1) % 2)
            j = listed[0, g * GROUP + u + 1] & (CODE - 1)
            m = mlist[g * GROUP + u].astype(F32)
            sums = jnp.zeros((8, block_len), F32)
            for s in range(block_len // STRIP):
                rows = slice(s * STRIP, (s + 1) * STRIP)
                d = jnp.maximum(dist[u % 2, rows, :], TINY)
                sc = d * lax.rsqrt(d)
                rem = jnp.maximum(1.0 - sc, 0.0)
                sq = rem * rem
                val = (sq * sq) * (sc * (4.0 * m) + m)
                target[slot, u, rows, :] = val.astype(BF16)
                for h in range(0, STRIP, 8):
                    sums = sums + val[h:h + 8]
            acc[j] += sums
        if not cfg.resident:
            copy_out(g).start()
        return carry

    lax.fori_loop(0, total, step, 0)
    if cfg.parts == 1 or not last:
        deg_ref[...] = jnp.sum(acc[...], axis=1)
    else:
        second = jnp.sum(acc[...], axis=1)
        for z in range(held):
            rows = slice(z * own_rows, (z + 1) * own_rows)
            for p, deg in enumerate((first_deg[rows, :], second[rows])):
                at = row_of(cfg, place, p, z) * own_rows
                for k in range(own_rows):
                    deg_ref[pl.ds(at + k, 1), :] = deg[k:k + 1]

    def drain(g, carry):
        copy_out(g).wait()
        return carry

    if not cfg.resident:
        lax.fori_loop(jnp.maximum(total - RING, 0), total, drain, 0)
    list_copy.wait()


def pieces_of(own, got):
    return own.at[0], got.at[0], own.at[1], got.at[1]


def walk(cfg, part, listed, k_mat, kbuf, sems, product, total_ref, by_row):
    total = listed[0, 0]
    base = part * cfg.part_groups

    def copy_in(g):
        slot = lax.rem(g, RING)
        return pltpu.make_async_copy(k_mat.at[g], kbuf.at[slot], sems.at[slot])

    if not cfg.resident:
        for p in range(RING - 1):

            @pl.when(p < total)
            def _(p=p):
                copy_in(p).start()

    def step(g, carry):
        slot, source = (base + g, k_mat) if cfg.resident else (lax.rem(g, RING), kbuf)
        if not cfg.resident:

            @pl.when(g + (RING - 1) < total)
            def _():
                copy_in(g + (RING - 1)).start()

            copy_in(g).wait()
        codes = [listed[0, g * GROUP + u + 1] for u in range(GROUP)]
        pairs = [(lax.shift_right_logical(code, CODE_BITS), code & (CODE - 1)) for code in codes]
        terms = [product(i, j, source[slot, u]) for u, (i, j) in enumerate(pairs)]
        for (i, j), term in zip(pairs, terms):
            total_ref[i if by_row else j] += term
        return carry

    lax.fori_loop(0, total, step, 0)


def first_kernel(cfg, k_mat, *refs):
    n = cfg.parts
    lists, pieces, inv_ref, refs = refs[:n], refs[n:2 * n], refs[2 * n], refs[2 * n + 1:]
    near, near_y, cross, own_inv, z_acc, w_all, listed, list_sems, *ring = refs
    kbuf, sems = ring or (None, None)
    place = position()
    col = place[1]
    copies = [
        pltpu.make_async_copy(lists[p], listed.at[p], list_sems.at[p]) for p in range(n)
    ]
    for copy in copies:
        copy.start()
    own_rows, block_len = cfg.own_rows, cfg.block_len
    z_acc[...] = jnp.zeros_like(z_acc)
    for part, piece in enumerate(pieces):
        held = piece.shape[0]

        def prepare(m, carry, part=part, piece=piece):
            z = slot_of(cfg, place, m)
            for k in range(own_rows):
                w = piece[m, :, k * block_len:(k + 1) * block_len]
                at = row_of(cfg, place, part, z) * own_rows + k
                w_all[z * own_rows + k] = (w * inv_ref[pl.ds(at, 1), :]).astype(BF16)
            return carry

        lax.fori_loop(0, held, prepare, 0, unroll=held <= 4)

        def product(i, j, block):
            return lax.dot_general(
                w_all[j], block, (((1,), (1,)), ((), ())), preferred_element_type=F32
            )

        copies[part].wait()
        walk(cfg, part, listed.at[part], k_mat, kbuf, sems, product, z_acc, True)
    for k in range(own_rows):
        cols = slice(k * block_len, (k + 1) * block_len)
        mine = inv_ref[pl.ds(place[0] * own_rows + k, 1), :]
        own_inv[:, cols] = jnp.broadcast_to(mine, (8, block_len))
        for e, ref in enumerate((near, cross.at[0], near_y, cross.at[1])):
            ref[:, cols] = z_acc[(col ^ e) * own_rows + k]


def second_kernel(cfg, part, k_mat, list_v, t_ref, s1_own, s1_got, out, z_acc, w_all, listed, list_sem, *ring):
    kbuf, sems = ring or (None, None)
    place = position()
    own_rows, block_len = cfg.own_rows, cfg.block_len
    outputs = t_ref.shape[0]
    list_copy = pltpu.make_async_copy(list_v, listed, list_sem)
    list_copy.start()
    for e, packed in enumerate(pieces_of(s1_own, s1_got)):
        share = place[1] ^ e
        for k in range(own_rows):
            cols = slice(k * block_len, (k + 1) * block_len)
            i = share * own_rows + k
            t = t_ref[:, pl.ds(pl.multiple_of(i * block_len, LANES), block_len)]
            g = (packed[:outputs, cols] - SHIFT * t) * packed[outputs:outputs + 1, cols]
            w_all[i] = g.astype(BF16)
    z_acc[...] = jnp.zeros_like(z_acc)

    def product(i, j, block):
        return jnp.dot(w_all[i], block, preferred_element_type=F32)

    list_copy.wait()
    walk(cfg, part, listed, k_mat, kbuf, sems, product, z_acc, False)

    def hand_out(m, carry):
        z = slot_of(cfg, place, m)
        for k in range(own_rows):
            out[m, :, k * block_len:(k + 1) * block_len] = z_acc[z * own_rows + k].astype(out.dtype)
        return carry

    held = out.shape[0]
    lax.fori_loop(0, held, hand_out, 0, unroll=held <= 4)


N_DOTS = 5


def meet_kernel(cfg, z_same, z_other, t_same, inv_ref, s1_own, *refs):
    gs, (own_z, own_dots, *outs) = refs[:4], refs[4:]
    own_rows, block_len = cfg.own_rows, cfg.block_len
    outputs, own_len = own_z.shape
    place = position()
    tz = jnp.zeros((outputs, 1), F32)
    gz = jnp.zeros((outputs, 1), F32)
    for n in range(4):
        z = z_same[n] + z_other[n].astype(F32)
        if n == 0:
            own_z[...] = z
        else:
            outs[n - 1][:, :own_len] = z.astype(BF16)
        gz += jnp.sum(gs[n][...].astype(F32) * z, axis=1, keepdims=True)
        at = row_of(cfg, place, 0, slot_of(cfg, place, n)) * own_rows
        for k in range(own_rows):
            cols = slice(k * block_len, (k + 1) * block_len)
            scaled = t_same[n, :, cols] * inv_ref[pl.ds(at + k, 1), :]
            tz += jnp.sum(scaled * z[:, cols], axis=1, keepdims=True)
    t, s1 = t_same[0], s1_own[0, :outputs, :]
    tt = jnp.sum(t * t, axis=1, keepdims=True)
    ts1 = jnp.sum(t * s1, axis=1, keepdims=True)
    s1s1 = jnp.sum(s1 * s1, axis=1, keepdims=True)
    dots = (tt, ts1, s1s1, tz + SHIFT * ts1, gz + SHIFT * (tz + s1s1))
    lane = lax.broadcasted_iota(jnp.int32, (outputs, LANES), 1)
    tile = jnp.zeros(lane.shape, F32)
    for n, v in enumerate(dots):
        for part in range(3):
            head = v.astype(BF16).astype(F32)
            tile = jnp.where(lane == part * N_DOTS + n, head, tile)
            v = v - head
    own_dots[...] = tile.astype(BF16)
    for out in outs:
        out[:, own_len:] = tile.astype(BF16)


def product_kernel(own_z, own_dots, s1_own, *refs):
    got, grown_ref, dot_ref = refs[2::-1], refs[3], refs[4]
    outputs, own_len = grown_ref.shape
    z = own_z[...]
    for ref in got:
        z = z + ref[:, :own_len].astype(F32)
    grown_ref[...] = z * s1_own[0, outputs:outputs + 1, :]
    tiles = [own_dots[...]] + [ref[:, own_len:] for ref in got]
    total = pair_sum([tile.astype(F32) for tile in tiles])
    out = total
    for part in range(1, 3):
        out = out + pltpu.roll(total, LANES - part * N_DOTS, 1)
    dot_ref[...] = out


def final_kernel(t_ref, s1_own, s1_got, *refs):
    grown, all_dots = pieces_of(refs[0], refs[1]), refs[2:4]
    sol_hbm, res_hbm, sol_ref, res_ref, sems = refs[4:]
    s1s = pieces_of(s1_own, s1_got)
    outputs, own_len = grown[0].shape
    place = position()
    dots = pair_sum([ref[...] for ref in all_dots])
    tt, ts1, s1s1, ts2, s1s2 = (dots[:, n:n + 1] for n in range(5))
    a1 = tt / (REG * tt + ts1)
    p = 1.0 - REG * a1
    new = p * p * tt - 2.0 * p * a1 * ts1 + a1 * a1 * s1s1
    u = p + new / tt
    dd = u * u * tt - 2.0 * u * a1 * ts1 + a1 * a1 * s1s1
    dmd = u * u * ts1 - u * a1 * (s1s1 + ts2) + a1 * a1 * s1s2
    a2 = new / (REG * dd + dmd)
    sol_t, sol_1 = a1 + a2 * u, a2 * a1
    res_t, res_1 = p - a2 * REG * u, a1 + a2 * (u - REG * a1)
    copies = []
    for e in range(4):
        at = pl.ds(pl.multiple_of((place[1] ^ e) * own_len, LANES), own_len)
        t, s1 = t_ref[:, at], s1s[e][:outputs, :]
        s2 = grown[e][...] + SHIFT * s1
        sol_ref[e] = sol_t * t - sol_1 * s1
        res_ref[e] = res_t * t - res_1 * s1 + sol_1 * s2
        for n, (ref, hbm) in enumerate(((sol_ref, sol_hbm), (res_ref, res_hbm))):
            copy = pltpu.make_async_copy(ref.at[e], hbm.at[:, at], sems.at[n, e])
            copy.start()
            copies.append(copy)
    for copy in copies:
        copy.wait()


def swap(x, axis, d):
    size = lax.axis_size(axis)
    return lax.ppermute(x, axis, [(i, i ^ d) for i in range(size)])


def both_swap(x, row_d, col_d):
    n_rows, n_cols = lax.axis_size("rows"), lax.axis_size("cols")
    pairs = [
        (r * n_cols + c, (r ^ row_d) * n_cols + (c ^ col_d))
        for r in range(n_rows)
        for c in range(n_cols)
    ]
    return lax.ppermute(x, ("rows", "cols"), pairs)


def along_z(x):
    return [x] + [swap(x, "rows", d) for d in range(2, lax.axis_size("rows"), 2)]


def across_x(same):
    return [same, swap(same, "rows", 1)]


def direct_cols(x):
    return [x] + [swap(x, "cols", e) for e in range(1, 4)]


def local(block_list, points, targets):
    n_rows = lax.axis_size("rows")
    n_cols = lax.axis_size("cols")
    row = lax.axis_index("rows")
    col = lax.axis_index("cols")
    block_rows, slots = block_list.shape
    dim, npoints = points.shape
    outputs = targets.shape[0]
    block_len = npoints // block_rows
    own_rows = block_rows // n_cols
    own_len = own_rows * block_len
    nb = block_rows * n_rows
    n_sub = own_rows * n_rows
    capacity = -(-block_rows * slots // n_rows)
    direct_rows = n_rows <= DIRECT_ROWS
    parts = 2 if direct_rows else 1
    n_part = n_sub // parts
    bound = min(block_rows * n_part, n_cols * capacity * (n_rows + 1))
    n_groups = -(-bound // GROUP)
    list_len = -(-(n_groups * GROUP + GROUP + 1) // LANES) * LANES
    resident = parts * 2 * n_groups * GROUP * block_len * block_len <= RESIDENT_BYTES
    k_shape = (parts * n_groups, GROUP, block_len, block_len)
    limit = pltpu.CompilerParams(vmem_limit_bytes=(8 if resident else 32) * 1024 * 1024)
    ring = [] if resident else [
        pltpu.VMEM((RING, GROUP, block_len, block_len), BF16),
        pltpu.SemaphoreType.DMA((RING,)),
    ]
    k_spec = VMEM if resident else HBM
    cfg = Sizes(
        parts, n_groups, resident, nb, block_len, own_rows, block_rows, -(-own_rows * nb // LANES)
    )

    def shape(*dims, dtype=F32):
        return jax.ShapeDtypeStruct(dims, dtype)

    def own(x):
        return lax.dynamic_slice_in_dim(x, col * own_len, own_len, 1)

    def total_rows(x):
        if direct_rows:
            near = pair_sum([x] + [swap(x, "rows", d) for d in range(1, 4)])
            return near + swap(near, "rows", 4)
        return lax.psum(x, "rows")

    lists = direct_cols(block_list)
    names = jnp.arange(nb, dtype=jnp.int32)
    direct = sum(jnp.sum((x[:, :, None] == names).astype(jnp.int32), axis=1) for x in lists)
    own_counts = lax.dynamic_slice_in_dim(direct, col * own_rows, own_rows, 0)
    coded = own_counts.reshape(-1)
    coded = jnp.pad(coded, (0, dim * LANES - coded.shape[0])).reshape(dim, LANES).astype(BF16)
    packed = jnp.concatenate([own(points), coded], axis=1)
    own_t = own(targets)

    def build(part, *operands):
        first, last = part == 0, part == parts - 1
        out = [
            pltpu.VMEM(k_shape, BF16) if resident else shape(*k_shape, dtype=BF16),
            shape(1, list_len, dtype=jnp.int32),
            shape(n_sub if last else n_part, block_len),
        ]
        out += [shape(block_rows, block_len, 2 * dim, dtype=BF16)] if first else []
        k_mat, *rest = pl.pallas_call(
            functools.partial(build_kernel, cfg, part),
            out_shape=out,
            in_specs=[VMEM] + ([HBM, VMEM] if first else [VMEM] * 3 + [k_spec]),
            out_specs=[k_spec] + [VMEM] * (len(out) - 1),
            scratch_shapes=([
                pltpu.VMEM((dim, npoints), BF16),
                pltpu.SemaphoreType.DMA,
            ] if first else []) + [
                pltpu.SMEM((1, list_len), jnp.int32),
                pltpu.SMEM((list_len,), jnp.int32),
                pltpu.VMEM((n_part, 8, block_len), F32),
                pltpu.VMEM((n_part, 2 * dim, block_len), BF16),
                pltpu.VMEM((2, block_len, block_len), F32),
                pltpu.SMEM((block_rows, nb), jnp.int32),
                pltpu.VMEM((n_part // own_rows, cfg.count_rows, LANES), jnp.int32),
                pltpu.SMEM((n_part // own_rows, cfg.count_rows, LANES), jnp.int32),
                pltpu.SemaphoreType.DMA((3,)),
                *ring,
            ],
            compiler_params=limit,
            input_output_aliases={} if first else {4: 0},
            cost_estimate=pl.CostEstimate(
                flops=10 * 2 * 2 * dim * bound * block_len * block_len,
                bytes_accessed=10 * 2 * bound * block_len * block_len,
                transcendentals=10 * bound * block_len * block_len,
            ),
            name="build",
        )(direct, *operands)
        if resident:
            k_mat = pltpu.with_memory_space_constraint(k_mat, pltpu.VMEM)
        return k_mat, *rest

    near = pltpu.with_memory_space_constraint(points, pltpu.HBM)
    if direct_rows:
        packed, early_t = lax.optimization_barrier((packed, own_t))
        same, other = across_x(jnp.stack(along_z(packed)))
        t_same = along_z(early_t)
        k_mat, list0, degree, lhs = build(0, near, same)
        degree, other, *t_same = lax.optimization_barrier((degree, other, *t_same))
        t_same, t_other = across_x(jnp.stack(t_same))
        other, t_same = lax.optimization_barrier((other, t_same))
        k_mat, list1, degree = build(1, lhs, degree, other, k_mat)
        degree, t_other = lax.optimization_barrier((degree, t_other))
        t_pieces, k_lists = [t_same, t_other], [list0, list1]
    else:
        k_mat, list0, degree, _ = build(0, near, lax.all_gather(packed, "rows"))
        t_pieces, k_lists = [lax.all_gather(own_t, "rows")], [list0]
    inv = 1.0 / jnp.sqrt(1.0 + total_rows(degree))

    def cost(n):
        return pl.CostEstimate(
            flops=2 * n * bound * outputs * block_len * block_len,
            bytes_accessed=n * bound * block_len * block_len,
            transcendentals=0,
        )

    near_z, near_y, cross_z, tail = pl.pallas_call(
        functools.partial(first_kernel, cfg),
        out_shape=[shape(outputs, own_len)] * 2 + [shape(2, outputs, own_len), shape(8, own_len)],
        in_specs=[k_spec] + [VMEM] * (2 * parts + 1),
        out_specs=[VMEM] * 4,
        scratch_shapes=[
            pltpu.VMEM((block_rows, outputs, block_len), F32),
            pltpu.VMEM((n_part, outputs, block_len), BF16),
            pltpu.SMEM((parts, 1, list_len), jnp.int32),
            pltpu.SemaphoreType.DMA((parts,)),
            *ring,
        ],
        compiler_params=limit,
        cost_estimate=cost(parts),
        name="first",
    )(k_mat, *k_lists, *t_pieces, inv)

    got = swap(cross_z, "cols", 1)
    half = jnp.concatenate([near_z + got[0], near_y + got[1], tail], axis=0)
    far = swap(half, "cols", 2)
    lo, hi, end = slice(0, outputs), slice(outputs, 2 * outputs), slice(2 * outputs, None)
    s1_own = jnp.stack([
        jnp.concatenate([(half[lo] + far[hi]) * tail[:1], tail], axis=0),
        jnp.concatenate([(half[hi] + far[lo]) * far[end][:1], far[end]], axis=0),
    ])
    s1_got = swap(s1_own, "cols", 1)
    held_t = pltpu.with_memory_space_constraint(targets, pltpu.VMEM)

    def second(part, dtype):
        return pl.pallas_call(
            functools.partial(second_kernel, cfg, part),
            out_shape=shape(n_part // own_rows, outputs, own_len, dtype=dtype),
            in_specs=[k_spec] + [VMEM] * 4,
            out_specs=VMEM,
            scratch_shapes=[
                pltpu.VMEM((n_part, outputs, block_len), F32),
                pltpu.VMEM((block_rows, outputs, block_len), BF16),
                pltpu.SMEM((1, list_len), jnp.int32),
                pltpu.SemaphoreType.DMA,
                *ring,
            ],
            compiler_params=limit,
            cost_estimate=cost(1),
            name="second",
        )(k_mat, k_lists[part], held_t, s1_own, s1_got)

    if direct_rows:
        g = ((s1_own[0, :outputs] - SHIFT * own_t) * tail[:1]).astype(BF16)
        z2_other, g = lax.optimization_barrier((second(1, BF16), g))
        z2_other = swap(z2_other, "rows", 1)
        gs = along_z(g)
        z2_same = second(0, F32)
        z2_same, z2_other, *gs = lax.optimization_barrier((z2_same, z2_other, *gs))
        row_piece = shape(outputs, own_len + LANES, dtype=BF16)
        own_z, own_dots, *sends = pl.pallas_call(
            functools.partial(meet_kernel, cfg),
            out_shape=[shape(outputs, own_len), shape(outputs, LANES, dtype=BF16)] + [row_piece] * 3,
            in_specs=[VMEM] * 9,
            out_specs=[VMEM] * 5,
            compiler_params=limit,
            name="meet",
        )(z2_same, z2_other, t_pieces[0], inv, s1_own, *gs)
        got = [swap(sends[n], "rows", 2 * n + 2) for n in (2, 1, 0)]
        grown, dots = pl.pallas_call(
            product_kernel,
            out_shape=(shape(outputs, own_len), shape(outputs, LANES)),
            in_specs=[VMEM] * 6,
            out_specs=(VMEM, VMEM),
            compiler_params=limit,
            name="products",
        )(own_z, own_dots, s1_own, *got)
        far = both_swap(dots, 1, 2)
        dots = pair_sum([dots, swap(dots, "rows", 1), swap(dots, "cols", 2), far])
    else:
        z2 = lax.psum_scatter(second(0, F32), "rows", scatter_dimension=0)
        grown = z2 * tail[:1]
        own_s1 = s1_own[0, :outputs]
        own_t, s2 = own(targets), grown + SHIFT * own_s1
        dots = [(own_t, own_t), (own_t, own_s1), (own_s1, own_s1), (own_t, s2), (own_s1, s2)]
        dots = jnp.stack([jnp.sum(x * y, axis=1) for x, y in dots], axis=1)
        dots = lax.psum(jnp.pad(dots, ((0, 0), (0, LANES - N_DOTS))), "rows")
        dots = dots + swap(dots, "cols", 2)
    grown = jnp.stack([grown, swap(grown, "cols", 2)])
    grown, dots = lax.optimization_barrier((grown, dots))
    ends = (s1_own, s1_got, grown, swap(grown, "cols", 1), dots, swap(dots, "cols", 1))
    ends = [pltpu.with_memory_space_constraint(x, pltpu.VMEM) for x in ends]

    return pl.pallas_call(
        final_kernel,
        out_shape=(shape(outputs, npoints), shape(outputs, npoints)),
        in_specs=[VMEM] * 7,
        out_specs=(HBM, HBM),
        scratch_shapes=[
            pltpu.VMEM((4, outputs, own_len), F32),
            pltpu.VMEM((4, outputs, own_len), F32),
            pltpu.SemaphoreType.DMA((2, 4)),
        ],
        compiler_params=limit,
        name="final",
    )(held_t, *ends)


def solution(mesh):
    placed = (P("rows", "cols"), P(None, "rows"), P(None, "rows"))
    return jax.shard_map(
        local,
        mesh=mesh,
        in_specs=placed,
        out_specs=(P(None, "rows"), P(None, "rows")),
        check_vma=False,
    )
```

```python
import functools
from typing import NamedTuple

import jax
import jax.numpy as jnp
from jax import lax
from jax.experimental import pallas as pl
from jax.experimental.pallas import tpu as pltpu
from jax.sharding import PartitionSpec as P

REG = 1.5
RADIUS = 0.25
GROUP_BITS = 2
GROUP = 1 << GROUP_BITS
CODE_BITS = 12
CODE = 1 << CODE_BITS
RING = 3
STRIP = 32
LANES = 128
TINY = 1e-30
SHIFT = 0.375
DIRECT_ROWS = 8
RESIDENT_BYTES = 20 * 1024 * 1024

VMEM = pl.BlockSpec(memory_space=pltpu.VMEM)
HBM = pl.BlockSpec(memory_space=pltpu.HBM)
F32 = jnp.float32
BF16 = jnp.bfloat16


def pair_sum(parts):
    while len(parts) > 1:
        parts = [a + b for a, b in zip(parts[::2], parts[1::2])]
    return parts[0]


def position():
    return lax.axis_index("rows"), lax.axis_index("cols")


class Sizes(NamedTuple):
    parts: int
    part_groups: int
    resident: bool
    nb: int
    block_len: int
    own_rows: int
    block_rows: int
    count_rows: int


def augment(x, first_ones):
    dim, n = x.shape
    norm = jnp.sum(x * x, axis=0, keepdims=True) / (RADIUS * RADIUS)
    high = norm.astype(BF16).astype(F32)
    rest = norm - high
    mid = rest.astype(BF16).astype(F32)
    low = rest - mid
    line = lax.broadcasted_iota(jnp.int32, (dim, n), 0)
    base = 3 if first_ones else 0
    ones_at = 0 if first_ones else 3
    tail = jnp.where((line >= ones_at) & (line < ones_at + 3), 1.0, 0.0)
    tail = jnp.where(line == base, high, tail)
    tail = jnp.where(line == base + 1, mid, tail)
    tail = jnp.where(line == base + 2, low, tail)
    return tail


def row_of(cfg, place, part, z):
    if cfg.parts == 1:
        return z
    return 2 * z + (place[0] & 1 if part == 0 else 1 - (place[0] & 1))


def slot_of(cfg, place, n):
    return n if cfg.parts == 1 else lax.shift_right_logical(place[0], 1) ^ n


def build_kernel(cfg, part, direct_v, *refs):
    last = part == cfg.parts - 1
    place = position()
    if part == 0:
        near_hbm, piece, refs = refs[0], refs[1], refs[2:]
        k_mat, list_v, deg_ref, lhs = refs[:4]
        near_ref, near_sem, refs = refs[4], refs[5], refs[6:]
        near_copy = pltpu.make_async_copy(near_hbm, near_ref, near_sem)
        near_copy.start()
    else:
        lhs, first_deg, piece, _ = refs[:4]
        k_mat, list_v, deg_ref = refs[4:7]
        refs = refs[7:]
    listed, mlist, acc, rhs, dist, direct, counts_v, counts, copy_sems = refs[:9]
    kbuf, sems = (None, None) if cfg.resident else refs[9:]
    direct_copy = pltpu.make_async_copy(direct_v, direct, copy_sems.at[0])
    direct_copy.start()
    row, col = place[0], place[1]
    own_rows, block_len, nb = cfg.own_rows, cfg.block_len, cfg.nb
    own_len = own_rows * block_len
    dim, held = piece.shape[1], piece.shape[0]
    scale = 1.0 / (RADIUS * RADIUS)

    def count(n, carry):
        named = piece[n, :, own_len:own_len + LANES]
        counts_v[slot_of(cfg, place, n)] = named.astype(F32)[:cfg.count_rows].astype(jnp.int32)
        return carry

    def prepare(n, carry):
        z = slot_of(cfg, place, n)
        for k in range(own_rows):
            far = piece[n, :, k * block_len:(k + 1) * block_len]
            rhs[z * own_rows + k, :dim, :] = far
            rhs[z * own_rows + k, dim:, :] = augment(far.astype(F32), False).astype(BF16)
        return carry

    lax.fori_loop(0, held, count, 0, unroll=held <= 4)
    fetch = pltpu.make_async_copy(counts_v, counts, copy_sems.at[1])
    fetch.start()
    lax.fori_loop(0, held, prepare, 0, unroll=held <= 4)
    acc[...] = jnp.zeros_like(acc)
    if part == 0:
        near_copy.wait()
        for i in range(cfg.block_rows):
            near = near_ref[:, i * block_len:(i + 1) * block_len].astype(F32)
            full = jnp.concatenate([near * (-2.0 * scale), augment(near, True)], axis=0)
            lhs[i] = full.T.astype(BF16)
    direct_copy.wait()
    fetch.wait()

    pos = jnp.int32(0)
    for i in range(cfg.block_rows):
        me = row * cfg.block_rows + i
        spots = [k * nb + me for k in range(own_rows)]
        spots = [(lax.shift_right_logical(p, 7), p & (LANES - 1)) for p in spots]

        def note(z, at, i=i, me=me, spots=spots):
            for k in range(own_rows):
                name = row_of(cfg, place, part, z) * cfg.block_rows + col * own_rows + k
                m = direct[i, name] + jnp.where(name == me, 0, counts[z, spots[k][0], spots[k][1]])
                listed[0, at + 1] = i * CODE + z * own_rows + k
                mlist[at] = m
                at = at + jnp.where(m > 0, 1, 0)
            return at

        if held <= 4:
            for z in range(held):
                pos = note(z, pos)
        else:
            pos = lax.fori_loop(0, held, note, pos, unroll=4)
    for u in range(GROUP):
        listed[0, pos + u + 1] = 0
        mlist[pos + u] = 0
    total = lax.shift_right_logical(pos + (GROUP - 1), GROUP_BITS)
    listed[0, 0] = total
    list_copy = pltpu.make_async_copy(listed, list_v, copy_sems.at[2])
    list_copy.start()

    def copy_out(g):
        slot = lax.rem(g, RING)
        return pltpu.make_async_copy(kbuf.at[slot], k_mat.at[g], sems.at[slot])

    base = part * cfg.part_groups

    def distances(e, slot):
        code = listed[0, e + 1]
        i, j = lax.shift_right_logical(code, CODE_BITS), code & (CODE - 1)
        dist[slot] = jnp.dot(lhs[i], rhs[j], preferred_element_type=F32)

    distances(0, 0)

    def step(g, carry):
        slot, target = (base + g, k_mat) if cfg.resident else (lax.rem(g, RING), kbuf)
        if not cfg.resident:

            @pl.when(g >= RING)
            def _():
                copy_out(g - RING).wait()

        for u in range(GROUP):
            distances(g * GROUP + u + 1, (u + 1) % 2)
            j = listed[0, g * GROUP + u + 1] & (CODE - 1)
            m = mlist[g * GROUP + u].astype(F32)
            sums = jnp.zeros((8, block_len), F32)
            for s in range(block_len // STRIP):
                rows = slice(s * STRIP, (s + 1) * STRIP)
                d = jnp.maximum(dist[u % 2, rows, :], TINY)
                sc = d * lax.rsqrt(d)
                rem = jnp.maximum(1.0 - sc, 0.0)
                sq = rem * rem
                val = (sq * sq) * (sc * (4.0 * m) + m)
                target[slot, u, rows, :] = val.astype(BF16)
                for h in range(0, STRIP, 8):
                    sums = sums + val[h:h + 8]
            acc[j] += sums
        if not cfg.resident:
            copy_out(g).start()
        return carry

    lax.fori_loop(0, total, step, 0)
    if cfg.parts == 1 or not last:
        deg_ref[...] = jnp.sum(acc[...], axis=1)
    else:
        second = jnp.sum(acc[...], axis=1)
        for z in range(held):
            rows = slice(z * own_rows, (z + 1) * own_rows)
            for p, deg in enumerate((first_deg[rows, :], second[rows])):
                at = row_of(cfg, place, p, z) * own_rows
                for k in range(own_rows):
                    deg_ref[pl.ds(at + k, 1), :] = deg[k:k + 1]

    def drain(g, carry):
        copy_out(g).wait()
        return carry

    if not cfg.resident:
        lax.fori_loop(jnp.maximum(total - RING, 0), total, drain, 0)
    list_copy.wait()


def pieces_of(own, got):
    return own.at[0], got.at[0], own.at[1], got.at[1]


def walk(cfg, part, listed, k_mat, kbuf, sems, product, total_ref, by_row):
    total = listed[0, 0]
    base = part * cfg.part_groups

    def copy_in(g):
        slot = lax.rem(g, RING)
        return pltpu.make_async_copy(k_mat.at[g], kbuf.at[slot], sems.at[slot])

    if not cfg.resident:
        for p in range(RING - 1):

            @pl.when(p < total)
            def _(p=p):
                copy_in(p).start()

    def step(g, carry):
        slot, source = (base + g, k_mat) if cfg.resident else (lax.rem(g, RING), kbuf)
        if not cfg.resident:

            @pl.when(g + (RING - 1) < total)
            def _():
                copy_in(g + (RING - 1)).start()

            copy_in(g).wait()
        codes = [listed[0, g * GROUP + u + 1] for u in range(GROUP)]
        pairs = [(lax.shift_right_logical(code, CODE_BITS), code & (CODE - 1)) for code in codes]
        terms = [product(i, j, source[slot, u]) for u, (i, j) in enumerate(pairs)]
        add(carry)
        return [i if by_row else j for i, j in pairs], terms

    def add(carry):
        for at, term in zip(*carry):
            total_ref[at] += term

    none = [jnp.int32(0)] * GROUP, [jnp.zeros(total_ref.shape[1:], F32)] * GROUP
    add(lax.fori_loop(0, total, step, none))


def first_kernel(cfg, k_mat, *refs):
    n = cfg.parts
    lists, pieces, inv_ref, refs = refs[:n], refs[n:2 * n], refs[2 * n], refs[2 * n + 1:]
    near, near_y, cross, own_inv, z_acc, w_all, listed, list_sems, *ring = refs
    kbuf, sems = ring or (None, None)
    place = position()
    col = place[1]
    copies = [
        pltpu.make_async_copy(lists[p], listed.at[p], list_sems.at[p]) for p in range(n)
    ]
    for copy in copies:
        copy.start()
    own_rows, block_len = cfg.own_rows, cfg.block_len
    z_acc[...] = jnp.zeros_like(z_acc)
    for part, piece in enumerate(pieces):
        held = piece.shape[0]

        def prepare(m, carry, part=part, piece=piece):
            z = slot_of(cfg, place, m)
            for k in range(own_rows):
                w = piece[m, :, k * block_len:(k + 1) * block_len]
                at = row_of(cfg, place, part, z) * own_rows + k
                w_all[z * own_rows + k] = (w * inv_ref[pl.ds(at, 1), :]).astype(BF16)
            return carry

        lax.fori_loop(0, held, prepare, 0, unroll=held <= 4)

        def product(i, j, block):
            return lax.dot_general(
                w_all[j], block, (((1,), (1,)), ((), ())), preferred_element_type=F32
            )

        copies[part].wait()
        walk(cfg, part, listed.at[part], k_mat, kbuf, sems, product, z_acc, True)
    for k in range(own_rows):
        cols = slice(k * block_len, (k + 1) * block_len)
        mine = inv_ref[pl.ds(place[0] * own_rows + k, 1), :]
        own_inv[:, cols] = jnp.broadcast_to(mine, (8, block_len))
        for e, ref in enumerate((near, cross.at[0], near_y, cross.at[1])):
            ref[:, cols] = z_acc[(col ^ e) * own_rows + k]


def second_kernel(cfg, part, k_mat, list_v, t_ref, s1_own, s1_got, out, z_acc, w_all, listed, list_sem, *ring):
    kbuf, sems = ring or (None, None)
    place = position()
    own_rows, block_len = cfg.own_rows, cfg.block_len
    outputs = t_ref.shape[0]
    list_copy = pltpu.make_async_copy(list_v, listed, list_sem)
    list_copy.start()
    for e, packed in enumerate(pieces_of(s1_own, s1_got)):
        share = place[1] ^ e
        for k in range(own_rows):
            cols = slice(k * block_len, (k + 1) * block_len)
            i = share * own_rows + k
            t = t_ref[:, pl.ds(pl.multiple_of(i * block_len, LANES), block_len)]
            g = (packed[:outputs, cols] - SHIFT * t) * packed[outputs:outputs + 1, cols]
            w_all[i] = g.astype(BF16)
    z_acc[...] = jnp.zeros_like(z_acc)

    def product(i, j, block):
        return jnp.dot(w_all[i], block, preferred_element_type=F32)

    list_copy.wait()
    walk(cfg, part, listed, k_mat, kbuf, sems, product, z_acc, False)

    def hand_out(m, carry):
        z = slot_of(cfg, place, m)
        for k in range(own_rows):
            out[m, :, k * block_len:(k + 1) * block_len] = z_acc[z * own_rows + k].astype(out.dtype)
        return carry

    held = out.shape[0]
    lax.fori_loop(0, held, hand_out, 0, unroll=held <= 4)


N_DOTS = 5


def meet_kernel(cfg, z_same, z_other, t_same, inv_ref, s1_own, *refs):
    gs, (own_z, own_dots, *outs) = refs[:4], refs[4:]
    own_rows, block_len = cfg.own_rows, cfg.block_len
    outputs, own_len = own_z.shape
    place = position()
    tz = jnp.zeros((outputs, 1), F32)
    gz = jnp.zeros((outputs, 1), F32)
    for n in range(4):
        z = z_same[n] + z_other[n].astype(F32)
        if n == 0:
            own_z[...] = z
        else:
            outs[n - 1][:, :own_len] = z.astype(BF16)
        gz += jnp.sum(gs[n][...].astype(F32) * z, axis=1, keepdims=True)
        at = row_of(cfg, place, 0, slot_of(cfg, place, n)) * own_rows
        for k in range(own_rows):
            cols = slice(k * block_len, (k + 1) * block_len)
            scaled = t_same[n, :, cols] * inv_ref[pl.ds(at + k, 1), :]
            tz += jnp.sum(scaled * z[:, cols], axis=1, keepdims=True)
    t, s1 = t_same[0], s1_own[0, :outputs, :]
    tt = jnp.sum(t * t, axis=1, keepdims=True)
    ts1 = jnp.sum(t * s1, axis=1, keepdims=True)
    s1s1 = jnp.sum(s1 * s1, axis=1, keepdims=True)
    dots = (tt, ts1, s1s1, tz + SHIFT * ts1, gz + SHIFT * (tz + s1s1))
    lane = lax.broadcasted_iota(jnp.int32, (outputs, LANES), 1)
    tile = jnp.zeros(lane.shape, F32)
    for n, v in enumerate(dots):
        for part in range(3):
            head = v.astype(BF16).astype(F32)
            tile = jnp.where(lane == part * N_DOTS + n, head, tile)
            v = v - head
    own_dots[...] = tile.astype(BF16)
    for out in outs:
        out[:, own_len:] = tile.astype(BF16)


def product_kernel(own_z, own_dots, s1_own, *refs):
    got, grown_ref, dot_ref = refs[2::-1], refs[3], refs[4]
    outputs, own_len = grown_ref.shape
    z = own_z[...]
    for ref in got:
        z = z + ref[:, :own_len].astype(F32)
    grown_ref[...] = z * s1_own[0, outputs:outputs + 1, :]
    tiles = [own_dots[...]] + [ref[:, own_len:] for ref in got]
    total = pair_sum([tile.astype(F32) for tile in tiles])
    out = total
    for part in range(1, 3):
        out = out + pltpu.roll(total, LANES - part * N_DOTS, 1)
    dot_ref[...] = out


def final_kernel(t_ref, s1_own, s1_got, *refs):
    grown, all_dots = pieces_of(refs[0], refs[1]), refs[2:4]
    sol_hbm, res_hbm, sol_ref, res_ref, sems = refs[4:]
    s1s = pieces_of(s1_own, s1_got)
    outputs, own_len = grown[0].shape
    place = position()
    dots = pair_sum([ref[...] for ref in all_dots])
    tt, ts1, s1s1, ts2, s1s2 = (dots[:, n:n + 1] for n in range(5))
    a1 = tt / (REG * tt + ts1)
    p = 1.0 - REG * a1
    new = p * p * tt - 2.0 * p * a1 * ts1 + a1 * a1 * s1s1
    u = p + new / tt
    dd = u * u * tt - 2.0 * u * a1 * ts1 + a1 * a1 * s1s1
    dmd = u * u * ts1 - u * a1 * (s1s1 + ts2) + a1 * a1 * s1s2
    a2 = new / (REG * dd + dmd)
    sol_t, sol_1 = a1 + a2 * u, a2 * a1
    res_t, res_1 = p - a2 * REG * u, a1 + a2 * (u - REG * a1)
    copies = []
    for e in range(4):
        at = pl.ds(pl.multiple_of((place[1] ^ e) * own_len, LANES), own_len)
        t, s1 = t_ref[:, at], s1s[e][:outputs, :]
        s2 = grown[e][...] + SHIFT * s1
        sol_ref[e] = sol_t * t - sol_1 * s1
        res_ref[e] = res_t * t - res_1 * s1 + sol_1 * s2
        for n, (ref, hbm) in enumerate(((sol_ref, sol_hbm), (res_ref, res_hbm))):
            copy = pltpu.make_async_copy(ref.at[e], hbm.at[:, at], sems.at[n, e])
            copy.start()
            copies.append(copy)
    for copy in copies:
        copy.wait()


def swap(x, axis, d):
    size = lax.axis_size(axis)
    return lax.ppermute(x, axis, [(i, i ^ d) for i in range(size)])


def both_swap(x, row_d, col_d):
    n_rows, n_cols = lax.axis_size("rows"), lax.axis_size("cols")
    pairs = [
        (r * n_cols + c, (r ^ row_d) * n_cols + (c ^ col_d))
        for r in range(n_rows)
        for c in range(n_cols)
    ]
    return lax.ppermute(x, ("rows", "cols"), pairs)


def along_z(x):
    return [x] + [swap(x, "rows", d) for d in range(2, lax.axis_size("rows"), 2)]


def across_x(same):
    return [same, swap(same, "rows", 1)]


def direct_cols(x):
    return [x] + [swap(x, "cols", e) for e in range(1, 4)]


def local(block_list, points, targets):
    n_rows = lax.axis_size("rows")
    n_cols = lax.axis_size("cols")
    row = lax.axis_index("rows")
    col = lax.axis_index("cols")
    block_rows, slots = block_list.shape
    dim, npoints = points.shape
    outputs = targets.shape[0]
    block_len = npoints // block_rows
    own_rows = block_rows // n_cols
    own_len = own_rows * block_len
    nb = block_rows * n_rows
    n_sub = own_rows * n_rows
    capacity = -(-block_rows * slots // n_rows)
    direct_rows = n_rows <= DIRECT_ROWS
    parts = 2 if direct_rows else 1
    n_part = n_sub // parts
    bound = min(block_rows * n_part, n_cols * capacity * (n_rows + 1))
    n_groups = -(-bound // GROUP)
    list_len = -(-(n_groups * GROUP + GROUP + 1) // LANES) * LANES
    resident = parts * 2 * n_groups * GROUP * block_len * block_len <= RESIDENT_BYTES
    k_shape = (parts * n_groups, GROUP, block_len, block_len)
    limit = pltpu.CompilerParams(vmem_limit_bytes=(8 if resident else 32) * 1024 * 1024)
    ring = [] if resident else [
        pltpu.VMEM((RING, GROUP, block_len, block_len), BF16),
        pltpu.SemaphoreType.DMA((RING,)),
    ]
    k_spec = VMEM if resident else HBM
    cfg = Sizes(
        parts, n_groups, resident, nb, block_len, own_rows, block_rows, -(-own_rows * nb // LANES)
    )

    def shape(*dims, dtype=F32):
        return jax.ShapeDtypeStruct(dims, dtype)

    def own(x):
        return lax.dynamic_slice_in_dim(x, col * own_len, own_len, 1)

    def total_rows(x):
        if direct_rows:
            near = pair_sum([x] + [swap(x, "rows", d) for d in range(1, 4)])
            return near + swap(near, "rows", 4)
        return lax.psum(x, "rows")

    lists = direct_cols(block_list)
    names = jnp.arange(nb, dtype=jnp.int32)
    direct = sum(jnp.sum((x[:, :, None] == names).astype(jnp.int32), axis=1) for x in lists)
    own_counts = lax.dynamic_slice_in_dim(direct, col * own_rows, own_rows, 0)
    coded = own_counts.reshape(-1)
    coded = jnp.pad(coded, (0, dim * LANES - coded.shape[0])).reshape(dim, LANES).astype(BF16)
    packed = jnp.concatenate([own(points), coded], axis=1)
    own_t = own(targets)

    def build(part, *operands):
        first, last = part == 0, part == parts - 1
        out = [
            pltpu.VMEM(k_shape, BF16) if resident else shape(*k_shape, dtype=BF16),
            shape(1, list_len, dtype=jnp.int32),
            shape(n_sub if last else n_part, block_len),
        ]
        out += [shape(block_rows, block_len, 2 * dim, dtype=BF16)] if first else []
        k_mat, *rest = pl.pallas_call(
            functools.partial(build_kernel, cfg, part),
            out_shape=out,
            in_specs=[VMEM] + ([HBM, VMEM] if first else [VMEM] * 3 + [k_spec]),
            out_specs=[k_spec] + [VMEM] * (len(out) - 1),
            scratch_shapes=([
                pltpu.VMEM((dim, npoints), BF16),
                pltpu.SemaphoreType.DMA,
            ] if first else []) + [
                pltpu.SMEM((1, list_len), jnp.int32),
                pltpu.SMEM((list_len,), jnp.int32),
                pltpu.VMEM((n_part, 8, block_len), F32),
                pltpu.VMEM((n_part, 2 * dim, block_len), BF16),
                pltpu.VMEM((2, block_len, block_len), F32),
                pltpu.SMEM((block_rows, nb), jnp.int32),
                pltpu.VMEM((n_part // own_rows, cfg.count_rows, LANES), jnp.int32),
                pltpu.SMEM((n_part // own_rows, cfg.count_rows, LANES), jnp.int32),
                pltpu.SemaphoreType.DMA((3,)),
                *ring,
            ],
            compiler_params=limit,
            input_output_aliases={} if first else {4: 0},
            cost_estimate=pl.CostEstimate(
                flops=10 * 2 * 2 * dim * bound * block_len * block_len,
                bytes_accessed=10 * 2 * bound * block_len * block_len,
                transcendentals=10 * bound * block_len * block_len,
            ),
            name="build",
        )(direct, *operands)
        if resident:
            k_mat = pltpu.with_memory_space_constraint(k_mat, pltpu.VMEM)
        return k_mat, *rest

    near = pltpu.with_memory_space_constraint(points, pltpu.HBM)
    if direct_rows:
        packed, early_t = lax.optimization_barrier((packed, own_t))
        same, other = across_x(jnp.stack(along_z(packed)))
        t_same = along_z(early_t)
        k_mat, list0, degree, lhs = build(0, near, same)
        degree, other, *t_same = lax.optimization_barrier((degree, other, *t_same))
        t_same, t_other = across_x(jnp.stack(t_same))
        other, t_same = lax.optimization_barrier((other, t_same))
        k_mat, list1, degree = build(1, lhs, degree, other, k_mat)
        t_pieces, k_lists = [t_same, t_other], [list0, list1]
    else:
        k_mat, list0, degree, _ = build(0, near, lax.all_gather(packed, "rows"))
        t_pieces, k_lists = [lax.all_gather(own_t, "rows")], [list0]
    inv = 1.0 / jnp.sqrt(1.0 + total_rows(degree))

    def cost(n):
        return pl.CostEstimate(
            flops=2 * n * bound * outputs * block_len * block_len,
            bytes_accessed=n * bound * block_len * block_len,
            transcendentals=0,
        )

    near_z, near_y, cross_z, tail = pl.pallas_call(
        functools.partial(first_kernel, cfg),
        out_shape=[shape(outputs, own_len)] * 2 + [shape(2, outputs, own_len), shape(8, own_len)],
        in_specs=[k_spec] + [VMEM] * (2 * parts + 1),
        out_specs=[VMEM] * 4,
        scratch_shapes=[
            pltpu.VMEM((block_rows, outputs, block_len), F32),
            pltpu.VMEM((n_part, outputs, block_len), BF16),
            pltpu.SMEM((parts, 1, list_len), jnp.int32),
            pltpu.SemaphoreType.DMA((parts,)),
            *ring,
        ],
        compiler_params=limit,
        cost_estimate=cost(parts),
        name="first",
    )(k_mat, *k_lists, *t_pieces, inv)

    got = swap(cross_z, "cols", 1)
    half = jnp.concatenate([near_z + got[0], near_y + got[1], tail], axis=0)
    far = swap(half, "cols", 2)
    lo, hi, end = slice(0, outputs), slice(outputs, 2 * outputs), slice(2 * outputs, None)
    s1_own = jnp.stack([
        jnp.concatenate([(half[lo] + far[hi]) * tail[:1], tail], axis=0),
        jnp.concatenate([(half[hi] + far[lo]) * far[end][:1], far[end]], axis=0),
    ])
    s1_got = swap(s1_own, "cols", 1)
    held_t = pltpu.with_memory_space_constraint(targets, pltpu.VMEM)

    def second(part, dtype):
        return pl.pallas_call(
            functools.partial(second_kernel, cfg, part),
            out_shape=shape(n_part // own_rows, outputs, own_len, dtype=dtype),
            in_specs=[k_spec] + [VMEM] * 4,
            out_specs=VMEM,
            scratch_shapes=[
                pltpu.VMEM((n_part, outputs, block_len), F32),
                pltpu.VMEM((block_rows, outputs, block_len), BF16),
                pltpu.SMEM((1, list_len), jnp.int32),
                pltpu.SemaphoreType.DMA,
                *ring,
            ],
            compiler_params=limit,
            cost_estimate=cost(1),
            name="second",
        )(k_mat, k_lists[part], held_t, s1_own, s1_got)

    if direct_rows:
        g = ((s1_own[0, :outputs] - SHIFT * own_t) * tail[:1]).astype(BF16)
        z2_other, g = lax.optimization_barrier((second(1, BF16), g))
        z2_other = swap(z2_other, "rows", 1)
        gs = along_z(g)
        z2_same = second(0, F32)
        z2_same, z2_other, *gs = lax.optimization_barrier((z2_same, z2_other, *gs))
        row_piece = shape(outputs, own_len + LANES, dtype=BF16)
        own_z, own_dots, *sends = pl.pallas_call(
            functools.partial(meet_kernel, cfg),
            out_shape=[shape(outputs, own_len), shape(outputs, LANES, dtype=BF16)] + [row_piece] * 3,
            in_specs=[VMEM] * 9,
            out_specs=[VMEM] * 5,
            compiler_params=limit,
            name="meet",
        )(z2_same, z2_other, t_pieces[0], inv, s1_own, *gs)
        got = [swap(sends[n], "rows", 2 * n + 2) for n in (2, 1, 0)]
        grown, dots = pl.pallas_call(
            product_kernel,
            out_shape=(shape(outputs, own_len), shape(outputs, LANES)),
            in_specs=[VMEM] * 6,
            out_specs=(VMEM, VMEM),
            compiler_params=limit,
            name="products",
        )(own_z, own_dots, s1_own, *got)
        far = both_swap(dots, 1, 2)
        dots = pair_sum([dots, swap(dots, "rows", 1), swap(dots, "cols", 2), far])
    else:
        z2 = lax.psum_scatter(second(0, F32), "rows", scatter_dimension=0)
        grown = z2 * tail[:1]
        own_s1 = s1_own[0, :outputs]
        own_t, s2 = own(targets), grown + SHIFT * own_s1
        dots = [(own_t, own_t), (own_t, own_s1), (own_s1, own_s1), (own_t, s2), (own_s1, s2)]
        dots = jnp.stack([jnp.sum(x * y, axis=1) for x, y in dots], axis=1)
        dots = lax.psum(jnp.pad(dots, ((0, 0), (0, LANES - N_DOTS))), "rows")
        dots = dots + swap(dots, "cols", 2)
    grown = jnp.stack([grown, swap(grown, "cols", 2)])
    grown, dots = lax.optimization_barrier((grown, dots))
    ends = (s1_own, s1_got, grown, swap(grown, "cols", 1), dots, swap(dots, "cols", 1))
    ends = [pltpu.with_memory_space_constraint(x, pltpu.VMEM) for x in ends]

    return pl.pallas_call(
        final_kernel,
        out_shape=(shape(outputs, npoints), shape(outputs, npoints)),
        in_specs=[VMEM] * 7,
        out_specs=(HBM, HBM),
        scratch_shapes=[
            pltpu.VMEM((4, outputs, own_len), F32),
            pltpu.VMEM((4, outputs, own_len), F32),
            pltpu.SemaphoreType.DMA((2, 4)),
        ],
        compiler_params=limit,
        name="final",
    )(held_t, *ends)


def solution(mesh):
    placed = (P("rows", "cols"), P(None, "rows"), P(None, "rows"))
    return jax.shard_map(
        local,
        mesh=mesh,
        in_specs=placed,
        out_specs=(P(None, "rows"), P(None, "rows")),
        check_vma=False,
    )
```

```python
import functools
from typing import NamedTuple

import jax
import jax.numpy as jnp
from jax import lax
from jax.experimental import pallas as pl
from jax.experimental.pallas import tpu as pltpu
from jax.sharding import PartitionSpec as P

REG = 1.5
RADIUS = 0.25
GROUP_BITS = 2
GROUP = 1 << GROUP_BITS
CODE_BITS = 12
CODE = 1 << CODE_BITS
RING = 3
STRIP = 32
LANES = 128
TINY = 1e-30
SHIFT = 0.375
DIRECT_ROWS = 8
RESIDENT_BYTES = 20 * 1024 * 1024

VMEM = pl.BlockSpec(memory_space=pltpu.VMEM)
HBM = pl.BlockSpec(memory_space=pltpu.HBM)
F32 = jnp.float32
BF16 = jnp.bfloat16


def pair_sum(parts):
    while len(parts) > 1:
        parts = [a + b for a, b in zip(parts[::2], parts[1::2])]
    return parts[0]


def position():
    return lax.axis_index("rows"), lax.axis_index("cols")


class Sizes(NamedTuple):
    parts: int
    part_groups: int
    resident: bool
    nb: int
    block_len: int
    own_rows: int
    block_rows: int
    count_rows: int


def augment(x, first_ones):
    dim, n = x.shape
    norm = jnp.sum(x * x, axis=0, keepdims=True) / (RADIUS * RADIUS)
    high = norm.astype(BF16).astype(F32)
    rest = norm - high
    mid = rest.astype(BF16).astype(F32)
    low = rest - mid
    line = lax.broadcasted_iota(jnp.int32, (dim, n), 0)
    base = 3 if first_ones else 0
    ones_at = 0 if first_ones else 3
    tail = jnp.where((line >= ones_at) & (line < ones_at + 3), 1.0, 0.0)
    tail = jnp.where(line == base, high, tail)
    tail = jnp.where(line == base + 1, mid, tail)
    tail = jnp.where(line == base + 2, low, tail)
    return tail


def row_of(cfg, place, part, z):
    if cfg.parts == 1:
        return z
    return 2 * z + (place[0] & 1 if part == 0 else 1 - (place[0] & 1))


def slot_of(cfg, place, n):
    return n if cfg.parts == 1 else lax.shift_right_logical(place[0], 1) ^ n


def build_kernel(cfg, part, direct_v, *refs):
    last = part == cfg.parts - 1
    place = position()
    if part == 0:
        near_hbm, piece, refs = refs[0], refs[1], refs[2:]
        k_mat, list_v, deg_ref, lhs = refs[:4]
        near_ref, near_sem, refs = refs[4], refs[5], refs[6:]
        near_copy = pltpu.make_async_copy(near_hbm, near_ref, near_sem)
        near_copy.start()
    else:
        lhs, first_deg, piece, _ = refs[:4]
        k_mat, list_v, deg_ref = refs[4:7]
        refs = refs[7:]
    listed, mlist, acc, rhs, dist, direct, counts_v, counts, copy_sems = refs[:9]
    kbuf, sems = (None, None) if cfg.resident else refs[9:]
    direct_copy = pltpu.make_async_copy(direct_v, direct, copy_sems.at[0])
    direct_copy.start()
    row, col = place[0], place[1]
    own_rows, block_len, nb = cfg.own_rows, cfg.block_len, cfg.nb
    own_len = own_rows * block_len
    dim, held = piece.shape[1], piece.shape[0]
    scale = 1.0 / (RADIUS * RADIUS)

    def count(n, carry):
        named = piece[n, :, own_len:own_len + LANES]
        counts_v[slot_of(cfg, place, n)] = named.astype(F32)[:cfg.count_rows].astype(jnp.int32)
        return carry

    def prepare(n, carry):
        z = slot_of(cfg, place, n)
        for k in range(own_rows):
            far = piece[n, :, k * block_len:(k + 1) * block_len]
            rhs[z * own_rows + k, :dim, :] = far
            rhs[z * own_rows + k, dim:, :] = augment(far.astype(F32), False).astype(BF16)
        return carry

    lax.fori_loop(0, held, count, 0, unroll=held <= 4)
    fetch = pltpu.make_async_copy(counts_v, counts, copy_sems.at[1])
    fetch.start()
    lax.fori_loop(0, held, prepare, 0, unroll=held <= 4)
    acc[...] = jnp.zeros_like(acc)
    if part == 0:
        near_copy.wait()
        for i in range(cfg.block_rows):
            near = near_ref[:, i * block_len:(i + 1) * block_len].astype(F32)
            full = jnp.concatenate([near * (-2.0 * scale), augment(near, True)], axis=0)
            lhs[i] = full.T.astype(BF16)
    direct_copy.wait()
    fetch.wait()

    pos = jnp.int32(0)
    for i in range(cfg.block_rows):
        me = row * cfg.block_rows + i
        spots = [k * nb + me for k in range(own_rows)]
        spots = [(lax.shift_right_logical(p, 7), p & (LANES - 1)) for p in spots]

        def note(z, at, i=i, me=me, spots=spots):
            for k in range(own_rows):
                name = row_of(cfg, place, part, z) * cfg.block_rows + col * own_rows + k
                m = direct[i, name] + jnp.where(name == me, 0, counts[z, spots[k][0], spots[k][1]])
                listed[0, at + 1] = i * CODE + z * own_rows + k
                mlist[at] = m
                at = at + jnp.where(m > 0, 1, 0)
            return at

        if held <= 4:
            for z in range(held):
                pos = note(z, pos)
        else:
            pos = lax.fori_loop(0, held, note, pos, unroll=4)
    for u in range(GROUP):
        listed[0, pos + u + 1] = 0
        mlist[pos + u] = 0
    total = lax.shift_right_logical(pos + (GROUP - 1), GROUP_BITS)
    listed[0, 0] = total
    list_copy = pltpu.make_async_copy(listed, list_v, copy_sems.at[2])
    list_copy.start()

    def copy_out(g):
        slot = lax.rem(g, RING)
        return pltpu.make_async_copy(kbuf.at[slot], k_mat.at[g], sems.at[slot])

    base = part * cfg.part_groups

    def distances(e, slot):
        code = listed[0, e + 1]
        i, j = lax.shift_right_logical(code, CODE_BITS), code & (CODE - 1)
        dist[slot] = jnp.dot(lhs[i], rhs[j], preferred_element_type=F32)

    distances(0, 0)
    ones = jnp.ones((8, block_len), BF16)

    def step(g, carry):
        slot, target = (base + g, k_mat) if cfg.resident else (lax.rem(g, RING), kbuf)
        if not cfg.resident:

            @pl.when(g >= RING)
            def _():
                copy_out(g - RING).wait()

        for u in range(GROUP):
            distances(g * GROUP + u + 1, (u + 1) % 2)
            j = listed[0, g * GROUP + u + 1] & (CODE - 1)
            m = mlist[g * GROUP + u].astype(F32)
            strips = []
            for s in range(block_len // STRIP):
                rows = slice(s * STRIP, (s + 1) * STRIP)
                d = jnp.maximum(dist[u % 2, rows, :], TINY)
                sc = d * lax.rsqrt(d)
                rem = jnp.maximum(1.0 - sc, 0.0)
                sq = rem * rem
                val = (sq * sq) * (sc * (4.0 * m) + m)
                strips.append(val.astype(BF16))
                target[slot, u, rows, :] = strips[-1]
            block = jnp.concatenate(strips, axis=0)
            acc[j] += jnp.dot(ones, block, preferred_element_type=F32)
        if not cfg.resident:
            copy_out(g).start()
        return carry

    lax.fori_loop(0, total, step, 0)
    if cfg.parts == 1 or not last:
        deg_ref[...] = acc[:, 0, :]
    else:
        second = acc[:, 0, :]
        for z in range(held):
            rows = slice(z * own_rows, (z + 1) * own_rows)
            for p, deg in enumerate((first_deg[rows, :], second[rows])):
                at = row_of(cfg, place, p, z) * own_rows
                for k in range(own_rows):
                    deg_ref[pl.ds(at + k, 1), :] = deg[k:k + 1]

    def drain(g, carry):
        copy_out(g).wait()
        return carry

    if not cfg.resident:
        lax.fori_loop(jnp.maximum(total - RING, 0), total, drain, 0)
    list_copy.wait()


def pieces_of(own, got):
    return own.at[0], got.at[0], own.at[1], got.at[1]


def walk(cfg, part, listed, k_mat, kbuf, sems, product, total_ref, by_row):
    total = listed[0, 0]
    base = part * cfg.part_groups

    def copy_in(g):
        slot = lax.rem(g, RING)
        return pltpu.make_async_copy(k_mat.at[g], kbuf.at[slot], sems.at[slot])

    if not cfg.resident:
        for p in range(RING - 1):

            @pl.when(p < total)
            def _(p=p):
                copy_in(p).start()

    def step(g, carry):
        slot, source = (base + g, k_mat) if cfg.resident else (lax.rem(g, RING), kbuf)
        if not cfg.resident:

            @pl.when(g + (RING - 1) < total)
            def _():
                copy_in(g + (RING - 1)).start()

            copy_in(g).wait()
        codes = [listed[0, g * GROUP + u + 1] for u in range(GROUP)]
        pairs = [(lax.shift_right_logical(code, CODE_BITS), code & (CODE - 1)) for code in codes]
        terms = [product(i, j, source[slot, u]) for u, (i, j) in enumerate(pairs)]
        add(carry)
        return [i if by_row else j for i, j in pairs], terms

    def add(carry):
        for at, term in zip(*carry):
            total_ref[at] += term

    none = [jnp.int32(0)] * GROUP, [jnp.zeros(total_ref.shape[1:], F32)] * GROUP
    add(lax.fori_loop(0, total, step, none))


def first_kernel(cfg, k_mat, *refs):
    n = cfg.parts
    lists, pieces, inv_ref, refs = refs[:n], refs[n:2 * n], refs[2 * n], refs[2 * n + 1:]
    near, near_y, cross, own_inv, z_acc, w_all, listed, list_sems, *ring = refs
    kbuf, sems = ring or (None, None)
    place = position()
    col = place[1]
    copies = [
        pltpu.make_async_copy(lists[p], listed.at[p], list_sems.at[p]) for p in range(n)
    ]
    for copy in copies:
        copy.start()
    own_rows, block_len = cfg.own_rows, cfg.block_len
    z_acc[...] = jnp.zeros_like(z_acc)
    for part, piece in enumerate(pieces):
        held = piece.shape[0]

        def prepare(m, carry, part=part, piece=piece):
            z = slot_of(cfg, place, m)
            for k in range(own_rows):
                w = piece[m, :, k * block_len:(k + 1) * block_len]
                at = row_of(cfg, place, part, z) * own_rows + k
                w_all[z * own_rows + k] = (w * inv_ref[pl.ds(at, 1), :]).astype(BF16)
            return carry

        lax.fori_loop(0, held, prepare, 0, unroll=held <= 4)

        def product(i, j, block):
            return lax.dot_general(
                w_all[j], block, (((1,), (1,)), ((), ())), preferred_element_type=F32
            )

        copies[part].wait()
        walk(cfg, part, listed.at[part], k_mat, kbuf, sems, product, z_acc, True)
    for k in range(own_rows):
        cols = slice(k * block_len, (k + 1) * block_len)
        mine = inv_ref[pl.ds(place[0] * own_rows + k, 1), :]
        own_inv[:, cols] = jnp.broadcast_to(mine, (8, block_len))
        for e, ref in enumerate((near, cross.at[0], near_y, cross.at[1])):
            ref[:, cols] = z_acc[(col ^ e) * own_rows + k]


def second_kernel(cfg, part, k_mat, list_v, t_ref, s1_own, s1_got, out, z_acc, w_all, listed, list_sem, *ring):
    kbuf, sems = ring or (None, None)
    place = position()
    own_rows, block_len = cfg.own_rows, cfg.block_len
    outputs = t_ref.shape[0]
    list_copy = pltpu.make_async_copy(list_v, listed, list_sem)
    list_copy.start()
    for e, packed in enumerate(pieces_of(s1_own, s1_got)):
        share = place[1] ^ e
        for k in range(own_rows):
            cols = slice(k * block_len, (k + 1) * block_len)
            i = share * own_rows + k
            t = t_ref[:, pl.ds(pl.multiple_of(i * block_len, LANES), block_len)]
            g = (packed[:outputs, cols] - SHIFT * t) * packed[outputs:outputs + 1, cols]
            w_all[i] = g.astype(BF16)
    z_acc[...] = jnp.zeros_like(z_acc)

    def product(i, j, block):
        return jnp.dot(w_all[i], block, preferred_element_type=F32)

    list_copy.wait()
    walk(cfg, part, listed, k_mat, kbuf, sems, product, z_acc, False)

    def hand_out(m, carry):
        z = slot_of(cfg, place, m)
        for k in range(own_rows):
            out[m, :, k * block_len:(k + 1) * block_len] = z_acc[z * own_rows + k].astype(out.dtype)
        return carry

    held = out.shape[0]
    lax.fori_loop(0, held, hand_out, 0, unroll=held <= 4)


N_DOTS = 5


def meet_kernel(cfg, z_same, z_other, t_same, inv_ref, s1_own, *refs):
    gs, (own_z, own_dots, *outs) = refs[:4], refs[4:]
    own_rows, block_len = cfg.own_rows, cfg.block_len
    outputs, own_len = own_z.shape
    place = position()
    tz = jnp.zeros((outputs, 1), F32)
    gz = jnp.zeros((outputs, 1), F32)
    for n in range(4):
        z = z_same[n] + z_other[n].astype(F32)
        if n == 0:
            own_z[...] = z
        else:
            outs[n - 1][:, :own_len] = z.astype(BF16)
        gz += jnp.sum(gs[n][...].astype(F32) * z, axis=1, keepdims=True)
        at = row_of(cfg, place, 0, slot_of(cfg, place, n)) * own_rows
        for k in range(own_rows):
            cols = slice(k * block_len, (k + 1) * block_len)
            scaled = t_same[n, :, cols] * inv_ref[pl.ds(at + k, 1), :]
            tz += jnp.sum(scaled * z[:, cols], axis=1, keepdims=True)
    t, s1 = t_same[0], s1_own[0, :outputs, :]
    tt = jnp.sum(t * t, axis=1, keepdims=True)
    ts1 = jnp.sum(t * s1, axis=1, keepdims=True)
    s1s1 = jnp.sum(s1 * s1, axis=1, keepdims=True)
    dots = (tt, ts1, s1s1, tz + SHIFT * ts1, gz + SHIFT * (tz + s1s1))
    lane = lax.broadcasted_iota(jnp.int32, (outputs, LANES), 1)
    tile = jnp.zeros(lane.shape, F32)
    for n, v in enumerate(dots):
        for part in range(3):
            head = v.astype(BF16).astype(F32)
            tile = jnp.where(lane == part * N_DOTS + n, head, tile)
            v = v - head
    own_dots[...] = tile.astype(BF16)
    for out in outs:
        out[:, own_len:] = tile.astype(BF16)


def product_kernel(own_z, own_dots, s1_own, *refs):
    got, end_ref, dot_ref = refs[2::-1], refs[3], refs[4]
    outputs, own_len = own_z.shape
    z = own_z[...]
    for ref in got:
        z = z + ref[:, :own_len].astype(F32)
    end_ref[:, :own_len] = z * s1_own[0, outputs:outputs + 1, :]
    tiles = [own_dots[...]] + [ref[:, own_len:] for ref in got]
    total = pair_sum([tile.astype(F32) for tile in tiles])
    out = total
    for part in range(1, 3):
        out = out + pltpu.roll(total, LANES - part * N_DOTS, 1)
    dot_ref[...] = out
    end_ref[:, own_len:] = out


def final_kernel(t_ref, s1_own, s1_got, *refs):
    ends = pieces_of(refs[0], refs[1])
    sol_hbm, res_hbm, sol_ref, res_ref, sems = refs[2:]
    s1s = pieces_of(s1_own, s1_got)
    outputs, own_len = ends[0].shape[0], ends[0].shape[1] - LANES
    place = position()
    dots = ends[0][:, own_len:] + ends[1][:, own_len:]
    tt, ts1, s1s1, ts2, s1s2 = (dots[:, n:n + 1] for n in range(5))
    a1 = tt / (REG * tt + ts1)
    p = 1.0 - REG * a1
    new = p * p * tt - 2.0 * p * a1 * ts1 + a1 * a1 * s1s1
    u = p + new / tt
    dd = u * u * tt - 2.0 * u * a1 * ts1 + a1 * a1 * s1s1
    dmd = u * u * ts1 - u * a1 * (s1s1 + ts2) + a1 * a1 * s1s2
    a2 = new / (REG * dd + dmd)
    sol_t, sol_1 = a1 + a2 * u, a2 * a1
    res_t, res_1 = p - a2 * REG * u, a1 + a2 * (u - REG * a1)
    copies = []
    for e in range(4):
        at = pl.ds(pl.multiple_of((place[1] ^ e) * own_len, LANES), own_len)
        t, s1 = t_ref[:, at], s1s[e][:outputs, :]
        s2 = ends[e][:, :own_len] + SHIFT * s1
        sol_ref[e] = sol_t * t - sol_1 * s1
        res_ref[e] = res_t * t - res_1 * s1 + sol_1 * s2
        for n, (ref, hbm) in enumerate(((sol_ref, sol_hbm), (res_ref, res_hbm))):
            copy = pltpu.make_async_copy(ref.at[e], hbm.at[:, at], sems.at[n, e])
            copy.start()
            copies.append(copy)
    for copy in copies:
        copy.wait()


def swap(x, axis, d):
    size = lax.axis_size(axis)
    return lax.ppermute(x, axis, [(i, i ^ d) for i in range(size)])


def both_swap(x, row_d, col_d):
    n_rows, n_cols = lax.axis_size("rows"), lax.axis_size("cols")
    pairs = [
        (r * n_cols + c, (r ^ row_d) * n_cols + (c ^ col_d))
        for r in range(n_rows)
        for c in range(n_cols)
    ]
    return lax.ppermute(x, ("rows", "cols"), pairs)


def along_z(x):
    return [x] + [swap(x, "rows", d) for d in range(2, lax.axis_size("rows"), 2)]


def across_x(same):
    return [same, swap(same, "rows", 1)]


def direct_cols(x):
    return [x] + [swap(x, "cols", e) for e in range(1, 4)]


def local(block_list, points, targets):
    n_rows = lax.axis_size("rows")
    n_cols = lax.axis_size("cols")
    row = lax.axis_index("rows")
    col = lax.axis_index("cols")
    block_rows, slots = block_list.shape
    dim, npoints = points.shape
    outputs = targets.shape[0]
    block_len = npoints // block_rows
    own_rows = block_rows // n_cols
    own_len = own_rows * block_len
    nb = block_rows * n_rows
    n_sub = own_rows * n_rows
    capacity = -(-block_rows * slots // n_rows)
    direct_rows = n_rows <= DIRECT_ROWS
    parts = 2 if direct_rows else 1
    n_part = n_sub // parts
    bound = min(block_rows * n_part, n_cols * capacity * (n_rows + 1))
    n_groups = -(-bound // GROUP)
    list_len = -(-(n_groups * GROUP + GROUP + 1) // LANES) * LANES
    resident = parts * 2 * n_groups * GROUP * block_len * block_len <= RESIDENT_BYTES
    k_shape = (parts * n_groups, GROUP, block_len, block_len)
    limit = pltpu.CompilerParams(vmem_limit_bytes=(8 if resident else 32) * 1024 * 1024)
    ring = [] if resident else [
        pltpu.VMEM((RING, GROUP, block_len, block_len), BF16),
        pltpu.SemaphoreType.DMA((RING,)),
    ]
    k_spec = VMEM if resident else HBM
    cfg = Sizes(
        parts, n_groups, resident, nb, block_len, own_rows, block_rows, -(-own_rows * nb // LANES)
    )

    def shape(*dims, dtype=F32):
        return jax.ShapeDtypeStruct(dims, dtype)

    def own(x):
        return lax.dynamic_slice_in_dim(x, col * own_len, own_len, 1)

    def total_rows(x):
        if direct_rows:
            near = pair_sum([x] + [swap(x, "rows", d) for d in range(1, 4)])
            return near + swap(near, "rows", 4)
        return lax.psum(x, "rows")

    lists = direct_cols(block_list)
    names = jnp.arange(nb, dtype=jnp.int32)
    direct = sum(jnp.sum((x[:, :, None] == names).astype(jnp.int32), axis=1) for x in lists)
    own_counts = lax.dynamic_slice_in_dim(direct, col * own_rows, own_rows, 0)
    coded = own_counts.reshape(-1)
    coded = jnp.pad(coded, (0, dim * LANES - coded.shape[0])).reshape(dim, LANES).astype(BF16)
    packed = jnp.concatenate([own(points), coded], axis=1)
    own_t = own(targets)

    def build(part, *operands):
        first, last = part == 0, part == parts - 1
        out = [
            pltpu.VMEM(k_shape, BF16) if resident else shape(*k_shape, dtype=BF16),
            shape(1, list_len, dtype=jnp.int32),
            shape(n_sub if last else n_part, block_len),
        ]
        out += [shape(block_rows, block_len, 2 * dim, dtype=BF16)] if first else []
        k_mat, *rest = pl.pallas_call(
            functools.partial(build_kernel, cfg, part),
            out_shape=out,
            in_specs=[VMEM] + ([HBM, VMEM] if first else [VMEM] * 3 + [k_spec]),
            out_specs=[k_spec] + [VMEM] * (len(out) - 1),
            scratch_shapes=([
                pltpu.VMEM((dim, npoints), BF16),
                pltpu.SemaphoreType.DMA,
            ] if first else []) + [
                pltpu.SMEM((1, list_len), jnp.int32),
                pltpu.SMEM((list_len,), jnp.int32),
                pltpu.VMEM((n_part, 8, block_len), F32),
                pltpu.VMEM((n_part, 2 * dim, block_len), BF16),
                pltpu.VMEM((2, block_len, block_len), F32),
                pltpu.SMEM((block_rows, nb), jnp.int32),
                pltpu.VMEM((n_part // own_rows, cfg.count_rows, LANES), jnp.int32),
                pltpu.SMEM((n_part // own_rows, cfg.count_rows, LANES), jnp.int32),
                pltpu.SemaphoreType.DMA((3,)),
                *ring,
            ],
            compiler_params=limit,
            input_output_aliases={} if first else {4: 0},
            cost_estimate=pl.CostEstimate(
                flops=10 * 2 * 2 * dim * bound * block_len * block_len,
                bytes_accessed=10 * 2 * bound * block_len * block_len,
                transcendentals=10 * bound * block_len * block_len,
            ),
            name="build",
        )(direct, *operands)
        if resident:
            k_mat = pltpu.with_memory_space_constraint(k_mat, pltpu.VMEM)
        return k_mat, *rest

    near = pltpu.with_memory_space_constraint(points, pltpu.HBM)
    if direct_rows:
        packed, early_t = lax.optimization_barrier((packed, own_t))
        same, other = across_x(jnp.stack(along_z(packed)))
        t_same = along_z(early_t)
        k_mat, list0, degree, lhs = build(0, near, same)
        degree, other, *t_same = lax.optimization_barrier((degree, other, *t_same))
        t_same, t_other = across_x(jnp.stack(t_same))
        other, t_same = lax.optimization_barrier((other, t_same))
        k_mat, list1, degree = build(1, lhs, degree, other, k_mat)
        t_pieces, k_lists = [t_same, t_other], [list0, list1]
    else:
        k_mat, list0, degree, _ = build(0, near, lax.all_gather(packed, "rows"))
        t_pieces, k_lists = [lax.all_gather(own_t, "rows")], [list0]
    inv = 1.0 / jnp.sqrt(1.0 + total_rows(degree))

    def cost(n):
        return pl.CostEstimate(
            flops=2 * n * bound * outputs * block_len * block_len,
            bytes_accessed=n * bound * block_len * block_len,
            transcendentals=0,
        )

    near_z, near_y, cross_z, tail = pl.pallas_call(
        functools.partial(first_kernel, cfg),
        out_shape=[shape(outputs, own_len)] * 2 + [shape(2, outputs, own_len), shape(8, own_len)],
        in_specs=[k_spec] + [VMEM] * (2 * parts + 1),
        out_specs=[VMEM] * 4,
        scratch_shapes=[
            pltpu.VMEM((block_rows, outputs, block_len), F32),
            pltpu.VMEM((n_part, outputs, block_len), BF16),
            pltpu.SMEM((parts, 1, list_len), jnp.int32),
            pltpu.SemaphoreType.DMA((parts,)),
            *ring,
        ],
        compiler_params=limit,
        cost_estimate=cost(parts),
        name="first",
    )(k_mat, *k_lists, *t_pieces, inv)

    got = swap(cross_z, "cols", 1)
    half = jnp.concatenate([near_z + got[0], near_y + got[1], tail], axis=0)
    far = swap(half, "cols", 2)
    lo, hi, end = slice(0, outputs), slice(outputs, 2 * outputs), slice(2 * outputs, None)
    s1_own = jnp.stack([
        jnp.concatenate([(half[lo] + far[hi]) * tail[:1], tail], axis=0),
        jnp.concatenate([(half[hi] + far[lo]) * far[end][:1], far[end]], axis=0),
    ])
    s1_got = swap(s1_own, "cols", 1)
    held_t = pltpu.with_memory_space_constraint(targets, pltpu.VMEM)

    def second(part, dtype):
        return pl.pallas_call(
            functools.partial(second_kernel, cfg, part),
            out_shape=shape(n_part // own_rows, outputs, own_len, dtype=dtype),
            in_specs=[k_spec] + [VMEM] * 4,
            out_specs=VMEM,
            scratch_shapes=[
                pltpu.VMEM((n_part, outputs, block_len), F32),
                pltpu.VMEM((block_rows, outputs, block_len), BF16),
                pltpu.SMEM((1, list_len), jnp.int32),
                pltpu.SemaphoreType.DMA,
                *ring,
            ],
            compiler_params=limit,
            cost_estimate=cost(1),
            name="second",
        )(k_mat, k_lists[part], held_t, s1_own, s1_got)

    if direct_rows:
        g = ((s1_own[0, :outputs] - SHIFT * own_t) * tail[:1]).astype(BF16)
        z2_other, g = lax.optimization_barrier((second(1, BF16), g))
        z2_other = swap(z2_other, "rows", 1)
        gs = along_z(g)
        z2_same = second(0, F32)
        z2_same, z2_other, *gs = lax.optimization_barrier((z2_same, z2_other, *gs))
        row_piece = shape(outputs, own_len + LANES, dtype=BF16)
        own_z, own_dots, *sends = pl.pallas_call(
            functools.partial(meet_kernel, cfg),
            out_shape=[shape(outputs, own_len), shape(outputs, LANES, dtype=BF16)] + [row_piece] * 3,
            in_specs=[VMEM] * 9,
            out_specs=[VMEM] * 5,
            compiler_params=limit,
            name="meet",
        )(z2_same, z2_other, t_pieces[0], inv, s1_own, *gs)
        got = [swap(sends[n], "rows", 2 * n + 2) for n in (2, 1, 0)]
        ends, dots = pl.pallas_call(
            product_kernel,
            out_shape=(shape(outputs, own_len + LANES), shape(outputs, LANES)),
            in_specs=[VMEM] * 6,
            out_specs=(VMEM, VMEM),
            compiler_params=limit,
            name="products",
        )(own_z, own_dots, s1_own, *got)
        far = both_swap(dots, 1, 2)
        across = swap(dots, "rows", 1)
        ends_y = swap(ends, "cols", 2)
        dots = (dots + across) + (ends_y[:, own_len:] + far)
    else:
        z2 = lax.psum_scatter(second(0, F32), "rows", scatter_dimension=0)
        grown = z2 * tail[:1]
        own_s1 = s1_own[0, :outputs]
        own_t, s2 = own(targets), grown + SHIFT * own_s1
        dots = [(own_t, own_t), (own_t, own_s1), (own_s1, own_s1), (own_t, s2), (own_s1, s2)]
        dots = jnp.stack([jnp.sum(x * y, axis=1) for x, y in dots], axis=1)
        dots = lax.psum(jnp.pad(dots, ((0, 0), (0, LANES - N_DOTS))), "rows")
        ends = jnp.concatenate([grown, dots], axis=1)
        ends_y = swap(ends, "cols", 2)
        dots = dots + ends_y[:, own_len:]
    ends = jnp.stack([jnp.concatenate([ends[:, :own_len], dots], axis=1), ends_y])
    ends = (s1_own, s1_got, ends, swap(ends, "cols", 1))
    ends = [pltpu.with_memory_space_constraint(x, pltpu.VMEM) for x in ends]

    return pl.pallas_call(
        final_kernel,
        out_shape=(shape(outputs, npoints), shape(outputs, npoints)),
        in_specs=[VMEM] * 5,
        out_specs=(HBM, HBM),
        scratch_shapes=[
            pltpu.VMEM((4, outputs, own_len), F32),
            pltpu.VMEM((4, outputs, own_len), F32),
            pltpu.SemaphoreType.DMA((2, 4)),
        ],
        compiler_params=limit,
        name="final",
    )(held_t, *ends)


def solution(mesh):
    placed = (P("rows", "cols"), P(None, "rows"), P(None, "rows"))
    return jax.shard_map(
        local,
        mesh=mesh,
        in_specs=placed,
        out_specs=(P(None, "rows"), P(None, "rows")),
        check_vma=False,
    )
```

```python
import functools
from typing import NamedTuple

import jax
import jax.numpy as jnp
from jax import lax
from jax.experimental import pallas as pl
from jax.experimental.pallas import tpu as pltpu
from jax.sharding import PartitionSpec as P

REG = 1.5
RADIUS = 0.25
GROUP_BITS = 2
GROUP = 1 << GROUP_BITS
CODE_BITS = 12
CODE = 1 << CODE_BITS
RING = 3
STRIP = 64
LANES = 128
TINY = 1e-30
SHIFT = 0.375
DIRECT_ROWS = 8
RESIDENT_BYTES = 20 * 1024 * 1024

VMEM = pl.BlockSpec(memory_space=pltpu.VMEM)
HBM = pl.BlockSpec(memory_space=pltpu.HBM)
F32 = jnp.float32
BF16 = jnp.bfloat16


def pair_sum(parts):
    while len(parts) > 1:
        parts = [a + b for a, b in zip(parts[::2], parts[1::2])]
    return parts[0]


def position():
    return lax.axis_index("rows"), lax.axis_index("cols")


class Sizes(NamedTuple):
    parts: int
    part_groups: int
    resident: bool
    nb: int
    block_len: int
    own_rows: int
    block_rows: int
    count_rows: int


def augment(x, first_ones):
    dim, n = x.shape
    norm = jnp.sum(x * x, axis=0, keepdims=True) / (RADIUS * RADIUS)
    high = norm.astype(BF16).astype(F32)
    rest = norm - high
    mid = rest.astype(BF16).astype(F32)
    low = rest - mid
    line = lax.broadcasted_iota(jnp.int32, (dim, n), 0)
    base = 3 if first_ones else 0
    ones_at = 0 if first_ones else 3
    tail = jnp.where((line >= ones_at) & (line < ones_at + 3), 1.0, 0.0)
    tail = jnp.where(line == base, high, tail)
    tail = jnp.where(line == base + 1, mid, tail)
    tail = jnp.where(line == base + 2, low, tail)
    return tail


def row_of(cfg, place, part, z):
    if cfg.parts == 1:
        return z
    return 2 * z + (place[0] & 1 if part == 0 else 1 - (place[0] & 1))


def slot_of(cfg, place, n):
    return n if cfg.parts == 1 else lax.shift_right_logical(place[0], 1) ^ n


def build_kernel(cfg, part, direct_v, *refs):
    last = part == cfg.parts - 1
    place = position()
    if part == 0:
        near_hbm, piece, refs = refs[0], refs[1], refs[2:]
        k_mat, list_v, deg_ref, lhs = refs[:4]
        near_ref, near_sem, refs = refs[4], refs[5], refs[6:]
        near_copy = pltpu.make_async_copy(near_hbm, near_ref, near_sem)
        near_copy.start()
    else:
        lhs, first_deg, piece, _ = refs[:4]
        k_mat, list_v, deg_ref = refs[4:7]
        refs = refs[7:]
    listed, mlist, acc, rhs, dist, direct, counts_v, counts, copy_sems = refs[:9]
    kbuf, sems = (None, None) if cfg.resident else refs[9:]
    direct_copy = pltpu.make_async_copy(direct_v, direct, copy_sems.at[0])
    direct_copy.start()
    row, col = place[0], place[1]
    own_rows, block_len, nb = cfg.own_rows, cfg.block_len, cfg.nb
    own_len = own_rows * block_len
    dim, held = piece.shape[1], piece.shape[0]
    scale = 1.0 / (RADIUS * RADIUS)

    def count(n, carry):
        named = piece[n, :, own_len:own_len + LANES]
        counts_v[slot_of(cfg, place, n)] = named.astype(F32)[:cfg.count_rows].astype(jnp.int32)
        return carry

    def prepare(n, carry):
        z = slot_of(cfg, place, n)
        for k in range(own_rows):
            far = piece[n, :, k * block_len:(k + 1) * block_len]
            rhs[z * own_rows + k, :dim, :] = far
            rhs[z * own_rows + k, dim:, :] = augment(far.astype(F32), False).astype(BF16)
        return carry

    lax.fori_loop(0, held, count, 0, unroll=held <= 4)
    fetch = pltpu.make_async_copy(counts_v, counts, copy_sems.at[1])
    fetch.start()
    lax.fori_loop(0, held, prepare, 0, unroll=held <= 4)
    acc[...] = jnp.zeros_like(acc)
    if part == 0:
        near_copy.wait()
        for i in range(cfg.block_rows):
            near = near_ref[:, i * block_len:(i + 1) * block_len].astype(F32)
            full = jnp.concatenate([near * (-2.0 * scale), augment(near, True)], axis=0)
            lhs[i] = full.T.astype(BF16)
    direct_copy.wait()
    fetch.wait()

    pos = jnp.int32(0)
    for i in range(cfg.block_rows):
        me = row * cfg.block_rows + i
        spots = [k * nb + me for k in range(own_rows)]
        spots = [(lax.shift_right_logical(p, 7), p & (LANES - 1)) for p in spots]

        def note(z, at, i=i, me=me, spots=spots):
            for k in range(own_rows):
                name = row_of(cfg, place, part, z) * cfg.block_rows + col * own_rows + k
                m = direct[i, name] + jnp.where(name == me, 0, counts[z, spots[k][0], spots[k][1]])
                listed[0, at + 1] = i * CODE + z * own_rows + k
                mlist[at] = m
                at = at + jnp.where(m > 0, 1, 0)
            return at

        if held <= 4:
            for z in range(held):
                pos = note(z, pos)
        else:
            pos = lax.fori_loop(0, held, note, pos, unroll=4)
    for u in range(GROUP):
        listed[0, pos + u + 1] = 0
        mlist[pos + u] = 0
    total = lax.shift_right_logical(pos + (GROUP - 1), GROUP_BITS)
    listed[0, 0] = total
    list_copy = pltpu.make_async_copy(listed, list_v, copy_sems.at[2])
    list_copy.start()

    def copy_out(g):
        slot = lax.rem(g, RING)
        return pltpu.make_async_copy(kbuf.at[slot], k_mat.at[g], sems.at[slot])

    base = part * cfg.part_groups

    def distances(e, slot):
        code = listed[0, e + 1]
        i, j = lax.shift_right_logical(code, CODE_BITS), code & (CODE - 1)
        dist[slot] = jnp.dot(lhs[i], rhs[j], preferred_element_type=F32)

    distances(0, 0)

    def step(g, carry):
        slot, target = (base + g, k_mat) if cfg.resident else (lax.rem(g, RING), kbuf)
        if not cfg.resident:

            @pl.when(g >= RING)
            def _():
                copy_out(g - RING).wait()

        for u in range(GROUP):
            distances(g * GROUP + u + 1, (u + 1) % 2)
            j = listed[0, g * GROUP + u + 1] & (CODE - 1)
            m = mlist[g * GROUP + u].astype(F32)
            sums = jnp.zeros((8, block_len), F32)
            for s in range(block_len // STRIP):
                rows = slice(s * STRIP, (s + 1) * STRIP)
                d = jnp.maximum(dist[u % 2, rows, :], TINY)
                sc = d * lax.rsqrt(d)
                rem = jnp.maximum(1.0 - sc, 0.0)
                sq = rem * rem
                val = (sq * sq) * (sc * (4.0 * m) + m)
                target[slot, u, rows, :] = val.astype(BF16)
                for h in range(0, STRIP, 8):
                    sums = sums + val[h:h + 8]
            acc[j] += sums
        if not cfg.resident:
            copy_out(g).start()
        return carry

    lax.fori_loop(0, total, step, 0)
    if cfg.parts == 1 or not last:
        deg_ref[...] = jnp.sum(acc[...], axis=1)
    else:
        second = jnp.sum(acc[...], axis=1)
        for z in range(held):
            rows = slice(z * own_rows, (z + 1) * own_rows)
            for p, deg in enumerate((first_deg[rows, :], second[rows])):
                at = row_of(cfg, place, p, z) * own_rows
                for k in range(own_rows):
                    deg_ref[pl.ds(at + k, 1), :] = deg[k:k + 1]

    def drain(g, carry):
        copy_out(g).wait()
        return carry

    if not cfg.resident:
        lax.fori_loop(jnp.maximum(total - RING, 0), total, drain, 0)
    list_copy.wait()


def pieces_of(own, got):
    return own.at[0], got.at[0], own.at[1], got.at[1]


def walk(cfg, part, listed, k_mat, kbuf, sems, product, total_ref, by_row):
    total = listed[0, 0]
    base = part * cfg.part_groups

    def copy_in(g):
        slot = lax.rem(g, RING)
        return pltpu.make_async_copy(k_mat.at[g], kbuf.at[slot], sems.at[slot])

    if not cfg.resident:
        for p in range(RING - 1):

            @pl.when(p < total)
            def _(p=p):
                copy_in(p).start()

    def step(g, carry):
        slot, source = (base + g, k_mat) if cfg.resident else (lax.rem(g, RING), kbuf)
        if not cfg.resident:

            @pl.when(g + (RING - 1) < total)
            def _():
                copy_in(g + (RING - 1)).start()

            copy_in(g).wait()
        codes = [listed[0, g * GROUP + u + 1] for u in range(GROUP)]
        pairs = [(lax.shift_right_logical(code, CODE_BITS), code & (CODE - 1)) for code in codes]
        terms = [product(i, j, source[slot, u]) for u, (i, j) in enumerate(pairs)]
        add(carry)
        return [i if by_row else j for i, j in pairs], terms

    def add(carry):
        for at, term in zip(*carry):
            total_ref[at] += term

    none = [jnp.int32(0)] * GROUP, [jnp.zeros(total_ref.shape[1:], F32)] * GROUP
    add(lax.fori_loop(0, total, step, none))


def first_kernel(cfg, k_mat, *refs):
    n = cfg.parts
    lists, pieces, inv_ref, refs = refs[:n], refs[n:2 * n], refs[2 * n], refs[2 * n + 1:]
    near, near_y, cross, own_inv, z_acc, w_all, listed, list_sems, *ring = refs
    kbuf, sems = ring or (None, None)
    place = position()
    col = place[1]
    copies = [
        pltpu.make_async_copy(lists[p], listed.at[p], list_sems.at[p]) for p in range(n)
    ]
    for copy in copies:
        copy.start()
    own_rows, block_len = cfg.own_rows, cfg.block_len
    z_acc[...] = jnp.zeros_like(z_acc)
    for part, piece in enumerate(pieces):
        held = piece.shape[0]

        def prepare(m, carry, part=part, piece=piece):
            z = slot_of(cfg, place, m)
            for k in range(own_rows):
                w = piece[m, :, k * block_len:(k + 1) * block_len]
                at = row_of(cfg, place, part, z) * own_rows + k
                w_all[z * own_rows + k] = (w * inv_ref[pl.ds(at, 1), :]).astype(BF16)
            return carry

        lax.fori_loop(0, held, prepare, 0, unroll=held <= 4)

        def product(i, j, block):
            return lax.dot_general(
                w_all[j], block, (((1,), (1,)), ((), ())), preferred_element_type=F32
            )

        copies[part].wait()
        walk(cfg, part, listed.at[part], k_mat, kbuf, sems, product, z_acc, True)
    for k in range(own_rows):
        cols = slice(k * block_len, (k + 1) * block_len)
        mine = inv_ref[pl.ds(place[0] * own_rows + k, 1), :]
        own_inv[:, cols] = jnp.broadcast_to(mine, (8, block_len))
        for e, ref in enumerate((near, cross.at[0], near_y, cross.at[1])):
            ref[:, cols] = z_acc[(col ^ e) * own_rows + k]


def second_kernel(cfg, part, k_mat, list_v, t_ref, s1_own, s1_got, out, z_acc, w_all, listed, list_sem, *ring):
    kbuf, sems = ring or (None, None)
    place = position()
    own_rows, block_len = cfg.own_rows, cfg.block_len
    outputs = t_ref.shape[0]
    list_copy = pltpu.make_async_copy(list_v, listed, list_sem)
    list_copy.start()
    for e, packed in enumerate(pieces_of(s1_own, s1_got)):
        share = place[1] ^ e
        for k in range(own_rows):
            cols = slice(k * block_len, (k + 1) * block_len)
            i = share * own_rows + k
            t = t_ref[:, pl.ds(pl.multiple_of(i * block_len, LANES), block_len)]
            g = (packed[:outputs, cols] - SHIFT * t) * packed[outputs:outputs + 1, cols]
            w_all[i] = g.astype(BF16)
    z_acc[...] = jnp.zeros_like(z_acc)

    def product(i, j, block):
        return jnp.dot(w_all[i], block, preferred_element_type=F32)

    list_copy.wait()
    walk(cfg, part, listed, k_mat, kbuf, sems, product, z_acc, False)

    def hand_out(m, carry):
        z = slot_of(cfg, place, m)
        for k in range(own_rows):
            out[m, :, k * block_len:(k + 1) * block_len] = z_acc[z * own_rows + k].astype(out.dtype)
        return carry

    held = out.shape[0]
    lax.fori_loop(0, held, hand_out, 0, unroll=held <= 4)


N_DOTS = 5


def meet_kernel(cfg, z_same, z_other, t_same, inv_ref, s1_own, *refs):
    gs, (own_z, own_dots, *outs) = refs[:4], refs[4:]
    own_rows, block_len = cfg.own_rows, cfg.block_len
    outputs, own_len = own_z.shape
    place = position()
    tz = jnp.zeros((outputs, 1), F32)
    gz = jnp.zeros((outputs, 1), F32)
    for n in range(4):
        z = z_same[n] + z_other[n].astype(F32)
        if n == 0:
            own_z[...] = z
        else:
            outs[n - 1][:, :own_len] = z.astype(BF16)
        gz += jnp.sum(gs[n][...].astype(F32) * z, axis=1, keepdims=True)
        at = row_of(cfg, place, 0, slot_of(cfg, place, n)) * own_rows
        for k in range(own_rows):
            cols = slice(k * block_len, (k + 1) * block_len)
            scaled = t_same[n, :, cols] * inv_ref[pl.ds(at + k, 1), :]
            tz += jnp.sum(scaled * z[:, cols], axis=1, keepdims=True)
    t, s1 = t_same[0], s1_own[0, :outputs, :]
    tt = jnp.sum(t * t, axis=1, keepdims=True)
    ts1 = jnp.sum(t * s1, axis=1, keepdims=True)
    s1s1 = jnp.sum(s1 * s1, axis=1, keepdims=True)
    dots = (tt, ts1, s1s1, tz + SHIFT * ts1, gz + SHIFT * (tz + s1s1))
    lane = lax.broadcasted_iota(jnp.int32, (outputs, LANES), 1)
    tile = jnp.zeros(lane.shape, F32)
    for n, v in enumerate(dots):
        for part in range(3):
            head = v.astype(BF16).astype(F32)
            tile = jnp.where(lane == part * N_DOTS + n, head, tile)
            v = v - head
    own_dots[...] = tile.astype(BF16)
    for out in outs:
        out[:, own_len:] = tile.astype(BF16)


def product_kernel(own_z, own_dots, s1_own, *refs):
    got, end_ref, dot_ref = refs[2::-1], refs[3], refs[4]
    outputs, own_len = own_z.shape
    z = own_z[...]
    for ref in got:
        z = z + ref[:, :own_len].astype(F32)
    end_ref[:, :own_len] = z * s1_own[0, outputs:outputs + 1, :]
    tiles = [own_dots[...]] + [ref[:, own_len:] for ref in got]
    total = pair_sum([tile.astype(F32) for tile in tiles])
    out = total
    for part in range(1, 3):
        out = out + pltpu.roll(total, LANES - part * N_DOTS, 1)
    dot_ref[...] = out
    end_ref[:, own_len:] = out


def final_kernel(t_ref, s1_own, s1_got, *refs):
    ends = pieces_of(refs[0], refs[1])
    sol_hbm, res_hbm, sol_ref, res_ref, sems = refs[2:]
    s1s = pieces_of(s1_own, s1_got)
    outputs, own_len = ends[0].shape[0], ends[0].shape[1] - LANES
    place = position()
    dots = ends[0][:, own_len:] + ends[1][:, own_len:]
    tt, ts1, s1s1, ts2, s1s2 = (dots[:, n:n + 1] for n in range(5))
    a1 = tt / (REG * tt + ts1)
    p = 1.0 - REG * a1
    new = p * p * tt - 2.0 * p * a1 * ts1 + a1 * a1 * s1s1
    u = p + new / tt
    dd = u * u * tt - 2.0 * u * a1 * ts1 + a1 * a1 * s1s1
    dmd = u * u * ts1 - u * a1 * (s1s1 + ts2) + a1 * a1 * s1s2
    a2 = new / (REG * dd + dmd)
    sol_t, sol_1 = a1 + a2 * u, a2 * a1
    res_t, res_1 = p - a2 * REG * u, a1 + a2 * (u - REG * a1)
    copies = []
    for e in range(4):
        at = pl.ds(pl.multiple_of((place[1] ^ e) * own_len, LANES), own_len)
        t, s1 = t_ref[:, at], s1s[e][:outputs, :]
        s2 = ends[e][:, :own_len] + SHIFT * s1
        sol_ref[e] = sol_t * t - sol_1 * s1
        res_ref[e] = res_t * t - res_1 * s1 + sol_1 * s2
        for n, (ref, hbm) in enumerate(((sol_ref, sol_hbm), (res_ref, res_hbm))):
            copy = pltpu.make_async_copy(ref.at[e], hbm.at[:, at], sems.at[n, e])
            copy.start()
            copies.append(copy)
    for copy in copies:
        copy.wait()


def swap(x, axis, d):
    size = lax.axis_size(axis)
    return lax.ppermute(x, axis, [(i, i ^ d) for i in range(size)])


def both_swap(x, row_d, col_d):
    n_rows, n_cols = lax.axis_size("rows"), lax.axis_size("cols")
    pairs = [
        (r * n_cols + c, (r ^ row_d) * n_cols + (c ^ col_d))
        for r in range(n_rows)
        for c in range(n_cols)
    ]
    return lax.ppermute(x, ("rows", "cols"), pairs)


def along_z(x):
    return [x] + [swap(x, "rows", d) for d in range(2, lax.axis_size("rows"), 2)]


def across_x(same):
    return [same, swap(same, "rows", 1)]


def direct_cols(x):
    return [x] + [swap(x, "cols", e) for e in range(1, 4)]


def local(block_list, points, targets):
    n_rows = lax.axis_size("rows")
    n_cols = lax.axis_size("cols")
    row = lax.axis_index("rows")
    col = lax.axis_index("cols")
    block_rows, slots = block_list.shape
    dim, npoints = points.shape
    outputs = targets.shape[0]
    block_len = npoints // block_rows
    own_rows = block_rows // n_cols
    own_len = own_rows * block_len
    nb = block_rows * n_rows
    n_sub = own_rows * n_rows
    capacity = -(-block_rows * slots // n_rows)
    direct_rows = n_rows <= DIRECT_ROWS
    parts = 2 if direct_rows else 1
    n_part = n_sub // parts
    bound = min(block_rows * n_part, n_cols * capacity * (n_rows + 1))
    n_groups = -(-bound // GROUP)
    list_len = -(-(n_groups * GROUP + GROUP + 1) // LANES) * LANES
    resident = parts * 2 * n_groups * GROUP * block_len * block_len <= RESIDENT_BYTES
    k_shape = (parts * n_groups, GROUP, block_len, block_len)
    limit = pltpu.CompilerParams(vmem_limit_bytes=(8 if resident else 32) * 1024 * 1024)
    ring = [] if resident else [
        pltpu.VMEM((RING, GROUP, block_len, block_len), BF16),
        pltpu.SemaphoreType.DMA((RING,)),
    ]
    k_spec = VMEM if resident else HBM
    cfg = Sizes(
        parts, n_groups, resident, nb, block_len, own_rows, block_rows, -(-own_rows * nb // LANES)
    )

    def shape(*dims, dtype=F32):
        return jax.ShapeDtypeStruct(dims, dtype)

    def own(x):
        return lax.dynamic_slice_in_dim(x, col * own_len, own_len, 1)

    def total_rows(x):
        if direct_rows:
            near = pair_sum([x] + [swap(x, "rows", d) for d in range(1, 4)])
            return near + swap(near, "rows", 4)
        return lax.psum(x, "rows")

    lists = direct_cols(block_list)
    names = jnp.arange(nb, dtype=jnp.int32)
    direct = sum(jnp.sum((x[:, :, None] == names).astype(jnp.int32), axis=1) for x in lists)
    own_counts = lax.dynamic_slice_in_dim(direct, col * own_rows, own_rows, 0)
    coded = own_counts.reshape(-1)
    coded = jnp.pad(coded, (0, dim * LANES - coded.shape[0])).reshape(dim, LANES).astype(BF16)
    packed = jnp.concatenate([own(points), coded], axis=1)
    own_t = own(targets)

    def build(part, *operands):
        first, last = part == 0, part == parts - 1
        out = [
            pltpu.VMEM(k_shape, BF16) if resident else shape(*k_shape, dtype=BF16),
            shape(1, list_len, dtype=jnp.int32),
            shape(n_sub if last else n_part, block_len),
        ]
        out += [shape(block_rows, block_len, 2 * dim, dtype=BF16)] if first else []
        k_mat, *rest = pl.pallas_call(
            functools.partial(build_kernel, cfg, part),
            out_shape=out,
            in_specs=[VMEM] + ([HBM, VMEM] if first else [VMEM] * 3 + [k_spec]),
            out_specs=[k_spec] + [VMEM] * (len(out) - 1),
            scratch_shapes=([
                pltpu.VMEM((dim, npoints), BF16),
                pltpu.SemaphoreType.DMA,
            ] if first else []) + [
                pltpu.SMEM((1, list_len), jnp.int32),
                pltpu.SMEM((list_len,), jnp.int32),
                pltpu.VMEM((n_part, 8, block_len), F32),
                pltpu.VMEM((n_part, 2 * dim, block_len), BF16),
                pltpu.VMEM((2, block_len, block_len), F32),
                pltpu.SMEM((block_rows, nb), jnp.int32),
                pltpu.VMEM((n_part // own_rows, cfg.count_rows, LANES), jnp.int32),
                pltpu.SMEM((n_part // own_rows, cfg.count_rows, LANES), jnp.int32),
                pltpu.SemaphoreType.DMA((3,)),
                *ring,
            ],
            compiler_params=limit,
            input_output_aliases={} if first else {4: 0},
            cost_estimate=pl.CostEstimate(
                flops=10 * 2 * 2 * dim * bound * block_len * block_len,
                bytes_accessed=10 * 2 * bound * block_len * block_len,
                transcendentals=10 * bound * block_len * block_len,
            ),
            name="build",
        )(direct, *operands)
        if resident:
            k_mat = pltpu.with_memory_space_constraint(k_mat, pltpu.VMEM)
        return k_mat, *rest

    near = pltpu.with_memory_space_constraint(points, pltpu.HBM)
    if direct_rows:
        packed, early_t = lax.optimization_barrier((packed, own_t))
        same, other = across_x(jnp.stack(along_z(packed)))
        t_same = along_z(early_t)
        k_mat, list0, degree, lhs = build(0, near, same)
        degree, other, *t_same = lax.optimization_barrier((degree, other, *t_same))
        t_same, t_other = across_x(jnp.stack(t_same))
        other, t_same = lax.optimization_barrier((other, t_same))
        k_mat, list1, degree = build(1, lhs, degree, other, k_mat)
        t_pieces, k_lists = [t_same, t_other], [list0, list1]
    else:
        k_mat, list0, degree, _ = build(0, near, lax.all_gather(packed, "rows"))
        t_pieces, k_lists = [lax.all_gather(own_t, "rows")], [list0]
    inv = 1.0 / jnp.sqrt(1.0 + total_rows(degree))

    def cost(n):
        return pl.CostEstimate(
            flops=2 * n * bound * outputs * block_len * block_len,
            bytes_accessed=n * bound * block_len * block_len,
            transcendentals=0,
        )

    near_z, near_y, cross_z, tail = pl.pallas_call(
        functools.partial(first_kernel, cfg),
        out_shape=[shape(outputs, own_len)] * 2 + [shape(2, outputs, own_len), shape(8, own_len)],
        in_specs=[k_spec] + [VMEM] * (2 * parts + 1),
        out_specs=[VMEM] * 4,
        scratch_shapes=[
            pltpu.VMEM((block_rows, outputs, block_len), F32),
            pltpu.VMEM((n_part, outputs, block_len), BF16),
            pltpu.SMEM((parts, 1, list_len), jnp.int32),
            pltpu.SemaphoreType.DMA((parts,)),
            *ring,
        ],
        compiler_params=limit,
        cost_estimate=cost(parts),
        name="first",
    )(k_mat, *k_lists, *t_pieces, inv)

    got = swap(cross_z, "cols", 1)
    half = jnp.concatenate([near_z + got[0], near_y + got[1], tail], axis=0)
    far = swap(half, "cols", 2)
    lo, hi, end = slice(0, outputs), slice(outputs, 2 * outputs), slice(2 * outputs, None)
    s1_own = jnp.stack([
        jnp.concatenate([(half[lo] + far[hi]) * tail[:1], tail], axis=0),
        jnp.concatenate([(half[hi] + far[lo]) * far[end][:1], far[end]], axis=0),
    ])
    s1_got = swap(s1_own, "cols", 1)
    held_t = pltpu.with_memory_space_constraint(targets, pltpu.VMEM)

    def second(part, dtype):
        return pl.pallas_call(
            functools.partial(second_kernel, cfg, part),
            out_shape=shape(n_part // own_rows, outputs, own_len, dtype=dtype),
            in_specs=[k_spec] + [VMEM] * 4,
            out_specs=VMEM,
            scratch_shapes=[
                pltpu.VMEM((n_part, outputs, block_len), F32),
                pltpu.VMEM((block_rows, outputs, block_len), BF16),
                pltpu.SMEM((1, list_len), jnp.int32),
                pltpu.SemaphoreType.DMA,
                *ring,
            ],
            compiler_params=limit,
            cost_estimate=cost(1),
            name="second",
        )(k_mat, k_lists[part], held_t, s1_own, s1_got)

    if direct_rows:
        g = ((s1_own[0, :outputs] - SHIFT * own_t) * tail[:1]).astype(BF16)
        z2_other, g = lax.optimization_barrier((second(1, BF16), g))
        z2_other = swap(z2_other, "rows", 1)
        gs = along_z(g)
        z2_same = second(0, F32)
        z2_same, z2_other, *gs = lax.optimization_barrier((z2_same, z2_other, *gs))
        row_piece = shape(outputs, own_len + LANES, dtype=BF16)
        own_z, own_dots, *sends = pl.pallas_call(
            functools.partial(meet_kernel, cfg),
            out_shape=[shape(outputs, own_len), shape(outputs, LANES, dtype=BF16)] + [row_piece] * 3,
            in_specs=[VMEM] * 9,
            out_specs=[VMEM] * 5,
            compiler_params=limit,
            name="meet",
        )(z2_same, z2_other, t_pieces[0], inv, s1_own, *gs)
        got = [swap(sends[n], "rows", 2 * n + 2) for n in (2, 1, 0)]
        ends, dots = pl.pallas_call(
            product_kernel,
            out_shape=(shape(outputs, own_len + LANES), shape(outputs, LANES)),
            in_specs=[VMEM] * 6,
            out_specs=(VMEM, VMEM),
            compiler_params=limit,
            name="products",
        )(own_z, own_dots, s1_own, *got)
        far = both_swap(dots, 1, 2)
        across = swap(dots, "rows", 1)
        ends_y = swap(ends, "cols", 2)
        dots = (dots + across) + (ends_y[:, own_len:] + far)
    else:
        z2 = lax.psum_scatter(second(0, F32), "rows", scatter_dimension=0)
        grown = z2 * tail[:1]
        own_s1 = s1_own[0, :outputs]
        own_t, s2 = own(targets), grown + SHIFT * own_s1
        dots = [(own_t, own_t), (own_t, own_s1), (own_s1, own_s1), (own_t, s2), (own_s1, s2)]
        dots = jnp.stack([jnp.sum(x * y, axis=1) for x, y in dots], axis=1)
        dots = lax.psum(jnp.pad(dots, ((0, 0), (0, LANES - N_DOTS))), "rows")
        ends = jnp.concatenate([grown, dots], axis=1)
        ends_y = swap(ends, "cols", 2)
        dots = dots + ends_y[:, own_len:]
    ends = jnp.stack([jnp.concatenate([ends[:, :own_len], dots], axis=1), ends_y])
    ends = (s1_own, s1_got, ends, swap(ends, "cols", 1))
    ends = [pltpu.with_memory_space_constraint(x, pltpu.VMEM) for x in ends]

    return pl.pallas_call(
        final_kernel,
        out_shape=(shape(outputs, npoints), shape(outputs, npoints)),
        in_specs=[VMEM] * 5,
        out_specs=(HBM, HBM),
        scratch_shapes=[
            pltpu.VMEM((4, outputs, own_len), F32),
            pltpu.VMEM((4, outputs, own_len), F32),
            pltpu.SemaphoreType.DMA((2, 4)),
        ],
        compiler_params=limit,
        name="final",
    )(held_t, *ends)


def solution(mesh):
    placed = (P("rows", "cols"), P(None, "rows"), P(None, "rows"))
    return jax.shard_map(
        local,
        mesh=mesh,
        in_specs=placed,
        out_specs=(P(None, "rows"), P(None, "rows")),
        check_vma=False,
    )
```

```python
import functools
from typing import NamedTuple

import jax
import jax.numpy as jnp
from jax import lax
from jax.experimental import pallas as pl
from jax.experimental.pallas import tpu as pltpu
from jax.sharding import PartitionSpec as P

REG = 1.5
RADIUS = 0.25
GROUP_BITS = 2
GROUP = 1 << GROUP_BITS
CODE_BITS = 12
CODE = 1 << CODE_BITS
RING = 3
STRIP = 64
LANES = 128
TINY = 1e-30
SHIFT = 0.375
DIRECT_ROWS = 8
RESIDENT_BYTES = 20 * 1024 * 1024

VMEM = pl.BlockSpec(memory_space=pltpu.VMEM)
HBM = pl.BlockSpec(memory_space=pltpu.HBM)
F32 = jnp.float32
BF16 = jnp.bfloat16


def pair_sum(parts):
    while len(parts) > 1:
        parts = [a + b for a, b in zip(parts[::2], parts[1::2])]
    return parts[0]


def position():
    return lax.axis_index("rows"), lax.axis_index("cols")


class Sizes(NamedTuple):
    parts: int
    part_groups: int
    resident: bool
    nb: int
    block_len: int
    own_rows: int
    block_rows: int
    count_rows: int


def augment(x, first_ones):
    dim, n = x.shape
    norm = jnp.sum(x * x, axis=0, keepdims=True) / (RADIUS * RADIUS)
    high = norm.astype(BF16).astype(F32)
    rest = norm - high
    mid = rest.astype(BF16).astype(F32)
    low = rest - mid
    line = lax.broadcasted_iota(jnp.int32, (dim, n), 0)
    base = 3 if first_ones else 0
    ones_at = 0 if first_ones else 3
    tail = jnp.where((line >= ones_at) & (line < ones_at + 3), 1.0, 0.0)
    tail = jnp.where(line == base, high, tail)
    tail = jnp.where(line == base + 1, mid, tail)
    tail = jnp.where(line == base + 2, low, tail)
    return tail


def row_of(cfg, place, part, z):
    if cfg.parts == 1:
        return z
    return 2 * z + (place[0] & 1 if part == 0 else 1 - (place[0] & 1))


def slot_of(cfg, place, n):
    return n if cfg.parts == 1 else lax.shift_right_logical(place[0], 1) ^ n


def build_kernel(cfg, part, direct_v, *refs):
    last = part == cfg.parts - 1
    place = position()
    if part == 0:
        near_hbm, piece, refs = refs[0], refs[1], refs[2:]
        k_mat, list_v, deg_ref, lhs = refs[:4]
        near_ref, near_sem, refs = refs[4], refs[5], refs[6:]
        near_copy = pltpu.make_async_copy(near_hbm, near_ref, near_sem)
        near_copy.start()
    else:
        lhs, first_deg, piece, _ = refs[:4]
        k_mat, list_v, deg_ref = refs[4:7]
        refs = refs[7:]
    listed, mlist, acc, rhs, dist, direct, counts_v, counts, copy_sems = refs[:9]
    kbuf, sems = (None, None) if cfg.resident else refs[9:]
    direct_copy = pltpu.make_async_copy(direct_v, direct, copy_sems.at[0])
    direct_copy.start()
    row, col = place[0], place[1]
    own_rows, block_len, nb = cfg.own_rows, cfg.block_len, cfg.nb
    own_len = own_rows * block_len
    dim, held = piece.shape[1], piece.shape[0]
    scale = 1.0 / (RADIUS * RADIUS)

    def count(n, carry):
        named = piece[n, :, own_len:own_len + LANES]
        counts_v[slot_of(cfg, place, n)] = named.astype(F32)[:cfg.count_rows].astype(jnp.int32)
        return carry

    def prepare(n, carry):
        z = slot_of(cfg, place, n)
        for k in range(own_rows):
            far = piece[n, :, k * block_len:(k + 1) * block_len]
            rhs[z * own_rows + k, :dim, :] = far
            rhs[z * own_rows + k, dim:, :] = augment(far.astype(F32), False).astype(BF16)
        return carry

    lax.fori_loop(0, held, count, 0, unroll=held <= 4)
    fetch = pltpu.make_async_copy(counts_v, counts, copy_sems.at[1])
    fetch.start()
    lax.fori_loop(0, held, prepare, 0, unroll=held <= 4)
    acc[...] = jnp.zeros_like(acc)
    if part == 0:
        near_copy.wait()
        for i in range(cfg.block_rows):
            near = near_ref[:, i * block_len:(i + 1) * block_len].astype(F32)
            full = jnp.concatenate([near * (-2.0 * scale), augment(near, True)], axis=0)
            lhs[i] = full.T.astype(BF16)
    direct_copy.wait()
    fetch.wait()

    pos = jnp.int32(0)
    for i in range(cfg.block_rows):
        me = row * cfg.block_rows + i
        spots = [k * nb + me for k in range(own_rows)]
        spots = [(lax.shift_right_logical(p, 7), p & (LANES - 1)) for p in spots]

        def note(z, at, i=i, me=me, spots=spots):
            for k in range(own_rows):
                name = row_of(cfg, place, part, z) * cfg.block_rows + col * own_rows + k
                m = direct[i, name] + jnp.where(name == me, 0, counts[z, spots[k][0], spots[k][1]])
                listed[0, at + 1] = i * CODE + z * own_rows + k
                mlist[at] = m
                at = at + jnp.where(m > 0, 1, 0)
            return at

        if held <= 4:
            for z in range(held):
                pos = note(z, pos)
        else:
            pos = lax.fori_loop(0, held, note, pos, unroll=4)
    for u in range(GROUP):
        listed[0, pos + u + 1] = 0
        mlist[pos + u] = 0
    total = lax.shift_right_logical(pos + (GROUP - 1), GROUP_BITS)
    listed[0, 0] = total
    list_copy = pltpu.make_async_copy(listed, list_v, copy_sems.at[2])
    list_copy.start()

    def copy_out(g):
        slot = lax.rem(g, RING)
        return pltpu.make_async_copy(kbuf.at[slot], k_mat.at[g], sems.at[slot])

    base = part * cfg.part_groups

    def distances(e, slot):
        code = listed[0, e + 1]
        i, j = lax.shift_right_logical(code, CODE_BITS), code & (CODE - 1)
        dist[slot] = jnp.dot(lhs[i], rhs[j], preferred_element_type=F32)

    distances(0, 0)

    def step(g, carry):
        slot, target = (base + g, k_mat) if cfg.resident else (lax.rem(g, RING), kbuf)
        if not cfg.resident:

            @pl.when(g >= RING)
            def _():
                copy_out(g - RING).wait()

        for u in range(GROUP):
            distances(g * GROUP + u + 1, (u + 1) % 2)
            j = listed[0, g * GROUP + u + 1] & (CODE - 1)
            m = mlist[g * GROUP + u].astype(F32)
            sums = jnp.zeros((8, block_len), F32)
            for s in range(block_len // STRIP):
                rows = slice(s * STRIP, (s + 1) * STRIP)
                d = jnp.maximum(dist[u % 2, rows, :], TINY)
                sc = d * lax.rsqrt(d)
                rem = jnp.maximum(1.0 - sc, 0.0)
                sq = rem * rem
                val = (sq * sq) * (sc * (4.0 * m) + m)
                target[slot, u, rows, :] = val.astype(BF16)
                for h in range(0, STRIP, 8):
                    sums = sums + val[h:h + 8]
            acc[j] += sums
        if not cfg.resident:
            copy_out(g).start()
        return carry

    lax.fori_loop(0, total, step, 0)
    if cfg.parts == 1 or not last:
        deg_ref[...] = jnp.sum(acc[...], axis=1)
    else:
        second = jnp.sum(acc[...], axis=1)
        for z in range(held):
            rows = slice(z * own_rows, (z + 1) * own_rows)
            for p, deg in enumerate((first_deg[rows, :], second[rows])):
                at = row_of(cfg, place, p, z) * own_rows
                for k in range(own_rows):
                    deg_ref[pl.ds(at + k, 1), :] = deg[k:k + 1]

    def drain(g, carry):
        copy_out(g).wait()
        return carry

    if not cfg.resident:
        lax.fori_loop(jnp.maximum(total - RING, 0), total, drain, 0)
    list_copy.wait()


def pieces_of(own, got):
    return own.at[0], got.at[0], own.at[1], got.at[1]


def walk(cfg, part, listed, k_mat, kbuf, sems, product, total_ref, by_row):
    total = listed[0, 0]
    base = part * cfg.part_groups

    def copy_in(g):
        slot = lax.rem(g, RING)
        return pltpu.make_async_copy(k_mat.at[g], kbuf.at[slot], sems.at[slot])

    if not cfg.resident:
        for p in range(RING - 1):

            @pl.when(p < total)
            def _(p=p):
                copy_in(p).start()

    def step(g, carry):
        slot, source = (base + g, k_mat) if cfg.resident else (lax.rem(g, RING), kbuf)
        if not cfg.resident:

            @pl.when(g + (RING - 1) < total)
            def _():
                copy_in(g + (RING - 1)).start()

            copy_in(g).wait()
        codes = [listed[0, g * GROUP + u + 1] for u in range(GROUP)]
        pairs = [(lax.shift_right_logical(code, CODE_BITS), code & (CODE - 1)) for code in codes]
        terms = [product(i, j, source[slot, u]) for u, (i, j) in enumerate(pairs)]
        add(carry)
        return [i if by_row else j for i, j in pairs], terms

    def add(carry):
        for at, term in zip(*carry):
            total_ref[at] += term

    none = [jnp.int32(0)] * GROUP, [jnp.zeros(total_ref.shape[1:], F32)] * GROUP
    add(lax.fori_loop(0, total, step, none))


def first_kernel(cfg, k_mat, *refs):
    n = cfg.parts
    lists, pieces, inv_ref, refs = refs[:n], refs[n:2 * n], refs[2 * n], refs[2 * n + 1:]
    near, near_y, cross, own_inv, z_acc, w_all, listed, list_sems, *ring = refs
    kbuf, sems = ring or (None, None)
    place = position()
    col = place[1]
    copies = [
        pltpu.make_async_copy(lists[p], listed.at[p], list_sems.at[p]) for p in range(n)
    ]
    for copy in copies:
        copy.start()
    own_rows, block_len = cfg.own_rows, cfg.block_len
    z_acc[...] = jnp.zeros_like(z_acc)
    for part, piece in enumerate(pieces):
        held = piece.shape[0]

        def prepare(m, carry, part=part, piece=piece):
            z = slot_of(cfg, place, m)
            for k in range(own_rows):
                w = piece[m, :, k * block_len:(k + 1) * block_len]
                at = row_of(cfg, place, part, z) * own_rows + k
                w_all[z * own_rows + k] = (w * inv_ref[pl.ds(at, 1), :]).astype(BF16)
            return carry

        lax.fori_loop(0, held, prepare, 0, unroll=held <= 4)

        def product(i, j, block):
            return lax.dot_general(
                w_all[j], block, (((1,), (1,)), ((), ())), preferred_element_type=F32
            )

        copies[part].wait()
        walk(cfg, part, listed.at[part], k_mat, kbuf, sems, product, z_acc, True)
    for k in range(own_rows):
        cols = slice(k * block_len, (k + 1) * block_len)
        mine = inv_ref[pl.ds(place[0] * own_rows + k, 1), :]
        own_inv[:, cols] = jnp.broadcast_to(mine, (8, block_len))
        for e, ref in enumerate((near, cross.at[0], near_y, cross.at[1])):
            ref[:, cols] = z_acc[(col ^ e) * own_rows + k]


def second_kernel(cfg, part, k_mat, list_v, t_ref, s1_own, s1_got, out, z_acc, w_all, listed, list_sem, *ring):
    kbuf, sems = ring or (None, None)
    place = position()
    own_rows, block_len = cfg.own_rows, cfg.block_len
    outputs = t_ref.shape[0]
    list_copy = pltpu.make_async_copy(list_v, listed, list_sem)
    list_copy.start()
    for e, packed in enumerate(pieces_of(s1_own, s1_got)):
        share = place[1] ^ e
        for k in range(own_rows):
            cols = slice(k * block_len, (k + 1) * block_len)
            i = share * own_rows + k
            t = t_ref[:, pl.ds(pl.multiple_of(i * block_len, LANES), block_len)]
            g = (packed[:outputs, cols] - SHIFT * t) * packed[outputs:outputs + 1, cols]
            w_all[i] = g.astype(BF16)
    z_acc[...] = jnp.zeros_like(z_acc)

    def product(i, j, block):
        return jnp.dot(w_all[i], block, preferred_element_type=F32)

    list_copy.wait()
    walk(cfg, part, listed, k_mat, kbuf, sems, product, z_acc, False)

    def hand_out(m, carry):
        z = slot_of(cfg, place, m)
        for k in range(own_rows):
            out[m, :, k * block_len:(k + 1) * block_len] = z_acc[z * own_rows + k].astype(out.dtype)
        return carry

    held = out.shape[0]
    lax.fori_loop(0, held, hand_out, 0, unroll=held <= 4)


N_DOTS = 5


def meet_kernel(cfg, z_same, z_other, t_same, inv_ref, s1_own, *refs):
    g_near, g_far, own_z, own_dots, *outs = refs
    gs = g_near[0], g_near[1], g_far[0], g_far[1]
    own_rows, block_len = cfg.own_rows, cfg.block_len
    outputs, own_len = own_z.shape
    place = position()
    tz = jnp.zeros((outputs, 1), F32)
    gz = jnp.zeros((outputs, 1), F32)
    for n in range(4):
        z = z_same[n] + z_other[n].astype(F32)
        if n == 0:
            own_z[...] = z
        else:
            outs[n - 1][:, :own_len] = z.astype(BF16)
        gz += jnp.sum(gs[n].astype(F32) * z, axis=1, keepdims=True)
        at = row_of(cfg, place, 0, slot_of(cfg, place, n)) * own_rows
        for k in range(own_rows):
            cols = slice(k * block_len, (k + 1) * block_len)
            scaled = t_same[n, :, cols] * inv_ref[pl.ds(at + k, 1), :]
            tz += jnp.sum(scaled * z[:, cols], axis=1, keepdims=True)
    t, s1 = t_same[0], s1_own[0, :outputs, :]
    tt = jnp.sum(t * t, axis=1, keepdims=True)
    ts1 = jnp.sum(t * s1, axis=1, keepdims=True)
    s1s1 = jnp.sum(s1 * s1, axis=1, keepdims=True)
    dots = (tt, ts1, s1s1, tz + SHIFT * ts1, gz + SHIFT * (tz + s1s1))
    lane = lax.broadcasted_iota(jnp.int32, (outputs, LANES), 1)
    tile = jnp.zeros(lane.shape, F32)
    for n, v in enumerate(dots):
        for part in range(3):
            head = v.astype(BF16).astype(F32)
            tile = jnp.where(lane == part * N_DOTS + n, head, tile)
            v = v - head
    own_dots[...] = tile.astype(BF16)
    for out in outs:
        out[:, own_len:] = tile.astype(BF16)


def product_kernel(own_z, own_dots, s1_own, *refs):
    got, end_ref, dot_ref = refs[2::-1], refs[3], refs[4]
    outputs, own_len = own_z.shape
    z = own_z[...]
    for ref in got:
        z = z + ref[:, :own_len].astype(F32)
    end_ref[:, :own_len] = z * s1_own[0, outputs:outputs + 1, :]
    tiles = [own_dots[...]] + [ref[:, own_len:] for ref in got]
    total = pair_sum([tile.astype(F32) for tile in tiles])
    out = total
    for part in range(1, 3):
        out = out + pltpu.roll(total, LANES - part * N_DOTS, 1)
    dot_ref[...] = out
    end_ref[:, own_len:] = out


def final_kernel(t_ref, s1_own, s1_got, *refs):
    ends = pieces_of(refs[0], refs[1])
    sol_hbm, res_hbm, sol_ref, res_ref, sems = refs[2:]
    s1s = pieces_of(s1_own, s1_got)
    outputs, own_len = ends[0].shape[0], ends[0].shape[1] - LANES
    place = position()
    dots = ends[0][:, own_len:] + ends[1][:, own_len:]
    tt, ts1, s1s1, ts2, s1s2 = (dots[:, n:n + 1] for n in range(5))
    a1 = tt / (REG * tt + ts1)
    p = 1.0 - REG * a1
    new = p * p * tt - 2.0 * p * a1 * ts1 + a1 * a1 * s1s1
    u = p + new / tt
    dd = u * u * tt - 2.0 * u * a1 * ts1 + a1 * a1 * s1s1
    dmd = u * u * ts1 - u * a1 * (s1s1 + ts2) + a1 * a1 * s1s2
    a2 = new / (REG * dd + dmd)
    sol_t, sol_1 = a1 + a2 * u, a2 * a1
    res_t, res_1 = p - a2 * REG * u, a1 + a2 * (u - REG * a1)
    copies = []
    for e in range(4):
        at = pl.ds(pl.multiple_of((place[1] ^ e) * own_len, LANES), own_len)
        t, s1 = t_ref[:, at], s1s[e][:outputs, :]
        s2 = ends[e][:, :own_len] + SHIFT * s1
        sol_ref[e] = sol_t * t - sol_1 * s1
        res_ref[e] = res_t * t - res_1 * s1 + sol_1 * s2
        for n, (ref, hbm) in enumerate(((sol_ref, sol_hbm), (res_ref, res_hbm))):
            copy = pltpu.make_async_copy(ref.at[e], hbm.at[:, at], sems.at[n, e])
            copy.start()
            copies.append(copy)
    for copy in copies:
        copy.wait()


def swap(x, axis, d):
    size = lax.axis_size(axis)
    return lax.ppermute(x, axis, [(i, i ^ d) for i in range(size)])


def both_swap(x, row_d, col_d):
    n_rows, n_cols = lax.axis_size("rows"), lax.axis_size("cols")
    pairs = [
        (r * n_cols + c, (r ^ row_d) * n_cols + (c ^ col_d))
        for r in range(n_rows)
        for c in range(n_cols)
    ]
    return lax.ppermute(x, ("rows", "cols"), pairs)


def along_z(x):
    return [x] + [swap(x, "rows", d) for d in range(2, lax.axis_size("rows"), 2)]


def across_x(same):
    return [same, swap(same, "rows", 1)]


def direct_cols(x):
    return [x] + [swap(x, "cols", e) for e in range(1, 4)]


def local(block_list, points, targets):
    n_rows = lax.axis_size("rows")
    n_cols = lax.axis_size("cols")
    row = lax.axis_index("rows")
    col = lax.axis_index("cols")
    block_rows, slots = block_list.shape
    dim, npoints = points.shape
    outputs = targets.shape[0]
    block_len = npoints // block_rows
    own_rows = block_rows // n_cols
    own_len = own_rows * block_len
    nb = block_rows * n_rows
    n_sub = own_rows * n_rows
    capacity = -(-block_rows * slots // n_rows)
    direct_rows = n_rows <= DIRECT_ROWS
    parts = 2 if direct_rows else 1
    n_part = n_sub // parts
    bound = min(block_rows * n_part, n_cols * capacity * (n_rows + 1))
    n_groups = -(-bound // GROUP)
    list_len = -(-(n_groups * GROUP + GROUP + 1) // LANES) * LANES
    resident = parts * 2 * n_groups * GROUP * block_len * block_len <= RESIDENT_BYTES
    k_shape = (parts * n_groups, GROUP, block_len, block_len)
    limit = pltpu.CompilerParams(vmem_limit_bytes=(8 if resident else 32) * 1024 * 1024)
    ring = [] if resident else [
        pltpu.VMEM((RING, GROUP, block_len, block_len), BF16),
        pltpu.SemaphoreType.DMA((RING,)),
    ]
    k_spec = VMEM if resident else HBM
    cfg = Sizes(
        parts, n_groups, resident, nb, block_len, own_rows, block_rows, -(-own_rows * nb // LANES)
    )

    def shape(*dims, dtype=F32):
        return jax.ShapeDtypeStruct(dims, dtype)

    def own(x):
        return lax.dynamic_slice_in_dim(x, col * own_len, own_len, 1)

    def total_rows(x):
        if direct_rows:
            near = pair_sum([x] + [swap(x, "rows", d) for d in range(1, 4)])
            return near + swap(near, "rows", 4)
        return lax.psum(x, "rows")

    lists = direct_cols(block_list)
    names = jnp.arange(nb, dtype=jnp.int32)
    direct = sum(jnp.sum((x[:, :, None] == names).astype(jnp.int32), axis=1) for x in lists)
    own_counts = lax.dynamic_slice_in_dim(direct, col * own_rows, own_rows, 0)
    coded = own_counts.reshape(-1)
    coded = jnp.pad(coded, (0, dim * LANES - coded.shape[0])).reshape(dim, LANES).astype(BF16)
    packed = jnp.concatenate([own(points), coded], axis=1)
    own_t = own(targets)

    def build(part, *operands):
        first, last = part == 0, part == parts - 1
        out = [
            pltpu.VMEM(k_shape, BF16) if resident else shape(*k_shape, dtype=BF16),
            shape(1, list_len, dtype=jnp.int32),
            shape(n_sub if last else n_part, block_len),
        ]
        out += [shape(block_rows, block_len, 2 * dim, dtype=BF16)] if first else []
        k_mat, *rest = pl.pallas_call(
            functools.partial(build_kernel, cfg, part),
            out_shape=out,
            in_specs=[VMEM] + ([HBM, VMEM] if first else [VMEM] * 3 + [k_spec]),
            out_specs=[k_spec] + [VMEM] * (len(out) - 1),
            scratch_shapes=([
                pltpu.VMEM((dim, npoints), BF16),
                pltpu.SemaphoreType.DMA,
            ] if first else []) + [
                pltpu.SMEM((1, list_len), jnp.int32),
                pltpu.SMEM((list_len,), jnp.int32),
                pltpu.VMEM((n_part, 8, block_len), F32),
                pltpu.VMEM((n_part, 2 * dim, block_len), BF16),
                pltpu.VMEM((2, block_len, block_len), F32),
                pltpu.SMEM((block_rows, nb), jnp.int32),
                pltpu.VMEM((n_part // own_rows, cfg.count_rows, LANES), jnp.int32),
                pltpu.SMEM((n_part // own_rows, cfg.count_rows, LANES), jnp.int32),
                pltpu.SemaphoreType.DMA((3,)),
                *ring,
            ],
            compiler_params=limit,
            input_output_aliases={} if first else {4: 0},
            cost_estimate=pl.CostEstimate(
                flops=10 * 2 * 2 * dim * bound * block_len * block_len,
                bytes_accessed=10 * 2 * bound * block_len * block_len,
                transcendentals=10 * bound * block_len * block_len,
            ),
            name="build",
        )(direct, *operands)
        if resident:
            k_mat = pltpu.with_memory_space_constraint(k_mat, pltpu.VMEM)
        return k_mat, *rest

    near = pltpu.with_memory_space_constraint(points, pltpu.HBM)
    if direct_rows:
        packed, early_t = lax.optimization_barrier((packed, own_t))
        same, other = across_x(jnp.stack(along_z(packed)))
        t_same = along_z(early_t)
        k_mat, list0, degree, lhs = build(0, near, same)
        degree, other, *t_same = lax.optimization_barrier((degree, other, *t_same))
        t_same, t_other = across_x(jnp.stack(t_same))
        other, t_same = lax.optimization_barrier((other, t_same))
        k_mat, list1, degree = build(1, lhs, degree, other, k_mat)
        t_pieces, k_lists = [t_same, t_other], [list0, list1]
    else:
        k_mat, list0, degree, _ = build(0, near, lax.all_gather(packed, "rows"))
        t_pieces, k_lists = [lax.all_gather(own_t, "rows")], [list0]
    inv = 1.0 / jnp.sqrt(1.0 + total_rows(degree))

    def cost(n):
        return pl.CostEstimate(
            flops=2 * n * bound * outputs * block_len * block_len,
            bytes_accessed=n * bound * block_len * block_len,
            transcendentals=0,
        )

    near_z, near_y, cross_z, tail = pl.pallas_call(
        functools.partial(first_kernel, cfg),
        out_shape=[shape(outputs, own_len)] * 2 + [shape(2, outputs, own_len), shape(8, own_len)],
        in_specs=[k_spec] + [VMEM] * (2 * parts + 1),
        out_specs=[VMEM] * 4,
        scratch_shapes=[
            pltpu.VMEM((block_rows, outputs, block_len), F32),
            pltpu.VMEM((n_part, outputs, block_len), BF16),
            pltpu.SMEM((parts, 1, list_len), jnp.int32),
            pltpu.SemaphoreType.DMA((parts,)),
            *ring,
        ],
        compiler_params=limit,
        cost_estimate=cost(parts),
        name="first",
    )(k_mat, *k_lists, *t_pieces, inv)

    got = swap(cross_z, "cols", 1)
    half = jnp.concatenate([near_z + got[0], near_y + got[1], tail], axis=0)
    far = swap(half, "cols", 2)
    lo, hi, end = slice(0, outputs), slice(outputs, 2 * outputs), slice(2 * outputs, None)
    s1_own = jnp.stack([
        jnp.concatenate([(half[lo] + far[hi]) * tail[:1], tail], axis=0),
        jnp.concatenate([(half[hi] + far[lo]) * far[end][:1], far[end]], axis=0),
    ])
    s1_got = swap(s1_own, "cols", 1)
    held_t = pltpu.with_memory_space_constraint(targets, pltpu.VMEM)

    def second(part, dtype):
        return pl.pallas_call(
            functools.partial(second_kernel, cfg, part),
            out_shape=shape(n_part // own_rows, outputs, own_len, dtype=dtype),
            in_specs=[k_spec] + [VMEM] * 4,
            out_specs=VMEM,
            scratch_shapes=[
                pltpu.VMEM((n_part, outputs, block_len), F32),
                pltpu.VMEM((block_rows, outputs, block_len), BF16),
                pltpu.SMEM((1, list_len), jnp.int32),
                pltpu.SemaphoreType.DMA,
                *ring,
            ],
            compiler_params=limit,
            cost_estimate=cost(1),
            name="second",
        )(k_mat, k_lists[part], held_t, s1_own, s1_got)

    if direct_rows:
        g = ((s1_own[0, :outputs] - SHIFT * own_t) * tail[:1]).astype(BF16)
        parts_of_g = (g, swap(g, "rows", 2))
        z2_other = second(1, BF16)
        _, *parts_of_g = lax.optimization_barrier((z2_other, *parts_of_g))
        g = jnp.stack(parts_of_g)
        z2_other = swap(z2_other, "rows", 1)
        far_g = swap(g, "rows", 4)
        z2_same = second(0, F32)
        z2_same, z2_other, far_g = lax.optimization_barrier((z2_same, z2_other, far_g))
        row_piece = shape(outputs, own_len + LANES, dtype=BF16)
        own_z, own_dots, *sends = pl.pallas_call(
            functools.partial(meet_kernel, cfg),
            out_shape=[shape(outputs, own_len), shape(outputs, LANES, dtype=BF16)] + [row_piece] * 3,
            in_specs=[VMEM] * 7,
            out_specs=[VMEM] * 5,
            compiler_params=limit,
            name="meet",
        )(z2_same, z2_other, t_pieces[0], inv, s1_own, g, far_g)
        got = [swap(sends[n], "rows", 2 * n + 2) for n in (2, 1, 0)]
        ends, dots = pl.pallas_call(
            product_kernel,
            out_shape=(shape(outputs, own_len + LANES), shape(outputs, LANES)),
            in_specs=[VMEM] * 6,
            out_specs=(VMEM, VMEM),
            compiler_params=limit,
            name="products",
        )(own_z, own_dots, s1_own, *got)
        far = both_swap(dots, 1, 2)
        across = swap(dots, "rows", 1)
        ends_y = swap(ends, "cols", 2)
        dots = (dots + across) + (ends_y[:, own_len:] + far)
    else:
        z2 = lax.psum_scatter(second(0, F32), "rows", scatter_dimension=0)
        grown = z2 * tail[:1]
        own_s1 = s1_own[0, :outputs]
        own_t, s2 = own(targets), grown + SHIFT * own_s1
        dots = [(own_t, own_t), (own_t, own_s1), (own_s1, own_s1), (own_t, s2), (own_s1, s2)]
        dots = jnp.stack([jnp.sum(x * y, axis=1) for x, y in dots], axis=1)
        dots = lax.psum(jnp.pad(dots, ((0, 0), (0, LANES - N_DOTS))), "rows")
        ends = jnp.concatenate([grown, dots], axis=1)
        ends_y = swap(ends, "cols", 2)
        dots = dots + ends_y[:, own_len:]
    ends = jnp.stack([jnp.concatenate([ends[:, :own_len], dots], axis=1), ends_y])
    ends = (s1_own, s1_got, ends, swap(ends, "cols", 1))
    ends = [pltpu.with_memory_space_constraint(x, pltpu.VMEM) for x in ends]

    return pl.pallas_call(
        final_kernel,
        out_shape=(shape(outputs, npoints), shape(outputs, npoints)),
        in_specs=[VMEM] * 5,
        out_specs=(HBM, HBM),
        scratch_shapes=[
            pltpu.VMEM((4, outputs, own_len), F32),
            pltpu.VMEM((4, outputs, own_len), F32),
            pltpu.SemaphoreType.DMA((2, 4)),
        ],
        compiler_params=limit,
        name="final",
    )(held_t, *ends)


def solution(mesh):
    placed = (P("rows", "cols"), P(None, "rows"), P(None, "rows"))
    return jax.shard_map(
        local,
        mesh=mesh,
        in_specs=placed,
        out_specs=(P(None, "rows"), P(None, "rows")),
        check_vma=False,
    )
```

```python
import functools
from typing import NamedTuple

import jax
import jax.numpy as jnp
from jax import lax
from jax.experimental import pallas as pl
from jax.experimental.pallas import tpu as pltpu
from jax.sharding import PartitionSpec as P

REG = 1.5
RADIUS = 0.25
GROUP_BITS = 2
GROUP = 1 << GROUP_BITS
CODE_BITS = 12
CODE = 1 << CODE_BITS
RING = 3
STRIP = 64
LANES = 128
TINY = 1e-30
SHIFT = 0.375
DIRECT_ROWS = 8
RESIDENT_BYTES = 20 * 1024 * 1024

VMEM = pl.BlockSpec(memory_space=pltpu.VMEM)
HBM = pl.BlockSpec(memory_space=pltpu.HBM)
F32 = jnp.float32
BF16 = jnp.bfloat16


def pair_sum(parts):
    while len(parts) > 1:
        parts = [a + b for a, b in zip(parts[::2], parts[1::2])]
    return parts[0]


def position():
    return lax.axis_index("rows"), lax.axis_index("cols")


class Sizes(NamedTuple):
    parts: int
    part_groups: int
    resident: bool
    nb: int
    block_len: int
    own_rows: int
    block_rows: int
    count_rows: int


def augment(x, first_ones):
    dim, n = x.shape
    norm = jnp.sum(x * x, axis=0, keepdims=True) / (RADIUS * RADIUS)
    high = norm.astype(BF16).astype(F32)
    rest = norm - high
    mid = rest.astype(BF16).astype(F32)
    low = rest - mid
    line = lax.broadcasted_iota(jnp.int32, (dim, n), 0)
    base = 3 if first_ones else 0
    ones_at = 0 if first_ones else 3
    tail = jnp.where((line >= ones_at) & (line < ones_at + 3), 1.0, 0.0)
    tail = jnp.where(line == base, high, tail)
    tail = jnp.where(line == base + 1, mid, tail)
    tail = jnp.where(line == base + 2, low, tail)
    return tail


def row_of(cfg, place, part, z):
    if cfg.parts == 1:
        return z
    return 2 * z + (place[0] & 1 if part == 0 else 1 - (place[0] & 1))


def slot_of(cfg, place, n):
    return n if cfg.parts == 1 else lax.shift_right_logical(place[0], 1) ^ n


def build_kernel(cfg, part, direct_v, *refs):
    last = part == cfg.parts - 1
    place = position()
    if part == 0:
        near_hbm, piece, refs = refs[0], refs[1], refs[2:]
        k_mat, list_v, deg_ref, lhs = refs[:4]
        near_ref, near_sem, refs = refs[4], refs[5], refs[6:]
        near_copy = pltpu.make_async_copy(near_hbm, near_ref, near_sem)
        near_copy.start()
    else:
        lhs, first_deg, piece, _ = refs[:4]
        k_mat, list_v, deg_ref = refs[4:7]
        refs = refs[7:]
    listed, mlist, acc, rhs, dist, direct, counts_v, counts, copy_sems = refs[:9]
    kbuf, sems = (None, None) if cfg.resident else refs[9:]
    direct_copy = pltpu.make_async_copy(direct_v, direct, copy_sems.at[0])
    direct_copy.start()
    row, col = place[0], place[1]
    own_rows, block_len, nb = cfg.own_rows, cfg.block_len, cfg.nb
    own_len = own_rows * block_len
    dim, held = piece.shape[1], piece.shape[0]
    scale = 1.0 / (RADIUS * RADIUS)

    def count(n, carry):
        named = piece[n, :, own_len:own_len + LANES]
        counts_v[slot_of(cfg, place, n)] = named.astype(F32)[:cfg.count_rows].astype(jnp.int32)
        return carry

    def prepare(n, carry):
        z = slot_of(cfg, place, n)
        for k in range(own_rows):
            far = piece[n, :, k * block_len:(k + 1) * block_len]
            rhs[z * own_rows + k, :dim, :] = far
            rhs[z * own_rows + k, dim:, :] = augment(far.astype(F32), False).astype(BF16)
        return carry

    lax.fori_loop(0, held, count, 0, unroll=held <= 4)
    fetch = pltpu.make_async_copy(counts_v, counts, copy_sems.at[1])
    fetch.start()
    lax.fori_loop(0, held, prepare, 0, unroll=held <= 4)
    acc[...] = jnp.zeros_like(acc)
    if part == 0:
        near_copy.wait()
        for i in range(cfg.block_rows):
            near = near_ref[:, i * block_len:(i + 1) * block_len].astype(F32)
            full = jnp.concatenate([near * (-2.0 * scale), augment(near, True)], axis=0)
            lhs[i] = full.T.astype(BF16)
    direct_copy.wait()
    fetch.wait()

    pos = jnp.int32(0)
    for i in range(cfg.block_rows):
        me = row * cfg.block_rows + i
        spots = [k * nb + me for k in range(own_rows)]
        spots = [(lax.shift_right_logical(p, 7), p & (LANES - 1)) for p in spots]

        def note(z, at, i=i, me=me, spots=spots):
            for k in range(own_rows):
                name = row_of(cfg, place, part, z) * cfg.block_rows + col * own_rows + k
                m = direct[i, name] + jnp.where(name == me, 0, counts[z, spots[k][0], spots[k][1]])
                listed[0, at + 1] = i * CODE + z * own_rows + k
                mlist[at] = m
                at = at + jnp.where(m > 0, 1, 0)
            return at

        if held <= 4:
            for z in range(held):
                pos = note(z, pos)
        else:
            pos = lax.fori_loop(0, held, note, pos, unroll=4)
    for u in range(GROUP):
        listed[0, pos + u + 1] = 0
        mlist[pos + u] = 0
    total = lax.shift_right_logical(pos + (GROUP - 1), GROUP_BITS)
    listed[0, 0] = total
    list_copy = pltpu.make_async_copy(listed, list_v, copy_sems.at[2])
    list_copy.start()

    def copy_out(g):
        slot = lax.rem(g, RING)
        return pltpu.make_async_copy(kbuf.at[slot], k_mat.at[g], sems.at[slot])

    base = part * cfg.part_groups

    def distances(e, slot):
        code = listed[0, e + 1]
        i, j = lax.shift_right_logical(code, CODE_BITS), code & (CODE - 1)
        dist[slot] = jnp.dot(lhs[i], rhs[j], preferred_element_type=F32)

    distances(0, 0)

    def step(g, carry):
        slot, target = (base + g, k_mat) if cfg.resident else (lax.rem(g, RING), kbuf)
        if not cfg.resident:

            @pl.when(g >= RING)
            def _():
                copy_out(g - RING).wait()

        for u in range(GROUP):
            distances(g * GROUP + u + 1, (u + 1) % 2)
            j = listed[0, g * GROUP + u + 1] & (CODE - 1)
            m = mlist[g * GROUP + u].astype(F32)
            sums = jnp.zeros((8, block_len), F32)
            for s in range(block_len // STRIP):
                rows = slice(s * STRIP, (s + 1) * STRIP)
                d = jnp.maximum(dist[u % 2, rows, :], TINY)
                sc = d * lax.rsqrt(d)
                rem = jnp.maximum(1.0 - sc, 0.0)
                sq = rem * rem
                val = (sq * sq) * (sc * (4.0 * m) + m)
                target[slot, u, rows, :] = val.astype(BF16)
                for h in range(0, STRIP, 8):
                    sums = sums + val[h:h + 8]
            acc[j] += sums
        if not cfg.resident:
            copy_out(g).start()
        return carry

    lax.fori_loop(0, total, step, 0)
    if cfg.parts == 1 or not last:
        deg_ref[...] = jnp.sum(acc[...], axis=1)
    else:
        second = jnp.sum(acc[...], axis=1)
        for z in range(held):
            rows = slice(z * own_rows, (z + 1) * own_rows)
            for p, deg in enumerate((first_deg[rows, :], second[rows])):
                at = row_of(cfg, place, p, z) * own_rows
                for k in range(own_rows):
                    deg_ref[pl.ds(at + k, 1), :] = deg[k:k + 1]

    def drain(g, carry):
        copy_out(g).wait()
        return carry

    if not cfg.resident:
        lax.fori_loop(jnp.maximum(total - RING, 0), total, drain, 0)
    list_copy.wait()


def pieces_of(own, got):
    return own.at[0], got.at[0], own.at[1], got.at[1]


def walk(cfg, part, listed, k_mat, kbuf, sems, product, total_ref, by_row):
    total = listed[0, 0]
    base = part * cfg.part_groups

    def copy_in(g):
        slot = lax.rem(g, RING)
        return pltpu.make_async_copy(k_mat.at[g], kbuf.at[slot], sems.at[slot])

    if not cfg.resident:
        for p in range(RING - 1):

            @pl.when(p < total)
            def _(p=p):
                copy_in(p).start()

    def step(g, carry):
        slot, source = (base + g, k_mat) if cfg.resident else (lax.rem(g, RING), kbuf)
        if not cfg.resident:

            @pl.when(g + (RING - 1) < total)
            def _():
                copy_in(g + (RING - 1)).start()

            copy_in(g).wait()
        codes = [listed[0, g * GROUP + u + 1] for u in range(GROUP)]
        pairs = [(lax.shift_right_logical(code, CODE_BITS), code & (CODE - 1)) for code in codes]
        terms = [product(i, j, source[slot, u]) for u, (i, j) in enumerate(pairs)]
        add(carry)
        return [i if by_row else j for i, j in pairs], terms

    def add(carry):
        for at, term in zip(*carry):
            total_ref[at] += term

    none = [jnp.int32(0)] * GROUP, [jnp.zeros(total_ref.shape[1:], F32)] * GROUP
    add(lax.fori_loop(0, total, step, none))


def first_kernel(cfg, k_mat, *refs):
    n = cfg.parts
    lists, pieces, inv_ref, refs = refs[:n], refs[n:2 * n], refs[2 * n], refs[2 * n + 1:]
    near, near_y, cross, own_inv, z_acc, w_all, listed, list_sems, *ring = refs
    kbuf, sems = ring or (None, None)
    place = position()
    col = place[1]
    copies = [
        pltpu.make_async_copy(lists[p], listed.at[p], list_sems.at[p]) for p in range(n)
    ]
    for copy in copies:
        copy.start()
    own_rows, block_len = cfg.own_rows, cfg.block_len
    z_acc[...] = jnp.zeros_like(z_acc)
    for part, piece in enumerate(pieces):
        held = piece.shape[0]

        def prepare(m, carry, part=part, piece=piece):
            z = slot_of(cfg, place, m)
            for k in range(own_rows):
                w = piece[m, :, k * block_len:(k + 1) * block_len]
                at = row_of(cfg, place, part, z) * own_rows + k
                w_all[z * own_rows + k] = (w * inv_ref[pl.ds(at, 1), :]).astype(BF16)
            return carry

        lax.fori_loop(0, held, prepare, 0, unroll=held <= 4)

        def product(i, j, block):
            return lax.dot_general(
                w_all[j], block, (((1,), (1,)), ((), ())), preferred_element_type=F32
            )

        copies[part].wait()
        walk(cfg, part, listed.at[part], k_mat, kbuf, sems, product, z_acc, True)
    for k in range(own_rows):
        cols = slice(k * block_len, (k + 1) * block_len)
        mine = inv_ref[pl.ds(place[0] * own_rows + k, 1), :]
        own_inv[:, cols] = jnp.broadcast_to(mine, (8, block_len))
        for e, ref in enumerate((near, cross.at[0], near_y, cross.at[1])):
            ref[:, cols] = z_acc[(col ^ e) * own_rows + k]


def terms_of(v, n):
    out = []
    for _ in range(n):
        out.append(v.astype(BF16))
        v = v - out[-1].astype(F32)
    return out


def part_kernel(near, near_y, got, tail, send, lo_ref, hi_ref):
    outputs = near.shape[0]
    hi = (near_y[...] + got[1]).astype(BF16)
    lo = terms_of(near[...] + got[0], 2)
    for n, v in enumerate((hi, *lo)):
        send[n * outputs:(n + 1) * outputs, :] = v
    hi_ref[...] = hi.astype(F32)
    lo_ref[...] = lo[0].astype(F32) + lo[1].astype(F32)
    line = lax.broadcasted_iota(jnp.int32, (16, tail.shape[1]), 0)
    rows = jnp.zeros(line.shape, F32)
    for n, v in enumerate(terms_of(tail[0:1, :], 3)):
        rows = jnp.where(line == n, v.astype(F32), rows)
    send[3 * outputs:, :] = rows.astype(BF16)


def join_kernel(lo_ref, hi_ref, tail, far, t_ref, s1_ref, g_ref):
    outputs = lo_ref.shape[0]
    far_hi, far_a, far_b = (far[n * outputs:(n + 1) * outputs, :].astype(F32) for n in range(3))
    rows = far[3 * outputs:, :].astype(F32)
    far_inv = (rows[0:1] + rows[1:2]) + rows[2:3]
    inv = tail[0:1, :]
    s1 = (lo_ref[...] + far_hi) * inv
    s1_ref[0, :outputs, :] = s1
    s1_ref[0, outputs:, :] = tail[...]
    s1_ref[1, :outputs, :] = ((far_a + far_b) + hi_ref[...]) * far_inv
    s1_ref[1, outputs:, :] = jnp.broadcast_to(far_inv, tail.shape)
    g_ref[...] = ((s1 - SHIFT * t_ref[...]) * inv).astype(BF16)


def second_kernel(cfg, part, k_mat, list_v, t_ref, s1_own, s1_got, out, z_acc, w_all, listed, list_sem, *ring):
    kbuf, sems = ring or (None, None)
    place = position()
    own_rows, block_len = cfg.own_rows, cfg.block_len
    outputs = t_ref.shape[0]
    list_copy = pltpu.make_async_copy(list_v, listed, list_sem)
    list_copy.start()
    for e, packed in enumerate(pieces_of(s1_own, s1_got)):
        share = place[1] ^ e
        for k in range(own_rows):
            cols = slice(k * block_len, (k + 1) * block_len)
            i = share * own_rows + k
            t = t_ref[:, pl.ds(pl.multiple_of(i * block_len, LANES), block_len)]
            g = (packed[:outputs, cols] - SHIFT * t) * packed[outputs:outputs + 1, cols]
            w_all[i] = g.astype(BF16)
    z_acc[...] = jnp.zeros_like(z_acc)

    def product(i, j, block):
        return jnp.dot(w_all[i], block, preferred_element_type=F32)

    list_copy.wait()
    walk(cfg, part, listed, k_mat, kbuf, sems, product, z_acc, False)

    def hand_out(m, carry):
        z = slot_of(cfg, place, m)
        for k in range(own_rows):
            out[m, :, k * block_len:(k + 1) * block_len] = z_acc[z * own_rows + k].astype(out.dtype)
        return carry

    held = out.shape[0]
    lax.fori_loop(0, held, hand_out, 0, unroll=held <= 4)


N_DOTS = 5


def meet_kernel(cfg, z_same, z_other, t_same, inv_ref, s1_own, *refs):
    g_near, g_far, own_z, own_dots, *outs = refs
    gs = g_near[0], g_near[1], g_far[0], g_far[1]
    own_rows, block_len = cfg.own_rows, cfg.block_len
    outputs, own_len = own_z.shape
    place = position()
    tz = jnp.zeros((outputs, 1), F32)
    gz = jnp.zeros((outputs, 1), F32)
    for n in range(4):
        z = z_same[n] + z_other[n].astype(F32)
        if n == 0:
            own_z[...] = z
        else:
            outs[n - 1][:, :own_len] = z.astype(BF16)
        gz += jnp.sum(gs[n].astype(F32) * z, axis=1, keepdims=True)
        at = row_of(cfg, place, 0, slot_of(cfg, place, n)) * own_rows
        for k in range(own_rows):
            cols = slice(k * block_len, (k + 1) * block_len)
            scaled = t_same[n, :, cols] * inv_ref[pl.ds(at + k, 1), :]
            tz += jnp.sum(scaled * z[:, cols], axis=1, keepdims=True)
    t, s1 = t_same[0], s1_own[0, :outputs, :]
    tt = jnp.sum(t * t, axis=1, keepdims=True)
    ts1 = jnp.sum(t * s1, axis=1, keepdims=True)
    s1s1 = jnp.sum(s1 * s1, axis=1, keepdims=True)
    dots = (tt, ts1, s1s1, tz + SHIFT * ts1, gz + SHIFT * (tz + s1s1))
    lane = lax.broadcasted_iota(jnp.int32, (outputs, LANES), 1)
    tile = jnp.zeros(lane.shape, F32)
    for n, v in enumerate(dots):
        for part in range(3):
            head = v.astype(BF16).astype(F32)
            tile = jnp.where(lane == part * N_DOTS + n, head, tile)
            v = v - head
    own_dots[...] = tile.astype(BF16)
    for out in outs:
        out[:, own_len:] = tile.astype(BF16)


def product_kernel(own_z, own_dots, s1_own, *refs):
    got, end_ref, dot_ref = refs[2::-1], refs[3], refs[4]
    outputs, own_len = own_z.shape
    z = own_z[...]
    for ref in got:
        z = z + ref[:, :own_len].astype(F32)
    end_ref[:, :own_len] = z * s1_own[0, outputs:outputs + 1, :]
    tiles = [own_dots[...]] + [ref[:, own_len:] for ref in got]
    total = pair_sum([tile.astype(F32) for tile in tiles])
    out = total
    for part in range(1, 3):
        out = out + pltpu.roll(total, LANES - part * N_DOTS, 1)
    dot_ref[...] = out
    end_ref[:, own_len:] = out


def final_kernel(t_ref, s1_own, s1_got, *refs):
    ends = pieces_of(refs[0], refs[1])
    sol_hbm, res_hbm, sol_ref, res_ref, sems = refs[2:]
    s1s = pieces_of(s1_own, s1_got)
    outputs, own_len = ends[0].shape[0], ends[0].shape[1] - LANES
    place = position()
    dots = ends[0][:, own_len:] + ends[1][:, own_len:]
    tt, ts1, s1s1, ts2, s1s2 = (dots[:, n:n + 1] for n in range(5))
    a1 = tt / (REG * tt + ts1)
    p = 1.0 - REG * a1
    new = p * p * tt - 2.0 * p * a1 * ts1 + a1 * a1 * s1s1
    u = p + new / tt
    dd = u * u * tt - 2.0 * u * a1 * ts1 + a1 * a1 * s1s1
    dmd = u * u * ts1 - u * a1 * (s1s1 + ts2) + a1 * a1 * s1s2
    a2 = new / (REG * dd + dmd)
    sol_t, sol_1 = a1 + a2 * u, a2 * a1
    res_t, res_1 = p - a2 * REG * u, a1 + a2 * (u - REG * a1)
    copies = []
    for e in range(4):
        at = pl.ds(pl.multiple_of((place[1] ^ e) * own_len, LANES), own_len)
        t, s1 = t_ref[:, at], s1s[e][:outputs, :]
        s2 = ends[e][:, :own_len] + SHIFT * s1
        sol_ref[e] = sol_t * t - sol_1 * s1
        res_ref[e] = res_t * t - res_1 * s1 + sol_1 * s2
        for n, (ref, hbm) in enumerate(((sol_ref, sol_hbm), (res_ref, res_hbm))):
            copy = pltpu.make_async_copy(ref.at[e], hbm.at[:, at], sems.at[n, e])
            copy.start()
            copies.append(copy)
    for copy in copies:
        copy.wait()


def swap(x, axis, d):
    size = lax.axis_size(axis)
    return lax.ppermute(x, axis, [(i, i ^ d) for i in range(size)])


def both_swap(x, row_d, col_d):
    n_rows, n_cols = lax.axis_size("rows"), lax.axis_size("cols")
    pairs = [
        (r * n_cols + c, (r ^ row_d) * n_cols + (c ^ col_d))
        for r in range(n_rows)
        for c in range(n_cols)
    ]
    return lax.ppermute(x, ("rows", "cols"), pairs)


def along_z(x):
    return [x] + [swap(x, "rows", d) for d in range(2, lax.axis_size("rows"), 2)]


def across_x(same):
    return [same, swap(same, "rows", 1)]


def direct_cols(x):
    return [x] + [swap(x, "cols", e) for e in range(1, 4)]


def local(block_list, points, targets):
    n_rows = lax.axis_size("rows")
    n_cols = lax.axis_size("cols")
    row = lax.axis_index("rows")
    col = lax.axis_index("cols")
    block_rows, slots = block_list.shape
    dim, npoints = points.shape
    outputs = targets.shape[0]
    block_len = npoints // block_rows
    own_rows = block_rows // n_cols
    own_len = own_rows * block_len
    nb = block_rows * n_rows
    n_sub = own_rows * n_rows
    capacity = -(-block_rows * slots // n_rows)
    direct_rows = n_rows <= DIRECT_ROWS
    parts = 2 if direct_rows else 1
    n_part = n_sub // parts
    bound = min(block_rows * n_part, n_cols * capacity * (n_rows + 1))
    n_groups = -(-bound // GROUP)
    list_len = -(-(n_groups * GROUP + GROUP + 1) // LANES) * LANES
    resident = parts * 2 * n_groups * GROUP * block_len * block_len <= RESIDENT_BYTES
    k_shape = (parts * n_groups, GROUP, block_len, block_len)
    limit = pltpu.CompilerParams(vmem_limit_bytes=(8 if resident else 32) * 1024 * 1024)
    ring = [] if resident else [
        pltpu.VMEM((RING, GROUP, block_len, block_len), BF16),
        pltpu.SemaphoreType.DMA((RING,)),
    ]
    k_spec = VMEM if resident else HBM
    cfg = Sizes(
        parts, n_groups, resident, nb, block_len, own_rows, block_rows, -(-own_rows * nb // LANES)
    )

    def shape(*dims, dtype=F32):
        return jax.ShapeDtypeStruct(dims, dtype)

    def own(x):
        return lax.dynamic_slice_in_dim(x, col * own_len, own_len, 1)

    def total_rows(x):
        if direct_rows:
            near = pair_sum([x] + [swap(x, "rows", d) for d in range(1, 4)])
            return near + swap(near, "rows", 4)
        return lax.psum(x, "rows")

    lists = direct_cols(block_list)
    names = jnp.arange(nb, dtype=jnp.int32)
    direct = sum(jnp.sum((x[:, :, None] == names).astype(jnp.int32), axis=1) for x in lists)
    own_counts = lax.dynamic_slice_in_dim(direct, col * own_rows, own_rows, 0)
    coded = own_counts.reshape(-1)
    coded = jnp.pad(coded, (0, dim * LANES - coded.shape[0])).reshape(dim, LANES).astype(BF16)
    packed = jnp.concatenate([own(points), coded], axis=1)
    own_t = own(targets)

    def build(part, *operands):
        first, last = part == 0, part == parts - 1
        out = [
            pltpu.VMEM(k_shape, BF16) if resident else shape(*k_shape, dtype=BF16),
            shape(1, list_len, dtype=jnp.int32),
            shape(n_sub if last else n_part, block_len),
        ]
        out += [shape(block_rows, block_len, 2 * dim, dtype=BF16)] if first else []
        k_mat, *rest = pl.pallas_call(
            functools.partial(build_kernel, cfg, part),
            out_shape=out,
            in_specs=[VMEM] + ([HBM, VMEM] if first else [VMEM] * 3 + [k_spec]),
            out_specs=[k_spec] + [VMEM] * (len(out) - 1),
            scratch_shapes=([
                pltpu.VMEM((dim, npoints), BF16),
                pltpu.SemaphoreType.DMA,
            ] if first else []) + [
                pltpu.SMEM((1, list_len), jnp.int32),
                pltpu.SMEM((list_len,), jnp.int32),
                pltpu.VMEM((n_part, 8, block_len), F32),
                pltpu.VMEM((n_part, 2 * dim, block_len), BF16),
                pltpu.VMEM((2, block_len, block_len), F32),
                pltpu.SMEM((block_rows, nb), jnp.int32),
                pltpu.VMEM((n_part // own_rows, cfg.count_rows, LANES), jnp.int32),
                pltpu.SMEM((n_part // own_rows, cfg.count_rows, LANES), jnp.int32),
                pltpu.SemaphoreType.DMA((3,)),
                *ring,
            ],
            compiler_params=limit,
            input_output_aliases={} if first else {4: 0},
            cost_estimate=pl.CostEstimate(
                flops=10 * 2 * 2 * dim * bound * block_len * block_len,
                bytes_accessed=10 * 2 * bound * block_len * block_len,
                transcendentals=10 * bound * block_len * block_len,
            ),
            name="build",
        )(direct, *operands)
        if resident:
            k_mat = pltpu.with_memory_space_constraint(k_mat, pltpu.VMEM)
        return k_mat, *rest

    near = pltpu.with_memory_space_constraint(points, pltpu.HBM)
    if direct_rows:
        packed, early_t = lax.optimization_barrier((packed, own_t))
        same, other = across_x(jnp.stack(along_z(packed)))
        t_same = along_z(early_t)
        k_mat, list0, degree, lhs = build(0, near, same)
        degree, other, *t_same = lax.optimization_barrier((degree, other, *t_same))
        t_same, t_other = across_x(jnp.stack(t_same))
        other, t_same = lax.optimization_barrier((other, t_same))
        k_mat, list1, degree = build(1, lhs, degree, other, k_mat)
        t_pieces, k_lists = [t_same, t_other], [list0, list1]
    else:
        k_mat, list0, degree, _ = build(0, near, lax.all_gather(packed, "rows"))
        t_pieces, k_lists = [lax.all_gather(own_t, "rows")], [list0]
    inv = 1.0 / jnp.sqrt(1.0 + total_rows(degree))

    def cost(n):
        return pl.CostEstimate(
            flops=2 * n * bound * outputs * block_len * block_len,
            bytes_accessed=n * bound * block_len * block_len,
            transcendentals=0,
        )

    near_z, near_y, cross_z, tail = pl.pallas_call(
        functools.partial(first_kernel, cfg),
        out_shape=[shape(outputs, own_len)] * 2 + [shape(2, outputs, own_len), shape(8, own_len)],
        in_specs=[k_spec] + [VMEM] * (2 * parts + 1),
        out_specs=[VMEM] * 4,
        scratch_shapes=[
            pltpu.VMEM((block_rows, outputs, block_len), F32),
            pltpu.VMEM((n_part, outputs, block_len), BF16),
            pltpu.SMEM((parts, 1, list_len), jnp.int32),
            pltpu.SemaphoreType.DMA((parts,)),
            *ring,
        ],
        compiler_params=limit,
        cost_estimate=cost(parts),
        name="first",
    )(k_mat, *k_lists, *t_pieces, inv)

    got = swap(cross_z, "cols", 1)
    send, lo, hi = pl.pallas_call(
        part_kernel,
        out_shape=[shape(3 * outputs + 16, own_len, dtype=BF16)] + [shape(outputs, own_len)] * 2,
        in_specs=[VMEM] * 4,
        out_specs=[VMEM] * 3,
        compiler_params=limit,
        name="part",
    )(near_z, near_y, got, tail)
    s1_own, g = pl.pallas_call(
        join_kernel,
        out_shape=(shape(2, outputs + 8, own_len), shape(outputs, own_len, dtype=BF16)),
        in_specs=[VMEM] * 5,
        out_specs=(VMEM, VMEM),
        compiler_params=limit,
        name="join",
    )(lo, hi, tail, swap(send, "cols", 2), own_t)
    s1_got = swap(s1_own, "cols", 1)
    held_t = pltpu.with_memory_space_constraint(targets, pltpu.VMEM)

    def second(part, dtype):
        return pl.pallas_call(
            functools.partial(second_kernel, cfg, part),
            out_shape=shape(n_part // own_rows, outputs, own_len, dtype=dtype),
            in_specs=[k_spec] + [VMEM] * 4,
            out_specs=VMEM,
            scratch_shapes=[
                pltpu.VMEM((n_part, outputs, block_len), F32),
                pltpu.VMEM((block_rows, outputs, block_len), BF16),
                pltpu.SMEM((1, list_len), jnp.int32),
                pltpu.SemaphoreType.DMA,
                *ring,
            ],
            compiler_params=limit,
            cost_estimate=cost(1),
            name="second",
        )(k_mat, k_lists[part], held_t, s1_own, s1_got)

    if direct_rows:
        parts_of_g = (g, swap(g, "rows", 2))
        z2_other = second(1, BF16)
        _, *parts_of_g = lax.optimization_barrier((z2_other, *parts_of_g))
        g = jnp.stack(parts_of_g)
        z2_other = swap(z2_other, "rows", 1)
        far_g = swap(g, "rows", 4)
        z2_same = second(0, F32)
        z2_same, z2_other, far_g = lax.optimization_barrier((z2_same, z2_other, far_g))
        row_piece = shape(outputs, own_len + LANES, dtype=BF16)
        own_z, own_dots, *sends = pl.pallas_call(
            functools.partial(meet_kernel, cfg),
            out_shape=[shape(outputs, own_len), shape(outputs, LANES, dtype=BF16)] + [row_piece] * 3,
            in_specs=[VMEM] * 7,
            out_specs=[VMEM] * 5,
            compiler_params=limit,
            name="meet",
        )(z2_same, z2_other, t_pieces[0], inv, s1_own, g, far_g)
        got = [swap(sends[n], "rows", 2 * n + 2) for n in (2, 1, 0)]
        ends, dots = pl.pallas_call(
            product_kernel,
            out_shape=(shape(outputs, own_len + LANES), shape(outputs, LANES)),
            in_specs=[VMEM] * 6,
            out_specs=(VMEM, VMEM),
            compiler_params=limit,
            name="products",
        )(own_z, own_dots, s1_own, *got)
        far = both_swap(dots, 1, 2)
        across = swap(dots, "rows", 1)
        ends_y = swap(ends, "cols", 2)
        dots = (dots + across) + (ends_y[:, own_len:] + far)
    else:
        z2 = lax.psum_scatter(second(0, F32), "rows", scatter_dimension=0)
        grown = z2 * tail[:1]
        own_s1 = s1_own[0, :outputs]
        s2 = grown + SHIFT * own_s1
        dots = [(own_t, own_t), (own_t, own_s1), (own_s1, own_s1), (own_t, s2), (own_s1, s2)]
        dots = jnp.stack([jnp.sum(x * y, axis=1) for x, y in dots], axis=1)
        dots = lax.psum(jnp.pad(dots, ((0, 0), (0, LANES - N_DOTS))), "rows")
        ends = jnp.concatenate([grown, dots], axis=1)
        ends_y = swap(ends, "cols", 2)
        dots = dots + ends_y[:, own_len:]
    ends = jnp.stack([jnp.concatenate([ends[:, :own_len], dots], axis=1), ends_y])
    ends = (s1_own, s1_got, ends, swap(ends, "cols", 1))
    ends = [pltpu.with_memory_space_constraint(x, pltpu.VMEM) for x in ends]

    return pl.pallas_call(
        final_kernel,
        out_shape=(shape(outputs, npoints), shape(outputs, npoints)),
        in_specs=[VMEM] * 5,
        out_specs=(HBM, HBM),
        scratch_shapes=[
            pltpu.VMEM((4, outputs, own_len), F32),
            pltpu.VMEM((4, outputs, own_len), F32),
            pltpu.SemaphoreType.DMA((2, 4)),
        ],
        compiler_params=limit,
        name="final",
    )(held_t, *ends)


def solution(mesh):
    placed = (P("rows", "cols"), P(None, "rows"), P(None, "rows"))
    return jax.shard_map(
        local,
        mesh=mesh,
        in_specs=placed,
        out_specs=(P(None, "rows"), P(None, "rows")),
        check_vma=False,
    )
```

```python
import functools
from typing import NamedTuple

import jax
import jax.numpy as jnp
from jax import lax
from jax.experimental import pallas as pl
from jax.experimental.pallas import tpu as pltpu
from jax.sharding import PartitionSpec as P

REG = 1.5
RADIUS = 0.25
GROUP_BITS = 2
GROUP = 1 << GROUP_BITS
CODE_BITS = 12
CODE = 1 << CODE_BITS
RING = 3
STRIP = 128
LANES = 128
TINY = 1e-30
SHIFT = 0.375
DIRECT_ROWS = 8
RESIDENT_BYTES = 20 * 1024 * 1024

VMEM = pl.BlockSpec(memory_space=pltpu.VMEM)
HBM = pl.BlockSpec(memory_space=pltpu.HBM)
F32 = jnp.float32
BF16 = jnp.bfloat16


def pair_sum(parts):
    while len(parts) > 1:
        parts = [a + b for a, b in zip(parts[::2], parts[1::2])]
    return parts[0]


def position():
    return lax.axis_index("rows"), lax.axis_index("cols")


class Sizes(NamedTuple):
    parts: int
    part_groups: int
    resident: bool
    nb: int
    block_len: int
    own_rows: int
    block_rows: int
    count_rows: int


def augment(x, first_ones):
    dim, n = x.shape
    norm = jnp.sum(x * x, axis=0, keepdims=True) / (RADIUS * RADIUS)
    high = norm.astype(BF16).astype(F32)
    rest = norm - high
    mid = rest.astype(BF16).astype(F32)
    low = rest - mid
    line = lax.broadcasted_iota(jnp.int32, (dim, n), 0)
    base = 3 if first_ones else 0
    ones_at = 0 if first_ones else 3
    tail = jnp.where((line >= ones_at) & (line < ones_at + 3), 1.0, 0.0)
    tail = jnp.where(line == base, high, tail)
    tail = jnp.where(line == base + 1, mid, tail)
    tail = jnp.where(line == base + 2, low, tail)
    return tail


def row_of(cfg, place, part, z):
    if cfg.parts == 1:
        return z
    return 2 * z + (place[0] & 1 if part == 0 else 1 - (place[0] & 1))


def slot_of(cfg, place, n):
    return n if cfg.parts == 1 else lax.shift_right_logical(place[0], 1) ^ n


def build_kernel(cfg, part, direct_v, *refs):
    last = part == cfg.parts - 1
    place = position()
    if part == 0:
        near_hbm, piece, refs = refs[0], refs[1], refs[2:]
        k_mat, list_v, deg_ref, lhs = refs[:4]
        near_ref, near_sem, refs = refs[4], refs[5], refs[6:]
        near_copy = pltpu.make_async_copy(near_hbm, near_ref, near_sem)
        near_copy.start()
    else:
        lhs, first_deg, piece, _ = refs[:4]
        k_mat, list_v, deg_ref = refs[4:7]
        refs = refs[7:]
    listed, mlist, acc, rhs, dist, direct, counts_v, counts, copy_sems = refs[:9]
    kbuf, sems = (None, None) if cfg.resident else refs[9:]
    direct_copy = pltpu.make_async_copy(direct_v, direct, copy_sems.at[0])
    direct_copy.start()
    row, col = place[0], place[1]
    own_rows, block_len, nb = cfg.own_rows, cfg.block_len, cfg.nb
    own_len = own_rows * block_len
    dim, held = piece.shape[1], piece.shape[0]
    scale = 1.0 / (RADIUS * RADIUS)

    def count(n, carry):
        named = piece[n, :, own_len:own_len + LANES]
        counts_v[slot_of(cfg, place, n)] = named.astype(F32)[:cfg.count_rows].astype(jnp.int32)
        return carry

    def prepare(n, carry):
        z = slot_of(cfg, place, n)
        for k in range(own_rows):
            far = piece[n, :, k * block_len:(k + 1) * block_len]
            rhs[z * own_rows + k, :dim, :] = far
            rhs[z * own_rows + k, dim:, :] = augment(far.astype(F32), False).astype(BF16)
        return carry

    lax.fori_loop(0, held, count, 0, unroll=held <= 4)
    fetch = pltpu.make_async_copy(counts_v, counts, copy_sems.at[1])
    fetch.start()
    lax.fori_loop(0, held, prepare, 0, unroll=held <= 4)
    acc[...] = jnp.zeros_like(acc)
    if part == 0:
        near_copy.wait()
        for i in range(cfg.block_rows):
            near = near_ref[:, i * block_len:(i + 1) * block_len].astype(F32)
            full = jnp.concatenate([near * (-2.0 * scale), augment(near, True)], axis=0)
            lhs[i] = full.T.astype(BF16)
    direct_copy.wait()
    fetch.wait()

    pos = jnp.int32(0)
    for i in range(cfg.block_rows):
        me = row * cfg.block_rows + i
        spots = [k * nb + me for k in range(own_rows)]
        spots = [(lax.shift_right_logical(p, 7), p & (LANES - 1)) for p in spots]

        def note(z, at, i=i, me=me, spots=spots):
            for k in range(own_rows):
                name = row_of(cfg, place, part, z) * cfg.block_rows + col * own_rows + k
                m = direct[i, name] + jnp.where(name == me, 0, counts[z, spots[k][0], spots[k][1]])
                listed[0, at + 1] = i * CODE + z * own_rows + k
                mlist[at] = m
                at = at + jnp.where(m > 0, 1, 0)
            return at

        if held <= 4:
            for z in range(held):
                pos = note(z, pos)
        else:
            pos = lax.fori_loop(0, held, note, pos, unroll=4)
    for u in range(GROUP):
        listed[0, pos + u + 1] = 0
        mlist[pos + u] = 0
    total = lax.shift_right_logical(pos + (GROUP - 1), GROUP_BITS)
    listed[0, 0] = total
    list_copy = pltpu.make_async_copy(listed, list_v, copy_sems.at[2])
    list_copy.start()

    def copy_out(g):
        slot = lax.rem(g, RING)
        return pltpu.make_async_copy(kbuf.at[slot], k_mat.at[g], sems.at[slot])

    base = part * cfg.part_groups

    def distances(e, slot):
        code = listed[0, e + 1]
        i, j = lax.shift_right_logical(code, CODE_BITS), code & (CODE - 1)
        dist[slot] = jnp.dot(lhs[i], rhs[j], preferred_element_type=F32)

    distances(0, 0)

    def step(g, carry):
        slot, target = (base + g, k_mat) if cfg.resident else (lax.rem(g, RING), kbuf)
        if not cfg.resident:

            @pl.when(g >= RING)
            def _():
                copy_out(g - RING).wait()

        for u in range(GROUP):
            distances(g * GROUP + u + 1, (u + 1) % 2)
            j = listed[0, g * GROUP + u + 1] & (CODE - 1)
            m = mlist[g * GROUP + u].astype(F32)
            sums = jnp.zeros((8, block_len), F32)
            for s in range(block_len // STRIP):
                rows = slice(s * STRIP, (s + 1) * STRIP)
                d = jnp.maximum(dist[u % 2, rows, :], TINY)
                sc = d * lax.rsqrt(d)
                rem = jnp.maximum(1.0 - sc, 0.0)
                sq = rem * rem
                val = (sq * sq) * (sc * (4.0 * m) + m)
                target[slot, u, rows, :] = val.astype(BF16)
                for h in range(0, STRIP, 8):
                    sums = sums + val[h:h + 8]
            acc[j] += sums
        if not cfg.resident:
            copy_out(g).start()
        return carry

    lax.fori_loop(0, total, step, 0)
    if cfg.parts == 1 or not last:
        deg_ref[...] = jnp.sum(acc[...], axis=1)
    else:
        second = jnp.sum(acc[...], axis=1)
        for z in range(held):
            rows = slice(z * own_rows, (z + 1) * own_rows)
            for p, deg in enumerate((first_deg[rows, :], second[rows])):
                at = row_of(cfg, place, p, z) * own_rows
                for k in range(own_rows):
                    deg_ref[pl.ds(at + k, 1), :] = deg[k:k + 1]

    def drain(g, carry):
        copy_out(g).wait()
        return carry

    if not cfg.resident:
        lax.fori_loop(jnp.maximum(total - RING, 0), total, drain, 0)
    list_copy.wait()


def pieces_of(own, got):
    return own.at[0], got.at[0], own.at[1], got.at[1]


def walk(cfg, part, listed, k_mat, kbuf, sems, product, total_ref, by_row):
    total = listed[0, 0]
    base = part * cfg.part_groups

    def copy_in(g):
        slot = lax.rem(g, RING)
        return pltpu.make_async_copy(k_mat.at[g], kbuf.at[slot], sems.at[slot])

    if not cfg.resident:
        for p in range(RING - 1):

            @pl.when(p < total)
            def _(p=p):
                copy_in(p).start()

    def step(g, carry):
        slot, source = (base + g, k_mat) if cfg.resident else (lax.rem(g, RING), kbuf)
        if not cfg.resident:

            @pl.when(g + (RING - 1) < total)
            def _():
                copy_in(g + (RING - 1)).start()

            copy_in(g).wait()
        codes = [listed[0, g * GROUP + u + 1] for u in range(GROUP)]
        pairs = [(lax.shift_right_logical(code, CODE_BITS), code & (CODE - 1)) for code in codes]
        terms = [product(i, j, source[slot, u]) for u, (i, j) in enumerate(pairs)]
        add(carry)
        return [i if by_row else j for i, j in pairs], terms

    def add(carry):
        for at, term in zip(*carry):
            total_ref[at] += term

    none = [jnp.int32(0)] * GROUP, [jnp.zeros(total_ref.shape[1:], F32)] * GROUP
    add(lax.fori_loop(0, total, step, none))


def first_kernel(cfg, k_mat, *refs):
    n = cfg.parts
    lists, pieces, inv_ref, refs = refs[:n], refs[n:2 * n], refs[2 * n], refs[2 * n + 1:]
    near, near_y, cross, own_inv, z_acc, w_all, listed, list_sems, *ring = refs
    kbuf, sems = ring or (None, None)
    place = position()
    col = place[1]
    copies = [
        pltpu.make_async_copy(lists[p], listed.at[p], list_sems.at[p]) for p in range(n)
    ]
    for copy in copies:
        copy.start()
    own_rows, block_len = cfg.own_rows, cfg.block_len
    z_acc[...] = jnp.zeros_like(z_acc)
    for part, piece in enumerate(pieces):
        held = piece.shape[0]

        def prepare(m, carry, part=part, piece=piece):
            z = slot_of(cfg, place, m)
            for k in range(own_rows):
                w = piece[m, :, k * block_len:(k + 1) * block_len]
                at = row_of(cfg, place, part, z) * own_rows + k
                w_all[z * own_rows + k] = (w * inv_ref[pl.ds(at, 1), :]).astype(BF16)
            return carry

        lax.fori_loop(0, held, prepare, 0, unroll=held <= 4)

        def product(i, j, block):
            return lax.dot_general(
                w_all[j], block, (((1,), (1,)), ((), ())), preferred_element_type=F32
            )

        copies[part].wait()
        walk(cfg, part, listed.at[part], k_mat, kbuf, sems, product, z_acc, True)
    for k in range(own_rows):
        cols = slice(k * block_len, (k + 1) * block_len)
        mine = inv_ref[pl.ds(place[0] * own_rows + k, 1), :]
        own_inv[:, cols] = jnp.broadcast_to(mine, (8, block_len))
        for e, ref in enumerate((near, cross.at[0], near_y, cross.at[1])):
            ref[:, cols] = z_acc[(col ^ e) * own_rows + k]


def terms_of(v, n):
    out = []
    for _ in range(n):
        out.append(v.astype(BF16))
        v = v - out[-1].astype(F32)
    return out


def part_kernel(near, near_y, got, tail, send, lo_ref, hi_ref):
    outputs = near.shape[0]
    hi = (near_y[...] + got[1]).astype(BF16)
    lo = terms_of(near[...] + got[0], 2)
    for n, v in enumerate((hi, *lo)):
        send[n * outputs:(n + 1) * outputs, :] = v
    hi_ref[...] = hi.astype(F32)
    lo_ref[...] = lo[0].astype(F32) + lo[1].astype(F32)
    line = lax.broadcasted_iota(jnp.int32, (16, tail.shape[1]), 0)
    rows = jnp.zeros(line.shape, F32)
    for n, v in enumerate(terms_of(tail[0:1, :], 3)):
        rows = jnp.where(line == n, v.astype(F32), rows)
    send[3 * outputs:, :] = rows.astype(BF16)


def join_kernel(lo_ref, hi_ref, tail, far, t_ref, s1_ref, g_ref):
    outputs = lo_ref.shape[0]
    far_hi, far_a, far_b = (far[n * outputs:(n + 1) * outputs, :].astype(F32) for n in range(3))
    rows = far[3 * outputs:, :].astype(F32)
    far_inv = (rows[0:1] + rows[1:2]) + rows[2:3]
    inv = tail[0:1, :]
    s1 = (lo_ref[...] + far_hi) * inv
    s1_ref[0, :outputs, :] = s1
    s1_ref[0, outputs:, :] = tail[...]
    s1_ref[1, :outputs, :] = ((far_a + far_b) + hi_ref[...]) * far_inv
    s1_ref[1, outputs:, :] = jnp.broadcast_to(far_inv, tail.shape)
    g_ref[...] = ((s1 - SHIFT * t_ref[...]) * inv).astype(BF16)


def second_kernel(cfg, part, k_mat, list_v, t_ref, s1_own, s1_got, out, z_acc, w_all, listed, list_sem, *ring):
    kbuf, sems = ring or (None, None)
    place = position()
    own_rows, block_len = cfg.own_rows, cfg.block_len
    outputs = t_ref.shape[0]
    list_copy = pltpu.make_async_copy(list_v, listed, list_sem)
    list_copy.start()
    for e, packed in enumerate(pieces_of(s1_own, s1_got)):
        share = place[1] ^ e
        for k in range(own_rows):
            cols = slice(k * block_len, (k + 1) * block_len)
            i = share * own_rows + k
            t = t_ref[:, pl.ds(pl.multiple_of(i * block_len, LANES), block_len)]
            g = (packed[:outputs, cols] - SHIFT * t) * packed[outputs:outputs + 1, cols]
            w_all[i] = g.astype(BF16)
    z_acc[...] = jnp.zeros_like(z_acc)

    def product(i, j, block):
        return jnp.dot(w_all[i], block, preferred_element_type=F32)

    list_copy.wait()
    walk(cfg, part, listed, k_mat, kbuf, sems, product, z_acc, False)

    def hand_out(m, carry):
        z = slot_of(cfg, place, m)
        for k in range(own_rows):
            out[m, :, k * block_len:(k + 1) * block_len] = z_acc[z * own_rows + k].astype(out.dtype)
        return carry

    held = out.shape[0]
    lax.fori_loop(0, held, hand_out, 0, unroll=held <= 4)


N_DOTS = 5


def meet_kernel(cfg, z_same, z_other, t_same, inv_ref, s1_own, *refs):
    g_near, g_far, own_z, own_dots, *outs = refs
    gs = g_near[0], g_near[1], g_far[0], g_far[1]
    own_rows, block_len = cfg.own_rows, cfg.block_len
    outputs, own_len = own_z.shape
    place = position()
    tz = jnp.zeros((outputs, 1), F32)
    gz = jnp.zeros((outputs, 1), F32)
    for n in range(4):
        z = z_same[n] + z_other[n].astype(F32)
        if n == 0:
            own_z[...] = z
        else:
            outs[n - 1][:, :own_len] = z.astype(BF16)
        gz += jnp.sum(gs[n].astype(F32) * z, axis=1, keepdims=True)
        at = row_of(cfg, place, 0, slot_of(cfg, place, n)) * own_rows
        for k in range(own_rows):
            cols = slice(k * block_len, (k + 1) * block_len)
            scaled = t_same[n, :, cols] * inv_ref[pl.ds(at + k, 1), :]
            tz += jnp.sum(scaled * z[:, cols], axis=1, keepdims=True)
    t, s1 = t_same[0], s1_own[0, :outputs, :]
    tt = jnp.sum(t * t, axis=1, keepdims=True)
    ts1 = jnp.sum(t * s1, axis=1, keepdims=True)
    s1s1 = jnp.sum(s1 * s1, axis=1, keepdims=True)
    dots = (tt, ts1, s1s1, tz + SHIFT * ts1, gz + SHIFT * (tz + s1s1))
    lane = lax.broadcasted_iota(jnp.int32, (outputs, LANES), 1)
    tile = jnp.zeros(lane.shape, F32)
    for n, v in enumerate(dots):
        for part in range(3):
            head = v.astype(BF16).astype(F32)
            tile = jnp.where(lane == part * N_DOTS + n, head, tile)
            v = v - head
    own_dots[...] = tile.astype(BF16)
    for out in outs:
        out[:, own_len:] = tile.astype(BF16)


def product_kernel(own_z, own_dots, s1_own, *refs):
    got, end_ref, dot_ref = refs[2::-1], refs[3], refs[4]
    outputs, own_len = own_z.shape
    z = own_z[...]
    for ref in got:
        z = z + ref[:, :own_len].astype(F32)
    end_ref[:, :own_len] = z * s1_own[0, outputs:outputs + 1, :]
    tiles = [own_dots[...]] + [ref[:, own_len:] for ref in got]
    total = pair_sum([tile.astype(F32) for tile in tiles])
    out = total
    for part in range(1, 3):
        out = out + pltpu.roll(total, LANES - part * N_DOTS, 1)
    dot_ref[...] = out
    end_ref[:, own_len:] = out


def final_kernel(t_ref, s1_own, s1_got, *refs):
    ends = pieces_of(refs[0], refs[1])
    sol_hbm, res_hbm, sol_ref, res_ref, sems = refs[2:]
    s1s = pieces_of(s1_own, s1_got)
    outputs, own_len = ends[0].shape[0], ends[0].shape[1] - LANES
    place = position()
    dots = ends[0][:, own_len:] + ends[1][:, own_len:]
    tt, ts1, s1s1, ts2, s1s2 = (dots[:, n:n + 1] for n in range(5))
    a1 = tt / (REG * tt + ts1)
    p = 1.0 - REG * a1
    new = p * p * tt - 2.0 * p * a1 * ts1 + a1 * a1 * s1s1
    u = p + new / tt
    dd = u * u * tt - 2.0 * u * a1 * ts1 + a1 * a1 * s1s1
    dmd = u * u * ts1 - u * a1 * (s1s1 + ts2) + a1 * a1 * s1s2
    a2 = new / (REG * dd + dmd)
    sol_t, sol_1 = a1 + a2 * u, a2 * a1
    res_t, res_1 = p - a2 * REG * u, a1 + a2 * (u - REG * a1)
    copies = []
    for e in range(4):
        at = pl.ds(pl.multiple_of((place[1] ^ e) * own_len, LANES), own_len)
        t, s1 = t_ref[:, at], s1s[e][:outputs, :]
        s2 = ends[e][:, :own_len] + SHIFT * s1
        sol_ref[e] = sol_t * t - sol_1 * s1
        res_ref[e] = res_t * t - res_1 * s1 + sol_1 * s2
        for n, (ref, hbm) in enumerate(((sol_ref, sol_hbm), (res_ref, res_hbm))):
            copy = pltpu.make_async_copy(ref.at[e], hbm.at[:, at], sems.at[n, e])
            copy.start()
            copies.append(copy)
    for copy in copies:
        copy.wait()


def swap(x, axis, d):
    size = lax.axis_size(axis)
    return lax.ppermute(x, axis, [(i, i ^ d) for i in range(size)])


def both_swap(x, row_d, col_d):
    n_rows, n_cols = lax.axis_size("rows"), lax.axis_size("cols")
    pairs = [
        (r * n_cols + c, (r ^ row_d) * n_cols + (c ^ col_d))
        for r in range(n_rows)
        for c in range(n_cols)
    ]
    return lax.ppermute(x, ("rows", "cols"), pairs)


def along_z(x):
    return [x] + [swap(x, "rows", d) for d in range(2, lax.axis_size("rows"), 2)]


def across_x(same):
    return [same, swap(same, "rows", 1)]


def direct_cols(x):
    return [x] + [swap(x, "cols", e) for e in range(1, 4)]


def local(block_list, points, targets):
    n_rows = lax.axis_size("rows")
    n_cols = lax.axis_size("cols")
    row = lax.axis_index("rows")
    col = lax.axis_index("cols")
    block_rows, slots = block_list.shape
    dim, npoints = points.shape
    outputs = targets.shape[0]
    block_len = npoints // block_rows
    own_rows = block_rows // n_cols
    own_len = own_rows * block_len
    nb = block_rows * n_rows
    n_sub = own_rows * n_rows
    capacity = -(-block_rows * slots // n_rows)
    direct_rows = n_rows <= DIRECT_ROWS
    parts = 2 if direct_rows else 1
    n_part = n_sub // parts
    bound = min(block_rows * n_part, n_cols * capacity * (n_rows + 1))
    n_groups = -(-bound // GROUP)
    list_len = -(-(n_groups * GROUP + GROUP + 1) // LANES) * LANES
    resident = parts * 2 * n_groups * GROUP * block_len * block_len <= RESIDENT_BYTES
    k_shape = (parts * n_groups, GROUP, block_len, block_len)
    limit = pltpu.CompilerParams(vmem_limit_bytes=(8 if resident else 32) * 1024 * 1024)
    ring = [] if resident else [
        pltpu.VMEM((RING, GROUP, block_len, block_len), BF16),
        pltpu.SemaphoreType.DMA((RING,)),
    ]
    k_spec = VMEM if resident else HBM
    cfg = Sizes(
        parts, n_groups, resident, nb, block_len, own_rows, block_rows, -(-own_rows * nb // LANES)
    )

    def shape(*dims, dtype=F32):
        return jax.ShapeDtypeStruct(dims, dtype)

    def own(x):
        return lax.dynamic_slice_in_dim(x, col * own_len, own_len, 1)

    def total_rows(x):
        if direct_rows:
            near = pair_sum([x] + [swap(x, "rows", d) for d in range(1, 4)])
            return near + swap(near, "rows", 4)
        return lax.psum(x, "rows")

    lists = direct_cols(block_list)
    names = jnp.arange(nb, dtype=jnp.int32)
    direct = sum(jnp.sum((x[:, :, None] == names).astype(jnp.int32), axis=1) for x in lists)
    own_counts = lax.dynamic_slice_in_dim(direct, col * own_rows, own_rows, 0)
    coded = own_counts.reshape(-1)
    coded = jnp.pad(coded, (0, dim * LANES - coded.shape[0])).reshape(dim, LANES).astype(BF16)
    packed = jnp.concatenate([own(points), coded], axis=1)
    own_t = own(targets)

    def build(part, *operands):
        first, last = part == 0, part == parts - 1
        out = [
            pltpu.VMEM(k_shape, BF16) if resident else shape(*k_shape, dtype=BF16),
            shape(1, list_len, dtype=jnp.int32),
            shape(n_sub if last else n_part, block_len),
        ]
        out += [shape(block_rows, block_len, 2 * dim, dtype=BF16)] if first else []
        k_mat, *rest = pl.pallas_call(
            functools.partial(build_kernel, cfg, part),
            out_shape=out,
            in_specs=[VMEM] + ([HBM, VMEM] if first else [VMEM] * 3 + [k_spec]),
            out_specs=[k_spec] + [VMEM] * (len(out) - 1),
            scratch_shapes=([
                pltpu.VMEM((dim, npoints), BF16),
                pltpu.SemaphoreType.DMA,
            ] if first else []) + [
                pltpu.SMEM((1, list_len), jnp.int32),
                pltpu.SMEM((list_len,), jnp.int32),
                pltpu.VMEM((n_part, 8, block_len), F32),
                pltpu.VMEM((n_part, 2 * dim, block_len), BF16),
                pltpu.VMEM((2, block_len, block_len), F32),
                pltpu.SMEM((block_rows, nb), jnp.int32),
                pltpu.VMEM((n_part // own_rows, cfg.count_rows, LANES), jnp.int32),
                pltpu.SMEM((n_part // own_rows, cfg.count_rows, LANES), jnp.int32),
                pltpu.SemaphoreType.DMA((3,)),
                *ring,
            ],
            compiler_params=limit,
            input_output_aliases={} if first else {4: 0},
            cost_estimate=pl.CostEstimate(
                flops=10 * 2 * 2 * dim * bound * block_len * block_len,
                bytes_accessed=10 * 2 * bound * block_len * block_len,
                transcendentals=10 * bound * block_len * block_len,
            ),
            name="build",
        )(direct, *operands)
        if resident:
            k_mat = pltpu.with_memory_space_constraint(k_mat, pltpu.VMEM)
        return k_mat, *rest

    near = pltpu.with_memory_space_constraint(points, pltpu.HBM)
    if direct_rows:
        packed, early_t = lax.optimization_barrier((packed, own_t))
        same, other = across_x(jnp.stack(along_z(packed)))
        t_same = along_z(early_t)
        k_mat, list0, degree, lhs = build(0, near, same)
        degree, other, *t_same = lax.optimization_barrier((degree, other, *t_same))
        t_same, t_other = across_x(jnp.stack(t_same))
        other, t_same = lax.optimization_barrier((other, t_same))
        k_mat, list1, degree = build(1, lhs, degree, other, k_mat)
        t_pieces, k_lists = [t_same, t_other], [list0, list1]
    else:
        k_mat, list0, degree, _ = build(0, near, lax.all_gather(packed, "rows"))
        t_pieces, k_lists = [lax.all_gather(own_t, "rows")], [list0]
    inv = 1.0 / jnp.sqrt(1.0 + total_rows(degree))

    def cost(n):
        return pl.CostEstimate(
            flops=2 * n * bound * outputs * block_len * block_len,
            bytes_accessed=n * bound * block_len * block_len,
            transcendentals=0,
        )

    near_z, near_y, cross_z, tail = pl.pallas_call(
        functools.partial(first_kernel, cfg),
        out_shape=[shape(outputs, own_len)] * 2 + [shape(2, outputs, own_len), shape(8, own_len)],
        in_specs=[k_spec] + [VMEM] * (2 * parts + 1),
        out_specs=[VMEM] * 4,
        scratch_shapes=[
            pltpu.VMEM((block_rows, outputs, block_len), F32),
            pltpu.VMEM((n_part, outputs, block_len), BF16),
            pltpu.SMEM((parts, 1, list_len), jnp.int32),
            pltpu.SemaphoreType.DMA((parts,)),
            *ring,
        ],
        compiler_params=limit,
        cost_estimate=cost(parts),
        name="first",
    )(k_mat, *k_lists, *t_pieces, inv)

    got = swap(cross_z, "cols", 1)
    send, lo, hi = pl.pallas_call(
        part_kernel,
        out_shape=[shape(3 * outputs + 16, own_len, dtype=BF16)] + [shape(outputs, own_len)] * 2,
        in_specs=[VMEM] * 4,
        out_specs=[VMEM] * 3,
        compiler_params=limit,
        name="part",
    )(near_z, near_y, got, tail)
    s1_own, g = pl.pallas_call(
        join_kernel,
        out_shape=(shape(2, outputs + 8, own_len), shape(outputs, own_len, dtype=BF16)),
        in_specs=[VMEM] * 5,
        out_specs=(VMEM, VMEM),
        compiler_params=limit,
        name="join",
    )(lo, hi, tail, swap(send, "cols", 2), own_t)
    s1_got = swap(s1_own, "cols", 1)
    held_t = pltpu.with_memory_space_constraint(targets, pltpu.VMEM)

    def second(part, dtype):
        return pl.pallas_call(
            functools.partial(second_kernel, cfg, part),
            out_shape=shape(n_part // own_rows, outputs, own_len, dtype=dtype),
            in_specs=[k_spec] + [VMEM] * 4,
            out_specs=VMEM,
            scratch_shapes=[
                pltpu.VMEM((n_part, outputs, block_len), F32),
                pltpu.VMEM((block_rows, outputs, block_len), BF16),
                pltpu.SMEM((1, list_len), jnp.int32),
                pltpu.SemaphoreType.DMA,
                *ring,
            ],
            compiler_params=limit,
            cost_estimate=cost(1),
            name="second",
        )(k_mat, k_lists[part], held_t, s1_own, s1_got)

    if direct_rows:
        parts_of_g = (g, swap(g, "rows", 2))
        z2_other = second(1, BF16)
        _, *parts_of_g = lax.optimization_barrier((z2_other, *parts_of_g))
        g = jnp.stack(parts_of_g)
        z2_other = swap(z2_other, "rows", 1)
        far_g = swap(g, "rows", 4)
        z2_same = second(0, F32)
        z2_same, z2_other, far_g = lax.optimization_barrier((z2_same, z2_other, far_g))
        row_piece = shape(outputs, own_len + LANES, dtype=BF16)
        own_z, own_dots, *sends = pl.pallas_call(
            functools.partial(meet_kernel, cfg),
            out_shape=[shape(outputs, own_len), shape(outputs, LANES, dtype=BF16)] + [row_piece] * 3,
            in_specs=[VMEM] * 7,
            out_specs=[VMEM] * 5,
            compiler_params=limit,
            name="meet",
        )(z2_same, z2_other, t_pieces[0], inv, s1_own, g, far_g)
        got = [swap(sends[n], "rows", 2 * n + 2) for n in (2, 1, 0)]
        ends, dots = pl.pallas_call(
            product_kernel,
            out_shape=(shape(outputs, own_len + LANES), shape(outputs, LANES)),
            in_specs=[VMEM] * 6,
            out_specs=(VMEM, VMEM),
            compiler_params=limit,
            name="products",
        )(own_z, own_dots, s1_own, *got)
        far = both_swap(dots, 1, 2)
        across = swap(dots, "rows", 1)
        ends_y = swap(ends, "cols", 2)
        dots = (dots + across) + (ends_y[:, own_len:] + far)
    else:
        z2 = lax.psum_scatter(second(0, F32), "rows", scatter_dimension=0)
        grown = z2 * tail[:1]
        own_s1 = s1_own[0, :outputs]
        s2 = grown + SHIFT * own_s1
        dots = [(own_t, own_t), (own_t, own_s1), (own_s1, own_s1), (own_t, s2), (own_s1, s2)]
        dots = jnp.stack([jnp.sum(x * y, axis=1) for x, y in dots], axis=1)
        dots = lax.psum(jnp.pad(dots, ((0, 0), (0, LANES - N_DOTS))), "rows")
        ends = jnp.concatenate([grown, dots], axis=1)
        ends_y = swap(ends, "cols", 2)
        dots = dots + ends_y[:, own_len:]
    ends = jnp.stack([jnp.concatenate([ends[:, :own_len], dots], axis=1), ends_y])
    ends = (s1_own, s1_got, ends, swap(ends, "cols", 1))
    ends = [pltpu.with_memory_space_constraint(x, pltpu.VMEM) for x in ends]

    return pl.pallas_call(
        final_kernel,
        out_shape=(shape(outputs, npoints), shape(outputs, npoints)),
        in_specs=[VMEM] * 5,
        out_specs=(HBM, HBM),
        scratch_shapes=[
            pltpu.VMEM((4, outputs, own_len), F32),
            pltpu.VMEM((4, outputs, own_len), F32),
            pltpu.SemaphoreType.DMA((2, 4)),
        ],
        compiler_params=limit,
        name="final",
    )(held_t, *ends)


def solution(mesh):
    placed = (P("rows", "cols"), P(None, "rows"), P(None, "rows"))
    return jax.shard_map(
        local,
        mesh=mesh,
        in_specs=placed,
        out_specs=(P(None, "rows"), P(None, "rows")),
        check_vma=False,
    )
```

```python
import functools
from typing import NamedTuple

import jax
import jax.numpy as jnp
from jax import lax
from jax.experimental import pallas as pl
from jax.experimental.pallas import tpu as pltpu
from jax.sharding import PartitionSpec as P

REG = 1.5
RADIUS = 0.25
GROUP_BITS = 2
GROUP = 1 << GROUP_BITS
CODE_BITS = 12
CODE = 1 << CODE_BITS
RING = 3
STRIP = 128
LANES = 128
TINY = 1e-30
SHIFT = 0.375
DIRECT_ROWS = 8
RESIDENT_BYTES = 20 * 1024 * 1024

VMEM = pl.BlockSpec(memory_space=pltpu.VMEM)
HBM = pl.BlockSpec(memory_space=pltpu.HBM)
F32 = jnp.float32
BF16 = jnp.bfloat16


def pair_sum(parts):
    while len(parts) > 1:
        parts = [a + b for a, b in zip(parts[::2], parts[1::2])]
    return parts[0]


def position():
    return lax.axis_index("rows"), lax.axis_index("cols")


class Sizes(NamedTuple):
    parts: int
    part_groups: int
    resident: bool
    nb: int
    block_len: int
    own_rows: int
    block_rows: int
    count_rows: int


def augment(x, first_ones):
    dim, n = x.shape
    norm = jnp.sum(x * x, axis=0, keepdims=True) / (RADIUS * RADIUS)
    high = norm.astype(BF16).astype(F32)
    rest = norm - high
    mid = rest.astype(BF16).astype(F32)
    low = rest - mid
    line = lax.broadcasted_iota(jnp.int32, (dim, n), 0)
    base = 3 if first_ones else 0
    ones_at = 0 if first_ones else 3
    tail = jnp.where((line >= ones_at) & (line < ones_at + 3), 1.0, 0.0)
    tail = jnp.where(line == base, high, tail)
    tail = jnp.where(line == base + 1, mid, tail)
    tail = jnp.where(line == base + 2, low, tail)
    return tail


def row_of(cfg, place, part, z):
    if cfg.parts == 1:
        return z
    return 2 * z + (place[0] & 1 if part == 0 else 1 - (place[0] & 1))


def slot_of(cfg, place, n):
    return n if cfg.parts == 1 else lax.shift_right_logical(place[0], 1) ^ n


def build_kernel(cfg, part, direct_v, *refs):
    last = part == cfg.parts - 1
    place = position()
    if part == 0:
        near_hbm, piece, refs = refs[0], refs[1], refs[2:]
        k_mat, list_v, deg_ref, lhs = refs[:4]
        near_ref, near_sem, refs = refs[4], refs[5], refs[6:]
        near_copy = pltpu.make_async_copy(near_hbm, near_ref, near_sem)
        near_copy.start()
    else:
        lhs, first_deg, piece, _ = refs[:4]
        k_mat, list_v, deg_ref = refs[4:7]
        refs = refs[7:]
    listed, mlist, acc, rhs, dist, direct, counts_v, counts, copy_sems = refs[:9]
    kbuf, sems = (None, None) if cfg.resident else refs[9:]
    direct_copy = pltpu.make_async_copy(direct_v, direct, copy_sems.at[0])
    direct_copy.start()
    row, col = place[0], place[1]
    own_rows, block_len, nb = cfg.own_rows, cfg.block_len, cfg.nb
    own_len = own_rows * block_len
    dim, held = piece.shape[1], piece.shape[0]
    scale = 1.0 / (RADIUS * RADIUS)

    def count(n, carry):
        named = piece[n, :, own_len:own_len + LANES]
        counts_v[slot_of(cfg, place, n)] = named.astype(F32)[:cfg.count_rows].astype(jnp.int32)
        return carry

    def prepare(n, carry):
        z = slot_of(cfg, place, n)
        for k in range(own_rows):
            far = piece[n, :, k * block_len:(k + 1) * block_len]
            rhs[z * own_rows + k, :dim, :] = far
            rhs[z * own_rows + k, dim:, :] = augment(far.astype(F32), False).astype(BF16)
        return carry

    lax.fori_loop(0, held, count, 0, unroll=held <= 4)
    fetch = pltpu.make_async_copy(counts_v, counts, copy_sems.at[1])
    fetch.start()
    lax.fori_loop(0, held, prepare, 0, unroll=held <= 4)
    acc[...] = jnp.zeros_like(acc)
    if part == 0:
        near_copy.wait()
        for i in range(cfg.block_rows):
            near = near_ref[:, i * block_len:(i + 1) * block_len].astype(F32)
            full = jnp.concatenate([near * (-2.0 * scale), augment(near, True)], axis=0)
            lhs[i] = full.T.astype(BF16)
    direct_copy.wait()
    fetch.wait()

    pos = jnp.int32(0)
    for i in range(cfg.block_rows):
        me = row * cfg.block_rows + i
        spots = [k * nb + me for k in range(own_rows)]
        spots = [(lax.shift_right_logical(p, 7), p & (LANES - 1)) for p in spots]

        def note(z, at, i=i, me=me, spots=spots):
            for k in range(own_rows):
                name = row_of(cfg, place, part, z) * cfg.block_rows + col * own_rows + k
                m = direct[i, name] + jnp.where(name == me, 0, counts[z, spots[k][0], spots[k][1]])
                listed[0, at + 1] = i * CODE + z * own_rows + k
                mlist[at] = m
                at = at + jnp.where(m > 0, 1, 0)
            return at

        if held <= 4:
            for z in range(held):
                pos = note(z, pos)
        else:
            pos = lax.fori_loop(0, held, note, pos, unroll=4)
    for u in range(GROUP):
        listed[0, pos + u + 1] = 0
        mlist[pos + u] = 0
    total = lax.shift_right_logical(pos + (GROUP - 1), GROUP_BITS)
    listed[0, 0] = total
    list_copy = pltpu.make_async_copy(listed, list_v, copy_sems.at[2])
    list_copy.start()

    def copy_out(g):
        slot = lax.rem(g, RING)
        return pltpu.make_async_copy(kbuf.at[slot], k_mat.at[g], sems.at[slot])

    base = part * cfg.part_groups

    def distances(e, slot):
        code = listed[0, e + 1]
        i, j = lax.shift_right_logical(code, CODE_BITS), code & (CODE - 1)
        dist[slot] = jnp.dot(lhs[i], rhs[j], preferred_element_type=F32)

    distances(0, 0)

    def step(g, carry):
        slot, target = (base + g, k_mat) if cfg.resident else (lax.rem(g, RING), kbuf)
        if not cfg.resident:

            @pl.when(g >= RING)
            def _():
                copy_out(g - RING).wait()

        for u in range(GROUP):
            distances(g * GROUP + u + 1, (u + 1) % 2)
            j = listed[0, g * GROUP + u + 1] & (CODE - 1)
            m = mlist[g * GROUP + u].astype(F32)
            sums = jnp.zeros((8, block_len), F32)
            for s in range(block_len // STRIP):
                rows = slice(s * STRIP, (s + 1) * STRIP)
                d = jnp.maximum(dist[u % 2, rows, :], TINY)
                sc = d * lax.rsqrt(d)
                rem = jnp.maximum(1.0 - sc, 0.0)
                sq = rem * rem
                val = (sq * sq) * (sc * (4.0 * m) + m)
                target[slot, u, rows, :] = val.astype(BF16)
                for h in range(0, STRIP, 8):
                    sums = sums + val[h:h + 8]
            acc[j] += sums
        if not cfg.resident:
            copy_out(g).start()
        return carry

    lax.fori_loop(0, total, step, 0)
    if cfg.parts == 1 or not last:
        deg_ref[...] = jnp.sum(acc[...], axis=1)
    else:
        second = jnp.sum(acc[...], axis=1)
        for z in range(held):
            rows = slice(z * own_rows, (z + 1) * own_rows)
            for p, deg in enumerate((first_deg[rows, :], second[rows])):
                at = row_of(cfg, place, p, z) * own_rows
                for k in range(own_rows):
                    deg_ref[pl.ds(at + k, 1), :] = deg[k:k + 1]

    def drain(g, carry):
        copy_out(g).wait()
        return carry

    if not cfg.resident:
        lax.fori_loop(jnp.maximum(total - RING, 0), total, drain, 0)
    list_copy.wait()


def pieces_of(own, got):
    return own.at[0], got.at[0], own.at[1], got.at[1]


def walk(cfg, part, listed, k_mat, kbuf, sems, product, total_ref, by_row):
    total = listed[0, 0]
    base = part * cfg.part_groups

    def copy_in(g):
        slot = lax.rem(g, RING)
        return pltpu.make_async_copy(k_mat.at[g], kbuf.at[slot], sems.at[slot])

    if not cfg.resident:
        for p in range(RING - 1):

            @pl.when(p < total)
            def _(p=p):
                copy_in(p).start()

    def step(g, carry):
        slot, source = (base + g, k_mat) if cfg.resident else (lax.rem(g, RING), kbuf)
        if not cfg.resident:

            @pl.when(g + (RING - 1) < total)
            def _():
                copy_in(g + (RING - 1)).start()

            copy_in(g).wait()
        codes = [listed[0, g * GROUP + u + 1] for u in range(GROUP)]
        pairs = [(lax.shift_right_logical(code, CODE_BITS), code & (CODE - 1)) for code in codes]
        terms = [product(i, j, source[slot, u]) for u, (i, j) in enumerate(pairs)]
        add(carry)
        return [i if by_row else j for i, j in pairs], terms

    def add(carry):
        for at, term in zip(*carry):
            total_ref[at] += term

    none = [jnp.int32(0)] * GROUP, [jnp.zeros(total_ref.shape[1:], F32)] * GROUP
    add(lax.fori_loop(0, total, step, none))


def first_kernel(cfg, k_mat, *refs):
    n = cfg.parts
    lists, pieces, inv_ref, refs = refs[:n], refs[n:2 * n], refs[2 * n], refs[2 * n + 1:]
    near, near_y, cross, own_inv, z_acc, w_all, listed, list_sems, *ring = refs
    kbuf, sems = ring or (None, None)
    place = position()
    col = place[1]
    copies = [
        pltpu.make_async_copy(lists[p], listed.at[p], list_sems.at[p]) for p in range(n)
    ]
    for copy in copies:
        copy.start()
    own_rows, block_len = cfg.own_rows, cfg.block_len
    z_acc[...] = jnp.zeros_like(z_acc)
    for part, piece in enumerate(pieces):
        held = piece.shape[0]

        def prepare(m, carry, part=part, piece=piece):
            z = slot_of(cfg, place, m)
            for k in range(own_rows):
                w = piece[m, :, k * block_len:(k + 1) * block_len]
                at = row_of(cfg, place, part, z) * own_rows + k
                w_all[z * own_rows + k] = (w * inv_ref[pl.ds(at, 1), :]).astype(BF16)
            return carry

        lax.fori_loop(0, held, prepare, 0, unroll=held <= 4)

        def product(i, j, block):
            return lax.dot_general(
                w_all[j], block, (((1,), (1,)), ((), ())), preferred_element_type=F32
            )

        copies[part].wait()
        walk(cfg, part, listed.at[part], k_mat, kbuf, sems, product, z_acc, True)
    for k in range(own_rows):
        cols = slice(k * block_len, (k + 1) * block_len)
        mine = inv_ref[pl.ds(place[0] * own_rows + k, 1), :]
        own_inv[:, cols] = jnp.broadcast_to(mine, (8, block_len))
        for e, ref in enumerate((near, cross.at[0], near_y, cross.at[1])):
            ref[:, cols] = z_acc[(col ^ e) * own_rows + k]


def terms_of(v, n):
    out = []
    for _ in range(n):
        out.append(v.astype(BF16))
        v = v - out[-1].astype(F32)
    return out


def part_kernel(near, near_y, got, tail, send, lo_ref, hi_ref):
    outputs = near.shape[0]
    hi = (near_y[...] + got[1]).astype(BF16)
    lo = terms_of(near[...] + got[0], 2)
    for n, v in enumerate((hi, *lo)):
        send[n * outputs:(n + 1) * outputs, :] = v
    hi_ref[...] = hi.astype(F32)
    lo_ref[...] = lo[0].astype(F32) + lo[1].astype(F32)
    line = lax.broadcasted_iota(jnp.int32, (16, tail.shape[1]), 0)
    rows = jnp.zeros(line.shape, F32)
    for n, v in enumerate(terms_of(tail[0:1, :], 3)):
        rows = jnp.where(line == n, v.astype(F32), rows)
    send[3 * outputs:, :] = rows.astype(BF16)


def join_kernel(lo_ref, hi_ref, tail, far, t_ref, s1_ref, g_ref):
    outputs = lo_ref.shape[0]
    far_hi, far_a, far_b = (far[n * outputs:(n + 1) * outputs, :].astype(F32) for n in range(3))
    rows = far[3 * outputs:, :].astype(F32)
    far_inv = (rows[0:1] + rows[1:2]) + rows[2:3]
    inv = tail[0:1, :]
    s1 = (lo_ref[...] + far_hi) * inv
    s1_ref[0, :outputs, :] = s1
    s1_ref[0, outputs:, :] = tail[...]
    s1_ref[1, :outputs, :] = ((far_a + far_b) + hi_ref[...]) * far_inv
    s1_ref[1, outputs:, :] = jnp.broadcast_to(far_inv, tail.shape)
    g_ref[...] = ((s1 - SHIFT * t_ref[...]) * inv).astype(BF16)


def second_kernel(cfg, part, k_mat, list_v, t_ref, s1_own, s1_got, out, z_acc, w_all, listed, list_sem, *ring):
    kbuf, sems = ring or (None, None)
    place = position()
    own_rows, block_len = cfg.own_rows, cfg.block_len
    outputs = t_ref.shape[0]
    list_copy = pltpu.make_async_copy(list_v, listed, list_sem)
    list_copy.start()
    for e, packed in enumerate(pieces_of(s1_own, s1_got)):
        share = place[1] ^ e
        for k in range(own_rows):
            cols = slice(k * block_len, (k + 1) * block_len)
            i = share * own_rows + k
            t = t_ref[:, pl.ds(pl.multiple_of(i * block_len, LANES), block_len)]
            g = (packed[:outputs, cols] - SHIFT * t) * packed[outputs:outputs + 1, cols]
            w_all[i] = g.astype(BF16)
    z_acc[...] = jnp.zeros_like(z_acc)

    def product(i, j, block):
        return jnp.dot(w_all[i], block, preferred_element_type=F32)

    list_copy.wait()
    walk(cfg, part, listed, k_mat, kbuf, sems, product, z_acc, False)

    def hand_out(m, carry):
        z = slot_of(cfg, place, m)
        for k in range(own_rows):
            out[m, :, k * block_len:(k + 1) * block_len] = z_acc[z * own_rows + k].astype(out.dtype)
        return carry

    held = out.shape[0]
    lax.fori_loop(0, held, hand_out, 0, unroll=held <= 4)


N_DOTS = 5


def meet_kernel(cfg, z_same, z_other, t_same, inv_ref, s1_own, *refs):
    g_near, g_far, own_z, own_dots, *outs = refs
    gs = g_near[0], g_far[0], g_near[1], g_far[1]
    own_rows, block_len = cfg.own_rows, cfg.block_len
    outputs, own_len = own_z.shape
    place = position()
    tz = jnp.zeros((outputs, 1), F32)
    gz = jnp.zeros((outputs, 1), F32)
    for n in range(4):
        z = z_same[n] + z_other[n].astype(F32)
        if n == 0:
            own_z[...] = z
        else:
            outs[n - 1][:, :own_len] = z.astype(BF16)
        gz += jnp.sum(gs[n].astype(F32) * z, axis=1, keepdims=True)
        at = row_of(cfg, place, 0, slot_of(cfg, place, n)) * own_rows
        for k in range(own_rows):
            cols = slice(k * block_len, (k + 1) * block_len)
            scaled = t_same[n, :, cols] * inv_ref[pl.ds(at + k, 1), :]
            tz += jnp.sum(scaled * z[:, cols], axis=1, keepdims=True)
    t, s1 = t_same[0], s1_own[0, :outputs, :]
    tt = jnp.sum(t * t, axis=1, keepdims=True)
    ts1 = jnp.sum(t * s1, axis=1, keepdims=True)
    s1s1 = jnp.sum(s1 * s1, axis=1, keepdims=True)
    dots = (tt, ts1, s1s1, tz + SHIFT * ts1, gz + SHIFT * (tz + s1s1))
    lane = lax.broadcasted_iota(jnp.int32, (outputs, LANES), 1)
    tile = jnp.zeros(lane.shape, F32)
    for n, v in enumerate(dots):
        for part in range(3):
            head = v.astype(BF16).astype(F32)
            tile = jnp.where(lane == part * N_DOTS + n, head, tile)
            v = v - head
    own_dots[...] = tile.astype(BF16)
    for out in outs:
        out[:, own_len:] = tile.astype(BF16)


def product_kernel(own_z, own_dots, s1_own, *refs):
    got, end_ref, dot_ref = refs[2::-1], refs[3], refs[4]
    outputs, own_len = own_z.shape
    z = own_z[...]
    for ref in got:
        z = z + ref[:, :own_len].astype(F32)
    end_ref[:, :own_len] = z * s1_own[0, outputs:outputs + 1, :]
    tiles = [own_dots[...]] + [ref[:, own_len:] for ref in got]
    total = pair_sum([tile.astype(F32) for tile in tiles])
    out = total
    for part in range(1, 3):
        out = out + pltpu.roll(total, LANES - part * N_DOTS, 1)
    dot_ref[...] = out
    end_ref[:, own_len:] = out


def final_kernel(t_ref, s1_own, s1_got, *refs):
    ends = pieces_of(refs[0], refs[1])
    sol_hbm, res_hbm, sol_ref, res_ref, sems = refs[2:]
    s1s = pieces_of(s1_own, s1_got)
    outputs, own_len = ends[0].shape[0], ends[0].shape[1] - LANES
    place = position()
    dots = ends[0][:, own_len:] + ends[1][:, own_len:]
    tt, ts1, s1s1, ts2, s1s2 = (dots[:, n:n + 1] for n in range(5))
    a1 = tt / (REG * tt + ts1)
    p = 1.0 - REG * a1
    new = p * p * tt - 2.0 * p * a1 * ts1 + a1 * a1 * s1s1
    u = p + new / tt
    dd = u * u * tt - 2.0 * u * a1 * ts1 + a1 * a1 * s1s1
    dmd = u * u * ts1 - u * a1 * (s1s1 + ts2) + a1 * a1 * s1s2
    a2 = new / (REG * dd + dmd)
    sol_t, sol_1 = a1 + a2 * u, a2 * a1
    res_t, res_1 = p - a2 * REG * u, a1 + a2 * (u - REG * a1)
    copies = []
    for e in range(4):
        at = pl.ds(pl.multiple_of((place[1] ^ e) * own_len, LANES), own_len)
        t, s1 = t_ref[:, at], s1s[e][:outputs, :]
        s2 = ends[e][:, :own_len] + SHIFT * s1
        sol_ref[e] = sol_t * t - sol_1 * s1
        res_ref[e] = res_t * t - res_1 * s1 + sol_1 * s2
        for n, (ref, hbm) in enumerate(((sol_ref, sol_hbm), (res_ref, res_hbm))):
            copy = pltpu.make_async_copy(ref.at[e], hbm.at[:, at], sems.at[n, e])
            copy.start()
            copies.append(copy)
    for copy in copies:
        copy.wait()


def swap(x, axis, d):
    size = lax.axis_size(axis)
    return lax.ppermute(x, axis, [(i, i ^ d) for i in range(size)])


def both_swap(x, row_d, col_d):
    n_rows, n_cols = lax.axis_size("rows"), lax.axis_size("cols")
    pairs = [
        (r * n_cols + c, (r ^ row_d) * n_cols + (c ^ col_d))
        for r in range(n_rows)
        for c in range(n_cols)
    ]
    return lax.ppermute(x, ("rows", "cols"), pairs)


def along_z(x):
    return [x] + [swap(x, "rows", d) for d in range(2, lax.axis_size("rows"), 2)]


def across_x(same):
    return [same, swap(same, "rows", 1)]


def direct_cols(x):
    return [x] + [swap(x, "cols", e) for e in range(1, 4)]


def local(block_list, points, targets):
    n_rows = lax.axis_size("rows")
    n_cols = lax.axis_size("cols")
    row = lax.axis_index("rows")
    col = lax.axis_index("cols")
    block_rows, slots = block_list.shape
    dim, npoints = points.shape
    outputs = targets.shape[0]
    block_len = npoints // block_rows
    own_rows = block_rows // n_cols
    own_len = own_rows * block_len
    nb = block_rows * n_rows
    n_sub = own_rows * n_rows
    capacity = -(-block_rows * slots // n_rows)
    direct_rows = n_rows <= DIRECT_ROWS
    parts = 2 if direct_rows else 1
    n_part = n_sub // parts
    bound = min(block_rows * n_part, n_cols * capacity * (n_rows + 1))
    n_groups = -(-bound // GROUP)
    list_len = -(-(n_groups * GROUP + GROUP + 1) // LANES) * LANES
    resident = parts * 2 * n_groups * GROUP * block_len * block_len <= RESIDENT_BYTES
    k_shape = (parts * n_groups, GROUP, block_len, block_len)
    limit = pltpu.CompilerParams(vmem_limit_bytes=(8 if resident else 32) * 1024 * 1024)
    ring = [] if resident else [
        pltpu.VMEM((RING, GROUP, block_len, block_len), BF16),
        pltpu.SemaphoreType.DMA((RING,)),
    ]
    k_spec = VMEM if resident else HBM
    cfg = Sizes(
        parts, n_groups, resident, nb, block_len, own_rows, block_rows, -(-own_rows * nb // LANES)
    )

    def shape(*dims, dtype=F32):
        return jax.ShapeDtypeStruct(dims, dtype)

    def own(x):
        return lax.dynamic_slice_in_dim(x, col * own_len, own_len, 1)

    def total_rows(x):
        if direct_rows:
            near = pair_sum([x] + [swap(x, "rows", d) for d in range(1, 4)])
            return near + swap(near, "rows", 4)
        return lax.psum(x, "rows")

    lists = direct_cols(block_list)
    names = jnp.arange(nb, dtype=jnp.int32)
    direct = sum(jnp.sum((x[:, :, None] == names).astype(jnp.int32), axis=1) for x in lists)
    own_counts = lax.dynamic_slice_in_dim(direct, col * own_rows, own_rows, 0)
    coded = own_counts.reshape(-1)
    coded = jnp.pad(coded, (0, dim * LANES - coded.shape[0])).reshape(dim, LANES).astype(BF16)
    packed = jnp.concatenate([own(points), coded], axis=1)
    own_t = own(targets)

    def build(part, *operands):
        first, last = part == 0, part == parts - 1
        out = [
            pltpu.VMEM(k_shape, BF16) if resident else shape(*k_shape, dtype=BF16),
            shape(1, list_len, dtype=jnp.int32),
            shape(n_sub if last else n_part, block_len),
        ]
        out += [shape(block_rows, block_len, 2 * dim, dtype=BF16)] if first else []
        k_mat, *rest = pl.pallas_call(
            functools.partial(build_kernel, cfg, part),
            out_shape=out,
            in_specs=[VMEM] + ([HBM, VMEM] if first else [VMEM] * 3 + [k_spec]),
            out_specs=[k_spec] + [VMEM] * (len(out) - 1),
            scratch_shapes=([
                pltpu.VMEM((dim, npoints), BF16),
                pltpu.SemaphoreType.DMA,
            ] if first else []) + [
                pltpu.SMEM((1, list_len), jnp.int32),
                pltpu.SMEM((list_len,), jnp.int32),
                pltpu.VMEM((n_part, 8, block_len), F32),
                pltpu.VMEM((n_part, 2 * dim, block_len), BF16),
                pltpu.VMEM((2, block_len, block_len), F32),
                pltpu.SMEM((block_rows, nb), jnp.int32),
                pltpu.VMEM((n_part // own_rows, cfg.count_rows, LANES), jnp.int32),
                pltpu.SMEM((n_part // own_rows, cfg.count_rows, LANES), jnp.int32),
                pltpu.SemaphoreType.DMA((3,)),
                *ring,
            ],
            compiler_params=limit,
            input_output_aliases={} if first else {4: 0},
            cost_estimate=pl.CostEstimate(
                flops=10 * 2 * 2 * dim * bound * block_len * block_len,
                bytes_accessed=10 * 2 * bound * block_len * block_len,
                transcendentals=10 * bound * block_len * block_len,
            ),
            name="build",
        )(direct, *operands)
        if resident:
            k_mat = pltpu.with_memory_space_constraint(k_mat, pltpu.VMEM)
        return k_mat, *rest

    near = pltpu.with_memory_space_constraint(points, pltpu.HBM)
    if direct_rows:
        packed, early_t = lax.optimization_barrier((packed, own_t))
        same, other = across_x(jnp.stack(along_z(packed)))
        t_same = along_z(early_t)
        k_mat, list0, degree, lhs = build(0, near, same)
        degree, other, *t_same = lax.optimization_barrier((degree, other, *t_same))
        t_same, t_other = across_x(jnp.stack(t_same))
        other, t_same = lax.optimization_barrier((other, t_same))
        k_mat, list1, degree = build(1, lhs, degree, other, k_mat)
        t_pieces, k_lists = [t_same, t_other], [list0, list1]
    else:
        k_mat, list0, degree, _ = build(0, near, lax.all_gather(packed, "rows"))
        t_pieces, k_lists = [lax.all_gather(own_t, "rows")], [list0]
    inv = 1.0 / jnp.sqrt(1.0 + total_rows(degree))

    def cost(n):
        return pl.CostEstimate(
            flops=2 * n * bound * outputs * block_len * block_len,
            bytes_accessed=n * bound * block_len * block_len,
            transcendentals=0,
        )

    near_z, near_y, cross_z, tail = pl.pallas_call(
        functools.partial(first_kernel, cfg),
        out_shape=[shape(outputs, own_len)] * 2 + [shape(2, outputs, own_len), shape(8, own_len)],
        in_specs=[k_spec] + [VMEM] * (2 * parts + 1),
        out_specs=[VMEM] * 4,
        scratch_shapes=[
            pltpu.VMEM((block_rows, outputs, block_len), F32),
            pltpu.VMEM((n_part, outputs, block_len), BF16),
            pltpu.SMEM((parts, 1, list_len), jnp.int32),
            pltpu.SemaphoreType.DMA((parts,)),
            *ring,
        ],
        compiler_params=limit,
        cost_estimate=cost(parts),
        name="first",
    )(k_mat, *k_lists, *t_pieces, inv)

    got = swap(cross_z, "cols", 1)
    send, lo, hi = pl.pallas_call(
        part_kernel,
        out_shape=[shape(3 * outputs + 16, own_len, dtype=BF16)] + [shape(outputs, own_len)] * 2,
        in_specs=[VMEM] * 4,
        out_specs=[VMEM] * 3,
        compiler_params=limit,
        name="part",
    )(near_z, near_y, got, tail)
    s1_own, g = pl.pallas_call(
        join_kernel,
        out_shape=(shape(2, outputs + 8, own_len), shape(outputs, own_len, dtype=BF16)),
        in_specs=[VMEM] * 5,
        out_specs=(VMEM, VMEM),
        compiler_params=limit,
        name="join",
    )(lo, hi, tail, swap(send, "cols", 2), own_t)
    s1_got = swap(s1_own, "cols", 1)
    held_t = pltpu.with_memory_space_constraint(targets, pltpu.VMEM)

    def second(part, dtype):
        return pl.pallas_call(
            functools.partial(second_kernel, cfg, part),
            out_shape=shape(n_part // own_rows, outputs, own_len, dtype=dtype),
            in_specs=[k_spec] + [VMEM] * 4,
            out_specs=VMEM,
            scratch_shapes=[
                pltpu.VMEM((n_part, outputs, block_len), F32),
                pltpu.VMEM((block_rows, outputs, block_len), BF16),
                pltpu.SMEM((1, list_len), jnp.int32),
                pltpu.SemaphoreType.DMA,
                *ring,
            ],
            compiler_params=limit,
            cost_estimate=cost(1),
            name="second",
        )(k_mat, k_lists[part], held_t, s1_own, s1_got)

    if direct_rows:
        parts_of_g = (g, swap(g, "rows", 4))
        z2_other = second(1, BF16)
        _, *parts_of_g = lax.optimization_barrier((z2_other, *parts_of_g))
        g = jnp.stack(parts_of_g)
        z2_other = swap(z2_other, "rows", 1)
        far_g = swap(g, "rows", 2)
        z2_same = second(0, F32)
        z2_same, z2_other, far_g = lax.optimization_barrier((z2_same, z2_other, far_g))
        row_piece = shape(outputs, own_len + LANES, dtype=BF16)
        own_z, own_dots, *sends = pl.pallas_call(
            functools.partial(meet_kernel, cfg),
            out_shape=[shape(outputs, own_len), shape(outputs, LANES, dtype=BF16)] + [row_piece] * 3,
            in_specs=[VMEM] * 7,
            out_specs=[VMEM] * 5,
            compiler_params=limit,
            name="meet",
        )(z2_same, z2_other, t_pieces[0], inv, s1_own, g, far_g)
        got = [swap(sends[n], "rows", 2 * n + 2) for n in (2, 1, 0)]
        ends, dots = pl.pallas_call(
            product_kernel,
            out_shape=(shape(outputs, own_len + LANES), shape(outputs, LANES)),
            in_specs=[VMEM] * 6,
            out_specs=(VMEM, VMEM),
            compiler_params=limit,
            name="products",
        )(own_z, own_dots, s1_own, *got)
        far = both_swap(dots, 1, 2)
        across = swap(dots, "rows", 1)
        ends_y = swap(ends, "cols", 2)
        dots = (dots + across) + (ends_y[:, own_len:] + far)
    else:
        z2 = lax.psum_scatter(second(0, F32), "rows", scatter_dimension=0)
        grown = z2 * tail[:1]
        own_s1 = s1_own[0, :outputs]
        s2 = grown + SHIFT * own_s1
        dots = [(own_t, own_t), (own_t, own_s1), (own_s1, own_s1), (own_t, s2), (own_s1, s2)]
        dots = jnp.stack([jnp.sum(x * y, axis=1) for x, y in dots], axis=1)
        dots = lax.psum(jnp.pad(dots, ((0, 0), (0, LANES - N_DOTS))), "rows")
        ends = jnp.concatenate([grown, dots], axis=1)
        ends_y = swap(ends, "cols", 2)
        dots = dots + ends_y[:, own_len:]
    ends = jnp.stack([jnp.concatenate([ends[:, :own_len], dots], axis=1), ends_y])
    ends = (s1_own, s1_got, ends, swap(ends, "cols", 1))
    ends = [pltpu.with_memory_space_constraint(x, pltpu.VMEM) for x in ends]

    return pl.pallas_call(
        final_kernel,
        out_shape=(shape(outputs, npoints), shape(outputs, npoints)),
        in_specs=[VMEM] * 5,
        out_specs=(HBM, HBM),
        scratch_shapes=[
            pltpu.VMEM((4, outputs, own_len), F32),
            pltpu.VMEM((4, outputs, own_len), F32),
            pltpu.SemaphoreType.DMA((2, 4)),
        ],
        compiler_params=limit,
        name="final",
    )(held_t, *ends)


def solution(mesh):
    placed = (P("rows", "cols"), P(None, "rows"), P(None, "rows"))
    return jax.shard_map(
        local,
        mesh=mesh,
        in_specs=placed,
        out_specs=(P(None, "rows"), P(None, "rows")),
        check_vma=False,
    )
```

```python
import functools
from typing import NamedTuple

import jax
import jax.numpy as jnp
from jax import lax
from jax.experimental import pallas as pl
from jax.experimental.pallas import tpu as pltpu
from jax.sharding import PartitionSpec as P

REG = 1.5
RADIUS = 0.25
GROUP_BITS = 1
GROUP = 1 << GROUP_BITS
CODE_BITS = 12
CODE = 1 << CODE_BITS
RING = 3
STRIP = 128
LANES = 128
TINY = 1e-30
SHIFT = 0.375
DIRECT_ROWS = 8
RESIDENT_BYTES = 20 * 1024 * 1024

VMEM = pl.BlockSpec(memory_space=pltpu.VMEM)
HBM = pl.BlockSpec(memory_space=pltpu.HBM)
F32 = jnp.float32
BF16 = jnp.bfloat16


def pair_sum(parts):
    while len(parts) > 1:
        parts = [a + b for a, b in zip(parts[::2], parts[1::2])]
    return parts[0]


def position():
    return lax.axis_index("rows"), lax.axis_index("cols")


class Sizes(NamedTuple):
    parts: int
    part_groups: int
    resident: bool
    nb: int
    block_len: int
    own_rows: int
    block_rows: int
    count_rows: int


def augment(x, first_ones):
    dim, n = x.shape
    norm = jnp.sum(x * x, axis=0, keepdims=True) / (RADIUS * RADIUS)
    high = norm.astype(BF16).astype(F32)
    rest = norm - high
    mid = rest.astype(BF16).astype(F32)
    low = rest - mid
    line = lax.broadcasted_iota(jnp.int32, (dim, n), 0)
    base = 3 if first_ones else 0
    ones_at = 0 if first_ones else 3
    tail = jnp.where((line >= ones_at) & (line < ones_at + 3), 1.0, 0.0)
    tail = jnp.where(line == base, high, tail)
    tail = jnp.where(line == base + 1, mid, tail)
    tail = jnp.where(line == base + 2, low, tail)
    return tail


def row_of(cfg, place, part, z):
    if cfg.parts == 1:
        return z
    return 2 * z + (place[0] & 1 if part == 0 else 1 - (place[0] & 1))


def slot_of(cfg, place, n):
    return n if cfg.parts == 1 else lax.shift_right_logical(place[0], 1) ^ n


def build_kernel(cfg, part, direct_v, *refs):
    last = part == cfg.parts - 1
    place = position()
    if part == 0:
        near_hbm, piece, refs = refs[0], refs[1], refs[2:]
        k_mat, list_v, deg_ref, lhs = refs[:4]
        near_ref, near_sem, refs = refs[4], refs[5], refs[6:]
        near_copy = pltpu.make_async_copy(near_hbm, near_ref, near_sem)
        near_copy.start()
    else:
        lhs, first_deg, piece, _ = refs[:4]
        k_mat, list_v, deg_ref = refs[4:7]
        refs = refs[7:]
    listed, mlist, acc, rhs, dist, direct, counts_v, counts, copy_sems = refs[:9]
    kbuf, sems = (None, None) if cfg.resident else refs[9:]
    direct_copy = pltpu.make_async_copy(direct_v, direct, copy_sems.at[0])
    direct_copy.start()
    row, col = place[0], place[1]
    own_rows, block_len, nb = cfg.own_rows, cfg.block_len, cfg.nb
    own_len = own_rows * block_len
    dim, held = piece.shape[1], piece.shape[0]
    scale = 1.0 / (RADIUS * RADIUS)

    def count(n, carry):
        named = piece[n, :, own_len:own_len + LANES]
        counts_v[slot_of(cfg, place, n)] = named.astype(F32)[:cfg.count_rows].astype(jnp.int32)
        return carry

    def prepare(n, carry):
        z = slot_of(cfg, place, n)
        for k in range(own_rows):
            far = piece[n, :, k * block_len:(k + 1) * block_len]
            rhs[z * own_rows + k, :dim, :] = far
            rhs[z * own_rows + k, dim:, :] = augment(far.astype(F32), False).astype(BF16)
        return carry

    lax.fori_loop(0, held, count, 0, unroll=held <= 4)
    fetch = pltpu.make_async_copy(counts_v, counts, copy_sems.at[1])
    fetch.start()
    lax.fori_loop(0, held, prepare, 0, unroll=held <= 4)
    acc[...] = jnp.zeros_like(acc)
    if part == 0:
        near_copy.wait()
        for i in range(cfg.block_rows):
            near = near_ref[:, i * block_len:(i + 1) * block_len].astype(F32)
            full = jnp.concatenate([near * (-2.0 * scale), augment(near, True)], axis=0)
            lhs[i] = full.T.astype(BF16)
    direct_copy.wait()
    fetch.wait()

    pos = jnp.int32(0)
    for i in range(cfg.block_rows):
        me = row * cfg.block_rows + i
        spots = [k * nb + me for k in range(own_rows)]
        spots = [(lax.shift_right_logical(p, 7), p & (LANES - 1)) for p in spots]

        def note(z, at, i=i, me=me, spots=spots):
            for k in range(own_rows):
                name = row_of(cfg, place, part, z) * cfg.block_rows + col * own_rows + k
                m = direct[i, name] + jnp.where(name == me, 0, counts[z, spots[k][0], spots[k][1]])
                listed[0, at + 1] = i * CODE + z * own_rows + k
                mlist[at] = m
                at = at + jnp.where(m > 0, 1, 0)
            return at

        if held <= 4:
            for z in range(held):
                pos = note(z, pos)
        else:
            pos = lax.fori_loop(0, held, note, pos, unroll=4)
    for u in range(GROUP):
        listed[0, pos + u + 1] = 0
        mlist[pos + u] = 0
    total = lax.shift_right_logical(pos + (GROUP - 1), GROUP_BITS)
    listed[0, 0] = total
    list_copy = pltpu.make_async_copy(listed, list_v, copy_sems.at[2])
    list_copy.start()

    def copy_out(g):
        slot = lax.rem(g, RING)
        return pltpu.make_async_copy(kbuf.at[slot], k_mat.at[g], sems.at[slot])

    base = part * cfg.part_groups

    def distances(e, slot):
        code = listed[0, e + 1]
        i, j = lax.shift_right_logical(code, CODE_BITS), code & (CODE - 1)
        dist[slot] = jnp.dot(lhs[i], rhs[j], preferred_element_type=F32)

    distances(0, 0)

    def step(g, carry):
        slot, target = (base + g, k_mat) if cfg.resident else (lax.rem(g, RING), kbuf)
        if not cfg.resident:

            @pl.when(g >= RING)
            def _():
                copy_out(g - RING).wait()

        for u in range(GROUP):
            distances(g * GROUP + u + 1, (u + 1) % 2)
            j = listed[0, g * GROUP + u + 1] & (CODE - 1)
            m = mlist[g * GROUP + u].astype(F32)
            sums = jnp.zeros((8, block_len), F32)
            for s in range(block_len // STRIP):
                rows = slice(s * STRIP, (s + 1) * STRIP)
                d = jnp.maximum(dist[u % 2, rows, :], TINY)
                sc = d * lax.rsqrt(d)
                rem = jnp.maximum(1.0 - sc, 0.0)
                sq = rem * rem
                val = (sq * sq) * (sc * (4.0 * m) + m)
                target[slot, u, rows, :] = val.astype(BF16)
                for h in range(0, STRIP, 8):
                    sums = sums + val[h:h + 8]
            acc[j] += sums
        if not cfg.resident:
            copy_out(g).start()
        return carry

    lax.fori_loop(0, total, step, 0)
    if cfg.parts == 1 or not last:
        deg_ref[...] = jnp.sum(acc[...], axis=1)
    else:
        second = jnp.sum(acc[...], axis=1)
        for z in range(held):
            rows = slice(z * own_rows, (z + 1) * own_rows)
            for p, deg in enumerate((first_deg[rows, :], second[rows])):
                at = row_of(cfg, place, p, z) * own_rows
                for k in range(own_rows):
                    deg_ref[pl.ds(at + k, 1), :] = deg[k:k + 1]

    def drain(g, carry):
        copy_out(g).wait()
        return carry

    if not cfg.resident:
        lax.fori_loop(jnp.maximum(total - RING, 0), total, drain, 0)
    list_copy.wait()


def pieces_of(own, got):
    return own.at[0], got.at[0], own.at[1], got.at[1]


def walk(cfg, part, listed, k_mat, kbuf, sems, product, total_ref, by_row):
    total = listed[0, 0]
    base = part * cfg.part_groups

    def copy_in(g):
        slot = lax.rem(g, RING)
        return pltpu.make_async_copy(k_mat.at[g], kbuf.at[slot], sems.at[slot])

    if not cfg.resident:
        for p in range(RING - 1):

            @pl.when(p < total)
            def _(p=p):
                copy_in(p).start()

    def step(g, carry):
        slot, source = (base + g, k_mat) if cfg.resident else (lax.rem(g, RING), kbuf)
        if not cfg.resident:

            @pl.when(g + (RING - 1) < total)
            def _():
                copy_in(g + (RING - 1)).start()

            copy_in(g).wait()
        codes = [listed[0, g * GROUP + u + 1] for u in range(GROUP)]
        pairs = [(lax.shift_right_logical(code, CODE_BITS), code & (CODE - 1)) for code in codes]
        terms = [product(i, j, source[slot, u]) for u, (i, j) in enumerate(pairs)]
        add(carry)
        return [i if by_row else j for i, j in pairs], terms

    def add(carry):
        for at, term in zip(*carry):
            total_ref[at] += term

    none = [jnp.int32(0)] * GROUP, [jnp.zeros(total_ref.shape[1:], F32)] * GROUP
    add(lax.fori_loop(0, total, step, none))


def first_kernel(cfg, k_mat, *refs):
    n = cfg.parts
    lists, pieces, inv_ref, refs = refs[:n], refs[n:2 * n], refs[2 * n], refs[2 * n + 1:]
    near, near_y, cross, own_inv, z_acc, w_all, listed, list_sems, *ring = refs
    kbuf, sems = ring or (None, None)
    place = position()
    col = place[1]
    copies = [
        pltpu.make_async_copy(lists[p], listed.at[p], list_sems.at[p]) for p in range(n)
    ]
    for copy in copies:
        copy.start()
    own_rows, block_len = cfg.own_rows, cfg.block_len
    z_acc[...] = jnp.zeros_like(z_acc)
    for part, piece in enumerate(pieces):
        held = piece.shape[0]

        def prepare(m, carry, part=part, piece=piece):
            z = slot_of(cfg, place, m)
            for k in range(own_rows):
                w = piece[m, :, k * block_len:(k + 1) * block_len]
                at = row_of(cfg, place, part, z) * own_rows + k
                w_all[z * own_rows + k] = (w * inv_ref[pl.ds(at, 1), :]).astype(BF16)
            return carry

        lax.fori_loop(0, held, prepare, 0, unroll=held <= 4)

        def product(i, j, block):
            return lax.dot_general(
                w_all[j], block, (((1,), (1,)), ((), ())), preferred_element_type=F32
            )

        copies[part].wait()
        walk(cfg, part, listed.at[part], k_mat, kbuf, sems, product, z_acc, True)
    for k in range(own_rows):
        cols = slice(k * block_len, (k + 1) * block_len)
        mine = inv_ref[pl.ds(place[0] * own_rows + k, 1), :]
        own_inv[:, cols] = jnp.broadcast_to(mine, (8, block_len))
        for e, ref in enumerate((near, cross.at[0], near_y, cross.at[1])):
            ref[:, cols] = z_acc[(col ^ e) * own_rows + k]


def terms_of(v, n):
    out = []
    for _ in range(n):
        out.append(v.astype(BF16))
        v = v - out[-1].astype(F32)
    return out


def part_kernel(near, near_y, got, tail, send, lo_ref, hi_ref):
    outputs = near.shape[0]
    hi = (near_y[...] + got[1]).astype(BF16)
    lo = terms_of(near[...] + got[0], 2)
    for n, v in enumerate((hi, *lo)):
        send[n * outputs:(n + 1) * outputs, :] = v
    hi_ref[...] = hi.astype(F32)
    lo_ref[...] = lo[0].astype(F32) + lo[1].astype(F32)
    line = lax.broadcasted_iota(jnp.int32, (16, tail.shape[1]), 0)
    rows = jnp.zeros(line.shape, F32)
    for n, v in enumerate(terms_of(tail[0:1, :], 3)):
        rows = jnp.where(line == n, v.astype(F32), rows)
    send[3 * outputs:, :] = rows.astype(BF16)


def join_kernel(lo_ref, hi_ref, tail, far, t_ref, s1_ref, g_ref):
    outputs = lo_ref.shape[0]
    far_hi, far_a, far_b = (far[n * outputs:(n + 1) * outputs, :].astype(F32) for n in range(3))
    rows = far[3 * outputs:, :].astype(F32)
    far_inv = (rows[0:1] + rows[1:2]) + rows[2:3]
    inv = tail[0:1, :]
    s1 = (lo_ref[...] + far_hi) * inv
    s1_ref[0, :outputs, :] = s1
    s1_ref[0, outputs:, :] = tail[...]
    s1_ref[1, :outputs, :] = ((far_a + far_b) + hi_ref[...]) * far_inv
    s1_ref[1, outputs:, :] = jnp.broadcast_to(far_inv, tail.shape)
    g_ref[...] = ((s1 - SHIFT * t_ref[...]) * inv).astype(BF16)


def second_kernel(cfg, part, k_mat, list_v, t_ref, s1_own, s1_got, out, z_acc, w_all, listed, list_sem, *ring):
    kbuf, sems = ring or (None, None)
    place = position()
    own_rows, block_len = cfg.own_rows, cfg.block_len
    outputs = t_ref.shape[0]
    list_copy = pltpu.make_async_copy(list_v, listed, list_sem)
    list_copy.start()
    for e, packed in enumerate(pieces_of(s1_own, s1_got)):
        share = place[1] ^ e
        for k in range(own_rows):
            cols = slice(k * block_len, (k + 1) * block_len)
            i = share * own_rows + k
            t = t_ref[:, pl.ds(pl.multiple_of(i * block_len, LANES), block_len)]
            g = (packed[:outputs, cols] - SHIFT * t) * packed[outputs:outputs + 1, cols]
            w_all[i] = g.astype(BF16)
    z_acc[...] = jnp.zeros_like(z_acc)

    def product(i, j, block):
        return jnp.dot(w_all[i], block, preferred_element_type=F32)

    list_copy.wait()
    walk(cfg, part, listed, k_mat, kbuf, sems, product, z_acc, False)

    def hand_out(m, carry):
        z = slot_of(cfg, place, m)
        for k in range(own_rows):
            out[m, :, k * block_len:(k + 1) * block_len] = z_acc[z * own_rows + k].astype(out.dtype)
        return carry

    held = out.shape[0]
    lax.fori_loop(0, held, hand_out, 0, unroll=held <= 4)


N_DOTS = 5


def meet_kernel(cfg, z_same, z_other, t_same, inv_ref, s1_own, *refs):
    g_near, g_far, own_z, own_dots, *outs = refs
    gs = g_near[0], g_far[0], g_near[1], g_far[1]
    own_rows, block_len = cfg.own_rows, cfg.block_len
    outputs, own_len = own_z.shape
    place = position()
    tz = jnp.zeros((outputs, 1), F32)
    gz = jnp.zeros((outputs, 1), F32)
    for n in range(4):
        z = z_same[n] + z_other[n].astype(F32)
        if n == 0:
            own_z[...] = z
        else:
            outs[n - 1][:, :own_len] = z.astype(BF16)
        gz += jnp.sum(gs[n].astype(F32) * z, axis=1, keepdims=True)
        at = row_of(cfg, place, 0, slot_of(cfg, place, n)) * own_rows
        for k in range(own_rows):
            cols = slice(k * block_len, (k + 1) * block_len)
            scaled = t_same[n, :, cols] * inv_ref[pl.ds(at + k, 1), :]
            tz += jnp.sum(scaled * z[:, cols], axis=1, keepdims=True)
    t, s1 = t_same[0], s1_own[0, :outputs, :]
    tt = jnp.sum(t * t, axis=1, keepdims=True)
    ts1 = jnp.sum(t * s1, axis=1, keepdims=True)
    s1s1 = jnp.sum(s1 * s1, axis=1, keepdims=True)
    dots = (tt, ts1, s1s1, tz + SHIFT * ts1, gz + SHIFT * (tz + s1s1))
    lane = lax.broadcasted_iota(jnp.int32, (outputs, LANES), 1)
    tile = jnp.zeros(lane.shape, F32)
    for n, v in enumerate(dots):
        for part in range(3):
            head = v.astype(BF16).astype(F32)
            tile = jnp.where(lane == part * N_DOTS + n, head, tile)
            v = v - head
    own_dots[...] = tile.astype(BF16)
    for out in outs:
        out[:, own_len:] = tile.astype(BF16)


def product_kernel(own_z, own_dots, s1_own, *refs):
    got, end_ref, dot_ref = refs[2::-1], refs[3], refs[4]
    outputs, own_len = own_z.shape
    z = own_z[...]
    for ref in got:
        z = z + ref[:, :own_len].astype(F32)
    end_ref[:, :own_len] = z * s1_own[0, outputs:outputs + 1, :]
    tiles = [own_dots[...]] + [ref[:, own_len:] for ref in got]
    total = pair_sum([tile.astype(F32) for tile in tiles])
    out = total
    for part in range(1, 3):
        out = out + pltpu.roll(total, LANES - part * N_DOTS, 1)
    dot_ref[...] = out
    end_ref[:, own_len:] = out


def final_kernel(t_ref, s1_own, s1_got, *refs):
    ends = pieces_of(refs[0], refs[1])
    sol_hbm, res_hbm, sol_ref, res_ref, sems = refs[2:]
    s1s = pieces_of(s1_own, s1_got)
    outputs, own_len = ends[0].shape[0], ends[0].shape[1] - LANES
    place = position()
    dots = ends[0][:, own_len:] + ends[1][:, own_len:]
    tt, ts1, s1s1, ts2, s1s2 = (dots[:, n:n + 1] for n in range(5))
    a1 = tt / (REG * tt + ts1)
    p = 1.0 - REG * a1
    new = p * p * tt - 2.0 * p * a1 * ts1 + a1 * a1 * s1s1
    u = p + new / tt
    dd = u * u * tt - 2.0 * u * a1 * ts1 + a1 * a1 * s1s1
    dmd = u * u * ts1 - u * a1 * (s1s1 + ts2) + a1 * a1 * s1s2
    a2 = new / (REG * dd + dmd)
    sol_t, sol_1 = a1 + a2 * u, a2 * a1
    res_t, res_1 = p - a2 * REG * u, a1 + a2 * (u - REG * a1)
    copies = []
    for e in range(4):
        at = pl.ds(pl.multiple_of((place[1] ^ e) * own_len, LANES), own_len)
        t, s1 = t_ref[:, at], s1s[e][:outputs, :]
        s2 = ends[e][:, :own_len] + SHIFT * s1
        sol_ref[e] = sol_t * t - sol_1 * s1
        res_ref[e] = res_t * t - res_1 * s1 + sol_1 * s2
        for n, (ref, hbm) in enumerate(((sol_ref, sol_hbm), (res_ref, res_hbm))):
            copy = pltpu.make_async_copy(ref.at[e], hbm.at[:, at], sems.at[n, e])
            copy.start()
            copies.append(copy)
    for copy in copies:
        copy.wait()


def swap(x, axis, d):
    size = lax.axis_size(axis)
    return lax.ppermute(x, axis, [(i, i ^ d) for i in range(size)])


def both_swap(x, row_d, col_d):
    n_rows, n_cols = lax.axis_size("rows"), lax.axis_size("cols")
    pairs = [
        (r * n_cols + c, (r ^ row_d) * n_cols + (c ^ col_d))
        for r in range(n_rows)
        for c in range(n_cols)
    ]
    return lax.ppermute(x, ("rows", "cols"), pairs)


def along_z(x):
    return [x] + [swap(x, "rows", d) for d in range(2, lax.axis_size("rows"), 2)]


def across_x(same):
    return [same, swap(same, "rows", 1)]


def direct_cols(x):
    return [x] + [swap(x, "cols", e) for e in range(1, 4)]


def local(block_list, points, targets):
    n_rows = lax.axis_size("rows")
    n_cols = lax.axis_size("cols")
    row = lax.axis_index("rows")
    col = lax.axis_index("cols")
    block_rows, slots = block_list.shape
    dim, npoints = points.shape
    outputs = targets.shape[0]
    block_len = npoints // block_rows
    own_rows = block_rows // n_cols
    own_len = own_rows * block_len
    nb = block_rows * n_rows
    n_sub = own_rows * n_rows
    capacity = -(-block_rows * slots // n_rows)
    direct_rows = n_rows <= DIRECT_ROWS
    parts = 2 if direct_rows else 1
    n_part = n_sub // parts
    bound = min(block_rows * n_part, n_cols * capacity * (n_rows + 1))
    n_groups = -(-bound // GROUP)
    list_len = -(-(n_groups * GROUP + GROUP + 1) // LANES) * LANES
    resident = parts * 2 * n_groups * GROUP * block_len * block_len <= RESIDENT_BYTES
    k_shape = (parts * n_groups, GROUP, block_len, block_len)
    limit = pltpu.CompilerParams(vmem_limit_bytes=(8 if resident else 32) * 1024 * 1024)
    ring = [] if resident else [
        pltpu.VMEM((RING, GROUP, block_len, block_len), BF16),
        pltpu.SemaphoreType.DMA((RING,)),
    ]
    k_spec = VMEM if resident else HBM
    cfg = Sizes(
        parts, n_groups, resident, nb, block_len, own_rows, block_rows, -(-own_rows * nb // LANES)
    )

    def shape(*dims, dtype=F32):
        return jax.ShapeDtypeStruct(dims, dtype)

    def own(x):
        return lax.dynamic_slice_in_dim(x, col * own_len, own_len, 1)

    def total_rows(x):
        if direct_rows:
            near = pair_sum([x] + [swap(x, "rows", d) for d in range(1, 4)])
            return near + swap(near, "rows", 4)
        return lax.psum(x, "rows")

    lists = direct_cols(block_list)
    names = jnp.arange(nb, dtype=jnp.int32)
    direct = sum(jnp.sum((x[:, :, None] == names).astype(jnp.int32), axis=1) for x in lists)
    own_counts = lax.dynamic_slice_in_dim(direct, col * own_rows, own_rows, 0)
    coded = own_counts.reshape(-1)
    coded = jnp.pad(coded, (0, dim * LANES - coded.shape[0])).reshape(dim, LANES).astype(BF16)
    packed = jnp.concatenate([own(points), coded], axis=1)
    own_t = own(targets)

    def build(part, *operands):
        first, last = part == 0, part == parts - 1
        out = [
            pltpu.VMEM(k_shape, BF16) if resident else shape(*k_shape, dtype=BF16),
            shape(1, list_len, dtype=jnp.int32),
            shape(n_sub if last else n_part, block_len),
        ]
        out += [shape(block_rows, block_len, 2 * dim, dtype=BF16)] if first else []
        k_mat, *rest = pl.pallas_call(
            functools.partial(build_kernel, cfg, part),
            out_shape=out,
            in_specs=[VMEM] + ([HBM, VMEM] if first else [VMEM] * 3 + [k_spec]),
            out_specs=[k_spec] + [VMEM] * (len(out) - 1),
            scratch_shapes=([
                pltpu.VMEM((dim, npoints), BF16),
                pltpu.SemaphoreType.DMA,
            ] if first else []) + [
                pltpu.SMEM((1, list_len), jnp.int32),
                pltpu.SMEM((list_len,), jnp.int32),
                pltpu.VMEM((n_part, 8, block_len), F32),
                pltpu.VMEM((n_part, 2 * dim, block_len), BF16),
                pltpu.VMEM((2, block_len, block_len), F32),
                pltpu.SMEM((block_rows, nb), jnp.int32),
                pltpu.VMEM((n_part // own_rows, cfg.count_rows, LANES), jnp.int32),
                pltpu.SMEM((n_part // own_rows, cfg.count_rows, LANES), jnp.int32),
                pltpu.SemaphoreType.DMA((3,)),
                *ring,
            ],
            compiler_params=limit,
            input_output_aliases={} if first else {4: 0},
            cost_estimate=pl.CostEstimate(
                flops=10 * 2 * 2 * dim * bound * block_len * block_len,
                bytes_accessed=10 * 2 * bound * block_len * block_len,
                transcendentals=10 * bound * block_len * block_len,
            ),
            name="build",
        )(direct, *operands)
        if resident:
            k_mat = pltpu.with_memory_space_constraint(k_mat, pltpu.VMEM)
        return k_mat, *rest

    near = pltpu.with_memory_space_constraint(points, pltpu.HBM)
    if direct_rows:
        packed, early_t = lax.optimization_barrier((packed, own_t))
        same, other = across_x(jnp.stack(along_z(packed)))
        t_same = along_z(early_t)
        k_mat, list0, degree, lhs = build(0, near, same)
        degree, other, *t_same = lax.optimization_barrier((degree, other, *t_same))
        t_same, t_other = across_x(jnp.stack(t_same))
        other, t_same = lax.optimization_barrier((other, t_same))
        k_mat, list1, degree = build(1, lhs, degree, other, k_mat)
        t_pieces, k_lists = [t_same, t_other], [list0, list1]
    else:
        k_mat, list0, degree, _ = build(0, near, lax.all_gather(packed, "rows"))
        t_pieces, k_lists = [lax.all_gather(own_t, "rows")], [list0]
    inv = 1.0 / jnp.sqrt(1.0 + total_rows(degree))

    def cost(n):
        return pl.CostEstimate(
            flops=2 * n * bound * outputs * block_len * block_len,
            bytes_accessed=n * bound * block_len * block_len,
            transcendentals=0,
        )

    near_z, near_y, cross_z, tail = pl.pallas_call(
        functools.partial(first_kernel, cfg),
        out_shape=[shape(outputs, own_len)] * 2 + [shape(2, outputs, own_len), shape(8, own_len)],
        in_specs=[k_spec] + [VMEM] * (2 * parts + 1),
        out_specs=[VMEM] * 4,
        scratch_shapes=[
            pltpu.VMEM((block_rows, outputs, block_len), F32),
            pltpu.VMEM((n_part, outputs, block_len), BF16),
            pltpu.SMEM((parts, 1, list_len), jnp.int32),
            pltpu.SemaphoreType.DMA((parts,)),
            *ring,
        ],
        compiler_params=limit,
        cost_estimate=cost(parts),
        name="first",
    )(k_mat, *k_lists, *t_pieces, inv)

    got = swap(cross_z, "cols", 1)
    send, lo, hi = pl.pallas_call(
        part_kernel,
        out_shape=[shape(3 * outputs + 16, own_len, dtype=BF16)] + [shape(outputs, own_len)] * 2,
        in_specs=[VMEM] * 4,
        out_specs=[VMEM] * 3,
        compiler_params=limit,
        name="part",
    )(near_z, near_y, got, tail)
    s1_own, g = pl.pallas_call(
        join_kernel,
        out_shape=(shape(2, outputs + 8, own_len), shape(outputs, own_len, dtype=BF16)),
        in_specs=[VMEM] * 5,
        out_specs=(VMEM, VMEM),
        compiler_params=limit,
        name="join",
    )(lo, hi, tail, swap(send, "cols", 2), own_t)
    s1_got = swap(s1_own, "cols", 1)
    held_t = pltpu.with_memory_space_constraint(targets, pltpu.VMEM)

    def second(part, dtype):
        return pl.pallas_call(
            functools.partial(second_kernel, cfg, part),
            out_shape=shape(n_part // own_rows, outputs, own_len, dtype=dtype),
            in_specs=[k_spec] + [VMEM] * 4,
            out_specs=VMEM,
            scratch_shapes=[
                pltpu.VMEM((n_part, outputs, block_len), F32),
                pltpu.VMEM((block_rows, outputs, block_len), BF16),
                pltpu.SMEM((1, list_len), jnp.int32),
                pltpu.SemaphoreType.DMA,
                *ring,
            ],
            compiler_params=limit,
            cost_estimate=cost(1),
            name="second",
        )(k_mat, k_lists[part], held_t, s1_own, s1_got)

    if direct_rows:
        parts_of_g = (g, swap(g, "rows", 4))
        z2_other = second(1, BF16)
        _, *parts_of_g = lax.optimization_barrier((z2_other, *parts_of_g))
        g = jnp.stack(parts_of_g)
        z2_other = swap(z2_other, "rows", 1)
        far_g = swap(g, "rows", 2)
        z2_same = second(0, F32)
        z2_same, z2_other, far_g = lax.optimization_barrier((z2_same, z2_other, far_g))
        row_piece = shape(outputs, own_len + LANES, dtype=BF16)
        own_z, own_dots, *sends = pl.pallas_call(
            functools.partial(meet_kernel, cfg),
            out_shape=[shape(outputs, own_len), shape(outputs, LANES, dtype=BF16)] + [row_piece] * 3,
            in_specs=[VMEM] * 7,
            out_specs=[VMEM] * 5,
            compiler_params=limit,
            name="meet",
        )(z2_same, z2_other, t_pieces[0], inv, s1_own, g, far_g)
        got = [swap(sends[n], "rows", 2 * n + 2) for n in (2, 1, 0)]
        ends, dots = pl.pallas_call(
            product_kernel,
            out_shape=(shape(outputs, own_len + LANES), shape(outputs, LANES)),
            in_specs=[VMEM] * 6,
            out_specs=(VMEM, VMEM),
            compiler_params=limit,
            name="products",
        )(own_z, own_dots, s1_own, *got)
        far = both_swap(dots, 1, 2)
        across = swap(dots, "rows", 1)
        ends_y = swap(ends, "cols", 2)
        dots = (dots + across) + (ends_y[:, own_len:] + far)
    else:
        z2 = lax.psum_scatter(second(0, F32), "rows", scatter_dimension=0)
        grown = z2 * tail[:1]
        own_s1 = s1_own[0, :outputs]
        s2 = grown + SHIFT * own_s1
        dots = [(own_t, own_t), (own_t, own_s1), (own_s1, own_s1), (own_t, s2), (own_s1, s2)]
        dots = jnp.stack([jnp.sum(x * y, axis=1) for x, y in dots], axis=1)
        dots = lax.psum(jnp.pad(dots, ((0, 0), (0, LANES - N_DOTS))), "rows")
        ends = jnp.concatenate([grown, dots], axis=1)
        ends_y = swap(ends, "cols", 2)
        dots = dots + ends_y[:, own_len:]
    ends = jnp.stack([jnp.concatenate([ends[:, :own_len], dots], axis=1), ends_y])
    ends = (s1_own, s1_got, ends, swap(ends, "cols", 1))
    ends = [pltpu.with_memory_space_constraint(x, pltpu.VMEM) for x in ends]

    return pl.pallas_call(
        final_kernel,
        out_shape=(shape(outputs, npoints), shape(outputs, npoints)),
        in_specs=[VMEM] * 5,
        out_specs=(HBM, HBM),
        scratch_shapes=[
            pltpu.VMEM((4, outputs, own_len), F32),
            pltpu.VMEM((4, outputs, own_len), F32),
            pltpu.SemaphoreType.DMA((2, 4)),
        ],
        compiler_params=limit,
        name="final",
    )(held_t, *ends)


def solution(mesh):
    placed = (P("rows", "cols"), P(None, "rows"), P(None, "rows"))
    return jax.shard_map(
        local,
        mesh=mesh,
        in_specs=placed,
        out_specs=(P(None, "rows"), P(None, "rows")),
        check_vma=False,
    )
```

```python
import functools
from typing import NamedTuple

import jax
import jax.numpy as jnp
from jax import lax
from jax.experimental import pallas as pl
from jax.experimental.pallas import tpu as pltpu
from jax.sharding import PartitionSpec as P

REG = 1.5
RADIUS = 0.25
GROUP_BITS = 3
GROUP = 1 << GROUP_BITS
CODE_BITS = 12
CODE = 1 << CODE_BITS
RING = 3
STRIP = 128
LANES = 128
TINY = 1e-30
SHIFT = 0.375
DIRECT_ROWS = 8
RESIDENT_BYTES = 20 * 1024 * 1024

VMEM = pl.BlockSpec(memory_space=pltpu.VMEM)
HBM = pl.BlockSpec(memory_space=pltpu.HBM)
F32 = jnp.float32
BF16 = jnp.bfloat16


def pair_sum(parts):
    while len(parts) > 1:
        parts = [a + b for a, b in zip(parts[::2], parts[1::2])]
    return parts[0]


def position():
    return lax.axis_index("rows"), lax.axis_index("cols")


class Sizes(NamedTuple):
    parts: int
    part_groups: int
    resident: bool
    nb: int
    block_len: int
    own_rows: int
    block_rows: int
    count_rows: int


def augment(x, first_ones):
    dim, n = x.shape
    norm = jnp.sum(x * x, axis=0, keepdims=True) / (RADIUS * RADIUS)
    high = norm.astype(BF16).astype(F32)
    rest = norm - high
    mid = rest.astype(BF16).astype(F32)
    low = rest - mid
    line = lax.broadcasted_iota(jnp.int32, (dim, n), 0)
    base = 3 if first_ones else 0
    ones_at = 0 if first_ones else 3
    tail = jnp.where((line >= ones_at) & (line < ones_at + 3), 1.0, 0.0)
    tail = jnp.where(line == base, high, tail)
    tail = jnp.where(line == base + 1, mid, tail)
    tail = jnp.where(line == base + 2, low, tail)
    return tail


def row_of(cfg, place, part, z):
    if cfg.parts == 1:
        return z
    return 2 * z + (place[0] & 1 if part == 0 else 1 - (place[0] & 1))


def slot_of(cfg, place, n):
    return n if cfg.parts == 1 else lax.shift_right_logical(place[0], 1) ^ n


def build_kernel(cfg, part, direct_v, *refs):
    last = part == cfg.parts - 1
    place = position()
    if part == 0:
        near_hbm, piece, refs = refs[0], refs[1], refs[2:]
        k_mat, list_v, deg_ref, lhs = refs[:4]
        near_ref, near_sem, refs = refs[4], refs[5], refs[6:]
        near_copy = pltpu.make_async_copy(near_hbm, near_ref, near_sem)
        near_copy.start()
    else:
        lhs, first_deg, piece, _ = refs[:4]
        k_mat, list_v, deg_ref = refs[4:7]
        refs = refs[7:]
    listed, mlist, acc, rhs, dist, direct, counts_v, counts, copy_sems = refs[:9]
    kbuf, sems = (None, None) if cfg.resident else refs[9:]
    direct_copy = pltpu.make_async_copy(direct_v, direct, copy_sems.at[0])
    direct_copy.start()
    row, col = place[0], place[1]
    own_rows, block_len, nb = cfg.own_rows, cfg.block_len, cfg.nb
    own_len = own_rows * block_len
    dim, held = piece.shape[1], piece.shape[0]
    scale = 1.0 / (RADIUS * RADIUS)

    def count(n, carry):
        named = piece[n, :, own_len:own_len + LANES]
        counts_v[slot_of(cfg, place, n)] = named.astype(F32)[:cfg.count_rows].astype(jnp.int32)
        return carry

    def prepare(n, carry):
        z = slot_of(cfg, place, n)
        for k in range(own_rows):
            far = piece[n, :, k * block_len:(k + 1) * block_len]
            rhs[z * own_rows + k, :dim, :] = far
            rhs[z * own_rows + k, dim:, :] = augment(far.astype(F32), False).astype(BF16)
        return carry

    lax.fori_loop(0, held, count, 0, unroll=held <= 4)
    fetch = pltpu.make_async_copy(counts_v, counts, copy_sems.at[1])
    fetch.start()
    lax.fori_loop(0, held, prepare, 0, unroll=held <= 4)
    acc[...] = jnp.zeros_like(acc)
    if part == 0:
        near_copy.wait()
        for i in range(cfg.block_rows):
            near = near_ref[:, i * block_len:(i + 1) * block_len].astype(F32)
            full = jnp.concatenate([near * (-2.0 * scale), augment(near, True)], axis=0)
            lhs[i] = full.T.astype(BF16)
    direct_copy.wait()
    fetch.wait()

    pos = jnp.int32(0)
    for i in range(cfg.block_rows):
        me = row * cfg.block_rows + i
        spots = [k * nb + me for k in range(own_rows)]
        spots = [(lax.shift_right_logical(p, 7), p & (LANES - 1)) for p in spots]

        def note(z, at, i=i, me=me, spots=spots):
            for k in range(own_rows):
                name = row_of(cfg, place, part, z) * cfg.block_rows + col * own_rows + k
                m = direct[i, name] + jnp.where(name == me, 0, counts[z, spots[k][0], spots[k][1]])
                listed[0, at + 1] = i * CODE + z * own_rows + k
                mlist[at] = m
                at = at + jnp.where(m > 0, 1, 0)
            return at

        if held <= 4:
            for z in range(held):
                pos = note(z, pos)
        else:
            pos = lax.fori_loop(0, held, note, pos, unroll=4)
    for u in range(GROUP):
        listed[0, pos + u + 1] = 0
        mlist[pos + u] = 0
    total = lax.shift_right_logical(pos + (GROUP - 1), GROUP_BITS)
    listed[0, 0] = total
    list_copy = pltpu.make_async_copy(listed, list_v, copy_sems.at[2])
    list_copy.start()

    def copy_out(g):
        slot = lax.rem(g, RING)
        return pltpu.make_async_copy(kbuf.at[slot], k_mat.at[g], sems.at[slot])

    base = part * cfg.part_groups

    def distances(e, slot):
        code = listed[0, e + 1]
        i, j = lax.shift_right_logical(code, CODE_BITS), code & (CODE - 1)
        dist[slot] = jnp.dot(lhs[i], rhs[j], preferred_element_type=F32)

    distances(0, 0)

    def step(g, carry):
        slot, target = (base + g, k_mat) if cfg.resident else (lax.rem(g, RING), kbuf)
        if not cfg.resident:

            @pl.when(g >= RING)
            def _():
                copy_out(g - RING).wait()

        for u in range(GROUP):
            distances(g * GROUP + u + 1, (u + 1) % 2)
            j = listed[0, g * GROUP + u + 1] & (CODE - 1)
            m = mlist[g * GROUP + u].astype(F32)
            sums = jnp.zeros((8, block_len), F32)
            for s in range(block_len // STRIP):
                rows = slice(s * STRIP, (s + 1) * STRIP)
                d = jnp.maximum(dist[u % 2, rows, :], TINY)
                sc = d * lax.rsqrt(d)
                rem = jnp.maximum(1.0 - sc, 0.0)
                sq = rem * rem
                val = (sq * sq) * (sc * (4.0 * m) + m)
                target[slot, u, rows, :] = val.astype(BF16)
                for h in range(0, STRIP, 8):
                    sums = sums + val[h:h + 8]
            acc[j] += sums
        if not cfg.resident:
            copy_out(g).start()
        return carry

    lax.fori_loop(0, total, step, 0)
    if cfg.parts == 1 or not last:
        deg_ref[...] = jnp.sum(acc[...], axis=1)
    else:
        second = jnp.sum(acc[...], axis=1)
        for z in range(held):
            rows = slice(z * own_rows, (z + 1) * own_rows)
            for p, deg in enumerate((first_deg[rows, :], second[rows])):
                at = row_of(cfg, place, p, z) * own_rows
                for k in range(own_rows):
                    deg_ref[pl.ds(at + k, 1), :] = deg[k:k + 1]

    def drain(g, carry):
        copy_out(g).wait()
        return carry

    if not cfg.resident:
        lax.fori_loop(jnp.maximum(total - RING, 0), total, drain, 0)
    list_copy.wait()


def pieces_of(own, got):
    return own.at[0], got.at[0], own.at[1], got.at[1]


def walk(cfg, part, listed, k_mat, kbuf, sems, product, total_ref, by_row):
    total = listed[0, 0]
    base = part * cfg.part_groups

    def copy_in(g):
        slot = lax.rem(g, RING)
        return pltpu.make_async_copy(k_mat.at[g], kbuf.at[slot], sems.at[slot])

    if not cfg.resident:
        for p in range(RING - 1):

            @pl.when(p < total)
            def _(p=p):
                copy_in(p).start()

    def step(g, carry):
        slot, source = (base + g, k_mat) if cfg.resident else (lax.rem(g, RING), kbuf)
        if not cfg.resident:

            @pl.when(g + (RING - 1) < total)
            def _():
                copy_in(g + (RING - 1)).start()

            copy_in(g).wait()
        codes = [listed[0, g * GROUP + u + 1] for u in range(GROUP)]
        pairs = [(lax.shift_right_logical(code, CODE_BITS), code & (CODE - 1)) for code in codes]
        terms = [product(i, j, source[slot, u]) for u, (i, j) in enumerate(pairs)]
        add(carry)
        return [i if by_row else j for i, j in pairs], terms

    def add(carry):
        for at, term in zip(*carry):
            total_ref[at] += term

    none = [jnp.int32(0)] * GROUP, [jnp.zeros(total_ref.shape[1:], F32)] * GROUP
    add(lax.fori_loop(0, total, step, none))


def first_kernel(cfg, k_mat, *refs):
    n = cfg.parts
    lists, pieces, inv_ref, refs = refs[:n], refs[n:2 * n], refs[2 * n], refs[2 * n + 1:]
    near, near_y, cross, own_inv, z_acc, w_all, listed, list_sems, *ring = refs
    kbuf, sems = ring or (None, None)
    place = position()
    col = place[1]
    copies = [
        pltpu.make_async_copy(lists[p], listed.at[p], list_sems.at[p]) for p in range(n)
    ]
    for copy in copies:
        copy.start()
    own_rows, block_len = cfg.own_rows, cfg.block_len
    z_acc[...] = jnp.zeros_like(z_acc)
    for part, piece in enumerate(pieces):
        held = piece.shape[0]

        def prepare(m, carry, part=part, piece=piece):
            z = slot_of(cfg, place, m)
            for k in range(own_rows):
                w = piece[m, :, k * block_len:(k + 1) * block_len]
                at = row_of(cfg, place, part, z) * own_rows + k
                w_all[z * own_rows + k] = (w * inv_ref[pl.ds(at, 1), :]).astype(BF16)
            return carry

        lax.fori_loop(0, held, prepare, 0, unroll=held <= 4)

        def product(i, j, block):
            return lax.dot_general(
                w_all[j], block, (((1,), (1,)), ((), ())), preferred_element_type=F32
            )

        copies[part].wait()
        walk(cfg, part, listed.at[part], k_mat, kbuf, sems, product, z_acc, True)
    for k in range(own_rows):
        cols = slice(k * block_len, (k + 1) * block_len)
        mine = inv_ref[pl.ds(place[0] * own_rows + k, 1), :]
        own_inv[:, cols] = jnp.broadcast_to(mine, (8, block_len))
        for e, ref in enumerate((near, cross.at[0], near_y, cross.at[1])):
            ref[:, cols] = z_acc[(col ^ e) * own_rows + k]


def terms_of(v, n):
    out = []
    for _ in range(n):
        out.append(v.astype(BF16))
        v = v - out[-1].astype(F32)
    return out


def part_kernel(near, near_y, got, tail, send, lo_ref, hi_ref):
    outputs = near.shape[0]
    hi = (near_y[...] + got[1]).astype(BF16)
    lo = terms_of(near[...] + got[0], 2)
    for n, v in enumerate((hi, *lo)):
        send[n * outputs:(n + 1) * outputs, :] = v
    hi_ref[...] = hi.astype(F32)
    lo_ref[...] = lo[0].astype(F32) + lo[1].astype(F32)
    line = lax.broadcasted_iota(jnp.int32, (16, tail.shape[1]), 0)
    rows = jnp.zeros(line.shape, F32)
    for n, v in enumerate(terms_of(tail[0:1, :], 3)):
        rows = jnp.where(line == n, v.astype(F32), rows)
    send[3 * outputs:, :] = rows.astype(BF16)


def join_kernel(lo_ref, hi_ref, tail, far, t_ref, s1_ref, g_ref):
    outputs = lo_ref.shape[0]
    far_hi, far_a, far_b = (far[n * outputs:(n + 1) * outputs, :].astype(F32) for n in range(3))
    rows = far[3 * outputs:, :].astype(F32)
    far_inv = (rows[0:1] + rows[1:2]) + rows[2:3]
    inv = tail[0:1, :]
    s1 = (lo_ref[...] + far_hi) * inv
    s1_ref[0, :outputs, :] = s1
    s1_ref[0, outputs:, :] = tail[...]
    s1_ref[1, :outputs, :] = ((far_a + far_b) + hi_ref[...]) * far_inv
    s1_ref[1, outputs:, :] = jnp.broadcast_to(far_inv, tail.shape)
    g_ref[...] = ((s1 - SHIFT * t_ref[...]) * inv).astype(BF16)


def second_kernel(cfg, part, k_mat, list_v, t_ref, s1_own, s1_got, out, z_acc, w_all, listed, list_sem, *ring):
    kbuf, sems = ring or (None, None)
    place = position()
    own_rows, block_len = cfg.own_rows, cfg.block_len
    outputs = t_ref.shape[0]
    list_copy = pltpu.make_async_copy(list_v, listed, list_sem)
    list_copy.start()
    for e, packed in enumerate(pieces_of(s1_own, s1_got)):
        share = place[1] ^ e
        for k in range(own_rows):
            cols = slice(k * block_len, (k + 1) * block_len)
            i = share * own_rows + k
            t = t_ref[:, pl.ds(pl.multiple_of(i * block_len, LANES), block_len)]
            g = (packed[:outputs, cols] - SHIFT * t) * packed[outputs:outputs + 1, cols]
            w_all[i] = g.astype(BF16)
    z_acc[...] = jnp.zeros_like(z_acc)

    def product(i, j, block):
        return jnp.dot(w_all[i], block, preferred_element_type=F32)

    list_copy.wait()
    walk(cfg, part, listed, k_mat, kbuf, sems, product, z_acc, False)

    def hand_out(m, carry):
        z = slot_of(cfg, place, m)
        for k in range(own_rows):
            out[m, :, k * block_len:(k + 1) * block_len] = z_acc[z * own_rows + k].astype(out.dtype)
        return carry

    held = out.shape[0]
    lax.fori_loop(0, held, hand_out, 0, unroll=held <= 4)


N_DOTS = 5


def meet_kernel(cfg, z_same, z_other, t_same, inv_ref, s1_own, *refs):
    g_near, g_far, own_z, own_dots, *outs = refs
    gs = g_near[0], g_far[0], g_near[1], g_far[1]
    own_rows, block_len = cfg.own_rows, cfg.block_len
    outputs, own_len = own_z.shape
    place = position()
    tz = jnp.zeros((outputs, 1), F32)
    gz = jnp.zeros((outputs, 1), F32)
    for n in range(4):
        z = z_same[n] + z_other[n].astype(F32)
        if n == 0:
            own_z[...] = z
        else:
            outs[n - 1][:, :own_len] = z.astype(BF16)
        gz += jnp.sum(gs[n].astype(F32) * z, axis=1, keepdims=True)
        at = row_of(cfg, place, 0, slot_of(cfg, place, n)) * own_rows
        for k in range(own_rows):
            cols = slice(k * block_len, (k + 1) * block_len)
            scaled = t_same[n, :, cols] * inv_ref[pl.ds(at + k, 1), :]
            tz += jnp.sum(scaled * z[:, cols], axis=1, keepdims=True)
    t, s1 = t_same[0], s1_own[0, :outputs, :]
    tt = jnp.sum(t * t, axis=1, keepdims=True)
    ts1 = jnp.sum(t * s1, axis=1, keepdims=True)
    s1s1 = jnp.sum(s1 * s1, axis=1, keepdims=True)
    dots = (tt, ts1, s1s1, tz + SHIFT * ts1, gz + SHIFT * (tz + s1s1))
    lane = lax.broadcasted_iota(jnp.int32, (outputs, LANES), 1)
    tile = jnp.zeros(lane.shape, F32)
    for n, v in enumerate(dots):
        for part in range(3):
            head = v.astype(BF16).astype(F32)
            tile = jnp.where(lane == part * N_DOTS + n, head, tile)
            v = v - head
    own_dots[...] = tile.astype(BF16)
    for out in outs:
        out[:, own_len:] = tile.astype(BF16)


def product_kernel(own_z, own_dots, s1_own, *refs):
    got, end_ref, dot_ref = refs[2::-1], refs[3], refs[4]
    outputs, own_len = own_z.shape
    z = own_z[...]
    for ref in got:
        z = z + ref[:, :own_len].astype(F32)
    end_ref[:, :own_len] = z * s1_own[0, outputs:outputs + 1, :]
    tiles = [own_dots[...]] + [ref[:, own_len:] for ref in got]
    total = pair_sum([tile.astype(F32) for tile in tiles])
    out = total
    for part in range(1, 3):
        out = out + pltpu.roll(total, LANES - part * N_DOTS, 1)
    dot_ref[...] = out
    end_ref[:, own_len:] = out


def final_kernel(t_ref, s1_own, s1_got, *refs):
    ends = pieces_of(refs[0], refs[1])
    sol_hbm, res_hbm, sol_ref, res_ref, sems = refs[2:]
    s1s = pieces_of(s1_own, s1_got)
    outputs, own_len = ends[0].shape[0], ends[0].shape[1] - LANES
    place = position()
    dots = ends[0][:, own_len:] + ends[1][:, own_len:]
    tt, ts1, s1s1, ts2, s1s2 = (dots[:, n:n + 1] for n in range(5))
    a1 = tt / (REG * tt + ts1)
    p = 1.0 - REG * a1
    new = p * p * tt - 2.0 * p * a1 * ts1 + a1 * a1 * s1s1
    u = p + new / tt
    dd = u * u * tt - 2.0 * u * a1 * ts1 + a1 * a1 * s1s1
    dmd = u * u * ts1 - u * a1 * (s1s1 + ts2) + a1 * a1 * s1s2
    a2 = new / (REG * dd + dmd)
    sol_t, sol_1 = a1 + a2 * u, a2 * a1
    res_t, res_1 = p - a2 * REG * u, a1 + a2 * (u - REG * a1)
    copies = []
    for e in range(4):
        at = pl.ds(pl.multiple_of((place[1] ^ e) * own_len, LANES), own_len)
        t, s1 = t_ref[:, at], s1s[e][:outputs, :]
        s2 = ends[e][:, :own_len] + SHIFT * s1
        sol_ref[e] = sol_t * t - sol_1 * s1
        res_ref[e] = res_t * t - res_1 * s1 + sol_1 * s2
        for n, (ref, hbm) in enumerate(((sol_ref, sol_hbm), (res_ref, res_hbm))):
            copy = pltpu.make_async_copy(ref.at[e], hbm.at[:, at], sems.at[n, e])
            copy.start()
            copies.append(copy)
    for copy in copies:
        copy.wait()


def swap(x, axis, d):
    size = lax.axis_size(axis)
    return lax.ppermute(x, axis, [(i, i ^ d) for i in range(size)])


def both_swap(x, row_d, col_d):
    n_rows, n_cols = lax.axis_size("rows"), lax.axis_size("cols")
    pairs = [
        (r * n_cols + c, (r ^ row_d) * n_cols + (c ^ col_d))
        for r in range(n_rows)
        for c in range(n_cols)
    ]
    return lax.ppermute(x, ("rows", "cols"), pairs)


def along_z(x):
    return [x] + [swap(x, "rows", d) for d in range(2, lax.axis_size("rows"), 2)]


def across_x(same):
    return [same, swap(same, "rows", 1)]


def direct_cols(x):
    return [x] + [swap(x, "cols", e) for e in range(1, 4)]


def local(block_list, points, targets):
    n_rows = lax.axis_size("rows")
    n_cols = lax.axis_size("cols")
    row = lax.axis_index("rows")
    col = lax.axis_index("cols")
    block_rows, slots = block_list.shape
    dim, npoints = points.shape
    outputs = targets.shape[0]
    block_len = npoints // block_rows
    own_rows = block_rows // n_cols
    own_len = own_rows * block_len
    nb = block_rows * n_rows
    n_sub = own_rows * n_rows
    capacity = -(-block_rows * slots // n_rows)
    direct_rows = n_rows <= DIRECT_ROWS
    parts = 2 if direct_rows else 1
    n_part = n_sub // parts
    bound = min(block_rows * n_part, n_cols * capacity * (n_rows + 1))
    n_groups = -(-bound // GROUP)
    list_len = -(-(n_groups * GROUP + GROUP + 1) // LANES) * LANES
    resident = parts * 2 * n_groups * GROUP * block_len * block_len <= RESIDENT_BYTES
    k_shape = (parts * n_groups, GROUP, block_len, block_len)
    limit = pltpu.CompilerParams(vmem_limit_bytes=(8 if resident else 32) * 1024 * 1024)
    ring = [] if resident else [
        pltpu.VMEM((RING, GROUP, block_len, block_len), BF16),
        pltpu.SemaphoreType.DMA((RING,)),
    ]
    k_spec = VMEM if resident else HBM
    cfg = Sizes(
        parts, n_groups, resident, nb, block_len, own_rows, block_rows, -(-own_rows * nb // LANES)
    )

    def shape(*dims, dtype=F32):
        return jax.ShapeDtypeStruct(dims, dtype)

    def own(x):
        return lax.dynamic_slice_in_dim(x, col * own_len, own_len, 1)

    def total_rows(x):
        if direct_rows:
            near = pair_sum([x] + [swap(x, "rows", d) for d in range(1, 4)])
            return near + swap(near, "rows", 4)
        return lax.psum(x, "rows")

    lists = direct_cols(block_list)
    names = jnp.arange(nb, dtype=jnp.int32)
    direct = sum(jnp.sum((x[:, :, None] == names).astype(jnp.int32), axis=1) for x in lists)
    own_counts = lax.dynamic_slice_in_dim(direct, col * own_rows, own_rows, 0)
    coded = own_counts.reshape(-1)
    coded = jnp.pad(coded, (0, dim * LANES - coded.shape[0])).reshape(dim, LANES).astype(BF16)
    packed = jnp.concatenate([own(points), coded], axis=1)
    own_t = own(targets)

    def build(part, *operands):
        first, last = part == 0, part == parts - 1
        out = [
            pltpu.VMEM(k_shape, BF16) if resident else shape(*k_shape, dtype=BF16),
            shape(1, list_len, dtype=jnp.int32),
            shape(n_sub if last else n_part, block_len),
        ]
        out += [shape(block_rows, block_len, 2 * dim, dtype=BF16)] if first else []
        k_mat, *rest = pl.pallas_call(
            functools.partial(build_kernel, cfg, part),
            out_shape=out,
            in_specs=[VMEM] + ([HBM, VMEM] if first else [VMEM] * 3 + [k_spec]),
            out_specs=[k_spec] + [VMEM] * (len(out) - 1),
            scratch_shapes=([
                pltpu.VMEM((dim, npoints), BF16),
                pltpu.SemaphoreType.DMA,
            ] if first else []) + [
                pltpu.SMEM((1, list_len), jnp.int32),
                pltpu.SMEM((list_len,), jnp.int32),
                pltpu.VMEM((n_part, 8, block_len), F32),
                pltpu.VMEM((n_part, 2 * dim, block_len), BF16),
                pltpu.VMEM((2, block_len, block_len), F32),
                pltpu.SMEM((block_rows, nb), jnp.int32),
                pltpu.VMEM((n_part // own_rows, cfg.count_rows, LANES), jnp.int32),
                pltpu.SMEM((n_part // own_rows, cfg.count_rows, LANES), jnp.int32),
                pltpu.SemaphoreType.DMA((3,)),
                *ring,
            ],
            compiler_params=limit,
            input_output_aliases={} if first else {4: 0},
            cost_estimate=pl.CostEstimate(
                flops=10 * 2 * 2 * dim * bound * block_len * block_len,
                bytes_accessed=10 * 2 * bound * block_len * block_len,
                transcendentals=10 * bound * block_len * block_len,
            ),
            name="build",
        )(direct, *operands)
        if resident:
            k_mat = pltpu.with_memory_space_constraint(k_mat, pltpu.VMEM)
        return k_mat, *rest

    near = pltpu.with_memory_space_constraint(points, pltpu.HBM)
    if direct_rows:
        packed, early_t = lax.optimization_barrier((packed, own_t))
        same, other = across_x(jnp.stack(along_z(packed)))
        t_same = along_z(early_t)
        k_mat, list0, degree, lhs = build(0, near, same)
        degree, other, *t_same = lax.optimization_barrier((degree, other, *t_same))
        t_same, t_other = across_x(jnp.stack(t_same))
        other, t_same = lax.optimization_barrier((other, t_same))
        k_mat, list1, degree = build(1, lhs, degree, other, k_mat)
        t_pieces, k_lists = [t_same, t_other], [list0, list1]
    else:
        k_mat, list0, degree, _ = build(0, near, lax.all_gather(packed, "rows"))
        t_pieces, k_lists = [lax.all_gather(own_t, "rows")], [list0]
    inv = 1.0 / jnp.sqrt(1.0 + total_rows(degree))

    def cost(n):
        return pl.CostEstimate(
            flops=2 * n * bound * outputs * block_len * block_len,
            bytes_accessed=n * bound * block_len * block_len,
            transcendentals=0,
        )

    near_z, near_y, cross_z, tail = pl.pallas_call(
        functools.partial(first_kernel, cfg),
        out_shape=[shape(outputs, own_len)] * 2 + [shape(2, outputs, own_len), shape(8, own_len)],
        in_specs=[k_spec] + [VMEM] * (2 * parts + 1),
        out_specs=[VMEM] * 4,
        scratch_shapes=[
            pltpu.VMEM((block_rows, outputs, block_len), F32),
            pltpu.VMEM((n_part, outputs, block_len), BF16),
            pltpu.SMEM((parts, 1, list_len), jnp.int32),
            pltpu.SemaphoreType.DMA((parts,)),
            *ring,
        ],
        compiler_params=limit,
        cost_estimate=cost(parts),
        name="first",
    )(k_mat, *k_lists, *t_pieces, inv)

    got = swap(cross_z, "cols", 1)
    send, lo, hi = pl.pallas_call(
        part_kernel,
        out_shape=[shape(3 * outputs + 16, own_len, dtype=BF16)] + [shape(outputs, own_len)] * 2,
        in_specs=[VMEM] * 4,
        out_specs=[VMEM] * 3,
        compiler_params=limit,
        name="part",
    )(near_z, near_y, got, tail)
    s1_own, g = pl.pallas_call(
        join_kernel,
        out_shape=(shape(2, outputs + 8, own_len), shape(outputs, own_len, dtype=BF16)),
        in_specs=[VMEM] * 5,
        out_specs=(VMEM, VMEM),
        compiler_params=limit,
        name="join",
    )(lo, hi, tail, swap(send, "cols", 2), own_t)
    s1_got = swap(s1_own, "cols", 1)
    held_t = pltpu.with_memory_space_constraint(targets, pltpu.VMEM)

    def second(part, dtype):
        return pl.pallas_call(
            functools.partial(second_kernel, cfg, part),
            out_shape=shape(n_part // own_rows, outputs, own_len, dtype=dtype),
            in_specs=[k_spec] + [VMEM] * 4,
            out_specs=VMEM,
            scratch_shapes=[
                pltpu.VMEM((n_part, outputs, block_len), F32),
                pltpu.VMEM((block_rows, outputs, block_len), BF16),
                pltpu.SMEM((1, list_len), jnp.int32),
                pltpu.SemaphoreType.DMA,
                *ring,
            ],
            compiler_params=limit,
            cost_estimate=cost(1),
            name="second",
        )(k_mat, k_lists[part], held_t, s1_own, s1_got)

    if direct_rows:
        parts_of_g = (g, swap(g, "rows", 4))
        z2_other = second(1, BF16)
        _, *parts_of_g = lax.optimization_barrier((z2_other, *parts_of_g))
        g = jnp.stack(parts_of_g)
        z2_other = swap(z2_other, "rows", 1)
        far_g = swap(g, "rows", 2)
        z2_same = second(0, F32)
        z2_same, z2_other, far_g = lax.optimization_barrier((z2_same, z2_other, far_g))
        row_piece = shape(outputs, own_len + LANES, dtype=BF16)
        own_z, own_dots, *sends = pl.pallas_call(
            functools.partial(meet_kernel, cfg),
            out_shape=[shape(outputs, own_len), shape(outputs, LANES, dtype=BF16)] + [row_piece] * 3,
            in_specs=[VMEM] * 7,
            out_specs=[VMEM] * 5,
            compiler_params=limit,
            name="meet",
        )(z2_same, z2_other, t_pieces[0], inv, s1_own, g, far_g)
        got = [swap(sends[n], "rows", 2 * n + 2) for n in (2, 1, 0)]
        ends, dots = pl.pallas_call(
            product_kernel,
            out_shape=(shape(outputs, own_len + LANES), shape(outputs, LANES)),
            in_specs=[VMEM] * 6,
            out_specs=(VMEM, VMEM),
            compiler_params=limit,
            name="products",
        )(own_z, own_dots, s1_own, *got)
        far = both_swap(dots, 1, 2)
        across = swap(dots, "rows", 1)
        ends_y = swap(ends, "cols", 2)
        dots = (dots + across) + (ends_y[:, own_len:] + far)
    else:
        z2 = lax.psum_scatter(second(0, F32), "rows", scatter_dimension=0)
        grown = z2 * tail[:1]
        own_s1 = s1_own[0, :outputs]
        s2 = grown + SHIFT * own_s1
        dots = [(own_t, own_t), (own_t, own_s1), (own_s1, own_s1), (own_t, s2), (own_s1, s2)]
        dots = jnp.stack([jnp.sum(x * y, axis=1) for x, y in dots], axis=1)
        dots = lax.psum(jnp.pad(dots, ((0, 0), (0, LANES - N_DOTS))), "rows")
        ends = jnp.concatenate([grown, dots], axis=1)
        ends_y = swap(ends, "cols", 2)
        dots = dots + ends_y[:, own_len:]
    ends = jnp.stack([jnp.concatenate([ends[:, :own_len], dots], axis=1), ends_y])
    ends = (s1_own, s1_got, ends, swap(ends, "cols", 1))
    ends = [pltpu.with_memory_space_constraint(x, pltpu.VMEM) for x in ends]

    return pl.pallas_call(
        final_kernel,
        out_shape=(shape(outputs, npoints), shape(outputs, npoints)),
        in_specs=[VMEM] * 5,
        out_specs=(HBM, HBM),
        scratch_shapes=[
            pltpu.VMEM((4, outputs, own_len), F32),
            pltpu.VMEM((4, outputs, own_len), F32),
            pltpu.SemaphoreType.DMA((2, 4)),
        ],
        compiler_params=limit,
        name="final",
    )(held_t, *ends)


def solution(mesh):
    placed = (P("rows", "cols"), P(None, "rows"), P(None, "rows"))
    return jax.shard_map(
        local,
        mesh=mesh,
        in_specs=placed,
        out_specs=(P(None, "rows"), P(None, "rows")),
        check_vma=False,
    )
```
